32 devices in a mesh: rows: 8 (over z, x), filt: 4 (over y, core).
Axes of the slice: x: 2, y: 2, z: 4, core: 2. Of those that a mesh axis runs over, the one named last changes fastest.
Arguments:
- features: bfloat16 [96, 48, 2048], P('rows'), may hold values from -6 to 6
- point_weight: bfloat16 [2048, 256], P(None, 'filt'), may hold values from -0.125 to 0.125
- dilated_weight: bfloat16 [3, 3, 3, 2048, 256], P(None, None, None, None, 'filt'), may hold values from -0.046875 to 0.046875
- branch_bias: float32 [4, 256], P(None, 'filt'), may hold values from -3 to 3
- project_weight: bfloat16 [4, 256, 256], replicated, may hold values from -0.1875 to 0.1875
- project_bias: float32 [256], replicated, may hold values from -3 to 3
- cotangent: bfloat16 [96, 48, 256], P('rows'), may hold values from -6 to 6
Outputs:
- head_output: bfloat16 [96, 48, 256], P('rows', None, 'filt')
- feature_grad: bfloat16 [96, 48, 2048], P('rows', None, 'filt')
The draws below stay inside these ranges and needn't reach their ends.
All inputs are finite; a program needn't handle non-finite values.
Results may differ from the reference program's by a relative error of at most 0.035.
The reference program's roundings to bfloat16 on the way count: a program that leaves them out, or rounds other values in their place, can miss the bound.
Values may be sent and summed in bfloat16 or wider, within the bound.
No kernel may reach another device: no remote copies, remote signals or barrier semaphores. Data moves between devices by JAX's collectives and lax.ppermute only.
A program may use at most 128 MiB of HBM per device.

```python
import jax
import jax.numpy as jnp
from jax import lax

C = 2048
BR = 256
OUTC = 256
FIRST_DILATION = 12
SECOND_DILATION = 24
THIRD_DILATION = 36
COLS = 48
ROWS = 96


def steps_of(rng, shape, split, least, top_value):
    gain = 1.0
    for dim, parts in split:
        steps = jax.random.uniform(jax.random.fold_in(jax.random.fold_in(rng, 6), dim), (parts,), jnp.float32, least / len(split), top_value / len(split))
        gain = gain * jnp.repeat(jnp.exp(steps), shape[dim] // parts).reshape((-1,) + (1,) * (len(shape) - 1 - dim))
    return gain


def centred(stream_key, shape, width, bound, pieces=(), dtype=jnp.bfloat16):
    level = steps_of(stream_key, shape, pieces, -0.22, 0.18) if pieces else 1.0
    drawn = jax.random.normal(stream_key, shape, jnp.float32) * width * level
    return jnp.minimum(jnp.maximum(drawn, -bound), bound).astype(dtype)


def setup_inputs(seed: int = 0) -> dict:
    streams_of = jax.random.split(jax.random.key(seed), 8)
    features = centred(streams_of[0], (ROWS, COLS, C), 1.0, 6.0, ((0, 8),))
    point_weight = centred(streams_of[1], (C, BR), C ** -0.5, 0.125, ((1, 4),))
    dilated_weight = centred(streams_of[2], (3, 3, 3, C, BR), (9 * C) ** -0.5, 0.046875, ((4, 4),))
    branch_bias = centred(streams_of[3], (4, BR), 0.5, 3.0, ((1, 4),), jnp.float32)
    project_weight = centred(streams_of[4], (4, BR, OUTC), (4 * BR) ** -0.5, 0.1875)
    project_bias = centred(streams_of[5], (OUTC,), 0.5, 3.0, (), jnp.float32)
    cotangent = centred(streams_of[6], (ROWS, COLS, OUTC), 1.0, 6.0, ((0, 8),))
    return dict(features=features, point_weight=point_weight, dilated_weight=dilated_weight, branch_bias=branch_bias, project_weight=project_weight, project_bias=project_bias, cotangent=cotangent)


def shift_axis(field, axis_index, amount):
    extent = field.shape[axis_index]
    if amount == 0:
        return field
    if abs(amount) >= extent:
        return jnp.zeros_like(field)
    padding = [(0, 0)] * field.ndim
    if amount > 0:
        kept = lax.slice_in_dim(field, amount, extent, axis=axis_index)
        padding[axis_index] = (0, amount)
    else:
        kept = lax.slice_in_dim(field, 0, extent + amount, axis=axis_index)
        padding[axis_index] = (-amount, 0)
    return jnp.pad(kept, padding)


def shift_field(field, rows_by, cols_by):
    return shift_axis(shift_axis(field, 0, rows_by), 1, cols_by)


def reference(features, point_weight, dilated_weight, branch_bias, project_weight, project_bias, cotangent):
    flattened = features.reshape(ROWS * COLS, C)
    dilation_rates = (FIRST_DILATION, SECOND_DILATION, THIRD_DILATION)
    point_pre = jnp.dot(flattened, point_weight, preferred_element_type=jnp.float32).reshape(ROWS, COLS, BR)
    pre_list = [point_pre + branch_bias[0]]
    for branch, dilation in enumerate(dilation_rates):
        summed_result = jnp.zeros((ROWS, COLS, BR), jnp.float32)
        for row_tap in range(3):
            for col_tap in range(3):
                product = jnp.dot(flattened, dilated_weight[branch, row_tap, col_tap], preferred_element_type=jnp.float32)
                product = product.reshape(ROWS, COLS, BR)
                summed_result = summed_result + shift_field(product, (row_tap - 1) * dilation, (col_tap - 1) * dilation)
        pre_list.append(summed_result + branch_bias[branch + 1])
    project_pre = jnp.zeros((ROWS * COLS, OUTC), jnp.float32) + project_bias
    for branch in range(4):
        activation = jnp.maximum(pre_list[branch], 0.0).astype(jnp.bfloat16).reshape(ROWS * COLS, BR)
        project_pre = project_pre + jnp.dot(activation, project_weight[branch], preferred_element_type=jnp.float32)
    head_output = jnp.maximum(project_pre, 0.0).astype(jnp.bfloat16).reshape(ROWS, COLS, OUTC)
    head_grad = jnp.where(project_pre > 0, cotangent.reshape(ROWS * COLS, OUTC).astype(jnp.float32), 0.0).astype(jnp.bfloat16)
    input_grad = jnp.zeros((ROWS * COLS, C), jnp.float32)
    for branch in range(4):
        act_grad = jnp.dot(head_grad, project_weight[branch].T, preferred_element_type=jnp.float32).reshape(ROWS, COLS, BR)
        branch_grad = jnp.where(pre_list[branch] > 0, act_grad, 0.0).astype(jnp.bfloat16)
        if branch == 0:
            input_grad = input_grad + jnp.dot(branch_grad.reshape(ROWS * COLS, BR), point_weight.T, preferred_element_type=jnp.float32)
        else:
            dilation = dilation_rates[branch - 1]
            for row_tap in range(3):
                for col_tap in range(3):
                    moved = shift_field(branch_grad, -(row_tap - 1) * dilation, -(col_tap - 1) * dilation)
                    input_grad = input_grad + jnp.dot(moved.reshape(ROWS * COLS, BR), dilated_weight[branch - 1, row_tap, col_tap].T, preferred_element_type=jnp.float32)
    feature_grad = input_grad.astype(jnp.bfloat16).reshape(ROWS, COLS, C)
    return head_output, feature_grad
```

```python
import functools

import jax
import jax.numpy as jnp
import numpy as np
from jax import lax
from jax.experimental import pallas as pl
from jax.experimental.pallas import tpu as pltpu
from jax.sharding import PartitionSpec as P

FIRST_DILATION = 12
SECOND_DILATION = 24
THIRD_DILATION = 36


def passed_along(x, axis, by):
    devices = lax.axis_size(axis)
    pairs = [(i, i + by) for i in range(devices) if 0 <= i + by < devices]
    return lax.ppermute(x, axis, pairs)


def shift_columns(field, amount):
    breadth = field.shape[1]
    if amount == 0:
        return field
    padding = [(0, 0)] * field.ndim
    if amount > 0:
        kept = field[:, amount:]
        padding[1] = (0, amount)
    else:
        kept = field[:, : breadth + amount]
        padding[1] = (-amount, 0)
    return jnp.pad(kept, padding)


def fetch_sums(field, offset):
    return passed_along(field, "rows", offset)


def fetch_grads(field, offset):
    return passed_along(field, "rows", offset)


def shift_rows(field, amount, fetcher):
    height = field.shape[0]
    quotient = amount // height

    def extract_block(offset):
        if offset == 0:
            return field
        return fetcher(field, offset)

    return extract_block(quotient)


def make_kernel_taps(variants, dilation_rates):
    stacked = [variants[:, :, 0]]
    for branch, dilation in enumerate(dilation_rates):
        for row_tap in range(3):
            source = variants[:, :, 1 + 3 * branch + row_tap]
            for col_tap in range(3):
                stacked.append(shift_columns(source, -(col_tap - 1) * dilation))
    return jnp.stack(stacked, 2)


def on_device_general(
    features, point_weight, dilated_weight, branch_bias, project_weight, project_bias, cotangent
):
    height, breadth, channels = features.shape
    pixels = height * breadth
    own_width = point_weight.shape[1]
    filters = lax.axis_size("filt")
    member = lax.axis_index("filt")
    branch_outputs = project_weight.shape[2]
    own_out = branch_outputs // filters
    own_channels = channels // filters
    dilation_rates = (FIRST_DILATION, SECOND_DILATION, THIRD_DILATION)
    all_weights = jnp.concatenate(
        [point_weight[None], dilated_weight.reshape(27, channels, own_width)], 0
    )
    flattened = features.reshape(pixels, channels)
    tap_terms = jnp.einsum(
        "pc,tco->pto", flattened, all_weights, preferred_element_type=jnp.float32
    )
    tap_terms = tap_terms.reshape(height, breadth, 28, own_width)
    pre_list = [tap_terms[:, :, 0, :] + branch_bias[0]]
    for branch, dilation in enumerate(dilation_rates):
        summed_result = jnp.zeros((height, breadth, own_width), jnp.float32)
        for row_tap in range(3):
            row_sum = jnp.zeros((height, breadth, own_width), jnp.float32)
            for col_tap in range(3):
                row_sum = row_sum + shift_columns(
                    tap_terms[:, :, 1 + 9 * branch + 3 * row_tap + col_tap, :],
                    (col_tap - 1) * dilation,
                )
            summed_result = summed_result + shift_rows(
                row_sum, -(row_tap - 1) * dilation, fetch_sums
            )
        pre_list.append(summed_result + branch_bias[branch + 1])
    branch_pre = jnp.stack(pre_list, 2)
    activations = jnp.maximum(branch_pre, 0.0).astype(jnp.bfloat16).reshape(pixels, 4 * own_width)
    grouped = project_weight.reshape(4, filters, own_width, branch_outputs)
    own_rows = lax.dynamic_index_in_dim(grouped, member, 1, keepdims=False).reshape(
        4 * own_width, branch_outputs
    )
    flat_cotangent = cotangent.reshape(pixels, branch_outputs)
    ordered = jnp.transpose(grouped, (1, 0, 2, 3)).reshape(filters * 4 * own_width, branch_outputs)
    project_pre = jnp.dot(
        lax.all_gather(activations, "filt", axis=1, tiled=True),
        ordered,
        preferred_element_type=jnp.float32,
    )
    project_pre = project_pre + project_bias
    head_grad = jnp.where(project_pre > 0, flat_cotangent.astype(jnp.float32), 0.0).astype(
        jnp.bfloat16
    )
    own_pre = lax.dynamic_slice_in_dim(project_pre, member * own_out, own_out, 1)
    act_grad = jnp.dot(head_grad, own_rows.T, preferred_element_type=jnp.float32)
    head_output = jnp.maximum(own_pre, 0.0).astype(jnp.bfloat16).reshape(height, breadth, own_out)
    branch_grad = jnp.where(
        branch_pre > 0, act_grad.reshape(height, breadth, 4, own_width), 0.0
    ).astype(jnp.bfloat16)
    variant_list = [branch_grad[:, :, 0, :]]
    for branch, dilation in enumerate(dilation_rates):
        for row_tap in range(3):
            variant_list.append(
                shift_rows(branch_grad[:, :, branch + 1, :], (row_tap - 1) * dilation, fetch_grads)
            )
    variants = jnp.stack(variant_list, 2)
    stacked = make_kernel_taps(variants, dilation_rates).reshape(pixels, 28, own_width)
    input_grad = lax.psum_scatter(
        jnp.einsum("pto,tco->cp", stacked, all_weights, preferred_element_type=jnp.float32),
        "filt",
        scatter_dimension=0,
        tiled=True,
    ).T
    feature_grad = input_grad.astype(jnp.bfloat16).reshape(height, breadth, own_channels)
    return (head_output, feature_grad)


W = 64
BLOCK = 144
PIXELS = 576
HALF = 288
CHANNELS = 2048
F32 = jnp.float32
BF16 = jnp.bfloat16
VMEM_BYTES = 60 * 2**20

OUT_PAIRS = ((3, 1), (1, 1), (2, 1), (3, 0), (1, 0), (2, 0), (1, 2), (2, 2), (3, 2))
OUT_TAPS = [(k, i, j) for k, j in OUT_PAIRS for i in (0, 2)]
OWN_TAPS = [(k, 1, j) for j in (1, 0, 2) for k in (1, 2, 3)]
GRAD_TAPS = (
    [(k, 1, 1) for k in (1, 2, 3)]
    + OUT_TAPS
    + [(k, 1, j) for k in (1, 2, 3) for j in (0, 2)]
)


def fits(mesh):
    return mesh.shape["rows"] == 8 and mesh.shape["filt"] == 4


def order_matrix():
    to = np.zeros((192, 192), np.float32)
    for m in range(4):
        for r in range(4):
            for c in range(12):
                to[m * 48 + r * 12 + c, r * 48 + m * 12 + c] = 1
    return to


def tap_index(tap):
    k, i, j = tap
    return (k - 1) * 9 + i * 3 + j


def nt(a, b):
    return lax.dot_general(a, b, (((1,), (1,)), ((), ())), preferred_element_type=F32)


def nn(a, b):
    return lax.dot_general(a, b, (((1,), (0,)), ((), ())), preferred_element_type=F32)


def into_blocks(order, read, write):
    for g in range(3):
        moved = nn(order, read(g * 192)).astype(BF16)
        for m in range(4):
            write(m * BLOCK + g * 48, moved[m * 48 : (m + 1) * 48])


def from_blocks(order_t, value, write):
    for g in range(3):
        parts = [value[m * BLOCK + g * 48 : m * BLOCK + g * 48 + 48] for m in range(4)]
        write(g * 192, nn(order_t, jnp.concatenate(parts, 0)).astype(BF16))


def low_lanes(shape):
    return lax.broadcasted_iota(jnp.int32, shape, 1) % 128 < W


def outward_kernel(features, dilated, order, *refs):
    plus, minus = refs[0:3], refs[3:6]
    ordered, raw, weights, sums, feature_sems, weight_sems = refs[6:]
    loads = []
    for g in range(3):
        rows = pl.ds(g * 192, 192)
        loads.append(pltpu.make_async_copy(features.at[rows], raw.at[rows], feature_sems.at[g]))
        loads[-1].start()
    fetches = []
    for q, tap in enumerate(OUT_TAPS):
        fetches.append(
            pltpu.make_async_copy(
                dilated.at[tap_index(tap)], weights.at[pl.ds(q * W, W)], weight_sems.at[q]
            )
        )
        fetches[-1].start()

    for g in range(3):
        loads[g].wait()
        moved = nn(order[...], raw[g * 192 : (g + 1) * 192, :]).astype(BF16)
        for m in range(4):
            at = m * BLOCK + g * 48
            ordered[at : at + 48, :] = moved[m * 48 : (m + 1) * 48]

    def product(pair, pairs, first, last):
        for q in range(2 * pair, 2 * (pair + pairs)):
            fetches[q].wait()
        return nt(
            ordered[first * BLOCK : last * BLOCK, :],
            weights[pair * 128 : (pair + pairs) * 128, :],
        )

    def add(k, first, value):
        rows = slice(first * BLOCK, first * BLOCK + value.shape[0])
        sums[k - 1, rows, :] = sums[k - 1, rows, :] + value

    d = product(0, 2, 0, 4)
    sums[2] = d[:, :128]
    sums[0] = d[:, 128:]
    d = product(2, 2, 0, 4)
    sums[1] = d[:, :128]
    add(3, 3, d[:BLOCK, 128:])
    d = product(4, 2, 0, 3)
    add(1, 1, d[:, :128])
    add(2, 2, d[: 2 * BLOCK, 128:])
    d = product(6, 2, 1, 4)
    add(1, 0, d[:, :128])
    add(2, 0, d[BLOCK:, 128:])
    d = product(8, 1, 3, 4)
    add(3, 0, d)

    low = low_lanes((HALF, 128))
    for k in range(3):
        top, bottom = sums[k, :HALF, :], sums[k, HALF:, :]
        plus[k][...] = jnp.where(low, top, pltpu.roll(bottom, W, 1))
        minus[k][...] = jnp.where(low, pltpu.roll(top, W, 1), bottom)


def outward_sums(features, dilated, order):
    flops = 2 * PIXELS * CHANNELS * 18 * W
    sent = jax.ShapeDtypeStruct((HALF, 128), F32)
    return pl.pallas_call(
        outward_kernel,
        out_shape=[sent] * 6 + [jax.ShapeDtypeStruct((PIXELS, CHANNELS), BF16)],
        in_specs=[
            pl.BlockSpec(memory_space=pl.ANY),
            pl.BlockSpec(memory_space=pl.ANY),
            pl.BlockSpec(memory_space=pltpu.VMEM),
        ],
        out_specs=[pl.BlockSpec(memory_space=pltpu.VMEM)] * 7,
        scratch_shapes=[
            pltpu.VMEM((PIXELS, CHANNELS), BF16),
            pltpu.VMEM((18 * W, CHANNELS), BF16),
            pltpu.VMEM((3, PIXELS, 128), F32),
            pltpu.SemaphoreType.DMA((3,)),
            pltpu.SemaphoreType.DMA((18,)),
        ],
        compiler_params=pltpu.CompilerParams(vmem_limit_bytes=VMEM_BYTES),
        cost_estimate=pl.CostEstimate(flops=flops, bytes_accessed=9 * 10**6, transcendentals=0),
        name="outward_sums",
    )(features, dilated, order)


def own_kernel(ordered, dilated, point, bias, out, weights, sems):
    fetches = [pltpu.make_async_copy(point, weights.at[pl.ds(0, W)], sems.at[9])]
    for q, tap in enumerate(OWN_TAPS):
        fetches.append(
            pltpu.make_async_copy(
                dilated.at[tap_index(tap)], weights.at[pl.ds((q + 1) * W, W)], sems.at[q]
            )
        )
    for fetch in fetches:
        fetch.start()
    for fetch in fetches[:4]:
        fetch.wait()
    out[...] = nt(ordered[...], weights[:256, :]) + bias[...]
    low = low_lanes((PIXELS, 128))

    def add(first, value, k):
        lanes = slice(0, 128) if k == 1 else slice(128, 256)
        rows = slice(first * BLOCK, first * BLOCK + value.shape[0])
        mask = low[: value.shape[0]]
        kept = jnp.where(mask, value[:, lanes], 0.0) if k == 2 else jnp.where(mask, 0.0, value[:, lanes])
        out[rows, lanes] = out[rows, lanes] + kept

    for fetch in fetches[4:7]:
        fetch.wait()
    d = nt(ordered[: 3 * BLOCK, :], weights[192:448, :])
    for k in (1, 2, 3):
        add(k, d[: (4 - k) * BLOCK], k)
    for fetch in fetches[7:]:
        fetch.wait()
    d = nt(ordered[BLOCK:, :], weights[384:640, :])
    for k in (1, 2, 3):
        add(0, d[(k - 1) * BLOCK :], k)


def own_sums(ordered, dilated, point, bias):
    flops = 2 * PIXELS * CHANNELS * 10 * W
    return pl.pallas_call(
        own_kernel,
        out_shape=jax.ShapeDtypeStruct((PIXELS, 4 * W), F32),
        in_specs=[
            pl.BlockSpec(memory_space=pltpu.VMEM),
            pl.BlockSpec(memory_space=pl.ANY),
            pl.BlockSpec(memory_space=pl.ANY),
            pl.BlockSpec(memory_space=pltpu.VMEM),
        ],
        out_specs=pl.BlockSpec(memory_space=pltpu.VMEM),
        scratch_shapes=[
            pltpu.VMEM((10 * W, CHANNELS), BF16),
            pltpu.SemaphoreType.DMA((10,)),
        ],
        compiler_params=pltpu.CompilerParams(vmem_limit_bytes=VMEM_BYTES),
        cost_estimate=pl.CostEstimate(flops=flops, bytes_accessed=6 * 10**6, transcendentals=0),
        name="own_sums",
    )(ordered, dilated, point, bias)


def activation_kernel(own, *refs):
    recv, acts = refs[:6], refs[6]
    low = low_lanes((HALF, 128))
    t1, t2, t3 = (recv[k][...] + recv[k + 3][...] for k in range(3))
    r1, r2, r3 = (pltpu.roll(t, W, 1) for t in (t1, t2, t3))
    for rows, a, b, c in ((slice(0, HALF), r1, t2, r3), (slice(HALF, PIXELS), t1, r2, t3)):
        left = own[rows, :128] + jnp.where(low, 0.0, a)
        right = own[rows, 128:] + jnp.where(low, b, c)
        acts[rows, :128] = jnp.maximum(left, 0.0).astype(BF16)
        acts[rows, 128:] = jnp.maximum(right, 0.0).astype(BF16)


def activations_of(own, received):
    return pl.pallas_call(
        activation_kernel,
        out_shape=jax.ShapeDtypeStruct((PIXELS, 4 * W), BF16),
        in_specs=[pl.BlockSpec(memory_space=pltpu.VMEM)] * 7,
        out_specs=pl.BlockSpec(memory_space=pltpu.VMEM),
        compiler_params=pltpu.CompilerParams(vmem_limit_bytes=VMEM_BYTES),
        name="activations",
    )(own, *received)


def head_kernel(member_ref, a0, a1, a2, a3, project, bias, cotangent, order, order_t, *refs):
    head_out, grads, sends, ordered = refs[0], refs[1], refs[2:5], refs[5]
    member = member_ref[0]

    def rows_of(who):
        at = pl.multiple_of(who * W, W)
        return jnp.concatenate([project[k, pl.ds(at, W), :] for k in range(4)], 0)

    own_rows = rows_of(member)
    pre = nn(a0[...], own_rows) + bias[...]
    for flip, acts in ((1, a1), (2, a2), (3, a3)):
        pre = pre + nn(acts[...], rows_of(member ^ flip))
    mine = jnp.zeros((PIXELS, W), F32)
    for q in range(4):
        mine = mine + jnp.where(member == q, pre[:, q * W : (q + 1) * W], 0.0)
    mine = jnp.maximum(mine, 0.0).astype(BF16)

    def put(at, value):
        head_out[at : at + 192, :] = value

    from_blocks(order_t[...], mine, put)
    for g in range(3):
        moved = nn(order[...], cotangent[g * 192 : (g + 1) * 192, :])
        for m in range(4):
            at = m * BLOCK + g * 48
            ordered[at : at + 48, :] = moved[m * 48 : (m + 1) * 48]
    head_grad = jnp.where(pre > 0, ordered[...], 0.0).astype(BF16)
    act_grad = nt(head_grad, own_rows)
    grad = jnp.where(a0[...].astype(F32) > 0, act_grad, 0.0)
    grads[...] = grad.astype(BF16)
    low = low_lanes((HALF, 128))
    left, right = grad[:, :128], grad[:, 128:]
    sends[0][...] = jnp.where(low, pltpu.roll(left[:HALF], W, 1), left[HALF:]).astype(BF16)
    sends[1][...] = jnp.where(low, right[:HALF], pltpu.roll(right[HALF:], W, 1)).astype(BF16)
    sends[2][...] = jnp.where(low, pltpu.roll(right[:HALF], W, 1), right[HALF:]).astype(BF16)


def head(member, acts, project, bias, cotangent, order, order_t):
    sent = jax.ShapeDtypeStruct((HALF, 128), BF16)
    return pl.pallas_call(
        head_kernel,
        out_shape=[
            jax.ShapeDtypeStruct((PIXELS, W), BF16),
            jax.ShapeDtypeStruct((PIXELS, 4 * W), BF16),
            sent,
            sent,
            sent,
        ],
        in_specs=[pl.BlockSpec(memory_space=pltpu.SMEM)]
        + [pl.BlockSpec(memory_space=pltpu.VMEM)] * 9,
        out_specs=[pl.BlockSpec(memory_space=pltpu.VMEM)] * 5,
        scratch_shapes=[pltpu.VMEM((PIXELS, 256), F32)],
        compiler_params=pltpu.CompilerParams(vmem_limit_bytes=VMEM_BYTES),
        name="head",
    )(member, *acts, project, bias, cotangent, order, order_t)


def grad_kernel(where_ref, own, *refs):
    recv, dilated, point = refs[:6], refs[6], refs[7]
    away, kept, stack, pairs, twice, weights, sems = refs[8:]
    first = pl.multiple_of(where_ref[0], 1024)
    columns = pl.ds(first, 1024)
    fetches = [
        pltpu.make_async_copy(point.at[:, columns], weights.at[pl.ds(0, W)], sems.at[27])
    ]
    for q, tap in enumerate(GRAD_TAPS):
        fetches.append(
            pltpu.make_async_copy(
                dilated.at[tap_index(tap), :, columns],
                weights.at[pl.ds((q + 1) * W, W)],
                sems.at[q],
            )
        )
    for fetch in fetches:
        fetch.start()
    low = low_lanes((HALF, 128))
    for k in range(3):
        p, m = recv[k][...].astype(F32), recv[k + 3][...].astype(F32)
        pairs[k, :HALF, :] = jnp.where(low, p, pltpu.roll(m, W, 1)).astype(BF16)
        pairs[k, HALF:, :] = jnp.where(low, pltpu.roll(p, W, 1), m).astype(BF16)
        g = own[:, :128].astype(F32) if k == 0 else own[:, 128:].astype(F32)
        other = pltpu.roll(g, W, 1)
        low_all = low_lanes((PIXELS, 128))
        both = jnp.where(low_all, g, other) if k == 1 else jnp.where(low_all, other, g)
        twice[k] = both.astype(BF16)
    stack[:, :256] = own[...]
    nothing = jnp.zeros((BLOCK, 128), BF16)
    for q, (k, j) in enumerate(OUT_PAIRS):
        lanes = slice(256 + q * 128, 384 + q * 128)
        for m in range(4):
            source = m - (j - 1) * k
            value = nothing
            if 0 <= source < 4:
                value = pairs[k - 1, source * BLOCK : (source + 1) * BLOCK, :]
            stack[m * BLOCK : (m + 1) * BLOCK, lanes] = value
    low_block = low_lanes((BLOCK, 128))
    for k in (1, 2, 3):
        lanes = slice(1408 + (k - 1) * 128, 1536 + (k - 1) * 128)
        for m in range(4):
            halves = []
            for source in (m + k, m - k):
                value = nothing
                if 0 <= source < 4:
                    value = twice[k - 1, source * BLOCK : (source + 1) * BLOCK, :]
                halves.append(value)
            stack[m * BLOCK : (m + 1) * BLOCK, lanes] = jnp.where(low_block, *halves)
    for fetch in fetches:
        fetch.wait()
    core = where_ref[1]
    for part, out in ((1 - core, away), (core, kept)):
        for n in range(2):
            at = pl.multiple_of(part * 512 + n * 256, 256)
            out[:, n * 256 : (n + 1) * 256] = nn(stack[...], weights[:, pl.ds(at, 256)]).astype(BF16)


def grad_half(where, own, received, dilated, point):
    out = jax.ShapeDtypeStruct((PIXELS, 512), BF16)
    return pl.pallas_call(
        grad_kernel,
        out_shape=[out, out],
        in_specs=[pl.BlockSpec(memory_space=pltpu.SMEM)]
        + [pl.BlockSpec(memory_space=pltpu.VMEM)] * 7
        + [pl.BlockSpec(memory_space=pl.ANY)] * 2,
        out_specs=[pl.BlockSpec(memory_space=pltpu.VMEM)] * 2,
        scratch_shapes=[
            pltpu.VMEM((PIXELS, 28 * W), BF16),
            pltpu.VMEM((3, PIXELS, 128), BF16),
            pltpu.VMEM((3, PIXELS, 128), BF16),
            pltpu.VMEM((28 * W, 1024), BF16),
            pltpu.SemaphoreType.DMA((28,)),
        ],
        compiler_params=pltpu.CompilerParams(vmem_limit_bytes=VMEM_BYTES),
        cost_estimate=pl.CostEstimate(
            flops=2 * PIXELS * 28 * W * 1024, bytes_accessed=6 * 10**6, transcendentals=0
        ),
        name="grad_half",
    )(where, own, *received, dilated, point)


def last_kernel(a, b, c, order_t, out):
    total = a[...].astype(F32) + b[...].astype(F32) + c[...].astype(F32)

    def put(at, value):
        out[at : at + 192, :] = value

    from_blocks(order_t[...], total.astype(BF16), put)


def last_sum(a, b, c, order_t):
    return pl.pallas_call(
        last_kernel,
        out_shape=jax.ShapeDtypeStruct((PIXELS, 512), BF16),
        in_specs=[pl.BlockSpec(memory_space=pltpu.VMEM)] * 4,
        out_specs=pl.BlockSpec(memory_space=pltpu.VMEM),
        compiler_params=pltpu.CompilerParams(vmem_limit_bytes=VMEM_BYTES),
        name="last_sum",
    )(a, b, c, order_t)


def flipped(x, bit):
    return lax.ppermute(x, "filt", [(i, i ^ bit) for i in range(lax.axis_size("filt"))])


def on_device(
    features, point_weight, dilated_weight, branch_bias, project_weight, project_bias, cotangent
):
    member = lax.axis_index("filt")
    order = jnp.asarray(order_matrix(), BF16)
    order_t = jnp.asarray(order_matrix().T, BF16)
    flat = features.reshape(PIXELS, CHANNELS)
    dilated = jnp.transpose(dilated_weight, (0, 1, 2, 4, 3)).reshape(27, W, CHANNELS)
    point = point_weight.T
    bias = branch_bias.reshape(1, 4 * W)
    *sums, ordered = outward_sums(flat, dilated, order)
    received = [
        passed_along(sums[3 * way + k], "rows", (1 - 2 * way) * (k + 1))
        for way in range(2)
        for k in range(3)
    ]
    own = own_sums(ordered, dilated, point, bias)
    acts = activations_of(own, received)
    across = flipped(acts, 2)
    beside = flipped(acts, 1)
    corner = flipped(across, 1)
    head_output, grads, *sends = head(
        member.astype(jnp.int32).reshape(1),
        (acts, beside, across, corner),
        project_weight,
        project_bias.reshape(1, 256),
        cotangent.reshape(PIXELS, 256),
        order,
        order_t,
    )
    arrived = [
        passed_along(sends[k], "rows", (2 * way - 1) * (k + 1)) for way in range(2) for k in range(3)
    ]
    row, core = member // 2, member % 2
    there = jnp.stack([(1 - row) * 1024, core]).astype(jnp.int32)
    here = jnp.stack([row * 1024, core]).astype(jnp.int32)
    away, kept = grad_half(there, grads, arrived, dilated, point)
    crossing = (flipped(away, 1).astype(F32) + kept.astype(F32)).astype(BF16)
    crossed = flipped(crossing, 2)
    away, kept = grad_half(here, grads, arrived, dilated, point)
    feature_grad = last_sum(kept, flipped(away, 1), crossed, order_t)
    return head_output.reshape(12, 48, W), feature_grad.reshape(12, 48, 512)


def solution(mesh):
    body = on_device if fits(mesh) else on_device_general
    in_specs = (
        P("rows", None, None),
        P(None, "filt"),
        P(None, None, None, None, "filt"),
        P(None, "filt"),
        P(),
        P(),
        P("rows", None, None),
    )
    out_specs = (P("rows", None, "filt"), P("rows", None, "filt"))
    return jax.shard_map(
        body, mesh=mesh, in_specs=in_specs, out_specs=out_specs, check_vma=False
    )
```

```python
import functools

import jax
import jax.numpy as jnp
import numpy as np
from jax import lax
from jax.experimental import pallas as pl
from jax.experimental.pallas import tpu as pltpu
from jax.sharding import PartitionSpec as P

FIRST_DILATION = 12
SECOND_DILATION = 24
THIRD_DILATION = 36


def passed_along(x, axis, by):
    devices = lax.axis_size(axis)
    pairs = [(i, i + by) for i in range(devices) if 0 <= i + by < devices]
    return lax.ppermute(x, axis, pairs)


def shift_columns(field, amount):
    breadth = field.shape[1]
    if amount == 0:
        return field
    padding = [(0, 0)] * field.ndim
    if amount > 0:
        kept = field[:, amount:]
        padding[1] = (0, amount)
    else:
        kept = field[:, : breadth + amount]
        padding[1] = (-amount, 0)
    return jnp.pad(kept, padding)


def fetch_sums(field, offset):
    return passed_along(field, "rows", offset)


def fetch_grads(field, offset):
    return passed_along(field, "rows", offset)


def shift_rows(field, amount, fetcher):
    height = field.shape[0]
    quotient = amount // height

    def extract_block(offset):
        if offset == 0:
            return field
        return fetcher(field, offset)

    return extract_block(quotient)


def make_kernel_taps(variants, dilation_rates):
    stacked = [variants[:, :, 0]]
    for branch, dilation in enumerate(dilation_rates):
        for row_tap in range(3):
            source = variants[:, :, 1 + 3 * branch + row_tap]
            for col_tap in range(3):
                stacked.append(shift_columns(source, -(col_tap - 1) * dilation))
    return jnp.stack(stacked, 2)


def on_device_general(
    features, point_weight, dilated_weight, branch_bias, project_weight, project_bias, cotangent
):
    height, breadth, channels = features.shape
    pixels = height * breadth
    own_width = point_weight.shape[1]
    filters = lax.axis_size("filt")
    member = lax.axis_index("filt")
    branch_outputs = project_weight.shape[2]
    own_out = branch_outputs // filters
    own_channels = channels // filters
    dilation_rates = (FIRST_DILATION, SECOND_DILATION, THIRD_DILATION)
    all_weights = jnp.concatenate(
        [point_weight[None], dilated_weight.reshape(27, channels, own_width)], 0
    )
    flattened = features.reshape(pixels, channels)
    tap_terms = jnp.einsum(
        "pc,tco->pto", flattened, all_weights, preferred_element_type=jnp.float32
    )
    tap_terms = tap_terms.reshape(height, breadth, 28, own_width)
    pre_list = [tap_terms[:, :, 0, :] + branch_bias[0]]
    for branch, dilation in enumerate(dilation_rates):
        summed_result = jnp.zeros((height, breadth, own_width), jnp.float32)
        for row_tap in range(3):
            row_sum = jnp.zeros((height, breadth, own_width), jnp.float32)
            for col_tap in range(3):
                row_sum = row_sum + shift_columns(
                    tap_terms[:, :, 1 + 9 * branch + 3 * row_tap + col_tap, :],
                    (col_tap - 1) * dilation,
                )
            summed_result = summed_result + shift_rows(
                row_sum, -(row_tap - 1) * dilation, fetch_sums
            )
        pre_list.append(summed_result + branch_bias[branch + 1])
    branch_pre = jnp.stack(pre_list, 2)
    activations = jnp.maximum(branch_pre, 0.0).astype(jnp.bfloat16).reshape(pixels, 4 * own_width)
    grouped = project_weight.reshape(4, filters, own_width, branch_outputs)
    own_rows = lax.dynamic_index_in_dim(grouped, member, 1, keepdims=False).reshape(
        4 * own_width, branch_outputs
    )
    flat_cotangent = cotangent.reshape(pixels, branch_outputs)
    ordered = jnp.transpose(grouped, (1, 0, 2, 3)).reshape(filters * 4 * own_width, branch_outputs)
    project_pre = jnp.dot(
        lax.all_gather(activations, "filt", axis=1, tiled=True),
        ordered,
        preferred_element_type=jnp.float32,
    )
    project_pre = project_pre + project_bias
    head_grad = jnp.where(project_pre > 0, flat_cotangent.astype(jnp.float32), 0.0).astype(
        jnp.bfloat16
    )
    own_pre = lax.dynamic_slice_in_dim(project_pre, member * own_out, own_out, 1)
    act_grad = jnp.dot(head_grad, own_rows.T, preferred_element_type=jnp.float32)
    head_output = jnp.maximum(own_pre, 0.0).astype(jnp.bfloat16).reshape(height, breadth, own_out)
    branch_grad = jnp.where(
        branch_pre > 0, act_grad.reshape(height, breadth, 4, own_width), 0.0
    ).astype(jnp.bfloat16)
    variant_list = [branch_grad[:, :, 0, :]]
    for branch, dilation in enumerate(dilation_rates):
        for row_tap in range(3):
            variant_list.append(
                shift_rows(branch_grad[:, :, branch + 1, :], (row_tap - 1) * dilation, fetch_grads)
            )
    variants = jnp.stack(variant_list, 2)
    stacked = make_kernel_taps(variants, dilation_rates).reshape(pixels, 28, own_width)
    input_grad = lax.psum_scatter(
        jnp.einsum("pto,tco->cp", stacked, all_weights, preferred_element_type=jnp.float32),
        "filt",
        scatter_dimension=0,
        tiled=True,
    ).T
    feature_grad = input_grad.astype(jnp.bfloat16).reshape(height, breadth, own_channels)
    return (head_output, feature_grad)


W = 64
BLOCK = 144
PIXELS = 576
HALF = 288
CHANNELS = 2048
F32 = jnp.float32
BF16 = jnp.bfloat16

OUT_PAIRS = ((3, 1), (1, 1), (3, 0), (1, 0), (3, 2), (1, 2), (2, 1), (2, 0), (2, 2))
OWN_TAPS = [(k, 1, j) for j in (1, 0, 2) for k in (1, 2, 3)]
GRAD_TAPS = (
    [(k, 1, 1) for k in (1, 2, 3)]
    + [(k, i, j) for k, j in OUT_PAIRS for i in (0, 2)]
    + [(k, 1, j) for k in (1, 2, 3) for j in (0, 2)]
)
SWAPS = (5, 7, 3, 1, 6, 2)


def fits(mesh):
    return mesh.shape["rows"] == 8 and mesh.shape["filt"] == 4


def order_matrix():
    to = np.zeros((192, 192), np.float32)
    for m in range(4):
        for r in range(4):
            for c in range(12):
                to[m * 48 + r * 12 + c, r * 48 + m * 12 + c] = 1
    return to


def tap_index(tap):
    k, i, j = tap
    return (k - 1) * 9 + i * 3 + j


def nt(a, b):
    return lax.dot_general(a, b, (((1,), (1,)), ((), ())), preferred_element_type=F32)


def nn(a, b):
    return lax.dot_general(a, b, (((1,), (0,)), ((), ())), preferred_element_type=F32)


def into_blocks(order, read, write):
    for g in range(3):
        moved = nn(order, read(g * 192)).astype(BF16)
        for m in range(4):
            write(m * BLOCK + g * 48, moved[m * 48 : (m + 1) * 48])


def from_blocks(order_t, value, write):
    for g in range(3):
        parts = [value[m * BLOCK + g * 48 : m * BLOCK + g * 48 + 48] for m in range(4)]
        write(g * 192, nn(order_t, jnp.concatenate(parts, 0)).astype(BF16))


def low_lanes(shape):
    return lax.broadcasted_iota(jnp.int32, shape, 1) % 128 < W


def outward_slot(row, x):
    other = row ^ x
    apart = jnp.abs(other - row)
    slot = apart - 1 + jnp.where(other < row, 3, 0)
    return jnp.where(apart <= 3, slot, 0)


def pack_rows(sums, packed, k):
    low = low_lanes((HALF, 128))
    top, bottom = sums[k - 1, :HALF, :], sums[k - 1, HALF:, :]
    packed[k - 1] = jnp.where(low, top, pltpu.roll(bottom, W, 1))
    packed[k + 2] = jnp.where(low, pltpu.roll(top, W, 1), bottom)


def fetch_taps(dilated, weights, sems, pairs):
    taps = [(k, i, j) for k, j in pairs for i in (0, 2)]
    fetches = [
        pltpu.make_async_copy(
            dilated.at[tap_index(tap)], weights.at[pl.ds(q * W, W)], sems.at[q]
        )
        for q, tap in enumerate(taps)
    ]
    for fetch in fetches:
        fetch.start()
    return fetches


def odd_kernel(row_ref, features, dilated, order, *refs):
    out, ordered = refs[0:4], refs[4]
    raw, weights, sums, packed, feature_sems, weight_sems = refs[5:]
    loads = []
    for g in range(3):
        rows = pl.ds(g * 192, 192)
        loads.append(pltpu.make_async_copy(features.at[rows], raw.at[rows], feature_sems.at[g]))
        loads[-1].start()
    fetches = fetch_taps(dilated, weights, weight_sems, OUT_PAIRS[:6])
    for g in range(3):
        loads[g].wait()
        moved = nn(order[...], raw[g * 192 : (g + 1) * 192, :]).astype(BF16)
        for m in range(4):
            at = m * BLOCK + g * 48
            ordered[at : at + 48, :] = moved[m * 48 : (m + 1) * 48]

    def product(pair, first, last):
        for fetch in fetches[2 * pair : 2 * pair + 4]:
            fetch.wait()
        return nt(
            ordered[first * BLOCK : last * BLOCK, :], weights[pair * 128 : pair * 128 + 256, :]
        )

    d = product(0, 0, 4)
    sums[2] = d[:, :128]
    sums[0] = d[:, 128:]
    d = product(2, 0, 3)
    sums[2, 3 * BLOCK :, :] = sums[2, 3 * BLOCK :, :] + d[:BLOCK, :128]
    sums[0, BLOCK:, :] = sums[0, BLOCK:, :] + d[:, 128:]
    d = product(4, 1, 4)
    sums[2, :BLOCK, :] = sums[2, :BLOCK, :] + d[2 * BLOCK :, :128]
    sums[0, : 3 * BLOCK, :] = sums[0, : 3 * BLOCK, :] + d[:, 128:]
    pack_rows(sums, packed, 3)
    pack_rows(sums, packed, 1)
    for n in range(4):
        out[n][...] = packed[outward_slot(row_ref[0], SWAPS[n])]


def odd_sums(row, features, dilated, order):
    return pl.pallas_call(
        odd_kernel,
        out_shape=[jax.ShapeDtypeStruct((HALF, 128), F32)] * 4
        + [jax.ShapeDtypeStruct((PIXELS, CHANNELS), BF16)],
        in_specs=[
            pl.BlockSpec(memory_space=pltpu.SMEM),
            pl.BlockSpec(memory_space=pl.ANY),
            pl.BlockSpec(memory_space=pl.ANY),
            pl.BlockSpec(memory_space=pltpu.VMEM),
        ],
        out_specs=[pl.BlockSpec(memory_space=pltpu.VMEM)] * 5,
        scratch_shapes=[
            pltpu.VMEM((PIXELS, CHANNELS), BF16),
            pltpu.VMEM((12 * W, CHANNELS), BF16),
            pltpu.VMEM((3, PIXELS, 128), F32),
            pltpu.VMEM((6, HALF, 128), F32),
            pltpu.SemaphoreType.DMA((3,)),
            pltpu.SemaphoreType.DMA((12,)),
        ],
        compiler_params=pltpu.CompilerParams(vmem_limit_bytes=20 * 2**20),
        cost_estimate=pl.CostEstimate(
            flops=2 * PIXELS * CHANNELS * 12 * W, bytes_accessed=8 * 10**6, transcendentals=0
        ),
        name="odd_sums",
    )(row, features, dilated, order)


def even_kernel(row_ref, ordered, dilated, *refs):
    out = refs[0:2]
    weights, sums, packed, sems = refs[2:]
    fetches = fetch_taps(dilated, weights, sems, OUT_PAIRS[6:])
    for fetch in fetches:
        fetch.wait()
    d = nt(ordered[...], weights[...])
    sums[1] = d[:, :128]
    sums[1, 2 * BLOCK :, :] = sums[1, 2 * BLOCK :, :] + d[: 2 * BLOCK, 128:256]
    sums[1, : 2 * BLOCK, :] = sums[1, : 2 * BLOCK, :] + d[2 * BLOCK :, 256:]
    pack_rows(sums, packed, 2)
    for n in range(2):
        slot = jnp.where((row_ref[0] ^ SWAPS[4 + n]) < row_ref[0], 4, 1)
        out[n][...] = packed[slot]


def even_sums(row, ordered, dilated):
    return pl.pallas_call(
        even_kernel,
        out_shape=[jax.ShapeDtypeStruct((HALF, 128), F32)] * 2,
        in_specs=[
            pl.BlockSpec(memory_space=pltpu.SMEM),
            pl.BlockSpec(memory_space=pltpu.VMEM),
            pl.BlockSpec(memory_space=pl.ANY),
        ],
        out_specs=[pl.BlockSpec(memory_space=pltpu.VMEM)] * 2,
        scratch_shapes=[
            pltpu.VMEM((6 * W, CHANNELS), BF16),
            pltpu.VMEM((3, PIXELS, 128), F32),
            pltpu.VMEM((6, HALF, 128), F32),
            pltpu.SemaphoreType.DMA((6,)),
        ],
        compiler_params=pltpu.CompilerParams(vmem_limit_bytes=14 * 2**20),
        cost_estimate=pl.CostEstimate(
            flops=2 * PIXELS * CHANNELS * 6 * W, bytes_accessed=4 * 10**6, transcendentals=0
        ),
        name="even_sums",
    )(row, ordered, dilated)


def own_kernel(ordered, dilated, point, bias, out, weights, sems):
    fetches = [pltpu.make_async_copy(point, weights.at[pl.ds(0, W)], sems.at[9])]
    for q, tap in enumerate(OWN_TAPS):
        fetches.append(
            pltpu.make_async_copy(
                dilated.at[tap_index(tap)], weights.at[pl.ds((q + 1) * W, W)], sems.at[q]
            )
        )
    for fetch in fetches:
        fetch.start()
    for fetch in fetches[:4]:
        fetch.wait()
    out[...] = nt(ordered[...], weights[:256, :]) + bias[...]
    low = low_lanes((PIXELS, 128))

    def add(first, value, k):
        lanes = slice(0, 128) if k == 1 else slice(128, 256)
        rows = slice(first * BLOCK, first * BLOCK + value.shape[0])
        mask = low[: value.shape[0]]
        kept = jnp.where(mask, value[:, lanes], 0.0) if k == 2 else jnp.where(mask, 0.0, value[:, lanes])
        out[rows, lanes] = out[rows, lanes] + kept

    for fetch in fetches[4:7]:
        fetch.wait()
    d = nt(ordered[: 3 * BLOCK, :], weights[192:448, :])
    for k in (1, 2, 3):
        add(k, d[: (4 - k) * BLOCK], k)
    for fetch in fetches[7:]:
        fetch.wait()
    d = nt(ordered[BLOCK:, :], weights[384:640, :])
    for k in (1, 2, 3):
        add(0, d[(k - 1) * BLOCK :], k)


def own_sums(ordered, dilated, point, bias):
    flops = 2 * PIXELS * CHANNELS * 10 * W
    return pl.pallas_call(
        own_kernel,
        out_shape=jax.ShapeDtypeStruct((PIXELS, 4 * W), F32),
        in_specs=[
            pl.BlockSpec(memory_space=pltpu.VMEM),
            pl.BlockSpec(memory_space=pl.ANY),
            pl.BlockSpec(memory_space=pl.ANY),
            pl.BlockSpec(memory_space=pltpu.VMEM),
        ],
        out_specs=pl.BlockSpec(memory_space=pltpu.VMEM),
        scratch_shapes=[
            pltpu.VMEM((10 * W, CHANNELS), BF16),
            pltpu.SemaphoreType.DMA((10,)),
        ],
        compiler_params=pltpu.CompilerParams(vmem_limit_bytes=14 * 2**20),
        cost_estimate=pl.CostEstimate(flops=flops, bytes_accessed=6 * 10**6, transcendentals=0),
        name="own_sums",
    )(ordered, dilated, point, bias)


def arrival_slot(row, other):
    return jnp.where((other >= 0) & (other < 8), row ^ other, 0)


def gather_arrivals(recv, arrivals):
    arrivals[0] = jnp.zeros((HALF, 128), arrivals.dtype)
    for n, x in enumerate(SWAPS):
        arrivals[x] = recv[n][...]


def activation_kernel(row_ref, own, *refs):
    recv, acts, arrivals = refs[:6], refs[6], refs[7]
    row = row_ref[0]
    gather_arrivals(recv, arrivals)
    low = low_lanes((HALF, 128))
    t1, t2, t3 = (
        arrivals[arrival_slot(row, row - k)] + arrivals[arrival_slot(row, row + k)]
        for k in (1, 2, 3)
    )
    r1, r2, r3 = (pltpu.roll(t, W, 1) for t in (t1, t2, t3))
    for rows, a, b, c in ((slice(0, HALF), r1, t2, r3), (slice(HALF, PIXELS), t1, r2, t3)):
        left = own[rows, :128] + jnp.where(low, 0.0, a)
        right = own[rows, 128:] + jnp.where(low, b, c)
        acts[rows, :128] = jnp.maximum(left, 0.0).astype(BF16)
        acts[rows, 128:] = jnp.maximum(right, 0.0).astype(BF16)


def activations_of(row, own, received):
    return pl.pallas_call(
        activation_kernel,
        out_shape=jax.ShapeDtypeStruct((PIXELS, 4 * W), BF16),
        in_specs=[pl.BlockSpec(memory_space=pltpu.SMEM)]
        + [pl.BlockSpec(memory_space=pltpu.VMEM)] * 7,
        out_specs=pl.BlockSpec(memory_space=pltpu.VMEM),
        scratch_shapes=[pltpu.VMEM((8, HALF, 128), F32)],
        compiler_params=pltpu.CompilerParams(vmem_limit_bytes=8 * 2**20),
        name="activations",
    )(row, own, *received)


def head_kernel(row_ref, member_ref, a0, a1, a2, a3, project, bias, cotangent, order, order_t, *refs):
    head_out, grads, sends, ordered, packed = refs[0], refs[1], refs[2:8], refs[8], refs[9]
    member = member_ref[0]

    def rows_of(who):
        at = pl.multiple_of(who * W, W)
        return jnp.concatenate([project[k, pl.ds(at, W), :] for k in range(4)], 0)

    own_rows = rows_of(member)
    pre = nn(a0[...], own_rows) + bias[...]
    for flip, acts in ((1, a1), (2, a2), (3, a3)):
        pre = pre + nn(acts[...], rows_of(member ^ flip))
    mine = jnp.zeros((PIXELS, W), F32)
    for q in range(4):
        mine = mine + jnp.where(member == q, pre[:, q * W : (q + 1) * W], 0.0)
    mine = jnp.maximum(mine, 0.0).astype(BF16)

    def put(at, value):
        head_out[at : at + 192, :] = value

    from_blocks(order_t[...], mine, put)
    for g in range(3):
        moved = nn(order[...], cotangent[g * 192 : (g + 1) * 192, :])
        for m in range(4):
            at = m * BLOCK + g * 48
            ordered[at : at + 48, :] = moved[m * 48 : (m + 1) * 48]
    head_grad = jnp.where(pre > 0, ordered[...], 0.0).astype(BF16)
    act_grad = nt(head_grad, own_rows)
    grad = jnp.where(a0[...].astype(F32) > 0, act_grad, 0.0)
    grads[...] = grad.astype(BF16)
    low = low_lanes((HALF, 128))
    left, right = grad[:, :128], grad[:, 128:]
    packed[0] = jnp.where(low, pltpu.roll(left[:HALF], W, 1), left[HALF:]).astype(BF16)
    packed[1] = jnp.where(low, right[:HALF], pltpu.roll(right[HALF:], W, 1)).astype(BF16)
    packed[2] = jnp.where(low, pltpu.roll(right[:HALF], W, 1), right[HALF:]).astype(BF16)
    for n, x in enumerate(SWAPS):
        apart = jnp.abs((row_ref[0] ^ x) - row_ref[0])
        sends[n][...] = packed[jnp.where(apart <= 3, apart - 1, 0)]


def head(row, member, acts, project, bias, cotangent, order, order_t):
    return pl.pallas_call(
        head_kernel,
        out_shape=[
            jax.ShapeDtypeStruct((PIXELS, W), BF16),
            jax.ShapeDtypeStruct((PIXELS, 4 * W), BF16),
        ]
        + [jax.ShapeDtypeStruct((HALF, 128), BF16)] * 6,
        in_specs=[pl.BlockSpec(memory_space=pltpu.SMEM)] * 2
        + [pl.BlockSpec(memory_space=pltpu.VMEM)] * 9,
        out_specs=[pl.BlockSpec(memory_space=pltpu.VMEM)] * 8,
        scratch_shapes=[pltpu.VMEM((PIXELS, 256), F32), pltpu.VMEM((3, HALF, 128), BF16)],
        compiler_params=pltpu.CompilerParams(vmem_limit_bytes=12 * 2**20),
        name="head",
    )(row, member, *acts, project, bias, cotangent, order, order_t)


def fetch_grad_taps(dilated, point, weights, sems, columns):
    fetches = [
        pltpu.make_async_copy(point.at[:, columns], weights.at[pl.ds(0, W)], sems.at[27])
    ]
    for q, tap in enumerate(GRAD_TAPS):
        fetches.append(
            pltpu.make_async_copy(
                dilated.at[tap_index(tap), :, columns],
                weights.at[pl.ds((q + 1) * W, W)],
                sems.at[q],
            )
        )
    for fetch in fetches:
        fetch.start()
    return fetches


def first_grad_kernel(row_ref, member_ref, own, *refs):
    recv, dilated, point = refs[:6], refs[6], refs[7]
    out, stack, arrivals, pairs, twice, weights, sems = refs[8:]
    row = row_ref[0]
    columns = pl.ds(pl.multiple_of((member_ref[0] ^ 3) * 512, 512), 512)
    fetches = fetch_grad_taps(dilated, point, weights, sems, columns)
    gather_arrivals(recv, arrivals)
    low = low_lanes((HALF, 128))
    low_all = low_lanes((PIXELS, 128))
    for k in (1, 2, 3):
        p = arrivals[arrival_slot(row, row + k)].astype(F32)
        m = arrivals[arrival_slot(row, row - k)].astype(F32)
        pairs[k - 1, :HALF, :] = jnp.where(low, p, pltpu.roll(m, W, 1)).astype(BF16)
        pairs[k - 1, HALF:, :] = jnp.where(low, pltpu.roll(p, W, 1), m).astype(BF16)
        g = own[:, :128].astype(F32) if k == 1 else own[:, 128:].astype(F32)
        other = pltpu.roll(g, W, 1)
        both = jnp.where(low_all, g, other) if k == 2 else jnp.where(low_all, other, g)
        twice[k - 1] = both.astype(BF16)
    stack[:, :256] = own[...]
    nothing = jnp.zeros((BLOCK, 128), BF16)
    for q, (k, j) in enumerate(OUT_PAIRS):
        lanes = slice(256 + q * 128, 384 + q * 128)
        for m in range(4):
            source = m - (j - 1) * k
            value = nothing
            if 0 <= source < 4:
                value = pairs[k - 1, source * BLOCK : (source + 1) * BLOCK, :]
            stack[m * BLOCK : (m + 1) * BLOCK, lanes] = value
    low_block = low_lanes((BLOCK, 128))
    for k in (1, 2, 3):
        lanes = slice(1408 + (k - 1) * 128, 1536 + (k - 1) * 128)
        for m in range(4):
            halves = []
            for source in (m + k, m - k):
                value = nothing
                if 0 <= source < 4:
                    value = twice[k - 1, source * BLOCK : (source + 1) * BLOCK, :]
                halves.append(value)
            stack[m * BLOCK : (m + 1) * BLOCK, lanes] = jnp.where(low_block, *halves)
    for fetch in fetches:
        fetch.wait()
    out[...] = nn(stack[...], weights[...]).astype(BF16)


def grad_cost(columns):
    return pl.CostEstimate(
        flops=2 * PIXELS * 28 * W * columns, bytes_accessed=6 * 10**6, transcendentals=0
    )


def first_grad(row, member, own, received, dilated, point):
    return pl.pallas_call(
        first_grad_kernel,
        out_shape=[
            jax.ShapeDtypeStruct((PIXELS, 512), BF16),
            jax.ShapeDtypeStruct((PIXELS, 28 * W), BF16),
        ],
        in_specs=[pl.BlockSpec(memory_space=pltpu.SMEM)] * 2
        + [pl.BlockSpec(memory_space=pltpu.VMEM)] * 7
        + [pl.BlockSpec(memory_space=pl.ANY)] * 2,
        out_specs=[pl.BlockSpec(memory_space=pltpu.VMEM)] * 2,
        scratch_shapes=[
            pltpu.VMEM((8, HALF, 128), BF16),
            pltpu.VMEM((3, PIXELS, 128), BF16),
            pltpu.VMEM((3, PIXELS, 128), BF16),
            pltpu.VMEM((28 * W, 512), BF16),
            pltpu.SemaphoreType.DMA((28,)),
        ],
        compiler_params=pltpu.CompilerParams(vmem_limit_bytes=16 * 2**20),
        cost_estimate=grad_cost(512),
        name="first_grad",
    )(row, member, own, *received, dilated, point)


def more_grad_kernel(flips, member_ref, stack, dilated, point, *refs):
    outs, (weights, sems) = refs[:-2], refs[-2:]
    fetches = []
    for n, flip in enumerate(flips):
        columns = pl.ds(pl.multiple_of((member_ref[0] ^ flip) * 512, 512), 512)
        fetches.append(fetch_grad_taps(dilated, point, weights.at[n], sems.at[n], columns))
    for n in range(len(flips)):
        for fetch in fetches[n]:
            fetch.wait()
        outs[n][...] = nn(stack[...], weights[n]).astype(BF16)


def more_grad(flips, member, stack, dilated, point):
    return pl.pallas_call(
        functools.partial(more_grad_kernel, flips),
        out_shape=[jax.ShapeDtypeStruct((PIXELS, 512), BF16)] * len(flips),
        in_specs=[pl.BlockSpec(memory_space=pltpu.SMEM)]
        + [pl.BlockSpec(memory_space=pltpu.VMEM)]
        + [pl.BlockSpec(memory_space=pl.ANY)] * 2,
        out_specs=[pl.BlockSpec(memory_space=pltpu.VMEM)] * len(flips),
        scratch_shapes=[
            pltpu.VMEM((len(flips), 28 * W, 512), BF16),
            pltpu.SemaphoreType.DMA((len(flips), 28)),
        ],
        compiler_params=pltpu.CompilerParams(vmem_limit_bytes=16 * 2**20),
        cost_estimate=grad_cost(512 * len(flips)),
        name="more_grad",
    )(member, stack, dilated, point)


def last_kernel(a, b, c, order_t, out):
    total = a[...].astype(F32) + b[...].astype(F32) + c[...].astype(F32)

    def put(at, value):
        out[at : at + 192, :] = value

    from_blocks(order_t[...], total.astype(BF16), put)


def last_sum(a, b, c, order_t):
    return pl.pallas_call(
        last_kernel,
        out_shape=jax.ShapeDtypeStruct((PIXELS, 512), BF16),
        in_specs=[pl.BlockSpec(memory_space=pltpu.VMEM)] * 4,
        out_specs=pl.BlockSpec(memory_space=pltpu.VMEM),
        compiler_params=pltpu.CompilerParams(vmem_limit_bytes=10 * 2**20),
        name="last_sum",
    )(a, b, c, order_t)


def flipped(x, bit):
    return lax.ppermute(x, "filt", [(i, i ^ bit) for i in range(lax.axis_size("filt"))])


def swapped(x, bits):
    pairs = [(r, r ^ bits) for r in range(8) if abs((r ^ bits) - r) <= 3]
    return lax.ppermute(x, "rows", pairs)


def on_device(
    features, point_weight, dilated_weight, branch_bias, project_weight, project_bias, cotangent
):
    row = lax.axis_index("rows").astype(jnp.int32).reshape(1)
    member = lax.axis_index("filt").astype(jnp.int32).reshape(1)
    order = jnp.asarray(order_matrix(), BF16)
    order_t = jnp.asarray(order_matrix().T, BF16)
    flat = features.reshape(PIXELS, CHANNELS)
    dilated = jnp.transpose(dilated_weight, (0, 1, 2, 4, 3)).reshape(27, W, CHANNELS)
    point = point_weight.T
    bias = branch_bias.reshape(1, 4 * W)
    *sums, ordered = odd_sums(row, flat, dilated, order)
    received = [swapped(sums[n], SWAPS[n]) for n in range(4)]
    sums = even_sums(row, ordered, dilated)
    received += [swapped(sums[n], SWAPS[4 + n]) for n in range(2)]
    own = own_sums(ordered, dilated, point, bias)
    acts = activations_of(row, own, received)
    across = flipped(acts, 2)
    beside = flipped(acts, 1)
    corner = flipped(across, 1)
    head_output, grads, *sends = head(
        row,
        member,
        (acts, beside, across, corner),
        project_weight,
        project_bias.reshape(1, 256),
        cotangent.reshape(PIXELS, 256),
        order,
        order_t,
    )
    arrived = [swapped(sends[n], x) for n, x in enumerate(SWAPS)]
    away, stack = first_grad(row, member, grads, arrived, dilated, point)
    shared = flipped(away, 1)
    (kept,) = more_grad((2,), member, stack, dilated, point)
    crossing = (shared.astype(F32) + kept.astype(F32)).astype(BF16)
    crossed = flipped(crossing, 2)
    crossing, later = lax.optimization_barrier((crossing, member))
    away, kept = more_grad((1, 0), later, stack, dilated, point)
    feature_grad = last_sum(kept, flipped(away, 1), crossed, order_t)
    return head_output.reshape(12, 48, W), feature_grad.reshape(12, 48, 512)


def solution(mesh):
    body = on_device if fits(mesh) else on_device_general
    in_specs = (
        P("rows", None, None),
        P(None, "filt"),
        P(None, None, None, None, "filt"),
        P(None, "filt"),
        P(),
        P(),
        P("rows", None, None),
    )
    out_specs = (P("rows", None, "filt"), P("rows", None, "filt"))
    return jax.shard_map(
        body, mesh=mesh, in_specs=in_specs, out_specs=out_specs, check_vma=False
    )
```

```python
import functools

import jax
import jax.numpy as jnp
import numpy as np
from jax import lax
from jax.experimental import pallas as pl
from jax.experimental.pallas import tpu as pltpu
from jax.sharding import PartitionSpec as P

FIRST_DILATION = 12
SECOND_DILATION = 24
THIRD_DILATION = 36


def passed_along(x, axis, by):
    devices = lax.axis_size(axis)
    pairs = [(i, i + by) for i in range(devices) if 0 <= i + by < devices]
    return lax.ppermute(x, axis, pairs)


def shift_columns(field, amount):
    breadth = field.shape[1]
    if amount == 0:
        return field
    padding = [(0, 0)] * field.ndim
    if amount > 0:
        kept = field[:, amount:]
        padding[1] = (0, amount)
    else:
        kept = field[:, : breadth + amount]
        padding[1] = (-amount, 0)
    return jnp.pad(kept, padding)


def fetch_sums(field, offset):
    return passed_along(field, "rows", offset)


def fetch_grads(field, offset):
    return passed_along(field, "rows", offset)


def shift_rows(field, amount, fetcher):
    height = field.shape[0]
    quotient = amount // height

    def extract_block(offset):
        if offset == 0:
            return field
        return fetcher(field, offset)

    return extract_block(quotient)


def make_kernel_taps(variants, dilation_rates):
    stacked = [variants[:, :, 0]]
    for branch, dilation in enumerate(dilation_rates):
        for row_tap in range(3):
            source = variants[:, :, 1 + 3 * branch + row_tap]
            for col_tap in range(3):
                stacked.append(shift_columns(source, -(col_tap - 1) * dilation))
    return jnp.stack(stacked, 2)


def on_device_general(
    features, point_weight, dilated_weight, branch_bias, project_weight, project_bias, cotangent
):
    height, breadth, channels = features.shape
    pixels = height * breadth
    own_width = point_weight.shape[1]
    filters = lax.axis_size("filt")
    member = lax.axis_index("filt")
    branch_outputs = project_weight.shape[2]
    own_out = branch_outputs // filters
    own_channels = channels // filters
    dilation_rates = (FIRST_DILATION, SECOND_DILATION, THIRD_DILATION)
    all_weights = jnp.concatenate(
        [point_weight[None], dilated_weight.reshape(27, channels, own_width)], 0
    )
    flattened = features.reshape(pixels, channels)
    tap_terms = jnp.einsum(
        "pc,tco->pto", flattened, all_weights, preferred_element_type=jnp.float32
    )
    tap_terms = tap_terms.reshape(height, breadth, 28, own_width)
    pre_list = [tap_terms[:, :, 0, :] + branch_bias[0]]
    for branch, dilation in enumerate(dilation_rates):
        summed_result = jnp.zeros((height, breadth, own_width), jnp.float32)
        for row_tap in range(3):
            row_sum = jnp.zeros((height, breadth, own_width), jnp.float32)
            for col_tap in range(3):
                row_sum = row_sum + shift_columns(
                    tap_terms[:, :, 1 + 9 * branch + 3 * row_tap + col_tap, :],
                    (col_tap - 1) * dilation,
                )
            summed_result = summed_result + shift_rows(
                row_sum, -(row_tap - 1) * dilation, fetch_sums
            )
        pre_list.append(summed_result + branch_bias[branch + 1])
    branch_pre = jnp.stack(pre_list, 2)
    activations = jnp.maximum(branch_pre, 0.0).astype(jnp.bfloat16).reshape(pixels, 4 * own_width)
    grouped = project_weight.reshape(4, filters, own_width, branch_outputs)
    own_rows = lax.dynamic_index_in_dim(grouped, member, 1, keepdims=False).reshape(
        4 * own_width, branch_outputs
    )
    flat_cotangent = cotangent.reshape(pixels, branch_outputs)
    ordered = jnp.transpose(grouped, (1, 0, 2, 3)).reshape(filters * 4 * own_width, branch_outputs)
    project_pre = jnp.dot(
        lax.all_gather(activations, "filt", axis=1, tiled=True),
        ordered,
        preferred_element_type=jnp.float32,
    )
    project_pre = project_pre + project_bias
    head_grad = jnp.where(project_pre > 0, flat_cotangent.astype(jnp.float32), 0.0).astype(
        jnp.bfloat16
    )
    own_pre = lax.dynamic_slice_in_dim(project_pre, member * own_out, own_out, 1)
    act_grad = jnp.dot(head_grad, own_rows.T, preferred_element_type=jnp.float32)
    head_output = jnp.maximum(own_pre, 0.0).astype(jnp.bfloat16).reshape(height, breadth, own_out)
    branch_grad = jnp.where(
        branch_pre > 0, act_grad.reshape(height, breadth, 4, own_width), 0.0
    ).astype(jnp.bfloat16)
    variant_list = [branch_grad[:, :, 0, :]]
    for branch, dilation in enumerate(dilation_rates):
        for row_tap in range(3):
            variant_list.append(
                shift_rows(branch_grad[:, :, branch + 1, :], (row_tap - 1) * dilation, fetch_grads)
            )
    variants = jnp.stack(variant_list, 2)
    stacked = make_kernel_taps(variants, dilation_rates).reshape(pixels, 28, own_width)
    input_grad = lax.psum_scatter(
        jnp.einsum("pto,tco->cp", stacked, all_weights, preferred_element_type=jnp.float32),
        "filt",
        scatter_dimension=0,
        tiled=True,
    ).T
    feature_grad = input_grad.astype(jnp.bfloat16).reshape(height, breadth, own_channels)
    return (head_output, feature_grad)


W = 64
BLOCK = 144
PIXELS = 576
HALF = 288
CHANNELS = 2048
F32 = jnp.float32
BF16 = jnp.bfloat16

OUT_PAIRS = ((3, 1), (1, 1), (3, 0), (1, 0), (3, 2), (1, 2), (2, 1), (2, 0), (2, 2))
TAPS = (
    [(k, 1, 1) for k in (1, 2, 3)]
    + [(k, i, j) for k, j in OUT_PAIRS for i in (0, 2)]
    + [(k, 1, j) for j in (0, 2) for k in (1, 2, 3)]
)
ODD_AT, EVEN_AT, LEFT_AT, RIGHT_AT = 4 * W, 16 * W, 22 * W, 25 * W
SWAPS = (5, 7, 3, 1, 6, 2)


def fits(mesh):
    return mesh.shape["rows"] == 8 and mesh.shape["filt"] == 4


def order_matrix():
    to = np.zeros((192, 192), np.float32)
    for m in range(4):
        for r in range(4):
            for c in range(12):
                to[m * 48 + r * 12 + c, r * 48 + m * 12 + c] = 1
    return to


def tap_index(tap):
    k, i, j = tap
    return (k - 1) * 9 + i * 3 + j


def nt(a, b):
    return lax.dot_general(a, b, (((1,), (1,)), ((), ())), preferred_element_type=F32)


def nn(a, b):
    return lax.dot_general(a, b, (((1,), (0,)), ((), ())), preferred_element_type=F32)


def into_blocks(order, read, write):
    for g in range(3):
        moved = nn(order, read(g * 192)).astype(BF16)
        for m in range(4):
            write(m * BLOCK + g * 48, moved[m * 48 : (m + 1) * 48])


def from_blocks(order_t, value, write):
    for g in range(3):
        parts = [value[m * BLOCK + g * 48 : m * BLOCK + g * 48 + 48] for m in range(4)]
        write(g * 192, nn(order_t, jnp.concatenate(parts, 0)).astype(BF16))


def low_lanes(shape):
    return lax.broadcasted_iota(jnp.int32, shape, 1) % 128 < W


def outward_slot(row, x):
    other = row ^ x
    apart = jnp.abs(other - row)
    slot = apart - 1 + jnp.where(other < row, 3, 0)
    return jnp.where(apart <= 3, slot, 0)


def pack_rows(sums, packed, k):
    low = low_lanes((HALF, 128))
    top, bottom = sums[k - 1, :HALF, :], sums[k - 1, HALF:, :]
    packed[k - 1] = jnp.where(low, top, pltpu.roll(bottom, W, 1))
    packed[k + 2] = jnp.where(low, pltpu.roll(top, W, 1), bottom)


def odd_kernel(row_ref, features, dilated, point, order, *refs):
    out, ordered, weights = refs[0:4], refs[4], refs[5]
    raw, sums, packed, feature_sems, weight_sems = refs[6:]
    loads = []
    for g in range(3):
        rows = pl.ds(g * 192, 192)
        loads.append(pltpu.make_async_copy(features.at[rows], raw.at[rows], feature_sems.at[g]))
        loads[-1].start()
    fetches = [pltpu.make_async_copy(point, weights.at[pl.ds(0, W)], weight_sems.at[0])]
    for q, tap in enumerate(TAPS):
        fetches.append(
            pltpu.make_async_copy(
                dilated.at[tap_index(tap)],
                weights.at[pl.ds((q + 1) * W, W)],
                weight_sems.at[q + 1],
            )
        )
    for fetch in fetches[4:] + fetches[:4]:
        fetch.start()
    for g in range(3):
        loads[g].wait()
        moved = nn(order[...], raw[g * 192 : (g + 1) * 192, :]).astype(BF16)
        for m in range(4):
            at = m * BLOCK + g * 48
            ordered[at : at + 48, :] = moved[m * 48 : (m + 1) * 48]

    def product(pair, first, last):
        for fetch in fetches[4 + 2 * pair : 8 + 2 * pair]:
            fetch.wait()
        at = ODD_AT + pair * 128
        return nt(ordered[first * BLOCK : last * BLOCK, :], weights[at : at + 256, :])

    d = product(0, 0, 4)
    sums[2] = d[:, :128]
    sums[0] = d[:, 128:]
    d = product(2, 0, 3)
    sums[2, 3 * BLOCK :, :] = sums[2, 3 * BLOCK :, :] + d[:BLOCK, :128]
    sums[0, BLOCK:, :] = sums[0, BLOCK:, :] + d[:, 128:]
    d = product(4, 1, 4)
    sums[2, :BLOCK, :] = sums[2, :BLOCK, :] + d[2 * BLOCK :, :128]
    sums[0, : 3 * BLOCK, :] = sums[0, : 3 * BLOCK, :] + d[:, 128:]
    pack_rows(sums, packed, 3)
    pack_rows(sums, packed, 1)
    for n in range(4):
        out[n][...] = packed[outward_slot(row_ref[0], SWAPS[n])]
    for fetch in fetches[:4] + fetches[16:]:
        fetch.wait()


def odd_sums(row, features, dilated, point, order):
    return pl.pallas_call(
        odd_kernel,
        out_shape=[jax.ShapeDtypeStruct((HALF, 128), F32)] * 4
        + [pltpu.VMEM((PIXELS, CHANNELS), BF16), pltpu.VMEM((28 * W, CHANNELS), BF16)],
        in_specs=[pl.BlockSpec(memory_space=pltpu.SMEM)]
        + [pl.BlockSpec(memory_space=pltpu.HBM)] * 3
        + [pl.BlockSpec(memory_space=pltpu.VMEM)],
        out_specs=[pl.BlockSpec(memory_space=pltpu.VMEM)] * 6,
        scratch_shapes=[
            pltpu.VMEM((PIXELS, CHANNELS), BF16),
            pltpu.VMEM((3, PIXELS, 128), F32),
            pltpu.VMEM((6, HALF, 128), F32),
            pltpu.SemaphoreType.DMA((3,)),
            pltpu.SemaphoreType.DMA((28,)),
        ],
        compiler_params=pltpu.CompilerParams(vmem_limit_bytes=28 * 2**20),
        name="odd_sums",
    )(row, features, dilated, point, order)


def even_kernel(row_ref, ordered, weights, *refs):
    out = refs[0:2]
    sums, packed = refs[2:]
    d = nt(ordered[...], weights[EVEN_AT : EVEN_AT + 384, :])
    sums[1] = d[:, :128]
    sums[1, 2 * BLOCK :, :] = sums[1, 2 * BLOCK :, :] + d[: 2 * BLOCK, 128:256]
    sums[1, : 2 * BLOCK, :] = sums[1, : 2 * BLOCK, :] + d[2 * BLOCK :, 256:]
    pack_rows(sums, packed, 2)
    for n in range(2):
        slot = jnp.where((row_ref[0] ^ SWAPS[4 + n]) < row_ref[0], 4, 1)
        out[n][...] = packed[slot]


def even_sums(row, ordered, weights):
    return pl.pallas_call(
        even_kernel,
        out_shape=[jax.ShapeDtypeStruct((HALF, 128), F32)] * 2,
        in_specs=[
            pl.BlockSpec(memory_space=pltpu.SMEM),
            pl.BlockSpec(memory_space=pltpu.VMEM),
            pl.BlockSpec(memory_space=pltpu.VMEM),
        ],
        out_specs=[pl.BlockSpec(memory_space=pltpu.VMEM)] * 2,
        scratch_shapes=[
            pltpu.VMEM((3, PIXELS, 128), F32),
            pltpu.VMEM((6, HALF, 128), F32),
        ],
        compiler_params=pltpu.CompilerParams(vmem_limit_bytes=18 * 2**20),
        cost_estimate=pl.CostEstimate(flops=10**6, bytes_accessed=10**4, transcendentals=0),
        name="even_sums",
    )(row, ordered, weights)


def own_kernel(ordered, weights, bias, out):
    out[...] = nt(ordered[...], weights[:256, :]) + bias[...]
    low = low_lanes((PIXELS, 128))

    def add(first, value, k):
        lanes = slice(0, 128) if k == 1 else slice(128, 256)
        rows = slice(first * BLOCK, first * BLOCK + value.shape[0])
        mask = low[: value.shape[0]]
        kept = jnp.where(mask, value[:, lanes], 0.0) if k == 2 else jnp.where(mask, 0.0, value[:, lanes])
        out[rows, lanes] = out[rows, lanes] + kept

    d = nt(ordered[: 3 * BLOCK, :], weights[LEFT_AT - W : LEFT_AT + 3 * W, :])
    for k in (1, 2, 3):
        add(k, d[: (4 - k) * BLOCK], k)
    d = nt(ordered[BLOCK:, :], weights[RIGHT_AT - W : RIGHT_AT + 3 * W, :])
    for k in (1, 2, 3):
        add(0, d[(k - 1) * BLOCK :], k)


def own_sums(ordered, weights, bias):
    return pl.pallas_call(
        own_kernel,
        out_shape=jax.ShapeDtypeStruct((PIXELS, 4 * W), F32),
        in_specs=[pl.BlockSpec(memory_space=pltpu.VMEM)] * 3,
        out_specs=pl.BlockSpec(memory_space=pltpu.VMEM),
        compiler_params=pltpu.CompilerParams(vmem_limit_bytes=18 * 2**20),
        cost_estimate=pl.CostEstimate(flops=10**6, bytes_accessed=10**4, transcendentals=0),
        name="own_sums",
    )(ordered, weights, bias)


def arrival_slot(row, other):
    return jnp.where((other >= 0) & (other < 8), row ^ other, 0)


def gather_arrivals(recv, arrivals):
    arrivals[0] = jnp.zeros((HALF, 128), arrivals.dtype)
    for n, x in enumerate(SWAPS):
        arrivals[x] = recv[n][...]


def activation_kernel(row_ref, own, *refs):
    recv, acts, arrivals = refs[:6], refs[6], refs[7]
    row = row_ref[0]
    gather_arrivals(recv, arrivals)
    low = low_lanes((HALF, 128))
    t1, t2, t3 = (
        arrivals[arrival_slot(row, row - k)] + arrivals[arrival_slot(row, row + k)]
        for k in (1, 2, 3)
    )
    r1, r2, r3 = (pltpu.roll(t, W, 1) for t in (t1, t2, t3))
    for rows, a, b, c in ((slice(0, HALF), r1, t2, r3), (slice(HALF, PIXELS), t1, r2, t3)):
        left = own[rows, :128] + jnp.where(low, 0.0, a)
        right = own[rows, 128:] + jnp.where(low, b, c)
        acts[rows, :128] = jnp.maximum(left, 0.0).astype(BF16)
        acts[rows, 128:] = jnp.maximum(right, 0.0).astype(BF16)


def activations_of(row, own, received):
    return pl.pallas_call(
        activation_kernel,
        out_shape=jax.ShapeDtypeStruct((PIXELS, 4 * W), BF16),
        in_specs=[pl.BlockSpec(memory_space=pltpu.SMEM)]
        + [pl.BlockSpec(memory_space=pltpu.VMEM)] * 7,
        out_specs=pl.BlockSpec(memory_space=pltpu.VMEM),
        scratch_shapes=[pltpu.VMEM((8, HALF, 128), F32)],
        compiler_params=pltpu.CompilerParams(vmem_limit_bytes=8 * 2**20),
        name="activations",
    )(row, own, *received)


def head_kernel(row_ref, member_ref, a0, a1, a2, a3, project, bias, cotangent, order, order_t, *refs):
    head_out, grads, sends, ordered, packed = refs[0], refs[1], refs[2:8], refs[8], refs[9]
    member = member_ref[0]

    def rows_of(who):
        at = pl.multiple_of(who * W, W)
        return jnp.concatenate([project[k, pl.ds(at, W), :] for k in range(4)], 0)

    own_rows = rows_of(member)
    pre = nn(a0[...], own_rows) + bias[...]
    for flip, acts in ((1, a1), (2, a2), (3, a3)):
        pre = pre + nn(acts[...], rows_of(member ^ flip))
    mine = jnp.zeros((PIXELS, W), F32)
    for q in range(4):
        mine = mine + jnp.where(member == q, pre[:, q * W : (q + 1) * W], 0.0)
    mine = jnp.maximum(mine, 0.0).astype(BF16)

    def put(at, value):
        head_out[at : at + 192, :] = value

    from_blocks(order_t[...], mine, put)
    for g in range(3):
        moved = nn(order[...], cotangent[g * 192 : (g + 1) * 192, :])
        for m in range(4):
            at = m * BLOCK + g * 48
            ordered[at : at + 48, :] = moved[m * 48 : (m + 1) * 48]
    head_grad = jnp.where(pre > 0, ordered[...], 0.0).astype(BF16)
    act_grad = nt(head_grad, own_rows)
    grad = jnp.where(a0[...].astype(F32) > 0, act_grad, 0.0)
    grads[...] = grad.astype(BF16)
    low = low_lanes((HALF, 128))
    left, right = grad[:, :128], grad[:, 128:]
    packed[0] = jnp.where(low, pltpu.roll(left[:HALF], W, 1), left[HALF:]).astype(BF16)
    packed[1] = jnp.where(low, right[:HALF], pltpu.roll(right[HALF:], W, 1)).astype(BF16)
    packed[2] = jnp.where(low, pltpu.roll(right[:HALF], W, 1), right[HALF:]).astype(BF16)
    for n, x in enumerate(SWAPS):
        apart = jnp.abs((row_ref[0] ^ x) - row_ref[0])
        sends[n][...] = packed[jnp.where(apart <= 3, apart - 1, 0)]


def head(row, member, acts, project, bias, cotangent, order, order_t):
    return pl.pallas_call(
        head_kernel,
        out_shape=[
            jax.ShapeDtypeStruct((PIXELS, W), BF16),
            jax.ShapeDtypeStruct((PIXELS, 4 * W), BF16),
        ]
        + [jax.ShapeDtypeStruct((HALF, 128), BF16)] * 6,
        in_specs=[pl.BlockSpec(memory_space=pltpu.SMEM)] * 2
        + [pl.BlockSpec(memory_space=pltpu.VMEM)] * 9,
        out_specs=[pl.BlockSpec(memory_space=pltpu.VMEM)] * 8,
        scratch_shapes=[pltpu.VMEM((PIXELS, 256), F32), pltpu.VMEM((3, HALF, 128), BF16)],
        compiler_params=pltpu.CompilerParams(vmem_limit_bytes=12 * 2**20),
        name="head",
    )(row, member, *acts, project, bias, cotangent, order, order_t)


def spread_kernel(row_ref, own, *refs):
    recv, stack, arrivals, pairs, twice = refs[:6], refs[6], refs[7], refs[8], refs[9]
    row = row_ref[0]
    gather_arrivals(recv, arrivals)
    low = low_lanes((HALF, 128))
    low_all = low_lanes((PIXELS, 128))
    for k in (1, 2, 3):
        p = arrivals[arrival_slot(row, row + k)].astype(F32)
        m = arrivals[arrival_slot(row, row - k)].astype(F32)
        pairs[k - 1, :HALF, :] = jnp.where(low, p, pltpu.roll(m, W, 1)).astype(BF16)
        pairs[k - 1, HALF:, :] = jnp.where(low, pltpu.roll(p, W, 1), m).astype(BF16)
        g = own[:, :128].astype(F32) if k == 1 else own[:, 128:].astype(F32)
        other = pltpu.roll(g, W, 1)
        both = jnp.where(low_all, g, other) if k == 2 else jnp.where(low_all, other, g)
        twice[k - 1] = both.astype(BF16)
    stack[:, : 4 * W] = own[...]
    nothing = jnp.zeros((BLOCK, 128), BF16)

    def block_of(ref, k, source):
        if 0 <= source < 4:
            return ref[k - 1, source * BLOCK : (source + 1) * BLOCK, :]
        return nothing

    for q, (k, j) in enumerate(OUT_PAIRS):
        lanes = slice(ODD_AT + q * 128, ODD_AT + q * 128 + 128)
        for m in range(4):
            stack[m * BLOCK : (m + 1) * BLOCK, lanes] = block_of(pairs, k, m - (j - 1) * k)
    low_block = low_lanes((BLOCK, 128))
    for q, (a, b) in enumerate(((1, 2), (3, -1), (-2, -3))):
        lanes = slice(LEFT_AT + q * 128, LEFT_AT + q * 128 + 128)
        for m in range(4):
            stack[m * BLOCK : (m + 1) * BLOCK, lanes] = jnp.where(
                low_block, block_of(twice, abs(a), m + a), block_of(twice, abs(b), m + b)
            )


def spread(row, own, received):
    return pl.pallas_call(
        spread_kernel,
        out_shape=pltpu.VMEM((PIXELS, 28 * W), BF16),
        in_specs=[pl.BlockSpec(memory_space=pltpu.SMEM)]
        + [pl.BlockSpec(memory_space=pltpu.VMEM)] * 7,
        out_specs=pl.BlockSpec(memory_space=pltpu.VMEM),
        scratch_shapes=[
            pltpu.VMEM((8, HALF, 128), BF16),
            pltpu.VMEM((3, PIXELS, 128), BF16),
            pltpu.VMEM((3, PIXELS, 128), BF16),
        ],
        compiler_params=pltpu.CompilerParams(vmem_limit_bytes=12 * 2**20),
        name="spread",
    )(row, own, *received)


def grad_kernel(flips, member_ref, stack, weights, *outs):
    for out, flip in zip(outs, flips):
        columns = pl.ds(pl.multiple_of((member_ref[0] ^ flip) * 512, 512), 512)
        out[...] = nn(stack[...], weights[:, columns]).astype(BF16)


def grads_for(flips, member, stack, weights):
    return pl.pallas_call(
        functools.partial(grad_kernel, flips),
        out_shape=[jax.ShapeDtypeStruct((PIXELS, 512), BF16)] * len(flips),
        in_specs=[pl.BlockSpec(memory_space=pltpu.SMEM)]
        + [pl.BlockSpec(memory_space=pltpu.VMEM)] * 2,
        out_specs=[pl.BlockSpec(memory_space=pltpu.VMEM)] * len(flips),
        compiler_params=pltpu.CompilerParams(vmem_limit_bytes=18 * 2**20),
        cost_estimate=pl.CostEstimate(
            flops=2 * PIXELS * 28 * W * 512 * len(flips), bytes_accessed=10**6, transcendentals=0
        ),
        name="grads_for",
    )(member, stack, weights)


def last_kernel(a, b, c, order_t, out):
    total = a[...].astype(F32) + b[...].astype(F32) + c[...].astype(F32)

    def put(at, value):
        out[at : at + 192, :] = value

    from_blocks(order_t[...], total.astype(BF16), put)


def last_sum(a, b, c, order_t):
    return pl.pallas_call(
        last_kernel,
        out_shape=jax.ShapeDtypeStruct((PIXELS, 512), BF16),
        in_specs=[pl.BlockSpec(memory_space=pltpu.VMEM)] * 4,
        out_specs=pl.BlockSpec(memory_space=pltpu.VMEM),
        compiler_params=pltpu.CompilerParams(vmem_limit_bytes=10 * 2**20),
        name="last_sum",
    )(a, b, c, order_t)


def flipped(x, bit):
    return lax.ppermute(x, "filt", [(i, i ^ bit) for i in range(lax.axis_size("filt"))])


def swapped(x, bits):
    pairs = [(r, r ^ bits) for r in range(8) if abs((r ^ bits) - r) <= 3]
    return lax.ppermute(x, "rows", pairs)


def on_device(
    features, point_weight, dilated_weight, branch_bias, project_weight, project_bias, cotangent
):
    row = lax.axis_index("rows").astype(jnp.int32).reshape(1)
    member = lax.axis_index("filt").astype(jnp.int32).reshape(1)
    order = jnp.asarray(order_matrix(), BF16)
    order_t = jnp.asarray(order_matrix().T, BF16)
    flat = features.reshape(PIXELS, CHANNELS)
    dilated = jnp.transpose(dilated_weight, (0, 1, 2, 4, 3)).reshape(27, W, CHANNELS)
    point = point_weight.T
    bias = branch_bias.reshape(1, 4 * W)
    flat, dilated, point = (
        pltpu.with_memory_space_constraint(x, pltpu.HBM) for x in (flat, dilated, point)
    )
    *sums, ordered, weights = odd_sums(row, flat, dilated, point, order)
    received = [swapped(sums[n], SWAPS[n]) for n in range(4)]
    sums = even_sums(row, ordered, weights)
    received += [swapped(sums[n], SWAPS[4 + n]) for n in range(2)]
    own = own_sums(ordered, weights, bias)
    acts = activations_of(row, own, received)
    across = flipped(acts, 2)
    beside = flipped(acts, 1)
    corner = flipped(across, 1)
    head_output, grads, *sends = head(
        row,
        member,
        (acts, beside, across, corner),
        project_weight,
        project_bias.reshape(1, 256),
        cotangent.reshape(PIXELS, 256),
        order,
        order_t,
    )
    arrived = [swapped(sends[n], x) for n, x in enumerate(SWAPS)]
    stack = spread(row, grads, arrived)
    near, far = grads_for((1, 3), member, stack, weights)
    near, far = flipped(near, 1), flipped(far, 1)
    (kept,) = grads_for((2,), member, stack, weights)
    crossing = (far.astype(F32) + kept.astype(F32)).astype(BF16)
    crossed = flipped(crossing, 2)
    later, crossing = lax.optimization_barrier((member, crossing))
    (kept,) = grads_for((0,), later, stack, weights)
    feature_grad = last_sum(kept, near, crossed, order_t)
    return head_output.reshape(12, 48, W), feature_grad.reshape(12, 48, 512)


def solution(mesh):
    body = on_device if fits(mesh) else on_device_general
    in_specs = (
        P("rows", None, None),
        P(None, "filt"),
        P(None, None, None, None, "filt"),
        P(None, "filt"),
        P(),
        P(),
        P("rows", None, None),
    )
    out_specs = (P("rows", None, "filt"), P("rows", None, "filt"))
    return jax.shard_map(
        body, mesh=mesh, in_specs=in_specs, out_specs=out_specs, check_vma=False
    )
```

```python
import functools

import jax
import jax.numpy as jnp
from jax import lax
from jax.experimental import pallas as pl
from jax.experimental.pallas import tpu as pltpu
from jax.sharding import PartitionSpec as P

FIRST_DILATION = 12
SECOND_DILATION = 24
THIRD_DILATION = 36


def passed_along(x, axis, by):
    devices = lax.axis_size(axis)
    pairs = [(i, i + by) for i in range(devices) if 0 <= i + by < devices]
    return lax.ppermute(x, axis, pairs)


def shift_columns(field, amount):
    breadth = field.shape[1]
    if amount == 0:
        return field
    padding = [(0, 0)] * field.ndim
    if amount > 0:
        kept = field[:, amount:]
        padding[1] = (0, amount)
    else:
        kept = field[:, : breadth + amount]
        padding[1] = (-amount, 0)
    return jnp.pad(kept, padding)


def fetch_sums(field, offset):
    return passed_along(field, "rows", offset)


def fetch_grads(field, offset):
    return passed_along(field, "rows", offset)


def shift_rows(field, amount, fetcher):
    height = field.shape[0]
    quotient = amount // height

    def extract_block(offset):
        if offset == 0:
            return field
        return fetcher(field, offset)

    return extract_block(quotient)


def make_kernel_taps(variants, dilation_rates):
    stacked = [variants[:, :, 0]]
    for branch, dilation in enumerate(dilation_rates):
        for row_tap in range(3):
            source = variants[:, :, 1 + 3 * branch + row_tap]
            for col_tap in range(3):
                stacked.append(shift_columns(source, -(col_tap - 1) * dilation))
    return jnp.stack(stacked, 2)


def on_device_general(
    features, point_weight, dilated_weight, branch_bias, project_weight, project_bias, cotangent
):
    height, breadth, channels = features.shape
    pixels = height * breadth
    own_width = point_weight.shape[1]
    filters = lax.axis_size("filt")
    member = lax.axis_index("filt")
    branch_outputs = project_weight.shape[2]
    own_out = branch_outputs // filters
    own_channels = channels // filters
    dilation_rates = (FIRST_DILATION, SECOND_DILATION, THIRD_DILATION)
    all_weights = jnp.concatenate(
        [point_weight[None], dilated_weight.reshape(27, channels, own_width)], 0
    )
    flattened = features.reshape(pixels, channels)
    tap_terms = jnp.einsum(
        "pc,tco->pto", flattened, all_weights, preferred_element_type=jnp.float32
    )
    tap_terms = tap_terms.reshape(height, breadth, 28, own_width)
    pre_list = [tap_terms[:, :, 0, :] + branch_bias[0]]
    for branch, dilation in enumerate(dilation_rates):
        summed_result = jnp.zeros((height, breadth, own_width), jnp.float32)
        for row_tap in range(3):
            row_sum = jnp.zeros((height, breadth, own_width), jnp.float32)
            for col_tap in range(3):
                row_sum = row_sum + shift_columns(
                    tap_terms[:, :, 1 + 9 * branch + 3 * row_tap + col_tap, :],
                    (col_tap - 1) * dilation,
                )
            summed_result = summed_result + shift_rows(
                row_sum, -(row_tap - 1) * dilation, fetch_sums
            )
        pre_list.append(summed_result + branch_bias[branch + 1])
    branch_pre = jnp.stack(pre_list, 2)
    activations = jnp.maximum(branch_pre, 0.0).astype(jnp.bfloat16).reshape(pixels, 4 * own_width)
    grouped = project_weight.reshape(4, filters, own_width, branch_outputs)
    own_rows = lax.dynamic_index_in_dim(grouped, member, 1, keepdims=False).reshape(
        4 * own_width, branch_outputs
    )
    flat_cotangent = cotangent.reshape(pixels, branch_outputs)
    ordered = jnp.transpose(grouped, (1, 0, 2, 3)).reshape(filters * 4 * own_width, branch_outputs)
    project_pre = jnp.dot(
        lax.all_gather(activations, "filt", axis=1, tiled=True),
        ordered,
        preferred_element_type=jnp.float32,
    )
    project_pre = project_pre + project_bias
    head_grad = jnp.where(project_pre > 0, flat_cotangent.astype(jnp.float32), 0.0).astype(
        jnp.bfloat16
    )
    own_pre = lax.dynamic_slice_in_dim(project_pre, member * own_out, own_out, 1)
    act_grad = jnp.dot(head_grad, own_rows.T, preferred_element_type=jnp.float32)
    head_output = jnp.maximum(own_pre, 0.0).astype(jnp.bfloat16).reshape(height, breadth, own_out)
    branch_grad = jnp.where(
        branch_pre > 0, act_grad.reshape(height, breadth, 4, own_width), 0.0
    ).astype(jnp.bfloat16)
    variant_list = [branch_grad[:, :, 0, :]]
    for branch, dilation in enumerate(dilation_rates):
        for row_tap in range(3):
            variant_list.append(
                shift_rows(branch_grad[:, :, branch + 1, :], (row_tap - 1) * dilation, fetch_grads)
            )
    variants = jnp.stack(variant_list, 2)
    stacked = make_kernel_taps(variants, dilation_rates).reshape(pixels, 28, own_width)
    input_grad = lax.psum_scatter(
        jnp.einsum("pto,tco->cp", stacked, all_weights, preferred_element_type=jnp.float32),
        "filt",
        scatter_dimension=0,
        tiled=True,
    ).T
    feature_grad = input_grad.astype(jnp.bfloat16).reshape(height, breadth, own_channels)
    return (head_output, feature_grad)


W = 64
BLOCK = 144
PIXELS = 576
HALF = 288
CHANNELS = 2048
F32 = jnp.float32
BF16 = jnp.bfloat16

OUT_PAIRS = ((3, 1), (1, 1), (3, 0), (1, 0), (3, 2), (1, 2), (2, 1), (2, 0), (2, 2))
TAPS = (
    [(k, 1, 1) for k in (1, 2, 3)]
    + [(k, i, j) for k, j in OUT_PAIRS for i in (0, 2)]
    + [(k, 1, j) for j in (0, 2) for k in (1, 2, 3)]
)
ODD_AT, EVEN_AT, LEFT_AT, RIGHT_AT = 4 * W, 16 * W, 22 * W, 25 * W
SWAPS = (5, 7, 3, 1, 6, 2)
GRAD_SWAPS = (1, 5, 7, 3, 6, 2)


def fits(mesh):
    return mesh.shape["rows"] == 8 and mesh.shape["filt"] == 4


def order_matrix(turned=False):
    to = lax.broadcasted_iota(jnp.int32, (192, 192), 1 if turned else 0)
    source = lax.broadcasted_iota(jnp.int32, (192, 192), 0 if turned else 1)

    def parts(value, width):
        return sum((value >= n * width).astype(jnp.int32) for n in (1, 2, 3))

    block = parts(to, 48)
    within = to - 48 * block
    line = parts(within, 12)
    wanted = line * 48 + block * 12 + within - 12 * line
    return (source == wanted).astype(F32).astype(BF16)


def tap_index(tap):
    k, i, j = tap
    return (k - 1) * 9 + i * 3 + j


def nt(a, b):
    return lax.dot_general(a, b, (((1,), (1,)), ((), ())), preferred_element_type=F32)


def nn(a, b):
    return lax.dot_general(a, b, (((1,), (0,)), ((), ())), preferred_element_type=F32)


def from_blocks(order_t, value, write):
    for g in range(3):
        parts = [value[m * BLOCK + g * 48 : m * BLOCK + g * 48 + 48] for m in range(4)]
        write(g * 192, nn(order_t, jnp.concatenate(parts, 0)).astype(BF16))


def low_lanes(shape):
    return lax.broadcasted_iota(jnp.int32, shape, 1) % 128 < W


def outward_slot(row, x):
    other = row ^ x
    apart = jnp.abs(other - row)
    slot = apart - 1 + jnp.where(other < row, 3, 0)
    return jnp.where(apart <= 3, slot, 0)


def pack_rows(sums, packed, k):
    low = low_lanes((HALF, 128))
    top, bottom = sums[k - 1, :HALF, :], sums[k - 1, HALF:, :]
    packed[k - 1] = jnp.where(low, top, pltpu.roll(bottom, W, 1))
    packed[k + 2] = jnp.where(low, pltpu.roll(top, W, 1), bottom)


def odd_kernel(features, dilated, point, *refs):
    row = lax.axis_index("rows")
    out, ordered, weights = refs[0:4], refs[4], refs[5]
    raw, sums, packed, feature_sems, weight_sems = refs[6:]
    loads = []
    for g in range(3):
        rows = pl.ds(g * 192, 192)
        loads.append(pltpu.make_async_copy(features.at[rows], raw.at[rows], feature_sems.at[g]))
        loads[-1].start()
    fetches = [pltpu.make_async_copy(point, weights.at[pl.ds(0, W)], weight_sems.at[0])]
    for q, tap in enumerate(TAPS):
        fetches.append(
            pltpu.make_async_copy(
                dilated.at[tap_index(tap)],
                weights.at[pl.ds((q + 1) * W, W)],
                weight_sems.at[q + 1],
            )
        )
    queue = fetches[4:] + fetches[:4]

    def start_loads(first, last):
        for fetch in queue[first:last]:
            fetch.start()

    start_loads(0, 4)
    order = order_matrix()
    for g in range(3):
        loads[g].wait()
        start_loads(4 + 4 * g, 8 + 4 * g)
        moved = nn(order, raw[g * 192 : (g + 1) * 192, :]).astype(BF16)
        for m in range(4):
            at = m * BLOCK + g * 48
            ordered[at : at + 48, :] = moved[m * 48 : (m + 1) * 48]

    def product(pair, first, last):
        for fetch in fetches[4 + 2 * pair : 8 + 2 * pair]:
            fetch.wait()
        at = ODD_AT + pair * 128
        return nt(ordered[first * BLOCK : last * BLOCK, :], weights[at : at + 256, :])

    d = product(0, 0, 4)
    start_loads(16, 22)
    sums[2] = d[:, :128]
    sums[0] = d[:, 128:]
    d = product(2, 0, 3)
    start_loads(22, 28)
    sums[2, 3 * BLOCK :, :] = sums[2, 3 * BLOCK :, :] + d[:BLOCK, :128]
    sums[0, BLOCK:, :] = sums[0, BLOCK:, :] + d[:, 128:]
    d = product(4, 1, 4)
    sums[2, :BLOCK, :] = sums[2, :BLOCK, :] + d[2 * BLOCK :, :128]
    sums[0, : 3 * BLOCK, :] = sums[0, : 3 * BLOCK, :] + d[:, 128:]
    pack_rows(sums, packed, 3)
    pack_rows(sums, packed, 1)
    for n in range(4):
        out[n][...] = packed[outward_slot(row, SWAPS[n])]
    for fetch in fetches[:4] + fetches[16:]:
        fetch.wait()


def odd_sums(features, dilated, point):
    return pl.pallas_call(
        odd_kernel,
        out_shape=[jax.ShapeDtypeStruct((HALF, 128), F32)] * 4
        + [pltpu.VMEM((PIXELS, CHANNELS), BF16), pltpu.VMEM((28 * W, CHANNELS), BF16)],
        in_specs=[pl.BlockSpec(memory_space=pltpu.HBM)] * 3,
        out_specs=[pl.BlockSpec(memory_space=pltpu.VMEM)] * 6,
        scratch_shapes=[
            pltpu.VMEM((PIXELS, CHANNELS), BF16),
            pltpu.VMEM((3, PIXELS, 128), F32),
            pltpu.VMEM((6, HALF, 128), F32),
            pltpu.SemaphoreType.DMA((3,)),
            pltpu.SemaphoreType.DMA((28,)),
        ],
        compiler_params=pltpu.CompilerParams(vmem_limit_bytes=28 * 2**20),
        name="odd_sums",
    )(features, dilated, point)


def even_kernel(ordered, weights, *refs):
    row = lax.axis_index("rows")
    out = refs[1:3]
    sums, packed = refs[3:]
    d = nt(ordered[...], weights[EVEN_AT : EVEN_AT + 384, :])
    sums[1] = d[:, :128]
    sums[1, 2 * BLOCK :, :] = sums[1, 2 * BLOCK :, :] + d[: 2 * BLOCK, 128:256]
    sums[1, : 2 * BLOCK, :] = sums[1, : 2 * BLOCK, :] + d[2 * BLOCK :, 256:]
    pack_rows(sums, packed, 2)
    for n in range(2):
        slot = jnp.where((row ^ SWAPS[4 + n]) < row, 4, 1)
        out[n][...] = packed[slot]


def even_sums(ordered, weights, started):
    return pl.pallas_call(
        even_kernel,
        out_shape=[jax.ShapeDtypeStruct((HALF, 128), F32)] * 2,
        in_specs=[
            pl.BlockSpec(memory_space=pltpu.VMEM),
            pl.BlockSpec(memory_space=pltpu.VMEM),
            pl.BlockSpec(memory_space=pl.ANY),
        ],
        out_specs=[pl.BlockSpec(memory_space=pltpu.VMEM)] * 2,
        scratch_shapes=[
            pltpu.VMEM((3, PIXELS, 128), F32),
            pltpu.VMEM((6, HALF, 128), F32),
        ],
        compiler_params=pltpu.CompilerParams(vmem_limit_bytes=18 * 2**20),
        cost_estimate=pl.CostEstimate(flops=10**6, bytes_accessed=10**4, transcendentals=0),
        name="even_sums",
    )(ordered, weights, started)


def own_kernel(ordered, weights, bias, out):
    line = jnp.concatenate([bias[k : k + 1, :] for k in range(4)], 1)
    out[...] = nt(ordered[...], weights[:256, :]) + line
    low = low_lanes((PIXELS, 128))

    def add(first, value, k):
        lanes = slice(0, 128) if k == 1 else slice(128, 256)
        rows = slice(first * BLOCK, first * BLOCK + value.shape[0])
        mask = low[: value.shape[0]]
        kept = jnp.where(mask, value[:, lanes], 0.0) if k == 2 else jnp.where(mask, 0.0, value[:, lanes])
        out[rows, lanes] = out[rows, lanes] + kept

    d = nt(ordered[: 3 * BLOCK, :], weights[LEFT_AT - W : LEFT_AT + 3 * W, :])
    for k in (1, 2, 3):
        add(k, d[: (4 - k) * BLOCK], k)
    d = nt(ordered[BLOCK:, :], weights[RIGHT_AT - W : RIGHT_AT + 3 * W, :])
    for k in (1, 2, 3):
        add(0, d[(k - 1) * BLOCK :], k)


def own_sums(ordered, weights, bias):
    return pl.pallas_call(
        own_kernel,
        out_shape=jax.ShapeDtypeStruct((PIXELS, 4 * W), F32),
        in_specs=[pl.BlockSpec(memory_space=pltpu.VMEM)] * 3,
        out_specs=pl.BlockSpec(memory_space=pltpu.VMEM),
        compiler_params=pltpu.CompilerParams(vmem_limit_bytes=18 * 2**20),
        cost_estimate=pl.CostEstimate(flops=10**6, bytes_accessed=10**4, transcendentals=0),
        name="own_sums",
    )(ordered, weights, bias)


def arrival_slot(row, other):
    return jnp.where((other >= 0) & (other < 8), row ^ other, 0)


def gather_arrivals(recv, arrivals, swaps):
    arrivals[0] = jnp.zeros((HALF, 128), arrivals.dtype)
    for n, x in enumerate(swaps):
        arrivals[x] = recv[n][...]


def activation_kernel(own, *refs):
    recv, acts, arrivals = refs[:6], refs[6], refs[7]
    row = lax.axis_index("rows")
    gather_arrivals(recv, arrivals, SWAPS)
    low = low_lanes((HALF, 128))
    t1, t2, t3 = (
        arrivals[arrival_slot(row, row - k)] + arrivals[arrival_slot(row, row + k)]
        for k in (1, 2, 3)
    )
    r1, r2, r3 = (pltpu.roll(t, W, 1) for t in (t1, t2, t3))
    for rows, a, b, c in ((slice(0, HALF), r1, t2, r3), (slice(HALF, PIXELS), t1, r2, t3)):
        left = own[rows, :128] + jnp.where(low, 0.0, a)
        right = own[rows, 128:] + jnp.where(low, b, c)
        acts[rows, :128] = jnp.maximum(left, 0.0).astype(BF16)
        acts[rows, 128:] = jnp.maximum(right, 0.0).astype(BF16)


def activations_of(own, received):
    return pl.pallas_call(
        activation_kernel,
        out_shape=jax.ShapeDtypeStruct((PIXELS, 4 * W), BF16),
        in_specs=[pl.BlockSpec(memory_space=pltpu.VMEM)] * 7,
        out_specs=pl.BlockSpec(memory_space=pltpu.VMEM),
        scratch_shapes=[pltpu.VMEM((8, HALF, 128), F32)],
        compiler_params=pltpu.CompilerParams(vmem_limit_bytes=8 * 2**20),
        name="activations",
    )(own, *received)


def head_kernel(a0, a1, a2, a3, project, bias, cotangent, *refs):
    head_out, grads, sends, ordered, packed = refs[0], refs[1], refs[2:8], refs[8], refs[9]
    row, member = lax.axis_index("rows"), lax.axis_index("filt")

    def rows_of(who):
        at = pl.multiple_of(who * W, W)
        return jnp.concatenate([project[k, pl.ds(at, W), :] for k in range(4)], 0)

    own_rows = rows_of(member)
    pre = nn(a0[...], own_rows) + bias[...]
    for flip, acts in ((1, a1), (2, a2), (3, a3)):
        pre = pre + nn(acts[...], rows_of(member ^ flip))
    mine = jnp.zeros((PIXELS, W), F32)
    for q in range(4):
        mine = mine + jnp.where(member == q, pre[:, q * W : (q + 1) * W], 0.0)
    mine = jnp.maximum(mine, 0.0).astype(BF16)

    def put(at, value):
        head_out[at : at + 192, :] = value

    from_blocks(order_matrix(True), mine, put)
    order = order_matrix()
    for g in range(3):
        moved = nn(order, cotangent[g * 192 : (g + 1) * 192, :])
        for m in range(4):
            at = m * BLOCK + g * 48
            ordered[at : at + 48, :] = moved[m * 48 : (m + 1) * 48]
    head_grad = jnp.where(pre > 0, ordered[...], 0.0).astype(BF16)
    act_grad = nt(head_grad, own_rows)
    grad = jnp.where(a0[...].astype(F32) > 0, act_grad, 0.0)
    grads[...] = grad.astype(BF16)
    low = low_lanes((HALF, 128))
    left, right = grad[:, :128], grad[:, 128:]
    packed[0] = jnp.where(low, pltpu.roll(left[:HALF], W, 1), left[HALF:]).astype(BF16)
    packed[1] = jnp.where(low, right[:HALF], pltpu.roll(right[HALF:], W, 1)).astype(BF16)
    packed[2] = jnp.where(low, pltpu.roll(right[:HALF], W, 1), right[HALF:]).astype(BF16)
    for n, x in enumerate(GRAD_SWAPS):
        apart = jnp.abs((row ^ x) - row)
        sends[n][...] = packed[jnp.where(apart <= 3, apart - 1, 0)]


def head(acts, project, bias, cotangent):
    return pl.pallas_call(
        head_kernel,
        out_shape=[
            jax.ShapeDtypeStruct((PIXELS, W), BF16),
            jax.ShapeDtypeStruct((PIXELS, 4 * W), BF16),
        ]
        + [jax.ShapeDtypeStruct((HALF, 128), BF16)] * 6,
        in_specs=[pl.BlockSpec(memory_space=pltpu.VMEM)] * 7,
        out_specs=[pl.BlockSpec(memory_space=pltpu.VMEM)] * 8,
        scratch_shapes=[pltpu.VMEM((PIXELS, 256), F32), pltpu.VMEM((3, HALF, 128), BF16)],
        compiler_params=pltpu.CompilerParams(vmem_limit_bytes=12 * 2**20),
        name="head",
    )(*acts, project, bias, cotangent)


def spread_kernel(own, *refs):
    recv, stack, arrivals, pairs, twice = refs[:6], refs[6], refs[7], refs[8], refs[9]
    row = lax.axis_index("rows")
    gather_arrivals(recv, arrivals, GRAD_SWAPS)
    low = low_lanes((HALF, 128))
    low_all = low_lanes((PIXELS, 128))
    for k in (1, 2, 3):
        p = arrivals[arrival_slot(row, row + k)].astype(F32)
        m = arrivals[arrival_slot(row, row - k)].astype(F32)
        pairs[k - 1, :HALF, :] = jnp.where(low, p, pltpu.roll(m, W, 1)).astype(BF16)
        pairs[k - 1, HALF:, :] = jnp.where(low, pltpu.roll(p, W, 1), m).astype(BF16)
        g = own[:, :128].astype(F32) if k == 1 else own[:, 128:].astype(F32)
        other = pltpu.roll(g, W, 1)
        both = jnp.where(low_all, g, other) if k == 2 else jnp.where(low_all, other, g)
        twice[k - 1] = both.astype(BF16)
    stack[:, : 4 * W] = own[...]
    nothing = jnp.zeros((BLOCK, 128), BF16)

    def block_of(ref, k, source):
        if 0 <= source < 4:
            return ref[k - 1, source * BLOCK : (source + 1) * BLOCK, :]
        return nothing

    for q, (k, j) in enumerate(OUT_PAIRS):
        lanes = slice(ODD_AT + q * 128, ODD_AT + q * 128 + 128)
        for m in range(4):
            stack[m * BLOCK : (m + 1) * BLOCK, lanes] = block_of(pairs, k, m - (j - 1) * k)
    low_block = low_lanes((BLOCK, 128))
    for q, (a, b) in enumerate(((1, 2), (3, -1), (-2, -3))):
        lanes = slice(LEFT_AT + q * 128, LEFT_AT + q * 128 + 128)
        for m in range(4):
            stack[m * BLOCK : (m + 1) * BLOCK, lanes] = jnp.where(
                low_block, block_of(twice, abs(a), m + a), block_of(twice, abs(b), m + b)
            )


def spread(own, received):
    return pl.pallas_call(
        spread_kernel,
        out_shape=pltpu.VMEM((PIXELS, 28 * W), BF16),
        in_specs=[pl.BlockSpec(memory_space=pltpu.VMEM)] * 7,
        out_specs=pl.BlockSpec(memory_space=pltpu.VMEM),
        scratch_shapes=[
            pltpu.VMEM((8, HALF, 128), BF16),
            pltpu.VMEM((3, PIXELS, 128), BF16),
            pltpu.VMEM((3, PIXELS, 128), BF16),
        ],
        compiler_params=pltpu.CompilerParams(vmem_limit_bytes=12 * 2**20),
        name="spread",
    )(own, *received)


def grad_kernel(flips, stack, weights, *outs):
    member = lax.axis_index("filt")
    for out, flip in zip(outs, flips):
        columns = pl.ds(pl.multiple_of((member ^ flip) * 512, 512), 512)
        out[...] = nn(stack[...], weights[:, columns]).astype(BF16)


def grads_for(flips, stack, weights):
    return pl.pallas_call(
        functools.partial(grad_kernel, flips),
        out_shape=[jax.ShapeDtypeStruct((PIXELS, 512), BF16)] * len(flips),
        in_specs=[pl.BlockSpec(memory_space=pltpu.VMEM)] * 2,
        out_specs=[pl.BlockSpec(memory_space=pltpu.VMEM)] * len(flips),
        compiler_params=pltpu.CompilerParams(vmem_limit_bytes=18 * 2**20),
        cost_estimate=pl.CostEstimate(
            flops=2 * PIXELS * 28 * W * 512 * len(flips), bytes_accessed=10**6, transcendentals=0
        ),
        name="grads_for",
    )(stack, weights)


def last_kernel(a, b, c, out):
    total = a[...].astype(F32) + b[...].astype(F32) + c[...].astype(F32)

    def put(at, value):
        out[at : at + 192, :] = value

    from_blocks(order_matrix(True), total.astype(BF16), put)


def last_sum(a, b, c):
    return pl.pallas_call(
        last_kernel,
        out_shape=jax.ShapeDtypeStruct((PIXELS, 512), BF16),
        in_specs=[pl.BlockSpec(memory_space=pltpu.VMEM)] * 3,
        out_specs=pl.BlockSpec(memory_space=pltpu.VMEM),
        compiler_params=pltpu.CompilerParams(vmem_limit_bytes=10 * 2**20),
        name="last_sum",
    )(a, b, c)


def flipped(x, bit):
    return lax.ppermute(x, "filt", [(i, i ^ bit) for i in range(lax.axis_size("filt"))])


def swapped(x, bits):
    pairs = [(r, r ^ bits) for r in range(8) if abs((r ^ bits) - r) <= 3]
    return lax.ppermute(x, "rows", pairs)


def on_device(
    features, point_weight, dilated_weight, branch_bias, project_weight, project_bias, cotangent
):
    flat = features.reshape(PIXELS, CHANNELS)
    dilated = jnp.transpose(dilated_weight, (0, 1, 2, 4, 3)).reshape(27, W, CHANNELS)
    point = point_weight.T
    flat, dilated, point = (
        pltpu.with_memory_space_constraint(x, pltpu.HBM) for x in (flat, dilated, point)
    )
    *sums, ordered, weights = odd_sums(flat, dilated, point)
    received = [swapped(sums[n], SWAPS[n]) for n in range(4)]
    sums = even_sums(ordered, weights, received[0])
    received += [swapped(sums[n], SWAPS[4 + n]) for n in range(2)]
    own = own_sums(ordered, weights, branch_bias)
    acts = activations_of(own, received)
    across = flipped(acts, 2)
    beside = flipped(acts, 1)
    corner = flipped(across, 1)
    head_output, grads, *sends = head(
        (acts, beside, across, corner),
        project_weight,
        project_bias.reshape(1, 256),
        cotangent.reshape(PIXELS, 256),
    )
    arrived = [swapped(sends[n], x) for n, x in enumerate(GRAD_SWAPS)]
    stack = spread(grads, arrived)
    near, far = grads_for((1, 3), stack, weights)
    near, far = flipped(near, 1), flipped(far, 1)
    (kept,) = grads_for((2,), stack, weights)
    crossing = (far.astype(F32) + kept.astype(F32)).astype(BF16)
    crossed = flipped(crossing, 2)
    later, crossing = lax.optimization_barrier((stack, crossing))
    (kept,) = grads_for((0,), later, weights)
    feature_grad = last_sum(kept, near, crossed)
    return head_output.reshape(12, 48, W), feature_grad.reshape(12, 48, 512)


def solution(mesh):
    body = on_device if fits(mesh) else on_device_general
    in_specs = (
        P("rows", None, None),
        P(None, "filt"),
        P(None, None, None, None, "filt"),
        P(None, "filt"),
        P(),
        P(),
        P("rows", None, None),
    )
    out_specs = (P("rows", None, "filt"), P("rows", None, "filt"))
    return jax.shard_map(
        body, mesh=mesh, in_specs=in_specs, out_specs=out_specs, check_vma=False
    )
```

```python
import functools

import jax
import jax.numpy as jnp
from jax import lax
from jax.experimental import pallas as pl
from jax.experimental.pallas import tpu as pltpu
from jax.sharding import PartitionSpec as P

FIRST_DILATION = 12
SECOND_DILATION = 24
THIRD_DILATION = 36


def passed_along(x, axis, by):
    devices = lax.axis_size(axis)
    pairs = [(i, i + by) for i in range(devices) if 0 <= i + by < devices]
    return lax.ppermute(x, axis, pairs)


def shift_columns(field, amount):
    breadth = field.shape[1]
    if amount == 0:
        return field
    padding = [(0, 0)] * field.ndim
    if amount > 0:
        kept = field[:, amount:]
        padding[1] = (0, amount)
    else:
        kept = field[:, : breadth + amount]
        padding[1] = (-amount, 0)
    return jnp.pad(kept, padding)


def fetch_sums(field, offset):
    return passed_along(field, "rows", offset)


def fetch_grads(field, offset):
    return passed_along(field, "rows", offset)


def shift_rows(field, amount, fetcher):
    height = field.shape[0]
    quotient = amount // height

    def extract_block(offset):
        if offset == 0:
            return field
        return fetcher(field, offset)

    return extract_block(quotient)


def make_kernel_taps(variants, dilation_rates):
    stacked = [variants[:, :, 0]]
    for branch, dilation in enumerate(dilation_rates):
        for row_tap in range(3):
            source = variants[:, :, 1 + 3 * branch + row_tap]
            for col_tap in range(3):
                stacked.append(shift_columns(source, -(col_tap - 1) * dilation))
    return jnp.stack(stacked, 2)


def on_device_general(
    features, point_weight, dilated_weight, branch_bias, project_weight, project_bias, cotangent
):
    height, breadth, channels = features.shape
    pixels = height * breadth
    own_width = point_weight.shape[1]
    filters = lax.axis_size("filt")
    member = lax.axis_index("filt")
    branch_outputs = project_weight.shape[2]
    own_out = branch_outputs // filters
    own_channels = channels // filters
    dilation_rates = (FIRST_DILATION, SECOND_DILATION, THIRD_DILATION)
    all_weights = jnp.concatenate(
        [point_weight[None], dilated_weight.reshape(27, channels, own_width)], 0
    )
    flattened = features.reshape(pixels, channels)
    tap_terms = jnp.einsum(
        "pc,tco->pto", flattened, all_weights, preferred_element_type=jnp.float32
    )
    tap_terms = tap_terms.reshape(height, breadth, 28, own_width)
    pre_list = [tap_terms[:, :, 0, :] + branch_bias[0]]
    for branch, dilation in enumerate(dilation_rates):
        summed_result = jnp.zeros((height, breadth, own_width), jnp.float32)
        for row_tap in range(3):
            row_sum = jnp.zeros((height, breadth, own_width), jnp.float32)
            for col_tap in range(3):
                row_sum = row_sum + shift_columns(
                    tap_terms[:, :, 1 + 9 * branch + 3 * row_tap + col_tap, :],
                    (col_tap - 1) * dilation,
                )
            summed_result = summed_result + shift_rows(
                row_sum, -(row_tap - 1) * dilation, fetch_sums
            )
        pre_list.append(summed_result + branch_bias[branch + 1])
    branch_pre = jnp.stack(pre_list, 2)
    activations = jnp.maximum(branch_pre, 0.0).astype(jnp.bfloat16).reshape(pixels, 4 * own_width)
    grouped = project_weight.reshape(4, filters, own_width, branch_outputs)
    own_rows = lax.dynamic_index_in_dim(grouped, member, 1, keepdims=False).reshape(
        4 * own_width, branch_outputs
    )
    flat_cotangent = cotangent.reshape(pixels, branch_outputs)
    ordered = jnp.transpose(grouped, (1, 0, 2, 3)).reshape(filters * 4 * own_width, branch_outputs)
    project_pre = jnp.dot(
        lax.all_gather(activations, "filt", axis=1, tiled=True),
        ordered,
        preferred_element_type=jnp.float32,
    )
    project_pre = project_pre + project_bias
    head_grad = jnp.where(project_pre > 0, flat_cotangent.astype(jnp.float32), 0.0).astype(
        jnp.bfloat16
    )
    own_pre = lax.dynamic_slice_in_dim(project_pre, member * own_out, own_out, 1)
    act_grad = jnp.dot(head_grad, own_rows.T, preferred_element_type=jnp.float32)
    head_output = jnp.maximum(own_pre, 0.0).astype(jnp.bfloat16).reshape(height, breadth, own_out)
    branch_grad = jnp.where(
        branch_pre > 0, act_grad.reshape(height, breadth, 4, own_width), 0.0
    ).astype(jnp.bfloat16)
    variant_list = [branch_grad[:, :, 0, :]]
    for branch, dilation in enumerate(dilation_rates):
        for row_tap in range(3):
            variant_list.append(
                shift_rows(branch_grad[:, :, branch + 1, :], (row_tap - 1) * dilation, fetch_grads)
            )
    variants = jnp.stack(variant_list, 2)
    stacked = make_kernel_taps(variants, dilation_rates).reshape(pixels, 28, own_width)
    input_grad = lax.psum_scatter(
        jnp.einsum("pto,tco->cp", stacked, all_weights, preferred_element_type=jnp.float32),
        "filt",
        scatter_dimension=0,
        tiled=True,
    ).T
    feature_grad = input_grad.astype(jnp.bfloat16).reshape(height, breadth, own_channels)
    return (head_output, feature_grad)


W = 64
BLOCK = 144
PIXELS = 576
HALF = 288
CHANNELS = 2048
F32 = jnp.float32
BF16 = jnp.bfloat16

OUT_PAIRS = ((3, 1), (1, 1), (3, 0), (1, 0), (3, 2), (1, 2), (2, 1), (2, 0), (2, 2))
TAPS = (
    [(k, 1, 1) for k in (2, 1, 3)]
    + [(k, i, j) for k, j in OUT_PAIRS for i in (0, 2)]
    + [(k, 1, j) for j in (0, 2) for k in (2, 1, 3)]
)
OUT_AT, LEFT_AT, RIGHT_AT = 4 * W, 22 * W, 25 * W
PARTS = ((0, 2), (1, 3))
SWAPS = (6, 2, 5, 7, 3, 1)
GRAD_SWAPS = (1, 5, 7, 3, 6, 2)


def fits(mesh):
    return mesh.shape["rows"] == 8 and mesh.shape["filt"] == 4


def order_matrix(turned=False):
    to = lax.broadcasted_iota(jnp.int32, (192, 192), 1 if turned else 0)
    source = lax.broadcasted_iota(jnp.int32, (192, 192), 0 if turned else 1)

    def parts(value, width):
        return sum((value >= n * width).astype(jnp.int32) for n in (1, 2, 3))

    block = parts(to, 48)
    within = to - 48 * block
    line = parts(within, 12)
    wanted = line * 48 + block * 12 + within - 12 * line
    return (source == wanted).astype(F32).astype(BF16)


def tap_index(tap):
    k, i, j = tap
    return (k - 1) * 9 + i * 3 + j


def nt(a, b):
    return lax.dot_general(a, b, (((1,), (1,)), ((), ())), preferred_element_type=F32)


def nn(a, b):
    return lax.dot_general(a, b, (((1,), (0,)), ((), ())), preferred_element_type=F32)


def from_blocks(order_t, value, write):
    for g in range(3):
        parts = [value[m * BLOCK + g * 48 : m * BLOCK + g * 48 + 48] for m in range(4)]
        write(g * 192, nn(order_t, jnp.concatenate(parts, 0)).astype(BF16))


def low_lanes(shape):
    return lax.broadcasted_iota(jnp.int32, shape, 1) % 128 < W


def outward_slot(row, x):
    other = row ^ x
    apart = jnp.abs(other - row)
    slot = apart - 1 + jnp.where(other < row, 3, 0)
    return jnp.where(apart <= 3, slot, 0)


def outward_kernel(features, dilated, point, *refs):
    row = lax.axis_index("rows")
    out, ordered, weights = refs[0:6], refs[6], refs[7]
    raw, sums, packed, feature_sems, weight_sems = refs[8:]
    loads = []
    for g in range(3):
        rows = pl.ds(g * 192, 192)
        loads.append(pltpu.make_async_copy(features.at[rows], raw.at[rows], feature_sems.at[g]))
        loads[-1].start()
    fetches = [pltpu.make_async_copy(point, weights.at[pl.ds(0, W)], weight_sems.at[0])]
    for q, tap in enumerate(TAPS):
        fetches.append(
            pltpu.make_async_copy(
                dilated.at[tap_index(tap)],
                weights.at[pl.ds((q + 1) * W, W)],
                weight_sems.at[q + 1],
            )
        )
    queue = fetches[4:] + fetches[:4]

    def start_loads(first, last):
        for fetch in queue[first:last]:
            fetch.start()

    start_loads(0, 4)
    order = order_matrix()
    for g in range(3):
        loads[g].wait()
        start_loads(4 + 4 * g, 8 + 4 * g)
        moved = nn(order, raw[g * 192 : (g + 1) * 192, :]).astype(BF16)
        for m in range(4):
            at = m * BLOCK + g * 48
            ordered[at : at + 48, :] = moved[m * 48 : (m + 1) * 48]

    def product(pair, pairs, first, last):
        for fetch in queue[2 * pair : 2 * (pair + pairs)]:
            fetch.wait()
        at = OUT_AT + pair * 128
        return nt(ordered[first * BLOCK : last * BLOCK, :], weights[at : at + pairs * 128, :])

    d = product(0, 2, 0, 4)
    start_loads(16, 22)
    sums[2] = d[:, :128]
    sums[0] = d[:, 128:]
    d = product(2, 2, 0, 3)
    start_loads(22, 28)
    sums[2, 3 * BLOCK :, :] = sums[2, 3 * BLOCK :, :] + d[:BLOCK, :128]
    sums[0, BLOCK:, :] = sums[0, BLOCK:, :] + d[:, 128:]
    d = product(4, 2, 1, 4)
    sums[2, :BLOCK, :] = sums[2, :BLOCK, :] + d[2 * BLOCK :, :128]
    sums[0, : 3 * BLOCK, :] = sums[0, : 3 * BLOCK, :] + d[:, 128:]
    d = product(6, 3, 0, 4)
    sums[1] = d[:, :128]
    sums[1, 2 * BLOCK :, :] = sums[1, 2 * BLOCK :, :] + d[: 2 * BLOCK, 128:256]
    sums[1, : 2 * BLOCK, :] = sums[1, : 2 * BLOCK, :] + d[2 * BLOCK :, 256:]
    low = low_lanes((HALF, 128))
    for k in range(3):
        top, bottom = sums[k, :HALF, :], sums[k, HALF:, :]
        packed[k] = jnp.where(low, top, pltpu.roll(bottom, W, 1))
        packed[k + 3] = jnp.where(low, pltpu.roll(top, W, 1), bottom)
    for n, x in enumerate(SWAPS):
        out[n][...] = packed[outward_slot(row, x)]
    for fetch in queue[18:]:
        fetch.wait()


def outward_sums(features, dilated, point):
    return pl.pallas_call(
        outward_kernel,
        out_shape=[jax.ShapeDtypeStruct((HALF, 128), F32)] * 6
        + [pltpu.VMEM((PIXELS, CHANNELS), BF16), pltpu.VMEM((28 * W, CHANNELS), BF16)],
        in_specs=[pl.BlockSpec(memory_space=pltpu.HBM)] * 3,
        out_specs=[pl.BlockSpec(memory_space=pltpu.VMEM)] * 8,
        scratch_shapes=[
            pltpu.VMEM((PIXELS, CHANNELS), BF16),
            pltpu.VMEM((3, PIXELS, 128), F32),
            pltpu.VMEM((6, HALF, 128), F32),
            pltpu.SemaphoreType.DMA((3,)),
            pltpu.SemaphoreType.DMA((28,)),
        ],
        compiler_params=pltpu.CompilerParams(vmem_limit_bytes=28 * 2**20),
        name="outward_sums",
    )(features, dilated, point)


def own_kernel(ordered, weights, bias, *outs):
    d = nt(ordered[...], weights[:256, :])
    for part, out in enumerate(outs):
        line = jnp.concatenate([bias[k : k + 1, :] for k in PARTS[part]], 1)
        out[...] = d[:, part * 128 : part * 128 + 128] + line
    low = low_lanes((PIXELS, 128))

    def add(first, value, k):
        part = k % 2
        rows = slice(first * BLOCK, first * BLOCK + value.shape[0])
        mask, value = low[: value.shape[0]], value[:, part * 128 : part * 128 + 128]
        kept = jnp.where(mask, value, 0.0) if k == 1 else jnp.where(mask, 0.0, value)
        outs[part][rows, :] = outs[part][rows, :] + kept

    d = nt(ordered[: 3 * BLOCK, :], weights[LEFT_AT - W : LEFT_AT + 3 * W, :])
    for k in (1, 2, 3):
        add(k, d[: (4 - k) * BLOCK], k)
    d = nt(ordered[BLOCK:, :], weights[RIGHT_AT - W : RIGHT_AT + 3 * W, :])
    for k in (1, 2, 3):
        add(0, d[(k - 1) * BLOCK :], k)


def own_sums(ordered, weights, bias):
    return pl.pallas_call(
        own_kernel,
        out_shape=[jax.ShapeDtypeStruct((PIXELS, 128), F32)] * 2,
        in_specs=[pl.BlockSpec(memory_space=pltpu.VMEM)] * 3,
        out_specs=[pl.BlockSpec(memory_space=pltpu.VMEM)] * 2,
        compiler_params=pltpu.CompilerParams(vmem_limit_bytes=18 * 2**20),
        cost_estimate=pl.CostEstimate(flops=10**6, bytes_accessed=10**4, transcendentals=0),
        name="own_sums",
    )(ordered, weights, bias)


def arrival_slot(row, other):
    return jnp.where((other >= 0) & (other < 8), row ^ other, 0)


def gather_arrivals(recv, arrivals, swaps):
    arrivals[0] = jnp.zeros((HALF, 128), arrivals.dtype)
    for n, x in enumerate(swaps):
        arrivals[x] = recv[n][...]


def activation_kernel(part, swaps, own, *refs):
    recv, acts, arrivals = refs[: len(swaps)], refs[-2], refs[-1]
    row = lax.axis_index("rows")
    gather_arrivals(recv, arrivals, swaps)
    low = low_lanes((HALF, 128))

    def total(k):
        return arrivals[arrival_slot(row, row - k)] + arrivals[arrival_slot(row, row + k)]

    high = total(PARTS[part][1])
    top, bottom = jnp.where(low, 0.0, pltpu.roll(high, W, 1)), jnp.where(low, 0.0, high)
    if part:
        left = total(PARTS[part][0])
        top = jnp.where(low, left, top)
        bottom = jnp.where(low, pltpu.roll(left, W, 1), bottom)
    acts[:HALF, :] = jnp.maximum(own[:HALF, :] + top, 0.0).astype(BF16)
    acts[HALF:, :] = jnp.maximum(own[HALF:, :] + bottom, 0.0).astype(BF16)


def activations_of(part, swaps, own, received):
    return pl.pallas_call(
        functools.partial(activation_kernel, part, swaps),
        out_shape=jax.ShapeDtypeStruct((PIXELS, 128), BF16),
        in_specs=[pl.BlockSpec(memory_space=pltpu.VMEM)] * (1 + len(swaps)),
        out_specs=pl.BlockSpec(memory_space=pltpu.VMEM),
        scratch_shapes=[pltpu.VMEM((8, HALF, 128), F32)],
        compiler_params=pltpu.CompilerParams(vmem_limit_bytes=8 * 2**20),
        name="activations",
    )(own, *received)


def project_rows(project, who):
    at = pl.multiple_of(who * W, W)
    return jnp.concatenate([project[k, pl.ds(at, W), :] for part in PARTS for k in part], 0)


def both(a, b):
    return jnp.concatenate([a[...], b[...]], 1)


def near_head_kernel(a0, b0, a1, b1, project, bias, cotangent, pre, ordered):
    member = lax.axis_index("filt")
    pre[...] = nn(both(a0, b0), project_rows(project, member)) + bias[...]
    pre[...] = pre[...] + nn(both(a1, b1), project_rows(project, member ^ 1))
    order = order_matrix()
    for g in range(3):
        moved = nn(order, cotangent[g * 192 : (g + 1) * 192, :])
        for m in range(4):
            at = m * BLOCK + g * 48
            ordered[at : at + 48, :] = moved[m * 48 : (m + 1) * 48]


def near_head(own, beside, project, bias, cotangent):
    return pl.pallas_call(
        near_head_kernel,
        out_shape=[jax.ShapeDtypeStruct((PIXELS, 256), F32)] * 2,
        in_specs=[pl.BlockSpec(memory_space=pltpu.VMEM)] * 7,
        out_specs=[pl.BlockSpec(memory_space=pltpu.VMEM)] * 2,
        compiler_params=pltpu.CompilerParams(vmem_limit_bytes=10 * 2**20),
        name="near_head",
    )(*own, *beside, project, bias, cotangent)


def far_head_kernel(a0, b0, a2, b2, a3, b3, project, near, cotangent, *refs):
    output, grads, sends, packed = refs[0], refs[1], refs[2:8], refs[8]
    row, member = lax.axis_index("rows"), lax.axis_index("filt")
    pre = near[...] + nn(both(a2, b2), project_rows(project, member ^ 2))
    pre = pre + nn(both(a3, b3), project_rows(project, member ^ 3))
    output[...] = jnp.maximum(pre, 0.0).astype(BF16)
    head_grad = jnp.where(pre > 0, cotangent[...], 0.0).astype(BF16)
    act_grad = nt(head_grad, project_rows(project, member))
    a = jnp.where(a0[...].astype(F32) > 0, act_grad[:, :128], 0.0)
    b = jnp.where(b0[...].astype(F32) > 0, act_grad[:, 128:], 0.0)
    grads[:, :128] = a.astype(BF16)
    grads[:, 128:] = b.astype(BF16)
    low = low_lanes((HALF, 128))
    packed[0] = jnp.where(low, b[:HALF], pltpu.roll(b[HALF:], W, 1)).astype(BF16)
    packed[1] = jnp.where(low, pltpu.roll(a[:HALF], W, 1), a[HALF:]).astype(BF16)
    packed[2] = jnp.where(low, pltpu.roll(b[:HALF], W, 1), b[HALF:]).astype(BF16)
    for n, x in enumerate(GRAD_SWAPS):
        apart = jnp.abs((row ^ x) - row)
        sends[n][...] = packed[jnp.where(apart <= 3, apart - 1, 0)]


def far_head(own, across, corner, project, near, cotangent):
    return pl.pallas_call(
        far_head_kernel,
        out_shape=[jax.ShapeDtypeStruct((PIXELS, 256), BF16)] * 2
        + [jax.ShapeDtypeStruct((HALF, 128), BF16)] * 6,
        in_specs=[pl.BlockSpec(memory_space=pltpu.VMEM)] * 9,
        out_specs=[pl.BlockSpec(memory_space=pltpu.VMEM)] * 8,
        scratch_shapes=[pltpu.VMEM((3, HALF, 128), BF16)],
        compiler_params=pltpu.CompilerParams(vmem_limit_bytes=12 * 2**20),
        name="far_head",
    )(*own, *across, *corner, project, near, cotangent)


def own_output_kernel(output, out):
    member = lax.axis_index("filt")
    mine = jnp.zeros((PIXELS, W), F32)
    for q in range(4):
        mine = jnp.where(member == q, output[:, q * W : (q + 1) * W].astype(F32), mine)

    def put(at, value):
        out[at : at + 192, :] = value

    from_blocks(order_matrix(True), mine.astype(BF16), put)


def own_output(output):
    return pl.pallas_call(
        own_output_kernel,
        out_shape=jax.ShapeDtypeStruct((PIXELS, W), BF16),
        in_specs=[pl.BlockSpec(memory_space=pltpu.VMEM)],
        out_specs=pl.BlockSpec(memory_space=pltpu.VMEM),
        compiler_params=pltpu.CompilerParams(vmem_limit_bytes=6 * 2**20),
        name="own_output",
    )(output)


def spread_kernel(own, *refs):
    recv, stack, arrivals, pairs, twice = refs[:6], refs[6], refs[7], refs[8], refs[9]
    row = lax.axis_index("rows")
    gather_arrivals(recv, arrivals, GRAD_SWAPS)
    low = low_lanes((HALF, 128))
    low_all = low_lanes((PIXELS, 128))
    for k in (1, 2, 3):
        p = arrivals[arrival_slot(row, row + k)].astype(F32)
        m = arrivals[arrival_slot(row, row - k)].astype(F32)
        pairs[k - 1, :HALF, :] = jnp.where(low, p, pltpu.roll(m, W, 1)).astype(BF16)
        pairs[k - 1, HALF:, :] = jnp.where(low, pltpu.roll(p, W, 1), m).astype(BF16)
        g = own[:, :128].astype(F32) if k == 2 else own[:, 128:].astype(F32)
        other = pltpu.roll(g, W, 1)
        two = jnp.where(low_all, g, other) if k == 1 else jnp.where(low_all, other, g)
        twice[k - 1] = two.astype(BF16)
    stack[:, : 4 * W] = own[...]
    nothing = jnp.zeros((BLOCK, 128), BF16)

    def block_of(ref, k, source):
        if 0 <= source < 4:
            return ref[k - 1, source * BLOCK : (source + 1) * BLOCK, :]
        return nothing

    for q, (k, j) in enumerate(OUT_PAIRS):
        lanes = slice(OUT_AT + q * 128, OUT_AT + q * 128 + 128)
        for m in range(4):
            stack[m * BLOCK : (m + 1) * BLOCK, lanes] = block_of(pairs, k, m - (j - 1) * k)
    low_block = low_lanes((BLOCK, 128))
    for q, (a, b) in enumerate(((2, 1), (3, -2), (-1, -3))):
        lanes = slice(LEFT_AT + q * 128, LEFT_AT + q * 128 + 128)
        for m in range(4):
            stack[m * BLOCK : (m + 1) * BLOCK, lanes] = jnp.where(
                low_block, block_of(twice, abs(a), m + a), block_of(twice, abs(b), m + b)
            )


def spread(own, received):
    return pl.pallas_call(
        spread_kernel,
        out_shape=pltpu.VMEM((PIXELS, 28 * W), BF16),
        in_specs=[pl.BlockSpec(memory_space=pltpu.VMEM)] * 7,
        out_specs=pl.BlockSpec(memory_space=pltpu.VMEM),
        scratch_shapes=[
            pltpu.VMEM((8, HALF, 128), BF16),
            pltpu.VMEM((3, PIXELS, 128), BF16),
            pltpu.VMEM((3, PIXELS, 128), BF16),
        ],
        compiler_params=pltpu.CompilerParams(vmem_limit_bytes=12 * 2**20),
        name="spread",
    )(own, *received)


def grad_kernel(flips, stack, weights, *outs):
    member = lax.axis_index("filt")
    for out, flip in zip(outs, flips):
        columns = pl.ds(pl.multiple_of((member ^ flip) * 512, 512), 512)
        out[...] = nn(stack[...], weights[:, columns]).astype(BF16)


def grads_for(flips, stack, weights, scale=1):
    return pl.pallas_call(
        functools.partial(grad_kernel, flips),
        out_shape=[jax.ShapeDtypeStruct((PIXELS, 512), BF16)] * len(flips),
        in_specs=[pl.BlockSpec(memory_space=pltpu.VMEM)] * 2,
        out_specs=[pl.BlockSpec(memory_space=pltpu.VMEM)] * len(flips),
        compiler_params=pltpu.CompilerParams(vmem_limit_bytes=18 * 2**20),
        cost_estimate=pl.CostEstimate(
            flops=2 * PIXELS * 28 * W * 512 * scale, bytes_accessed=10**6, transcendentals=0
        ),
        name="grads_for",
    )(stack, weights)


def last_kernel(a, b, c, out):
    total = a[...].astype(F32) + b[...].astype(F32) + c[...].astype(F32)

    def put(at, value):
        out[at : at + 192, :] = value

    from_blocks(order_matrix(True), total.astype(BF16), put)


def last_sum(a, b, c):
    return pl.pallas_call(
        last_kernel,
        out_shape=jax.ShapeDtypeStruct((PIXELS, 512), BF16),
        in_specs=[pl.BlockSpec(memory_space=pltpu.VMEM)] * 3,
        out_specs=pl.BlockSpec(memory_space=pltpu.VMEM),
        compiler_params=pltpu.CompilerParams(vmem_limit_bytes=10 * 2**20),
        name="last_sum",
    )(a, b, c)


def flipped(x, bit):
    return lax.ppermute(x, "filt", [(i, i ^ bit) for i in range(lax.axis_size("filt"))])


def swapped(x, bits):
    pairs = [(r, r ^ bits) for r in range(8) if abs((r ^ bits) - r) <= 3]
    return lax.ppermute(x, "rows", pairs)


def on_device(
    features, point_weight, dilated_weight, branch_bias, project_weight, project_bias, cotangent
):
    flat = features.reshape(PIXELS, CHANNELS)
    dilated = jnp.transpose(dilated_weight, (0, 1, 2, 4, 3)).reshape(27, W, CHANNELS)
    point = point_weight.T
    flat, dilated, point = (
        pltpu.with_memory_space_constraint(x, pltpu.HBM) for x in (flat, dilated, point)
    )
    *sums, ordered, weights = outward_sums(flat, dilated, point)
    received = {x: swapped(sums[n], x) for n, x in enumerate(SWAPS)}
    own = own_sums(ordered, weights, branch_bias)
    acts = [
        activations_of(part, swaps, own[part], [received[x] for x in swaps])
        for part, swaps in ((0, SWAPS[:2]), (1, SWAPS[2:]))
    ]
    across = [flipped(x, 2) for x in acts]
    beside = [flipped(x, 1) for x in acts]
    corner = [flipped(x, 1) for x in across]
    near, ordered_cotangent = near_head(
        acts,
        beside,
        project_weight,
        project_bias.reshape(1, 256),
        cotangent.reshape(PIXELS, 256),
    )
    output, grads, *sends = far_head(
        acts, across, corner, project_weight, near, ordered_cotangent
    )
    arrived = [swapped(sends[n], x) for n, x in enumerate(GRAD_SWAPS)]
    stack = spread(grads, arrived)
    (far,) = grads_for((3,), stack, weights)
    far = flipped(far, 1)
    (kept,) = grads_for((2,), stack, weights)
    crossing = (far.astype(F32) + kept.astype(F32)).astype(BF16)
    crossed = flipped(crossing, 2)
    later, output, crossing = lax.optimization_barrier((stack, output, crossing))
    head_output = own_output(output)
    (near,) = grads_for((1,), later, weights)
    near = flipped(near, 1)
    (kept,) = grads_for((0,), later, weights, 8)
    feature_grad = last_sum(kept, near, crossed)
    return head_output.reshape(12, 48, W), feature_grad.reshape(12, 48, 512)


def solution(mesh):
    body = on_device if fits(mesh) else on_device_general
    in_specs = (
        P("rows", None, None),
        P(None, "filt"),
        P(None, None, None, None, "filt"),
        P(None, "filt"),
        P(),
        P(),
        P("rows", None, None),
    )
    out_specs = (P("rows", None, "filt"), P("rows", None, "filt"))
    return jax.shard_map(
        body, mesh=mesh, in_specs=in_specs, out_specs=out_specs, check_vma=False
    )
```

```python
import functools

import jax
import jax.numpy as jnp
from jax import lax
from jax.experimental import pallas as pl
from jax.experimental.pallas import tpu as pltpu
from jax.sharding import PartitionSpec as P

FIRST_DILATION = 12
SECOND_DILATION = 24
THIRD_DILATION = 36


def passed_along(x, axis, by):
    devices = lax.axis_size(axis)
    pairs = [(i, i + by) for i in range(devices) if 0 <= i + by < devices]
    return lax.ppermute(x, axis, pairs)


def shift_columns(field, amount):
    breadth = field.shape[1]
    if amount == 0:
        return field
    padding = [(0, 0)] * field.ndim
    if amount > 0:
        kept = field[:, amount:]
        padding[1] = (0, amount)
    else:
        kept = field[:, : breadth + amount]
        padding[1] = (-amount, 0)
    return jnp.pad(kept, padding)


def fetch_sums(field, offset):
    return passed_along(field, "rows", offset)


def fetch_grads(field, offset):
    return passed_along(field, "rows", offset)


def shift_rows(field, amount, fetcher):
    height = field.shape[0]
    quotient = amount // height

    def extract_block(offset):
        if offset == 0:
            return field
        return fetcher(field, offset)

    return extract_block(quotient)


def make_kernel_taps(variants, dilation_rates):
    stacked = [variants[:, :, 0]]
    for branch, dilation in enumerate(dilation_rates):
        for row_tap in range(3):
            source = variants[:, :, 1 + 3 * branch + row_tap]
            for col_tap in range(3):
                stacked.append(shift_columns(source, -(col_tap - 1) * dilation))
    return jnp.stack(stacked, 2)


def on_device_general(
    features, point_weight, dilated_weight, branch_bias, project_weight, project_bias, cotangent
):
    height, breadth, channels = features.shape
    pixels = height * breadth
    own_width = point_weight.shape[1]
    filters = lax.axis_size("filt")
    member = lax.axis_index("filt")
    branch_outputs = project_weight.shape[2]
    own_out = branch_outputs // filters
    own_channels = channels // filters
    dilation_rates = (FIRST_DILATION, SECOND_DILATION, THIRD_DILATION)
    all_weights = jnp.concatenate(
        [point_weight[None], dilated_weight.reshape(27, channels, own_width)], 0
    )
    flattened = features.reshape(pixels, channels)
    tap_terms = jnp.einsum(
        "pc,tco->pto", flattened, all_weights, preferred_element_type=jnp.float32
    )
    tap_terms = tap_terms.reshape(height, breadth, 28, own_width)
    pre_list = [tap_terms[:, :, 0, :] + branch_bias[0]]
    for branch, dilation in enumerate(dilation_rates):
        summed_result = jnp.zeros((height, breadth, own_width), jnp.float32)
        for row_tap in range(3):
            row_sum = jnp.zeros((height, breadth, own_width), jnp.float32)
            for col_tap in range(3):
                row_sum = row_sum + shift_columns(
                    tap_terms[:, :, 1 + 9 * branch + 3 * row_tap + col_tap, :],
                    (col_tap - 1) * dilation,
                )
            summed_result = summed_result + shift_rows(
                row_sum, -(row_tap - 1) * dilation, fetch_sums
            )
        pre_list.append(summed_result + branch_bias[branch + 1])
    branch_pre = jnp.stack(pre_list, 2)
    activations = jnp.maximum(branch_pre, 0.0).astype(jnp.bfloat16).reshape(pixels, 4 * own_width)
    grouped = project_weight.reshape(4, filters, own_width, branch_outputs)
    own_rows = lax.dynamic_index_in_dim(grouped, member, 1, keepdims=False).reshape(
        4 * own_width, branch_outputs
    )
    flat_cotangent = cotangent.reshape(pixels, branch_outputs)
    ordered = jnp.transpose(grouped, (1, 0, 2, 3)).reshape(filters * 4 * own_width, branch_outputs)
    project_pre = jnp.dot(
        lax.all_gather(activations, "filt", axis=1, tiled=True),
        ordered,
        preferred_element_type=jnp.float32,
    )
    project_pre = project_pre + project_bias
    head_grad = jnp.where(project_pre > 0, flat_cotangent.astype(jnp.float32), 0.0).astype(
        jnp.bfloat16
    )
    own_pre = lax.dynamic_slice_in_dim(project_pre, member * own_out, own_out, 1)
    act_grad = jnp.dot(head_grad, own_rows.T, preferred_element_type=jnp.float32)
    head_output = jnp.maximum(own_pre, 0.0).astype(jnp.bfloat16).reshape(height, breadth, own_out)
    branch_grad = jnp.where(
        branch_pre > 0, act_grad.reshape(height, breadth, 4, own_width), 0.0
    ).astype(jnp.bfloat16)
    variant_list = [branch_grad[:, :, 0, :]]
    for branch, dilation in enumerate(dilation_rates):
        for row_tap in range(3):
            variant_list.append(
                shift_rows(branch_grad[:, :, branch + 1, :], (row_tap - 1) * dilation, fetch_grads)
            )
    variants = jnp.stack(variant_list, 2)
    stacked = make_kernel_taps(variants, dilation_rates).reshape(pixels, 28, own_width)
    input_grad = lax.psum_scatter(
        jnp.einsum("pto,tco->cp", stacked, all_weights, preferred_element_type=jnp.float32),
        "filt",
        scatter_dimension=0,
        tiled=True,
    ).T
    feature_grad = input_grad.astype(jnp.bfloat16).reshape(height, breadth, own_channels)
    return (head_output, feature_grad)


W = 64
BLOCK = 144
PIXELS = 576
HALF = 288
SENT = 304
CHANNELS = 2048
F32 = jnp.float32
BF16 = jnp.bfloat16

OUT_PAIRS = ((3, 1), (1, 1), (3, 0), (1, 0), (3, 2), (1, 2), (2, 1), (2, 0), (2, 2))
TAPS = (
    [(k, 1, 1) for k in (2, 1, 3)]
    + [(k, i, j) for k, j in OUT_PAIRS for i in (0, 2)]
    + [(k, 1, j) for j in (0, 2) for k in (2, 1, 3)]
)
OUT_AT, LEFT_AT, RIGHT_AT = 4 * W, 22 * W, 25 * W
PARTS = ((0, 2), (1, 3))
SWAPS = (6, 2, 1, 3, 7, 5)
GRAD_SWAPS = (1, 5, 7, 3, 6, 2)


def fits(mesh):
    return mesh.shape["rows"] == 8 and mesh.shape["filt"] == 4


def order_matrix(turned=False):
    to = lax.broadcasted_iota(jnp.int32, (192, 192), 1 if turned else 0)
    source = lax.broadcasted_iota(jnp.int32, (192, 192), 0 if turned else 1)

    def parts(value, width):
        return sum((value >= n * width).astype(jnp.int32) for n in (1, 2, 3))

    block = parts(to, 48)
    within = to - 48 * block
    line = parts(within, 12)
    wanted = line * 48 + block * 12 + within - 12 * line
    return (source == wanted).astype(F32).astype(BF16)


def tap_index(tap):
    k, i, j = tap
    return (k - 1) * 9 + i * 3 + j


def nt(a, b):
    return lax.dot_general(a, b, (((1,), (1,)), ((), ())), preferred_element_type=F32)


def nn(a, b):
    return lax.dot_general(a, b, (((1,), (0,)), ((), ())), preferred_element_type=F32)


def from_blocks(order_t, value, write):
    for g in range(3):
        parts = [value[m * BLOCK + g * 48 : m * BLOCK + g * 48 + 48] for m in range(4)]
        write(g * 192, nn(order_t, jnp.concatenate(parts, 0)).astype(BF16))


def low_lanes(shape):
    return lax.broadcasted_iota(jnp.int32, shape, 1) % 128 < W


def scaled(value):
    most = jnp.maximum(jnp.max(jnp.abs(value), axis=0, keepdims=True), 1e-30)
    power = jnp.floor(jnp.log(most) * 1.4426950408889634)
    return value * jnp.exp2(13.0 - power), power


def unscaled(sent):
    return sent[:HALF, :] * jnp.exp2(sent[HALF : HALF + 1, :] - 13.0)


def outward_slot(row, x):
    other = row ^ x
    apart = jnp.abs(other - row)
    slot = apart - 1 + jnp.where(other < row, 3, 0)
    return jnp.where(apart <= 3, slot, 0)


def fetch_tap(dilated, weights, sem, place):
    return pltpu.make_async_copy(
        dilated.at[tap_index(TAPS[place - 1])], weights.at[pl.ds(place * W, W)], sem
    )


def outward_kernel(features, dilated, *refs):
    row = lax.axis_index("rows")
    out, ordered, weights = refs[0:6], refs[6], refs[7]
    raw, sums, packed, feature_sems, weight_sems = refs[8:]
    loads = []
    for g in range(3):
        rows = pl.ds(g * 192, 192)
        loads.append(pltpu.make_async_copy(features.at[rows], raw.at[rows], feature_sems.at[g]))
        loads[-1].start()
    queue = [fetch_tap(dilated, weights, weight_sems.at[q], q + 4) for q in range(18)]

    def start_loads(first, last):
        for fetch in queue[first:last]:
            fetch.start()

    start_loads(0, 4)
    order = order_matrix()
    for g in range(3):
        loads[g].wait()
        start_loads(4 + 4 * g, 8 + 4 * g if g < 2 else 18)
        moved = nn(order, raw[g * 192 : (g + 1) * 192, :]).astype(BF16)
        for m in range(4):
            at = m * BLOCK + g * 48
            ordered[at : at + 48, :] = moved[m * 48 : (m + 1) * 48]

    def product(pair, pairs, first, last):
        for fetch in queue[2 * pair : 2 * (pair + pairs)]:
            fetch.wait()
        at = OUT_AT + pair * 128
        return nt(ordered[first * BLOCK : last * BLOCK, :], weights[at : at + pairs * 128, :])

    d = product(0, 2, 0, 4)
    sums[2] = d[:, :128]
    sums[0] = d[:, 128:]
    d = product(2, 2, 0, 3)
    sums[2, 3 * BLOCK :, :] = sums[2, 3 * BLOCK :, :] + d[:BLOCK, :128]
    sums[0, BLOCK:, :] = sums[0, BLOCK:, :] + d[:, 128:]
    d = product(4, 2, 1, 4)
    sums[2, :BLOCK, :] = sums[2, :BLOCK, :] + d[2 * BLOCK :, :128]
    sums[0, : 3 * BLOCK, :] = sums[0, : 3 * BLOCK, :] + d[:, 128:]
    d = product(6, 3, 0, 4)
    sums[1] = d[:, :128]
    sums[1, 2 * BLOCK :, :] = sums[1, 2 * BLOCK :, :] + d[: 2 * BLOCK, 128:256]
    sums[1, : 2 * BLOCK, :] = sums[1, : 2 * BLOCK, :] + d[2 * BLOCK :, 256:]
    low = low_lanes((HALF, 128))
    for k in range(3):
        top, bottom = sums[k, :HALF, :], sums[k, HALF:, :]
        halves = (
            jnp.where(low, top, pltpu.roll(bottom, W, 1)),
            jnp.where(low, pltpu.roll(top, W, 1), bottom),
        )
        for way, value in enumerate(halves):
            value, power = scaled(value)
            packed[k + 3 * way, :HALF, :] = value
            packed[k + 3 * way, HALF:, :] = jnp.broadcast_to(power, (SENT - HALF, 128))
    for n, x in enumerate(SWAPS):
        out[n][...] = packed[outward_slot(row, x)]


def outward_sums(features, dilated):
    return pl.pallas_call(
        outward_kernel,
        out_shape=[jax.ShapeDtypeStruct((SENT, 128), F32)] * 6
        + [pltpu.VMEM((PIXELS, CHANNELS), BF16), pltpu.VMEM((28 * W, CHANNELS), BF16)],
        in_specs=[pl.BlockSpec(memory_space=pltpu.HBM)] * 2,
        out_specs=[pl.BlockSpec(memory_space=pltpu.VMEM)] * 8,
        scratch_shapes=[
            pltpu.VMEM((PIXELS, CHANNELS), BF16),
            pltpu.VMEM((3, PIXELS, 128), F32),
            pltpu.VMEM((6, SENT, 128), F32),
            pltpu.SemaphoreType.DMA((3,)),
            pltpu.SemaphoreType.DMA((18,)),
        ],
        compiler_params=pltpu.CompilerParams(vmem_limit_bytes=28 * 2**20),
        name="outward_sums",
    )(features, dilated)


def own_kernel(ordered, _, bias, dilated, point, *refs):
    outs, weights, sems = refs[0:2], refs[2], refs[3]
    fetches = [pltpu.make_async_copy(point, weights.at[pl.ds(0, W)], sems.at[0])]
    for q, place in enumerate((1, 2, 3, 22, 23, 24, 25, 26, 27)):
        fetches.append(fetch_tap(dilated, weights, sems.at[q + 1], place))
    for fetch in fetches:
        fetch.start()
    for fetch in fetches[:4]:
        fetch.wait()
    d = nt(ordered[...], weights[:256, :])
    for part, out in enumerate(outs):
        line = jnp.concatenate([bias[k : k + 1, :] for k in PARTS[part]], 1)
        out[...] = d[:, part * 128 : part * 128 + 128] + line
    low = low_lanes((PIXELS, 128))

    def add(first, value, k):
        part = k % 2
        rows = slice(first * BLOCK, first * BLOCK + value.shape[0])
        mask, value = low[: value.shape[0]], value[:, part * 128 : part * 128 + 128]
        kept = jnp.where(mask, value, 0.0) if k == 1 else jnp.where(mask, 0.0, value)
        outs[part][rows, :] = outs[part][rows, :] + kept

    for fetch in fetches[4:7]:
        fetch.wait()
    d = nt(ordered[: 3 * BLOCK, :], weights[LEFT_AT - W : LEFT_AT + 3 * W, :])
    for k in (1, 2, 3):
        add(k, d[: (4 - k) * BLOCK], k)
    for fetch in fetches[7:]:
        fetch.wait()
    d = nt(ordered[BLOCK:, :], weights[RIGHT_AT - W : RIGHT_AT + 3 * W, :])
    for k in (1, 2, 3):
        add(0, d[(k - 1) * BLOCK :], k)


def own_sums(ordered, weights, bias, dilated, point):
    return pl.pallas_call(
        own_kernel,
        out_shape=[jax.ShapeDtypeStruct((PIXELS, 128), F32)] * 2
        + [pltpu.VMEM((28 * W, CHANNELS), BF16)],
        in_specs=[pl.BlockSpec(memory_space=pltpu.VMEM)] * 3
        + [pl.BlockSpec(memory_space=pltpu.HBM)] * 2,
        out_specs=[pl.BlockSpec(memory_space=pltpu.VMEM)] * 3,
        scratch_shapes=[pltpu.SemaphoreType.DMA((10,))],
        input_output_aliases={1: 2},
        compiler_params=pltpu.CompilerParams(vmem_limit_bytes=18 * 2**20),
        cost_estimate=pl.CostEstimate(flops=10**6, bytes_accessed=10**4, transcendentals=0),
        name="own_sums",
    )(ordered, weights, bias, dilated, point)


def arrival_slot(row, other):
    return jnp.where((other >= 0) & (other < 8), row ^ other, 0)


def gather_arrivals(recv, arrivals, swaps):
    arrivals[0] = jnp.zeros((HALF, 128), arrivals.dtype)
    for n, x in enumerate(swaps):
        arrivals[x] = recv[n][...] if recv[n].shape[0] == HALF else unscaled(recv[n][...])


def activation_kernel(part, swaps, own, *refs):
    recv, acts, arrivals = refs[: len(swaps)], refs[-2], refs[-1]
    row = lax.axis_index("rows")
    gather_arrivals(recv, arrivals, swaps)
    low = low_lanes((HALF, 128))

    def total(k):
        return arrivals[arrival_slot(row, row - k)] + arrivals[arrival_slot(row, row + k)]

    high = total(PARTS[part][1])
    top, bottom = jnp.where(low, 0.0, pltpu.roll(high, W, 1)), jnp.where(low, 0.0, high)
    if part:
        left = total(PARTS[part][0])
        top = jnp.where(low, left, top)
        bottom = jnp.where(low, pltpu.roll(left, W, 1), bottom)
    acts[:HALF, :] = jnp.maximum(own[:HALF, :] + top, 0.0).astype(BF16)
    acts[HALF:, :] = jnp.maximum(own[HALF:, :] + bottom, 0.0).astype(BF16)


def activations_of(part, swaps, own, received):
    return pl.pallas_call(
        functools.partial(activation_kernel, part, swaps),
        out_shape=jax.ShapeDtypeStruct((PIXELS, 128), BF16),
        in_specs=[pl.BlockSpec(memory_space=pltpu.VMEM)] * (1 + len(swaps)),
        out_specs=pl.BlockSpec(memory_space=pltpu.VMEM),
        scratch_shapes=[pltpu.VMEM((8, HALF, 128), F32)],
        compiler_params=pltpu.CompilerParams(vmem_limit_bytes=8 * 2**20),
        name="activations",
    )(own, *received)


def project_rows(project, who):
    at = pl.multiple_of(who * W, W)
    return jnp.concatenate([project[k, pl.ds(at, W), :] for part in PARTS for k in part], 0)


def both(a, b):
    return jnp.concatenate([a[...], b[...]], 1)


def near_head_kernel(a0, b0, a1, b1, project, bias, cotangent, pre, ordered):
    member = lax.axis_index("filt")
    pre[...] = nn(both(a0, b0), project_rows(project, member)) + bias[...]
    pre[...] = pre[...] + nn(both(a1, b1), project_rows(project, member ^ 1))
    order = order_matrix()
    for g in range(3):
        moved = nn(order, cotangent[g * 192 : (g + 1) * 192, :])
        for m in range(4):
            at = m * BLOCK + g * 48
            ordered[at : at + 48, :] = moved[m * 48 : (m + 1) * 48]


def near_head(own, beside, project, bias, cotangent):
    return pl.pallas_call(
        near_head_kernel,
        out_shape=[jax.ShapeDtypeStruct((PIXELS, 256), F32)] * 2,
        in_specs=[pl.BlockSpec(memory_space=pltpu.VMEM)] * 7,
        out_specs=[pl.BlockSpec(memory_space=pltpu.VMEM)] * 2,
        compiler_params=pltpu.CompilerParams(vmem_limit_bytes=10 * 2**20),
        name="near_head",
    )(*own, *beside, project, bias, cotangent)


def far_head_kernel(a0, b0, a2, b2, a3, b3, project, near, cotangent, *refs):
    output, grads, sends, packed = refs[0], refs[1], refs[2:8], refs[8]
    row, member = lax.axis_index("rows"), lax.axis_index("filt")
    pre = near[...] + nn(both(a2, b2), project_rows(project, member ^ 2))
    pre = pre + nn(both(a3, b3), project_rows(project, member ^ 3))
    output[...] = jnp.maximum(pre, 0.0).astype(BF16)
    head_grad = jnp.where(pre > 0, cotangent[...], 0.0).astype(BF16)
    act_grad = nt(head_grad, project_rows(project, member))
    a = jnp.where(a0[...].astype(F32) > 0, act_grad[:, :128], 0.0)
    b = jnp.where(b0[...].astype(F32) > 0, act_grad[:, 128:], 0.0)
    grads[:, :128] = a.astype(BF16)
    grads[:, 128:] = b.astype(BF16)
    low = low_lanes((HALF, 128))
    packed[0] = jnp.where(low, b[:HALF], pltpu.roll(b[HALF:], W, 1)).astype(BF16)
    packed[1] = jnp.where(low, pltpu.roll(a[:HALF], W, 1), a[HALF:]).astype(BF16)
    packed[2] = jnp.where(low, pltpu.roll(b[:HALF], W, 1), b[HALF:]).astype(BF16)
    for n, x in enumerate(GRAD_SWAPS):
        apart = jnp.abs((row ^ x) - row)
        sends[n][...] = packed[jnp.where(apart <= 3, apart - 1, 0)]


def far_head(own, across, corner, project, near, cotangent):
    return pl.pallas_call(
        far_head_kernel,
        out_shape=[jax.ShapeDtypeStruct((PIXELS, 256), BF16)] * 2
        + [jax.ShapeDtypeStruct((HALF, 128), BF16)] * 6,
        in_specs=[pl.BlockSpec(memory_space=pltpu.VMEM)] * 9,
        out_specs=[pl.BlockSpec(memory_space=pltpu.VMEM)] * 8,
        scratch_shapes=[pltpu.VMEM((3, HALF, 128), BF16)],
        compiler_params=pltpu.CompilerParams(vmem_limit_bytes=12 * 2**20),
        name="far_head",
    )(*own, *across, *corner, project, near, cotangent)


def own_output_kernel(output, out):
    member = lax.axis_index("filt")
    mine = jnp.zeros((PIXELS, W), F32)
    for q in range(4):
        mine = jnp.where(member == q, output[:, q * W : (q + 1) * W].astype(F32), mine)

    def put(at, value):
        out[at : at + 192, :] = value

    from_blocks(order_matrix(True), mine.astype(BF16), put)


def own_output(output):
    return pl.pallas_call(
        own_output_kernel,
        out_shape=jax.ShapeDtypeStruct((PIXELS, W), BF16),
        in_specs=[pl.BlockSpec(memory_space=pltpu.VMEM)],
        out_specs=pl.BlockSpec(memory_space=pltpu.VMEM),
        compiler_params=pltpu.CompilerParams(vmem_limit_bytes=6 * 2**20),
        name="own_output",
    )(output)


def spread_kernel(own, *refs):
    recv, stack, arrivals, pairs, twice = refs[:6], refs[6], refs[7], refs[8], refs[9]
    row = lax.axis_index("rows")
    gather_arrivals(recv, arrivals, GRAD_SWAPS)
    low = low_lanes((HALF, 128))
    low_all = low_lanes((PIXELS, 128))
    for k in (1, 2, 3):
        p = arrivals[arrival_slot(row, row + k)].astype(F32)
        m = arrivals[arrival_slot(row, row - k)].astype(F32)
        pairs[k - 1, :HALF, :] = jnp.where(low, p, pltpu.roll(m, W, 1)).astype(BF16)
        pairs[k - 1, HALF:, :] = jnp.where(low, pltpu.roll(p, W, 1), m).astype(BF16)
        g = own[:, :128].astype(F32) if k == 2 else own[:, 128:].astype(F32)
        other = pltpu.roll(g, W, 1)
        two = jnp.where(low_all, g, other) if k == 1 else jnp.where(low_all, other, g)
        twice[k - 1] = two.astype(BF16)
    stack[:, : 4 * W] = own[...]
    nothing = jnp.zeros((BLOCK, 128), BF16)

    def block_of(ref, k, source):
        if 0 <= source < 4:
            return ref[k - 1, source * BLOCK : (source + 1) * BLOCK, :]
        return nothing

    for q, (k, j) in enumerate(OUT_PAIRS):
        lanes = slice(OUT_AT + q * 128, OUT_AT + q * 128 + 128)
        for m in range(4):
            stack[m * BLOCK : (m + 1) * BLOCK, lanes] = block_of(pairs, k, m - (j - 1) * k)
    low_block = low_lanes((BLOCK, 128))
    for q, (a, b) in enumerate(((2, 1), (3, -2), (-1, -3))):
        lanes = slice(LEFT_AT + q * 128, LEFT_AT + q * 128 + 128)
        for m in range(4):
            stack[m * BLOCK : (m + 1) * BLOCK, lanes] = jnp.where(
                low_block, block_of(twice, abs(a), m + a), block_of(twice, abs(b), m + b)
            )


def spread(own, received):
    return pl.pallas_call(
        spread_kernel,
        out_shape=pltpu.VMEM((PIXELS, 28 * W), BF16),
        in_specs=[pl.BlockSpec(memory_space=pltpu.VMEM)] * 7,
        out_specs=pl.BlockSpec(memory_space=pltpu.VMEM),
        scratch_shapes=[
            pltpu.VMEM((8, HALF, 128), BF16),
            pltpu.VMEM((3, PIXELS, 128), BF16),
            pltpu.VMEM((3, PIXELS, 128), BF16),
        ],
        compiler_params=pltpu.CompilerParams(vmem_limit_bytes=12 * 2**20),
        name="spread",
    )(own, *received)


def grad_kernel(flips, stack, weights, *outs):
    member = lax.axis_index("filt")
    for out, flip in zip(outs, flips):
        columns = pl.ds(pl.multiple_of((member ^ flip) * 512, 512), 512)
        out[...] = nn(stack[...], weights[:, columns]).astype(BF16)


def grads_for(flips, stack, weights, scale=1):
    return pl.pallas_call(
        functools.partial(grad_kernel, flips),
        out_shape=[jax.ShapeDtypeStruct((PIXELS, 512), BF16)] * len(flips),
        in_specs=[pl.BlockSpec(memory_space=pltpu.VMEM)] * 2,
        out_specs=[pl.BlockSpec(memory_space=pltpu.VMEM)] * len(flips),
        compiler_params=pltpu.CompilerParams(vmem_limit_bytes=18 * 2**20),
        cost_estimate=pl.CostEstimate(
            flops=2 * PIXELS * 28 * W * 512 * scale, bytes_accessed=10**6, transcendentals=0
        ),
        name="grads_for",
    )(stack, weights)


def last_kernel(a, b, c, out):
    total = a[...].astype(F32) + b[...].astype(F32) + c[...].astype(F32)

    def put(at, value):
        out[at : at + 192, :] = value

    from_blocks(order_matrix(True), total.astype(BF16), put)


def last_sum(a, b, c):
    return pl.pallas_call(
        last_kernel,
        out_shape=jax.ShapeDtypeStruct((PIXELS, 512), BF16),
        in_specs=[pl.BlockSpec(memory_space=pltpu.VMEM)] * 3,
        out_specs=pl.BlockSpec(memory_space=pltpu.VMEM),
        compiler_params=pltpu.CompilerParams(vmem_limit_bytes=10 * 2**20),
        name="last_sum",
    )(a, b, c)


def flipped(x, bit):
    return lax.ppermute(x, "filt", [(i, i ^ bit) for i in range(lax.axis_size("filt"))])


def swapped(x, bits):
    pairs = [(r, r ^ bits) for r in range(8) if abs((r ^ bits) - r) <= 3]
    return lax.ppermute(x, "rows", pairs)


def on_device(
    features, point_weight, dilated_weight, branch_bias, project_weight, project_bias, cotangent
):
    flat = features.reshape(PIXELS, CHANNELS)
    dilated = jnp.transpose(dilated_weight, (0, 1, 2, 4, 3)).reshape(27, W, CHANNELS)
    point = point_weight.T
    flat, dilated, point = (
        pltpu.with_memory_space_constraint(x, pltpu.HBM) for x in (flat, dilated, point)
    )
    *sums, ordered, weights = outward_sums(flat, dilated)
    received = {
        x: swapped(sums[n].astype(jnp.float16), x).astype(F32) for n, x in enumerate(SWAPS)
    }
    *own, weights = own_sums(ordered, weights, branch_bias, dilated, point)
    acts = [
        activations_of(part, swaps, own[part], [received[x] for x in swaps])
        for part, swaps in ((0, SWAPS[:2]), (1, SWAPS[2:]))
    ]
    across = [flipped(x, 2) for x in acts]
    beside = [flipped(x, 1) for x in acts]
    corner = [flipped(x, 1) for x in across]
    near, ordered_cotangent = near_head(
        acts,
        beside,
        project_weight,
        project_bias.reshape(1, 256),
        cotangent.reshape(PIXELS, 256),
    )
    output, grads, *sends = far_head(
        acts, across, corner, project_weight, near, ordered_cotangent
    )
    arrived = [swapped(sends[n], x) for n, x in enumerate(GRAD_SWAPS)]
    stack = spread(grads, arrived)
    (far,) = grads_for((3,), stack, weights)
    far = flipped(far, 1)
    (kept,) = grads_for((2,), stack, weights)
    crossing = (far.astype(F32) + kept.astype(F32)).astype(BF16)
    crossed = flipped(crossing, 2)
    later, output, crossing = lax.optimization_barrier((stack, output, crossing))
    head_output = own_output(output)
    (near,) = grads_for((1,), later, weights)
    near = flipped(near, 1)
    (kept,) = grads_for((0,), later, weights, 8)
    feature_grad = last_sum(kept, near, crossed)
    return head_output.reshape(12, 48, W), feature_grad.reshape(12, 48, 512)


def solution(mesh):
    body = on_device if fits(mesh) else on_device_general
    in_specs = (
        P("rows", None, None),
        P(None, "filt"),
        P(None, None, None, None, "filt"),
        P(None, "filt"),
        P(),
        P(),
        P("rows", None, None),
    )
    out_specs = (P("rows", None, "filt"), P("rows", None, "filt"))
    return jax.shard_map(
        body, mesh=mesh, in_specs=in_specs, out_specs=out_specs, check_vma=False
    )
```

```python
import functools

import jax
import jax.numpy as jnp
from jax import lax
from jax.experimental import pallas as pl
from jax.experimental.pallas import tpu as pltpu
from jax.sharding import PartitionSpec as P

FIRST_DILATION = 12
SECOND_DILATION = 24
THIRD_DILATION = 36


def passed_along(x, axis, by):
    devices = lax.axis_size(axis)
    pairs = [(i, i + by) for i in range(devices) if 0 <= i + by < devices]
    return lax.ppermute(x, axis, pairs)


def shift_columns(field, amount):
    breadth = field.shape[1]
    if amount == 0:
        return field
    padding = [(0, 0)] * field.ndim
    if amount > 0:
        kept = field[:, amount:]
        padding[1] = (0, amount)
    else:
        kept = field[:, : breadth + amount]
        padding[1] = (-amount, 0)
    return jnp.pad(kept, padding)


def fetch_sums(field, offset):
    return passed_along(field, "rows", offset)


def fetch_grads(field, offset):
    return passed_along(field, "rows", offset)


def shift_rows(field, amount, fetcher):
    height = field.shape[0]
    quotient = amount // height

    def extract_block(offset):
        if offset == 0:
            return field
        return fetcher(field, offset)

    return extract_block(quotient)


def make_kernel_taps(variants, dilation_rates):
    stacked = [variants[:, :, 0]]
    for branch, dilation in enumerate(dilation_rates):
        for row_tap in range(3):
            source = variants[:, :, 1 + 3 * branch + row_tap]
            for col_tap in range(3):
                stacked.append(shift_columns(source, -(col_tap - 1) * dilation))
    return jnp.stack(stacked, 2)


def on_device_general(
    features, point_weight, dilated_weight, branch_bias, project_weight, project_bias, cotangent
):
    height, breadth, channels = features.shape
    pixels = height * breadth
    own_width = point_weight.shape[1]
    filters = lax.axis_size("filt")
    member = lax.axis_index("filt")
    branch_outputs = project_weight.shape[2]
    own_out = branch_outputs // filters
    own_channels = channels // filters
    dilation_rates = (FIRST_DILATION, SECOND_DILATION, THIRD_DILATION)
    all_weights = jnp.concatenate(
        [point_weight[None], dilated_weight.reshape(27, channels, own_width)], 0
    )
    flattened = features.reshape(pixels, channels)
    tap_terms = jnp.einsum(
        "pc,tco->pto", flattened, all_weights, preferred_element_type=jnp.float32
    )
    tap_terms = tap_terms.reshape(height, breadth, 28, own_width)
    pre_list = [tap_terms[:, :, 0, :] + branch_bias[0]]
    for branch, dilation in enumerate(dilation_rates):
        summed_result = jnp.zeros((height, breadth, own_width), jnp.float32)
        for row_tap in range(3):
            row_sum = jnp.zeros((height, breadth, own_width), jnp.float32)
            for col_tap in range(3):
                row_sum = row_sum + shift_columns(
                    tap_terms[:, :, 1 + 9 * branch + 3 * row_tap + col_tap, :],
                    (col_tap - 1) * dilation,
                )
            summed_result = summed_result + shift_rows(
                row_sum, -(row_tap - 1) * dilation, fetch_sums
            )
        pre_list.append(summed_result + branch_bias[branch + 1])
    branch_pre = jnp.stack(pre_list, 2)
    activations = jnp.maximum(branch_pre, 0.0).astype(jnp.bfloat16).reshape(pixels, 4 * own_width)
    grouped = project_weight.reshape(4, filters, own_width, branch_outputs)
    own_rows = lax.dynamic_index_in_dim(grouped, member, 1, keepdims=False).reshape(
        4 * own_width, branch_outputs
    )
    flat_cotangent = cotangent.reshape(pixels, branch_outputs)
    ordered = jnp.transpose(grouped, (1, 0, 2, 3)).reshape(filters * 4 * own_width, branch_outputs)
    project_pre = jnp.dot(
        lax.all_gather(activations, "filt", axis=1, tiled=True),
        ordered,
        preferred_element_type=jnp.float32,
    )
    project_pre = project_pre + project_bias
    head_grad = jnp.where(project_pre > 0, flat_cotangent.astype(jnp.float32), 0.0).astype(
        jnp.bfloat16
    )
    own_pre = lax.dynamic_slice_in_dim(project_pre, member * own_out, own_out, 1)
    act_grad = jnp.dot(head_grad, own_rows.T, preferred_element_type=jnp.float32)
    head_output = jnp.maximum(own_pre, 0.0).astype(jnp.bfloat16).reshape(height, breadth, own_out)
    branch_grad = jnp.where(
        branch_pre > 0, act_grad.reshape(height, breadth, 4, own_width), 0.0
    ).astype(jnp.bfloat16)
    variant_list = [branch_grad[:, :, 0, :]]
    for branch, dilation in enumerate(dilation_rates):
        for row_tap in range(3):
            variant_list.append(
                shift_rows(branch_grad[:, :, branch + 1, :], (row_tap - 1) * dilation, fetch_grads)
            )
    variants = jnp.stack(variant_list, 2)
    stacked = make_kernel_taps(variants, dilation_rates).reshape(pixels, 28, own_width)
    input_grad = lax.psum_scatter(
        jnp.einsum("pto,tco->cp", stacked, all_weights, preferred_element_type=jnp.float32),
        "filt",
        scatter_dimension=0,
        tiled=True,
    ).T
    feature_grad = input_grad.astype(jnp.bfloat16).reshape(height, breadth, own_channels)
    return (head_output, feature_grad)


W = 64
BLOCK = 144
PIXELS = 576
HALF = 288
SENT = 304
CHANNELS = 2048
F32 = jnp.float32
BF16 = jnp.bfloat16

OUT_PAIRS = ((3, 1), (1, 1), (3, 0), (1, 0), (3, 2), (1, 2), (2, 1), (2, 0), (2, 2))
TAPS = (
    [(k, 1, 1) for k in (2, 1, 3)]
    + [(k, i, j) for k, j in OUT_PAIRS for i in (0, 2)]
    + [(k, 1, j) for j in (0, 2) for k in (2, 1, 3)]
)
OUT_AT, LEFT_AT, RIGHT_AT = 4 * W, 22 * W, 25 * W
PARTS = ((0, 2), (1, 3))
SWAPS = (6, 2, 1, 3, 7, 5)
GRAD_SWAPS = (1, 5, 7, 3, 6, 2)


def fits(mesh):
    return mesh.shape["rows"] == 8 and mesh.shape["filt"] == 4


def order_matrix(turned=False):
    to = lax.broadcasted_iota(jnp.int32, (192, 192), 1 if turned else 0)
    source = lax.broadcasted_iota(jnp.int32, (192, 192), 0 if turned else 1)

    def parts(value, width):
        return sum((value >= n * width).astype(jnp.int32) for n in (1, 2, 3))

    block = parts(to, 48)
    within = to - 48 * block
    line = parts(within, 12)
    wanted = line * 48 + block * 12 + within - 12 * line
    return (source == wanted).astype(F32).astype(BF16)


def tap_index(tap):
    k, i, j = tap
    return (k - 1) * 9 + i * 3 + j


def nt(a, b):
    return lax.dot_general(a, b, (((1,), (1,)), ((), ())), preferred_element_type=F32)


def nn(a, b):
    return lax.dot_general(a, b, (((1,), (0,)), ((), ())), preferred_element_type=F32)


def from_blocks(order_t, value, write):
    for g in range(3):
        parts = [value[m * BLOCK + g * 48 : m * BLOCK + g * 48 + 48] for m in range(4)]
        write(g * 192, nn(order_t, jnp.concatenate(parts, 0)).astype(BF16))


def low_lanes(shape):
    return lax.broadcasted_iota(jnp.int32, shape, 1) % 128 < W


def scaled(value):
    most = jnp.maximum(jnp.max(jnp.abs(value), axis=0, keepdims=True), 1e-30)
    power = jnp.floor(jnp.log(most) * 1.4426950408889634)
    return value * jnp.exp2(13.0 - power), power


def unscaled(sent):
    return sent[:HALF, :] * jnp.exp2(sent[HALF : HALF + 1, :] - 13.0)


def outward_slot(row, x):
    other = row ^ x
    apart = jnp.abs(other - row)
    slot = apart - 1 + jnp.where(other < row, 3, 0)
    return jnp.where(apart <= 3, slot, 0)


def fetch_tap(dilated, weights, sem, place):
    return pltpu.make_async_copy(
        dilated.at[tap_index(TAPS[place - 1])], weights.at[pl.ds(place * W, W)], sem
    )


def outward_kernel(features, dilated, point, *refs):
    row = lax.axis_index("rows")
    out, ordered, weights = refs[0:6], refs[6], refs[7]
    raw, sums, packed, feature_sems, weight_sems = refs[8:]
    loads = []
    for g in range(3):
        rows = pl.ds(g * 192, 192)
        loads.append(pltpu.make_async_copy(features.at[rows], raw.at[rows], feature_sems.at[g]))
        loads[-1].start()
    queue = [
        fetch_tap(dilated, weights, weight_sems.at[q], place)
        for q, place in enumerate((*range(4, 28), 1, 2, 3))
    ]
    queue.append(pltpu.make_async_copy(point, weights.at[pl.ds(0, W)], weight_sems.at[27]))

    def start_loads(first, last):
        for fetch in queue[first:last]:
            fetch.start()

    start_loads(0, 4)
    order = order_matrix()
    for g in range(3):
        loads[g].wait()
        start_loads((4, 12, 18)[g], (12, 18, 28)[g])
        moved = nn(order, raw[g * 192 : (g + 1) * 192, :]).astype(BF16)
        for m in range(4):
            at = m * BLOCK + g * 48
            ordered[at : at + 48, :] = moved[m * 48 : (m + 1) * 48]

    def product(pair, pairs, first, last):
        for fetch in queue[2 * pair : 2 * (pair + pairs)]:
            fetch.wait()
        at = OUT_AT + pair * 128
        return nt(ordered[first * BLOCK : last * BLOCK, :], weights[at : at + pairs * 128, :])

    d = product(0, 2, 0, 4)
    sums[2] = d[:, :128]
    sums[0] = d[:, 128:]
    d = product(2, 2, 0, 3)
    sums[2, 3 * BLOCK :, :] = sums[2, 3 * BLOCK :, :] + d[:BLOCK, :128]
    sums[0, BLOCK:, :] = sums[0, BLOCK:, :] + d[:, 128:]
    d = product(4, 2, 1, 4)
    sums[2, :BLOCK, :] = sums[2, :BLOCK, :] + d[2 * BLOCK :, :128]
    sums[0, : 3 * BLOCK, :] = sums[0, : 3 * BLOCK, :] + d[:, 128:]
    low = low_lanes((HALF, 128))

    def pack(k):
        top, bottom = sums[k, :HALF, :], sums[k, HALF:, :]
        halves = (
            jnp.where(low, top, pltpu.roll(bottom, W, 1)),
            jnp.where(low, pltpu.roll(top, W, 1), bottom),
        )
        for way, value in enumerate(halves):
            value, power = scaled(value)
            packed[k + 3 * way, :HALF, :] = value
            packed[k + 3 * way, HALF:, :] = jnp.broadcast_to(power, (SENT - HALF, 128))

    pack(2)
    pack(0)
    d = product(6, 3, 0, 4)
    sums[1] = d[:, :128]
    sums[1, 2 * BLOCK :, :] = sums[1, 2 * BLOCK :, :] + d[: 2 * BLOCK, 128:256]
    sums[1, : 2 * BLOCK, :] = sums[1, : 2 * BLOCK, :] + d[2 * BLOCK :, 256:]
    pack(1)
    for n, x in enumerate(SWAPS):
        out[n][...] = packed[outward_slot(row, x)]
    for fetch in queue[18:]:
        fetch.wait()


def outward_sums(features, dilated, point):
    return pl.pallas_call(
        outward_kernel,
        out_shape=[jax.ShapeDtypeStruct((SENT, 128), F32)] * 6
        + [pltpu.VMEM((PIXELS, CHANNELS), BF16), pltpu.VMEM((28 * W, CHANNELS), BF16)],
        in_specs=[pl.BlockSpec(memory_space=pltpu.HBM)] * 3,
        out_specs=[pl.BlockSpec(memory_space=pltpu.VMEM)] * 8,
        scratch_shapes=[
            pltpu.VMEM((PIXELS, CHANNELS), BF16),
            pltpu.VMEM((3, PIXELS, 128), F32),
            pltpu.VMEM((6, SENT, 128), F32),
            pltpu.SemaphoreType.DMA((3,)),
            pltpu.SemaphoreType.DMA((28,)),
        ],
        compiler_params=pltpu.CompilerParams(vmem_limit_bytes=28 * 2**20),
        name="outward_sums",
    )(features, dilated, point)


def own_kernel(ordered, weights, bias, *outs):
    d = nt(ordered[...], weights[:256, :])
    for part, out in enumerate(outs):
        line = jnp.concatenate([bias[k : k + 1, :] for k in PARTS[part]], 1)
        out[...] = d[:, part * 128 : part * 128 + 128] + line
    low = low_lanes((PIXELS, 128))

    def add(first, value, k):
        part = k % 2
        rows = slice(first * BLOCK, first * BLOCK + value.shape[0])
        mask, value = low[: value.shape[0]], value[:, part * 128 : part * 128 + 128]
        kept = jnp.where(mask, value, 0.0) if k == 1 else jnp.where(mask, 0.0, value)
        outs[part][rows, :] = outs[part][rows, :] + kept

    d = nt(ordered[: 3 * BLOCK, :], weights[LEFT_AT - W : LEFT_AT + 3 * W, :])
    for k in (1, 2, 3):
        add(k, d[: (4 - k) * BLOCK], k)
    d = nt(ordered[BLOCK:, :], weights[RIGHT_AT - W : RIGHT_AT + 3 * W, :])
    for k in (1, 2, 3):
        add(0, d[(k - 1) * BLOCK :], k)


def own_sums(ordered, weights, bias):
    return pl.pallas_call(
        own_kernel,
        out_shape=[jax.ShapeDtypeStruct((PIXELS, 128), F32)] * 2,
        in_specs=[pl.BlockSpec(memory_space=pltpu.VMEM)] * 3,
        out_specs=[pl.BlockSpec(memory_space=pltpu.VMEM)] * 2,
        compiler_params=pltpu.CompilerParams(vmem_limit_bytes=18 * 2**20),
        cost_estimate=pl.CostEstimate(flops=10**6, bytes_accessed=10**4, transcendentals=0),
        name="own_sums",
    )(ordered, weights, bias)


def arrival_slot(row, other):
    return jnp.where((other >= 0) & (other < 8), row ^ other, 0)


def gather_arrivals(recv, arrivals, swaps):
    arrivals[0] = jnp.zeros((HALF, 128), arrivals.dtype)
    for n, x in enumerate(swaps):
        arrivals[x] = recv[n][...] if recv[n].shape[0] == HALF else unscaled(recv[n][...])


def activation_kernel(part, swaps, own, *refs):
    recv, acts, arrivals = refs[: len(swaps)], refs[-2], refs[-1]
    row = lax.axis_index("rows")
    gather_arrivals(recv, arrivals, swaps)
    low = low_lanes((HALF, 128))

    def total(k):
        return arrivals[arrival_slot(row, row - k)] + arrivals[arrival_slot(row, row + k)]

    high = total(PARTS[part][1])
    top, bottom = jnp.where(low, 0.0, pltpu.roll(high, W, 1)), jnp.where(low, 0.0, high)
    if part:
        left = total(PARTS[part][0])
        top = jnp.where(low, left, top)
        bottom = jnp.where(low, pltpu.roll(left, W, 1), bottom)
    acts[:HALF, :] = jnp.maximum(own[:HALF, :] + top, 0.0).astype(BF16)
    acts[HALF:, :] = jnp.maximum(own[HALF:, :] + bottom, 0.0).astype(BF16)


def activations_of(part, swaps, own, received):
    return pl.pallas_call(
        functools.partial(activation_kernel, part, swaps),
        out_shape=jax.ShapeDtypeStruct((PIXELS, 128), BF16),
        in_specs=[pl.BlockSpec(memory_space=pltpu.VMEM)] * (1 + len(swaps)),
        out_specs=pl.BlockSpec(memory_space=pltpu.VMEM),
        scratch_shapes=[pltpu.VMEM((8, HALF, 128), F32)],
        compiler_params=pltpu.CompilerParams(vmem_limit_bytes=8 * 2**20),
        name="activations",
    )(own, *received)


def project_rows(project, who):
    at = pl.multiple_of(who * W, W)
    return jnp.concatenate([project[k, pl.ds(at, W), :] for part in PARTS for k in part], 0)


def both(a, b):
    return jnp.concatenate([a[...], b[...]], 1)


def near_head_kernel(a0, b0, a1, b1, project, bias, cotangent, pre, ordered):
    member = lax.axis_index("filt")
    pre[...] = nn(both(a0, b0), project_rows(project, member)) + bias[...]
    pre[...] = pre[...] + nn(both(a1, b1), project_rows(project, member ^ 1))
    order = order_matrix()
    for g in range(3):
        moved = nn(order, cotangent[g * 192 : (g + 1) * 192, :])
        for m in range(4):
            at = m * BLOCK + g * 48
            ordered[at : at + 48, :] = moved[m * 48 : (m + 1) * 48]


def near_head(own, beside, project, bias, cotangent):
    return pl.pallas_call(
        near_head_kernel,
        out_shape=[jax.ShapeDtypeStruct((PIXELS, 256), F32)] * 2,
        in_specs=[pl.BlockSpec(memory_space=pltpu.VMEM)] * 7,
        out_specs=[pl.BlockSpec(memory_space=pltpu.VMEM)] * 2,
        compiler_params=pltpu.CompilerParams(vmem_limit_bytes=10 * 2**20),
        name="near_head",
    )(*own, *beside, project, bias, cotangent)


def far_head_kernel(a0, b0, a2, b2, a3, b3, project, near, cotangent, *refs):
    output, grads, sends, packed = refs[0], refs[1], refs[2:8], refs[8]
    row, member = lax.axis_index("rows"), lax.axis_index("filt")
    pre = near[...] + nn(both(a2, b2), project_rows(project, member ^ 2))
    pre = pre + nn(both(a3, b3), project_rows(project, member ^ 3))
    output[...] = jnp.maximum(pre, 0.0).astype(BF16)
    head_grad = jnp.where(pre > 0, cotangent[...], 0.0).astype(BF16)
    act_grad = nt(head_grad, project_rows(project, member))
    a = jnp.where(a0[...].astype(F32) > 0, act_grad[:, :128], 0.0)
    b = jnp.where(b0[...].astype(F32) > 0, act_grad[:, 128:], 0.0)
    grads[:, :128] = a.astype(BF16)
    grads[:, 128:] = b.astype(BF16)
    low = low_lanes((HALF, 128))
    packed[0] = jnp.where(low, b[:HALF], pltpu.roll(b[HALF:], W, 1)).astype(BF16)
    packed[1] = jnp.where(low, pltpu.roll(a[:HALF], W, 1), a[HALF:]).astype(BF16)
    packed[2] = jnp.where(low, pltpu.roll(b[:HALF], W, 1), b[HALF:]).astype(BF16)
    for n, x in enumerate(GRAD_SWAPS):
        apart = jnp.abs((row ^ x) - row)
        sends[n][...] = packed[jnp.where(apart <= 3, apart - 1, 0)]


def far_head(own, across, corner, project, near, cotangent):
    return pl.pallas_call(
        far_head_kernel,
        out_shape=[jax.ShapeDtypeStruct((PIXELS, 256), BF16)] * 2
        + [jax.ShapeDtypeStruct((HALF, 128), BF16)] * 6,
        in_specs=[pl.BlockSpec(memory_space=pltpu.VMEM)] * 9,
        out_specs=[pl.BlockSpec(memory_space=pltpu.VMEM)] * 8,
        scratch_shapes=[pltpu.VMEM((3, HALF, 128), BF16)],
        compiler_params=pltpu.CompilerParams(vmem_limit_bytes=12 * 2**20),
        name="far_head",
    )(*own, *across, *corner, project, near, cotangent)


def own_output_kernel(output, out):
    member = lax.axis_index("filt")
    mine = jnp.zeros((PIXELS, W), F32)
    for q in range(4):
        mine = jnp.where(member == q, output[:, q * W : (q + 1) * W].astype(F32), mine)

    def put(at, value):
        out[at : at + 192, :] = value

    from_blocks(order_matrix(True), mine.astype(BF16), put)


def own_output(output):
    return pl.pallas_call(
        own_output_kernel,
        out_shape=jax.ShapeDtypeStruct((PIXELS, W), BF16),
        in_specs=[pl.BlockSpec(memory_space=pltpu.VMEM)],
        out_specs=pl.BlockSpec(memory_space=pltpu.VMEM),
        compiler_params=pltpu.CompilerParams(vmem_limit_bytes=6 * 2**20),
        name="own_output",
    )(output)


def spread_kernel(own, *refs):
    recv, stack, arrivals, pairs, twice = refs[:6], refs[6], refs[7], refs[8], refs[9]
    row = lax.axis_index("rows")
    gather_arrivals(recv, arrivals, GRAD_SWAPS)
    low = low_lanes((HALF, 128))
    low_all = low_lanes((PIXELS, 128))
    for k in (1, 2, 3):
        p = arrivals[arrival_slot(row, row + k)].astype(F32)
        m = arrivals[arrival_slot(row, row - k)].astype(F32)
        pairs[k - 1, :HALF, :] = jnp.where(low, p, pltpu.roll(m, W, 1)).astype(BF16)
        pairs[k - 1, HALF:, :] = jnp.where(low, pltpu.roll(p, W, 1), m).astype(BF16)
        g = own[:, :128].astype(F32) if k == 2 else own[:, 128:].astype(F32)
        other = pltpu.roll(g, W, 1)
        two = jnp.where(low_all, g, other) if k == 1 else jnp.where(low_all, other, g)
        twice[k - 1] = two.astype(BF16)
    stack[:, : 4 * W] = own[...]
    nothing = jnp.zeros((BLOCK, 128), BF16)

    def block_of(ref, k, source):
        if 0 <= source < 4:
            return ref[k - 1, source * BLOCK : (source + 1) * BLOCK, :]
        return nothing

    for q, (k, j) in enumerate(OUT_PAIRS):
        lanes = slice(OUT_AT + q * 128, OUT_AT + q * 128 + 128)
        for m in range(4):
            stack[m * BLOCK : (m + 1) * BLOCK, lanes] = block_of(pairs, k, m - (j - 1) * k)
    low_block = low_lanes((BLOCK, 128))
    for q, (a, b) in enumerate(((2, 1), (3, -2), (-1, -3))):
        lanes = slice(LEFT_AT + q * 128, LEFT_AT + q * 128 + 128)
        for m in range(4):
            stack[m * BLOCK : (m + 1) * BLOCK, lanes] = jnp.where(
                low_block, block_of(twice, abs(a), m + a), block_of(twice, abs(b), m + b)
            )


def spread(own, received):
    return pl.pallas_call(
        spread_kernel,
        out_shape=pltpu.VMEM((PIXELS, 28 * W), BF16),
        in_specs=[pl.BlockSpec(memory_space=pltpu.VMEM)] * 7,
        out_specs=pl.BlockSpec(memory_space=pltpu.VMEM),
        scratch_shapes=[
            pltpu.VMEM((8, HALF, 128), BF16),
            pltpu.VMEM((3, PIXELS, 128), BF16),
            pltpu.VMEM((3, PIXELS, 128), BF16),
        ],
        compiler_params=pltpu.CompilerParams(vmem_limit_bytes=12 * 2**20),
        name="spread",
    )(own, *received)


def grad_kernel(flips, stack, weights, *outs):
    member = lax.axis_index("filt")
    for out, flip in zip(outs, flips):
        columns = pl.ds(pl.multiple_of((member ^ flip) * 512, 512), 512)
        out[...] = nn(stack[...], weights[:, columns]).astype(BF16)


def grads_for(flips, stack, weights, scale=1):
    return pl.pallas_call(
        functools.partial(grad_kernel, flips),
        out_shape=[jax.ShapeDtypeStruct((PIXELS, 512), BF16)] * len(flips),
        in_specs=[pl.BlockSpec(memory_space=pltpu.VMEM)] * 2,
        out_specs=[pl.BlockSpec(memory_space=pltpu.VMEM)] * len(flips),
        compiler_params=pltpu.CompilerParams(vmem_limit_bytes=18 * 2**20),
        cost_estimate=pl.CostEstimate(
            flops=2 * PIXELS * 28 * W * 512 * scale, bytes_accessed=10**6, transcendentals=0
        ),
        name="grads_for",
    )(stack, weights)


def last_kernel(a, b, c, out):
    total = a[...].astype(F32) + b[...].astype(F32) + c[...].astype(F32)

    def put(at, value):
        out[at : at + 192, :] = value

    from_blocks(order_matrix(True), total.astype(BF16), put)


def last_sum(a, b, c):
    return pl.pallas_call(
        last_kernel,
        out_shape=jax.ShapeDtypeStruct((PIXELS, 512), BF16),
        in_specs=[pl.BlockSpec(memory_space=pltpu.VMEM)] * 3,
        out_specs=pl.BlockSpec(memory_space=pltpu.VMEM),
        compiler_params=pltpu.CompilerParams(vmem_limit_bytes=10 * 2**20),
        name="last_sum",
    )(a, b, c)


def flipped(x, bit):
    return lax.ppermute(x, "filt", [(i, i ^ bit) for i in range(lax.axis_size("filt"))])


def swapped(x, bits):
    pairs = [(r, r ^ bits) for r in range(8) if abs((r ^ bits) - r) <= 3]
    return lax.ppermute(x, "rows", pairs)


def on_device(
    features, point_weight, dilated_weight, branch_bias, project_weight, project_bias, cotangent
):
    flat = features.reshape(PIXELS, CHANNELS)
    dilated = jnp.transpose(dilated_weight, (0, 1, 2, 4, 3)).reshape(27, W, CHANNELS)
    point = point_weight.T
    flat, dilated, point = (
        pltpu.with_memory_space_constraint(x, pltpu.HBM) for x in (flat, dilated, point)
    )
    *sums, ordered, weights = outward_sums(flat, dilated, point)
    received = {
        x: swapped(sums[n].astype(jnp.float16), x).astype(F32) for n, x in enumerate(SWAPS)
    }
    own = own_sums(ordered, weights, branch_bias)
    acts = [
        activations_of(part, swaps, own[part], [received[x] for x in swaps])
        for part, swaps in ((0, SWAPS[:2]), (1, SWAPS[2:]))
    ]
    across = [flipped(x, 2) for x in acts]
    beside = [flipped(x, 1) for x in acts]
    corner = [flipped(x, 1) for x in across]
    near, ordered_cotangent = near_head(
        acts,
        beside,
        project_weight,
        project_bias.reshape(1, 256),
        cotangent.reshape(PIXELS, 256),
    )
    output, grads, *sends = far_head(
        acts, across, corner, project_weight, near, ordered_cotangent
    )
    arrived = [swapped(sends[n], x) for n, x in enumerate(GRAD_SWAPS)]
    stack = spread(grads, arrived)
    (far,) = grads_for((3,), stack, weights)
    far = flipped(far, 1)
    (kept,) = grads_for((2,), stack, weights)
    crossing = (far.astype(F32) + kept.astype(F32)).astype(BF16)
    crossed = flipped(crossing, 2)
    later, output, crossing = lax.optimization_barrier((stack, output, crossing))
    head_output = own_output(output)
    (near,) = grads_for((1,), later, weights)
    near = flipped(near, 1)
    (kept,) = grads_for((0,), later, weights, 8)
    feature_grad = last_sum(kept, near, crossed)
    return head_output.reshape(12, 48, W), feature_grad.reshape(12, 48, 512)


def solution(mesh):
    body = on_device if fits(mesh) else on_device_general
    in_specs = (
        P("rows", None, None),
        P(None, "filt"),
        P(None, None, None, None, "filt"),
        P(None, "filt"),
        P(),
        P(),
        P("rows", None, None),
    )
    out_specs = (P("rows", None, "filt"), P("rows", None, "filt"))
    return jax.shard_map(
        body, mesh=mesh, in_specs=in_specs, out_specs=out_specs, check_vma=False
    )
```

```python
import functools

import jax
import jax.numpy as jnp
from jax import lax
from jax.experimental import pallas as pl
from jax.experimental.pallas import tpu as pltpu
from jax.sharding import PartitionSpec as P

FIRST_DILATION = 12
SECOND_DILATION = 24
THIRD_DILATION = 36


def passed_along(x, axis, by):
    devices = lax.axis_size(axis)
    pairs = [(i, i + by) for i in range(devices) if 0 <= i + by < devices]
    return lax.ppermute(x, axis, pairs)


def shift_columns(field, amount):
    breadth = field.shape[1]
    if amount == 0:
        return field
    padding = [(0, 0)] * field.ndim
    if amount > 0:
        kept = field[:, amount:]
        padding[1] = (0, amount)
    else:
        kept = field[:, : breadth + amount]
        padding[1] = (-amount, 0)
    return jnp.pad(kept, padding)


def fetch_sums(field, offset):
    return passed_along(field, "rows", offset)


def fetch_grads(field, offset):
    return passed_along(field, "rows", offset)


def shift_rows(field, amount, fetcher):
    height = field.shape[0]
    quotient = amount // height

    def extract_block(offset):
        if offset == 0:
            return field
        return fetcher(field, offset)

    return extract_block(quotient)


def make_kernel_taps(variants, dilation_rates):
    stacked = [variants[:, :, 0]]
    for branch, dilation in enumerate(dilation_rates):
        for row_tap in range(3):
            source = variants[:, :, 1 + 3 * branch + row_tap]
            for col_tap in range(3):
                stacked.append(shift_columns(source, -(col_tap - 1) * dilation))
    return jnp.stack(stacked, 2)


def on_device_general(
    features, point_weight, dilated_weight, branch_bias, project_weight, project_bias, cotangent
):
    height, breadth, channels = features.shape
    pixels = height * breadth
    own_width = point_weight.shape[1]
    filters = lax.axis_size("filt")
    member = lax.axis_index("filt")
    branch_outputs = project_weight.shape[2]
    own_out = branch_outputs // filters
    own_channels = channels // filters
    dilation_rates = (FIRST_DILATION, SECOND_DILATION, THIRD_DILATION)
    all_weights = jnp.concatenate(
        [point_weight[None], dilated_weight.reshape(27, channels, own_width)], 0
    )
    flattened = features.reshape(pixels, channels)
    tap_terms = jnp.einsum(
        "pc,tco->pto", flattened, all_weights, preferred_element_type=jnp.float32
    )
    tap_terms = tap_terms.reshape(height, breadth, 28, own_width)
    pre_list = [tap_terms[:, :, 0, :] + branch_bias[0]]
    for branch, dilation in enumerate(dilation_rates):
        summed_result = jnp.zeros((height, breadth, own_width), jnp.float32)
        for row_tap in range(3):
            row_sum = jnp.zeros((height, breadth, own_width), jnp.float32)
            for col_tap in range(3):
                row_sum = row_sum + shift_columns(
                    tap_terms[:, :, 1 + 9 * branch + 3 * row_tap + col_tap, :],
                    (col_tap - 1) * dilation,
                )
            summed_result = summed_result + shift_rows(
                row_sum, -(row_tap - 1) * dilation, fetch_sums
            )
        pre_list.append(summed_result + branch_bias[branch + 1])
    branch_pre = jnp.stack(pre_list, 2)
    activations = jnp.maximum(branch_pre, 0.0).astype(jnp.bfloat16).reshape(pixels, 4 * own_width)
    grouped = project_weight.reshape(4, filters, own_width, branch_outputs)
    own_rows = lax.dynamic_index_in_dim(grouped, member, 1, keepdims=False).reshape(
        4 * own_width, branch_outputs
    )
    flat_cotangent = cotangent.reshape(pixels, branch_outputs)
    ordered = jnp.transpose(grouped, (1, 0, 2, 3)).reshape(filters * 4 * own_width, branch_outputs)
    project_pre = jnp.dot(
        lax.all_gather(activations, "filt", axis=1, tiled=True),
        ordered,
        preferred_element_type=jnp.float32,
    )
    project_pre = project_pre + project_bias
    head_grad = jnp.where(project_pre > 0, flat_cotangent.astype(jnp.float32), 0.0).astype(
        jnp.bfloat16
    )
    own_pre = lax.dynamic_slice_in_dim(project_pre, member * own_out, own_out, 1)
    act_grad = jnp.dot(head_grad, own_rows.T, preferred_element_type=jnp.float32)
    head_output = jnp.maximum(own_pre, 0.0).astype(jnp.bfloat16).reshape(height, breadth, own_out)
    branch_grad = jnp.where(
        branch_pre > 0, act_grad.reshape(height, breadth, 4, own_width), 0.0
    ).astype(jnp.bfloat16)
    variant_list = [branch_grad[:, :, 0, :]]
    for branch, dilation in enumerate(dilation_rates):
        for row_tap in range(3):
            variant_list.append(
                shift_rows(branch_grad[:, :, branch + 1, :], (row_tap - 1) * dilation, fetch_grads)
            )
    variants = jnp.stack(variant_list, 2)
    stacked = make_kernel_taps(variants, dilation_rates).reshape(pixels, 28, own_width)
    input_grad = lax.psum_scatter(
        jnp.einsum("pto,tco->cp", stacked, all_weights, preferred_element_type=jnp.float32),
        "filt",
        scatter_dimension=0,
        tiled=True,
    ).T
    feature_grad = input_grad.astype(jnp.bfloat16).reshape(height, breadth, own_channels)
    return (head_output, feature_grad)


W = 64
BLOCK = 144
PIXELS = 576
HALF = 288
SENT = 304
CHANNELS = 2048
F32 = jnp.float32
BF16 = jnp.bfloat16

OUT_PAIRS = ((3, 1), (1, 1), (3, 0), (1, 0), (3, 2), (1, 2), (2, 1), (2, 0), (2, 2))
TAPS = (
    [(k, 1, 1) for k in (2, 1, 3)]
    + [(k, i, j) for k, j in OUT_PAIRS for i in (0, 2)]
    + [(k, 1, j) for j in (0, 2) for k in (2, 1, 3)]
)
OUT_AT, LEFT_AT, RIGHT_AT = 4 * W, 22 * W, 25 * W
PARTS = ((0, 2), (1, 3))
SWAPS = (6, 2, 1, 3, 7, 5)
GRAD_SWAPS = (6, 7, 5)
QUARTETS = ((0, 1, 2, 3), (4, 5, 6, 7))


def fits(mesh):
    return mesh.shape["rows"] == 8 and mesh.shape["filt"] == 4


def order_matrix(turned=False):
    to = lax.broadcasted_iota(jnp.int32, (192, 192), 1 if turned else 0)
    source = lax.broadcasted_iota(jnp.int32, (192, 192), 0 if turned else 1)

    def parts(value, width):
        return sum((value >= n * width).astype(jnp.int32) for n in (1, 2, 3))

    block = parts(to, 48)
    within = to - 48 * block
    line = parts(within, 12)
    wanted = line * 48 + block * 12 + within - 12 * line
    return (source == wanted).astype(F32).astype(BF16)


def tap_index(tap):
    k, i, j = tap
    return (k - 1) * 9 + i * 3 + j


def nt(a, b):
    return lax.dot_general(a, b, (((1,), (1,)), ((), ())), preferred_element_type=F32)


def nn(a, b):
    return lax.dot_general(a, b, (((1,), (0,)), ((), ())), preferred_element_type=F32)


def from_blocks(order_t, value, write):
    for g in range(3):
        parts = [value[m * BLOCK + g * 48 : m * BLOCK + g * 48 + 48] for m in range(4)]
        write(g * 192, nn(order_t, jnp.concatenate(parts, 0)).astype(BF16))


def low_lanes(shape):
    return lax.broadcasted_iota(jnp.int32, shape, 1) % 128 < W


def scaled(value):
    most = jnp.maximum(jnp.max(jnp.abs(value), axis=0, keepdims=True), 1e-30)
    power = jnp.floor(jnp.log(most) * 1.4426950408889634)
    return value * jnp.exp2(13.0 - power), power


def unscaled(sent):
    return sent[:HALF, :] * jnp.exp2(sent[HALF : HALF + 1, :] - 13.0)


def outward_slot(row, x):
    other = row ^ x
    apart = jnp.abs(other - row)
    slot = apart - 1 + jnp.where(other < row, 3, 0)
    return jnp.where(apart <= 3, slot, 0)


def fetch_tap(dilated, weights, sem, place):
    return pltpu.make_async_copy(
        dilated.at[tap_index(TAPS[place - 1])], weights.at[pl.ds(place * W, W)], sem
    )


def outward_kernel(features, dilated, point, *refs):
    row = lax.axis_index("rows")
    out, ordered, weights = refs[0:6], refs[6], refs[7]
    raw, sums, packed, feature_sems, weight_sems = refs[8:]
    loads = []
    for g in range(3):
        rows = pl.ds(g * 192, 192)
        loads.append(pltpu.make_async_copy(features.at[rows], raw.at[rows], feature_sems.at[g]))
        loads[-1].start()
    queue = [
        fetch_tap(dilated, weights, weight_sems.at[q], place)
        for q, place in enumerate((*range(4, 28), 1, 2, 3))
    ]
    queue.append(pltpu.make_async_copy(point, weights.at[pl.ds(0, W)], weight_sems.at[27]))

    def start_loads(first, last):
        for fetch in queue[first:last]:
            fetch.start()

    start_loads(0, 4)
    order = order_matrix()
    for g in range(3):
        loads[g].wait()
        start_loads((4, 12, 18)[g], (12, 18, 28)[g])
        moved = nn(order, raw[g * 192 : (g + 1) * 192, :]).astype(BF16)
        for m in range(4):
            at = m * BLOCK + g * 48
            ordered[at : at + 48, :] = moved[m * 48 : (m + 1) * 48]

    def product(pair, pairs, first, last):
        for fetch in queue[2 * pair : 2 * (pair + pairs)]:
            fetch.wait()
        at = OUT_AT + pair * 128
        return nt(ordered[first * BLOCK : last * BLOCK, :], weights[at : at + pairs * 128, :])

    d = product(0, 2, 0, 4)
    sums[2] = d[:, :128]
    sums[0] = d[:, 128:]
    d = product(2, 2, 0, 3)
    sums[2, 3 * BLOCK :, :] = sums[2, 3 * BLOCK :, :] + d[:BLOCK, :128]
    sums[0, BLOCK:, :] = sums[0, BLOCK:, :] + d[:, 128:]
    d = product(4, 2, 1, 4)
    sums[2, :BLOCK, :] = sums[2, :BLOCK, :] + d[2 * BLOCK :, :128]
    sums[0, : 3 * BLOCK, :] = sums[0, : 3 * BLOCK, :] + d[:, 128:]
    low = low_lanes((HALF, 128))

    def pack(k):
        top, bottom = sums[k, :HALF, :], sums[k, HALF:, :]
        halves = (
            jnp.where(low, top, pltpu.roll(bottom, W, 1)),
            jnp.where(low, pltpu.roll(top, W, 1), bottom),
        )
        for way, value in enumerate(halves):
            value, power = scaled(value)
            packed[k + 3 * way, :HALF, :] = value
            packed[k + 3 * way, HALF:, :] = jnp.broadcast_to(power, (SENT - HALF, 128))

    pack(2)
    pack(0)
    d = product(6, 3, 0, 4)
    sums[1] = d[:, :128]
    sums[1, 2 * BLOCK :, :] = sums[1, 2 * BLOCK :, :] + d[: 2 * BLOCK, 128:256]
    sums[1, : 2 * BLOCK, :] = sums[1, : 2 * BLOCK, :] + d[2 * BLOCK :, 256:]
    pack(1)
    for n, x in enumerate(SWAPS):
        out[n][...] = packed[outward_slot(row, x)]
    for fetch in queue[18:]:
        fetch.wait()


def outward_sums(features, dilated, point):
    return pl.pallas_call(
        outward_kernel,
        out_shape=[jax.ShapeDtypeStruct((SENT, 128), F32)] * 6
        + [pltpu.VMEM((PIXELS, CHANNELS), BF16), pltpu.VMEM((28 * W, CHANNELS), BF16)],
        in_specs=[pl.BlockSpec(memory_space=pltpu.HBM)] * 3,
        out_specs=[pl.BlockSpec(memory_space=pltpu.VMEM)] * 8,
        scratch_shapes=[
            pltpu.VMEM((PIXELS, CHANNELS), BF16),
            pltpu.VMEM((3, PIXELS, 128), F32),
            pltpu.VMEM((6, SENT, 128), F32),
            pltpu.SemaphoreType.DMA((3,)),
            pltpu.SemaphoreType.DMA((28,)),
        ],
        compiler_params=pltpu.CompilerParams(vmem_limit_bytes=28 * 2**20),
        name="outward_sums",
    )(features, dilated, point)


def own_kernel(ordered, weights, bias, *outs):
    d = nt(ordered[...], weights[:256, :])
    for part, out in enumerate(outs):
        line = jnp.concatenate([bias[k : k + 1, :] for k in PARTS[part]], 1)
        out[...] = d[:, part * 128 : part * 128 + 128] + line
    low = low_lanes((PIXELS, 128))

    def add(first, value, k):
        part = k % 2
        rows = slice(first * BLOCK, first * BLOCK + value.shape[0])
        mask, value = low[: value.shape[0]], value[:, part * 128 : part * 128 + 128]
        kept = jnp.where(mask, value, 0.0) if k == 1 else jnp.where(mask, 0.0, value)
        outs[part][rows, :] = outs[part][rows, :] + kept

    d = nt(ordered[: 3 * BLOCK, :], weights[LEFT_AT - W : LEFT_AT + 3 * W, :])
    for k in (1, 2, 3):
        add(k, d[: (4 - k) * BLOCK], k)
    d = nt(ordered[BLOCK:, :], weights[RIGHT_AT - W : RIGHT_AT + 3 * W, :])
    for k in (1, 2, 3):
        add(0, d[(k - 1) * BLOCK :], k)


def own_sums(ordered, weights, bias):
    return pl.pallas_call(
        own_kernel,
        out_shape=[jax.ShapeDtypeStruct((PIXELS, 128), F32)] * 2,
        in_specs=[pl.BlockSpec(memory_space=pltpu.VMEM)] * 3,
        out_specs=[pl.BlockSpec(memory_space=pltpu.VMEM)] * 2,
        compiler_params=pltpu.CompilerParams(vmem_limit_bytes=18 * 2**20),
        cost_estimate=pl.CostEstimate(flops=10**6, bytes_accessed=10**4, transcendentals=0),
        name="own_sums",
    )(ordered, weights, bias)


def arrival_slot(row, other):
    return jnp.where((other >= 0) & (other < 8), row ^ other, 0)


def gather_arrivals(recv, arrivals, swaps):
    arrivals[0] = jnp.zeros((HALF, 128), arrivals.dtype)
    for n, x in enumerate(swaps):
        arrivals[x] = recv[n][...] if recv[n].shape[0] == HALF else unscaled(recv[n][...])


def activation_kernel(part, swaps, own, *refs):
    recv, acts, arrivals = refs[: len(swaps)], refs[-2], refs[-1]
    row = lax.axis_index("rows")
    gather_arrivals(recv, arrivals, swaps)
    low = low_lanes((HALF, 128))

    def total(k):
        return arrivals[arrival_slot(row, row - k)] + arrivals[arrival_slot(row, row + k)]

    high = total(PARTS[part][1])
    top, bottom = jnp.where(low, 0.0, pltpu.roll(high, W, 1)), jnp.where(low, 0.0, high)
    if part:
        left = total(PARTS[part][0])
        top = jnp.where(low, left, top)
        bottom = jnp.where(low, pltpu.roll(left, W, 1), bottom)
    acts[:HALF, :] = jnp.maximum(own[:HALF, :] + top, 0.0).astype(BF16)
    acts[HALF:, :] = jnp.maximum(own[HALF:, :] + bottom, 0.0).astype(BF16)


def activations_of(part, swaps, own, received):
    return pl.pallas_call(
        functools.partial(activation_kernel, part, swaps),
        out_shape=jax.ShapeDtypeStruct((PIXELS, 128), BF16),
        in_specs=[pl.BlockSpec(memory_space=pltpu.VMEM)] * (1 + len(swaps)),
        out_specs=pl.BlockSpec(memory_space=pltpu.VMEM),
        scratch_shapes=[pltpu.VMEM((8, HALF, 128), F32)],
        compiler_params=pltpu.CompilerParams(vmem_limit_bytes=8 * 2**20),
        name="activations",
    )(own, *received)


def project_rows(project, who):
    at = pl.multiple_of(who * W, W)
    return jnp.concatenate([project[k, pl.ds(at, W), :] for part in PARTS for k in part], 0)


def both(a, b):
    return jnp.concatenate([a[...], b[...]], 1)


def near_head_kernel(a0, b0, a1, b1, project, bias, cotangent, pre, ordered):
    member = lax.axis_index("filt")
    pre[...] = nn(both(a0, b0), project_rows(project, member)) + bias[...]
    pre[...] = pre[...] + nn(both(a1, b1), project_rows(project, member ^ 1))
    order = order_matrix()
    for g in range(3):
        moved = nn(order, cotangent[g * 192 : (g + 1) * 192, :])
        for m in range(4):
            at = m * BLOCK + g * 48
            ordered[at : at + 48, :] = moved[m * 48 : (m + 1) * 48]


def near_head(own, beside, project, bias, cotangent):
    return pl.pallas_call(
        near_head_kernel,
        out_shape=[jax.ShapeDtypeStruct((PIXELS, 256), F32)] * 2,
        in_specs=[pl.BlockSpec(memory_space=pltpu.VMEM)] * 7,
        out_specs=[pl.BlockSpec(memory_space=pltpu.VMEM)] * 2,
        compiler_params=pltpu.CompilerParams(vmem_limit_bytes=10 * 2**20),
        name="near_head",
    )(*own, *beside, project, bias, cotangent)


def far_head_kernel(a0, b0, a2, b2, a3, b3, project, near, cotangent, *refs):
    output, grads, sends, quartet, packed = refs[0], refs[1], refs[2:5], refs[5], refs[6]
    row, member = lax.axis_index("rows"), lax.axis_index("filt")
    pre = near[...] + nn(both(a2, b2), project_rows(project, member ^ 2))
    pre = pre + nn(both(a3, b3), project_rows(project, member ^ 3))
    output[...] = jnp.maximum(pre, 0.0).astype(BF16)
    head_grad = jnp.where(pre > 0, cotangent[...], 0.0).astype(BF16)
    act_grad = nt(head_grad, project_rows(project, member))
    a = jnp.where(a0[...].astype(F32) > 0, act_grad[:, :128], 0.0)
    b = jnp.where(b0[...].astype(F32) > 0, act_grad[:, 128:], 0.0)
    grads[:, :128] = a.astype(BF16)
    grads[:, 128:] = b.astype(BF16)
    low = low_lanes((HALF, 128))
    packed[0] = jnp.where(low, b[:HALF], pltpu.roll(b[HALF:], W, 1)).astype(BF16)
    packed[1] = jnp.where(low, pltpu.roll(a[:HALF], W, 1), a[HALF:]).astype(BF16)
    packed[2] = jnp.where(low, pltpu.roll(b[:HALF], W, 1), b[HALF:]).astype(BF16)
    for n, x in enumerate(GRAD_SWAPS):
        apart = jnp.abs((row ^ x) - row)
        sends[n][...] = packed[jnp.where(apart <= 3, apart - 1, 0)]
    for q in range(4):
        apart = jnp.abs(q - (row & 3))
        quartet[q] = packed[jnp.where(apart > 0, apart - 1, 0)]


def far_head(own, across, corner, project, near, cotangent):
    return pl.pallas_call(
        far_head_kernel,
        out_shape=[jax.ShapeDtypeStruct((PIXELS, 256), BF16)] * 2
        + [jax.ShapeDtypeStruct((HALF, 128), BF16)] * 3
        + [jax.ShapeDtypeStruct((4, HALF, 128), BF16)],
        in_specs=[pl.BlockSpec(memory_space=pltpu.VMEM)] * 9,
        out_specs=[pl.BlockSpec(memory_space=pltpu.VMEM)] * 6,
        scratch_shapes=[pltpu.VMEM((3, HALF, 128), BF16)],
        compiler_params=pltpu.CompilerParams(vmem_limit_bytes=12 * 2**20),
        name="far_head",
    )(*own, *across, *corner, project, near, cotangent)


def own_output_kernel(output, out):
    member = lax.axis_index("filt")
    mine = jnp.zeros((PIXELS, W), F32)
    for q in range(4):
        mine = jnp.where(member == q, output[:, q * W : (q + 1) * W].astype(F32), mine)

    def put(at, value):
        out[at : at + 192, :] = value

    from_blocks(order_matrix(True), mine.astype(BF16), put)


def own_output(output):
    return pl.pallas_call(
        own_output_kernel,
        out_shape=jax.ShapeDtypeStruct((PIXELS, W), BF16),
        in_specs=[pl.BlockSpec(memory_space=pltpu.VMEM)],
        out_specs=pl.BlockSpec(memory_space=pltpu.VMEM),
        compiler_params=pltpu.CompilerParams(vmem_limit_bytes=6 * 2**20),
        name="own_output",
    )(output)


def spread_kernel(own, *refs):
    recv, quartet, stack, arrivals, pairs, twice = refs[:3], *refs[3:]
    row = lax.axis_index("rows")
    gather_arrivals(recv, arrivals, GRAD_SWAPS)
    for x in (1, 2, 3):
        arrivals[x] = quartet[(row & 3) ^ x]
    low = low_lanes((HALF, 128))
    low_all = low_lanes((PIXELS, 128))
    for k in (1, 2, 3):
        p = arrivals[arrival_slot(row, row + k)].astype(F32)
        m = arrivals[arrival_slot(row, row - k)].astype(F32)
        pairs[k - 1, :HALF, :] = jnp.where(low, p, pltpu.roll(m, W, 1)).astype(BF16)
        pairs[k - 1, HALF:, :] = jnp.where(low, pltpu.roll(p, W, 1), m).astype(BF16)
        g = own[:, :128].astype(F32) if k == 2 else own[:, 128:].astype(F32)
        other = pltpu.roll(g, W, 1)
        two = jnp.where(low_all, g, other) if k == 1 else jnp.where(low_all, other, g)
        twice[k - 1] = two.astype(BF16)
    stack[:, : 4 * W] = own[...]
    nothing = jnp.zeros((BLOCK, 128), BF16)

    def block_of(ref, k, source):
        if 0 <= source < 4:
            return ref[k - 1, source * BLOCK : (source + 1) * BLOCK, :]
        return nothing

    for q, (k, j) in enumerate(OUT_PAIRS):
        lanes = slice(OUT_AT + q * 128, OUT_AT + q * 128 + 128)
        for m in range(4):
            stack[m * BLOCK : (m + 1) * BLOCK, lanes] = block_of(pairs, k, m - (j - 1) * k)
    low_block = low_lanes((BLOCK, 128))
    for q, (a, b) in enumerate(((2, 1), (3, -2), (-1, -3))):
        lanes = slice(LEFT_AT + q * 128, LEFT_AT + q * 128 + 128)
        for m in range(4):
            stack[m * BLOCK : (m + 1) * BLOCK, lanes] = jnp.where(
                low_block, block_of(twice, abs(a), m + a), block_of(twice, abs(b), m + b)
            )


def spread(own, received, quartet):
    return pl.pallas_call(
        spread_kernel,
        out_shape=pltpu.VMEM((PIXELS, 28 * W), BF16),
        in_specs=[pl.BlockSpec(memory_space=pltpu.VMEM)] * 5,
        out_specs=pl.BlockSpec(memory_space=pltpu.VMEM),
        scratch_shapes=[
            pltpu.VMEM((8, HALF, 128), BF16),
            pltpu.VMEM((3, PIXELS, 128), BF16),
            pltpu.VMEM((3, PIXELS, 128), BF16),
        ],
        compiler_params=pltpu.CompilerParams(vmem_limit_bytes=12 * 2**20),
        name="spread",
    )(own, *received, quartet)


def grad_kernel(flips, stack, weights, *outs):
    member = lax.axis_index("filt")
    for out, flip in zip(outs, flips):
        columns = pl.ds(pl.multiple_of((member ^ flip) * 512, 512), 512)
        out[...] = nn(stack[...], weights[:, columns]).astype(BF16)


def grads_for(flips, stack, weights, scale=1):
    return pl.pallas_call(
        functools.partial(grad_kernel, flips),
        out_shape=[jax.ShapeDtypeStruct((PIXELS, 512), BF16)] * len(flips),
        in_specs=[pl.BlockSpec(memory_space=pltpu.VMEM)] * 2,
        out_specs=[pl.BlockSpec(memory_space=pltpu.VMEM)] * len(flips),
        compiler_params=pltpu.CompilerParams(vmem_limit_bytes=18 * 2**20),
        cost_estimate=pl.CostEstimate(
            flops=2 * PIXELS * 28 * W * 512 * scale, bytes_accessed=10**6, transcendentals=0
        ),
        name="grads_for",
    )(stack, weights)


def last_kernel(a, b, c, out):
    total = a[...].astype(F32) + b[...].astype(F32) + c[...].astype(F32)

    def put(at, value):
        out[at : at + 192, :] = value

    from_blocks(order_matrix(True), total.astype(BF16), put)


def last_sum(a, b, c):
    return pl.pallas_call(
        last_kernel,
        out_shape=jax.ShapeDtypeStruct((PIXELS, 512), BF16),
        in_specs=[pl.BlockSpec(memory_space=pltpu.VMEM)] * 3,
        out_specs=pl.BlockSpec(memory_space=pltpu.VMEM),
        compiler_params=pltpu.CompilerParams(vmem_limit_bytes=10 * 2**20),
        name="last_sum",
    )(a, b, c)


def flipped(x, bit):
    return lax.ppermute(x, "filt", [(i, i ^ bit) for i in range(lax.axis_size("filt"))])


def swapped(x, bits):
    pairs = [(r, r ^ bits) for r in range(8) if abs((r ^ bits) - r) <= 3]
    return lax.ppermute(x, "rows", pairs)


def on_device(
    features, point_weight, dilated_weight, branch_bias, project_weight, project_bias, cotangent
):
    flat = features.reshape(PIXELS, CHANNELS)
    dilated = jnp.transpose(dilated_weight, (0, 1, 2, 4, 3)).reshape(27, W, CHANNELS)
    point = point_weight.T
    flat, dilated, point = (
        pltpu.with_memory_space_constraint(x, pltpu.HBM) for x in (flat, dilated, point)
    )
    *sums, ordered, weights = outward_sums(flat, dilated, point)
    received = {
        x: swapped(sums[n].astype(jnp.float16), x).astype(F32) for n, x in enumerate(SWAPS)
    }
    own = own_sums(ordered, weights, branch_bias)
    acts = [
        activations_of(part, swaps, own[part], [received[x] for x in swaps])
        for part, swaps in ((0, SWAPS[:2]), (1, SWAPS[2:]))
    ]
    across = [flipped(x, 2) for x in acts]
    beside = [flipped(x, 1) for x in acts]
    corner = [flipped(x, 1) for x in across]
    near, ordered_cotangent = near_head(
        acts,
        beside,
        project_weight,
        project_bias.reshape(1, 256),
        cotangent.reshape(PIXELS, 256),
    )
    output, grads, *sends, quartet = far_head(
        acts, across, corner, project_weight, near, ordered_cotangent
    )
    arrived = [swapped(sends[n], x) for n, x in enumerate(GRAD_SWAPS)]
    quartet = lax.all_to_all(quartet, "rows", 0, 0, axis_index_groups=QUARTETS)
    stack = spread(grads, arrived, quartet)
    (far,) = grads_for((3,), stack, weights)
    far = flipped(far, 1)
    (kept,) = grads_for((2,), stack, weights)
    crossing = (far.astype(F32) + kept.astype(F32)).astype(BF16)
    crossed = flipped(crossing, 2)
    later, output, crossing = lax.optimization_barrier((stack, output, crossing))
    head_output = own_output(output)
    (near,) = grads_for((1,), later, weights)
    near = flipped(near, 1)
    (kept,) = grads_for((0,), later, weights, 8)
    feature_grad = last_sum(kept, near, crossed)
    return head_output.reshape(12, 48, W), feature_grad.reshape(12, 48, 512)


def solution(mesh):
    body = on_device if fits(mesh) else on_device_general
    in_specs = (
        P("rows", None, None),
        P(None, "filt"),
        P(None, None, None, None, "filt"),
        P(None, "filt"),
        P(),
        P(),
        P("rows", None, None),
    )
    out_specs = (P("rows", None, "filt"), P("rows", None, "filt"))
    return jax.shard_map(
        body, mesh=mesh, in_specs=in_specs, out_specs=out_specs, check_vma=False
    )
```

```python
import functools

import jax
import jax.numpy as jnp
from jax import lax
from jax.experimental import pallas as pl
from jax.experimental.pallas import tpu as pltpu
from jax.sharding import PartitionSpec as P

FIRST_DILATION = 12
SECOND_DILATION = 24
THIRD_DILATION = 36


def passed_along(x, axis, by):
    devices = lax.axis_size(axis)
    pairs = [(i, i + by) for i in range(devices) if 0 <= i + by < devices]
    return lax.ppermute(x, axis, pairs)


def shift_columns(field, amount):
    breadth = field.shape[1]
    if amount == 0:
        return field
    padding = [(0, 0)] * field.ndim
    if amount > 0:
        kept = field[:, amount:]
        padding[1] = (0, amount)
    else:
        kept = field[:, : breadth + amount]
        padding[1] = (-amount, 0)
    return jnp.pad(kept, padding)


def fetch_sums(field, offset):
    return passed_along(field, "rows", offset)


def fetch_grads(field, offset):
    return passed_along(field, "rows", offset)


def shift_rows(field, amount, fetcher):
    height = field.shape[0]
    quotient = amount // height

    def extract_block(offset):
        if offset == 0:
            return field
        return fetcher(field, offset)

    return extract_block(quotient)


def make_kernel_taps(variants, dilation_rates):
    stacked = [variants[:, :, 0]]
    for branch, dilation in enumerate(dilation_rates):
        for row_tap in range(3):
            source = variants[:, :, 1 + 3 * branch + row_tap]
            for col_tap in range(3):
                stacked.append(shift_columns(source, -(col_tap - 1) * dilation))
    return jnp.stack(stacked, 2)


def on_device_general(
    features, point_weight, dilated_weight, branch_bias, project_weight, project_bias, cotangent
):
    height, breadth, channels = features.shape
    pixels = height * breadth
    own_width = point_weight.shape[1]
    filters = lax.axis_size("filt")
    member = lax.axis_index("filt")
    branch_outputs = project_weight.shape[2]
    own_out = branch_outputs // filters
    own_channels = channels // filters
    dilation_rates = (FIRST_DILATION, SECOND_DILATION, THIRD_DILATION)
    all_weights = jnp.concatenate(
        [point_weight[None], dilated_weight.reshape(27, channels, own_width)], 0
    )
    flattened = features.reshape(pixels, channels)
    tap_terms = jnp.einsum(
        "pc,tco->pto", flattened, all_weights, preferred_element_type=jnp.float32
    )
    tap_terms = tap_terms.reshape(height, breadth, 28, own_width)
    pre_list = [tap_terms[:, :, 0, :] + branch_bias[0]]
    for branch, dilation in enumerate(dilation_rates):
        summed_result = jnp.zeros((height, breadth, own_width), jnp.float32)
        for row_tap in range(3):
            row_sum = jnp.zeros((height, breadth, own_width), jnp.float32)
            for col_tap in range(3):
                row_sum = row_sum + shift_columns(
                    tap_terms[:, :, 1 + 9 * branch + 3 * row_tap + col_tap, :],
                    (col_tap - 1) * dilation,
                )
            summed_result = summed_result + shift_rows(
                row_sum, -(row_tap - 1) * dilation, fetch_sums
            )
        pre_list.append(summed_result + branch_bias[branch + 1])
    branch_pre = jnp.stack(pre_list, 2)
    activations = jnp.maximum(branch_pre, 0.0).astype(jnp.bfloat16).reshape(pixels, 4 * own_width)
    grouped = project_weight.reshape(4, filters, own_width, branch_outputs)
    own_rows = lax.dynamic_index_in_dim(grouped, member, 1, keepdims=False).reshape(
        4 * own_width, branch_outputs
    )
    flat_cotangent = cotangent.reshape(pixels, branch_outputs)
    ordered = jnp.transpose(grouped, (1, 0, 2, 3)).reshape(filters * 4 * own_width, branch_outputs)
    project_pre = jnp.dot(
        lax.all_gather(activations, "filt", axis=1, tiled=True),
        ordered,
        preferred_element_type=jnp.float32,
    )
    project_pre = project_pre + project_bias
    head_grad = jnp.where(project_pre > 0, flat_cotangent.astype(jnp.float32), 0.0).astype(
        jnp.bfloat16
    )
    own_pre = lax.dynamic_slice_in_dim(project_pre, member * own_out, own_out, 1)
    act_grad = jnp.dot(head_grad, own_rows.T, preferred_element_type=jnp.float32)
    head_output = jnp.maximum(own_pre, 0.0).astype(jnp.bfloat16).reshape(height, breadth, own_out)
    branch_grad = jnp.where(
        branch_pre > 0, act_grad.reshape(height, breadth, 4, own_width), 0.0
    ).astype(jnp.bfloat16)
    variant_list = [branch_grad[:, :, 0, :]]
    for branch, dilation in enumerate(dilation_rates):
        for row_tap in range(3):
            variant_list.append(
                shift_rows(branch_grad[:, :, branch + 1, :], (row_tap - 1) * dilation, fetch_grads)
            )
    variants = jnp.stack(variant_list, 2)
    stacked = make_kernel_taps(variants, dilation_rates).reshape(pixels, 28, own_width)
    input_grad = lax.psum_scatter(
        jnp.einsum("pto,tco->cp", stacked, all_weights, preferred_element_type=jnp.float32),
        "filt",
        scatter_dimension=0,
        tiled=True,
    ).T
    feature_grad = input_grad.astype(jnp.bfloat16).reshape(height, breadth, own_channels)
    return (head_output, feature_grad)


W = 64
BLOCK = 144
PIXELS = 576
HALF = 288
SENT = 304
CHANNELS = 2048
F32 = jnp.float32
BF16 = jnp.bfloat16

OUT_PAIRS = ((3, 1), (1, 1), (3, 0), (1, 0), (3, 2), (1, 2), (2, 1), (2, 0), (2, 2))
TAPS = (
    [(k, 1, 1) for k in (2, 1, 3)]
    + [(k, i, j) for k, j in OUT_PAIRS for i in (0, 2)]
    + [(k, 1, j) for j in (0, 2) for k in (2, 1, 3)]
)
OUT_AT, LEFT_AT, RIGHT_AT = 4 * W, 22 * W, 25 * W
PARTS = ((0, 2), (1, 3))
SWAPS = (6, 2, 1, 3, 7, 5)
GRAD_SWAPS = ((5, 7), (2, 6), (1, 3))


def fits(mesh):
    return mesh.shape["rows"] == 8 and mesh.shape["filt"] == 4


def order_matrix(turned=False):
    to = lax.broadcasted_iota(jnp.int32, (192, 192), 1 if turned else 0)
    source = lax.broadcasted_iota(jnp.int32, (192, 192), 0 if turned else 1)

    def parts(value, width):
        return sum((value >= n * width).astype(jnp.int32) for n in (1, 2, 3))

    block = parts(to, 48)
    within = to - 48 * block
    line = parts(within, 12)
    wanted = line * 48 + block * 12 + within - 12 * line
    return (source == wanted).astype(F32).astype(BF16)


def tap_index(tap):
    k, i, j = tap
    return (k - 1) * 9 + i * 3 + j


def nt(a, b):
    return lax.dot_general(a, b, (((1,), (1,)), ((), ())), preferred_element_type=F32)


def nn(a, b):
    return lax.dot_general(a, b, (((1,), (0,)), ((), ())), preferred_element_type=F32)


def from_blocks(order_t, value, write):
    for g in range(3):
        parts = [value[m * BLOCK + g * 48 : m * BLOCK + g * 48 + 48] for m in range(4)]
        write(g * 192, nn(order_t, jnp.concatenate(parts, 0)).astype(BF16))


def low_lanes(shape):
    return lax.broadcasted_iota(jnp.int32, shape, 1) % 128 < W


def scaled(value):
    most = jnp.maximum(jnp.max(jnp.abs(value), axis=0, keepdims=True), 1e-30)
    power = jnp.floor(jnp.log(most) * 1.4426950408889634)
    return value * jnp.exp2(13.0 - power), power


def unscaled(sent):
    return sent[:HALF, :] * jnp.exp2(sent[HALF : HALF + 1, :] - 13.0)


def outward_slot(row, x):
    other = row ^ x
    apart = jnp.abs(other - row)
    slot = apart - 1 + jnp.where(other < row, 3, 0)
    return jnp.where(apart <= 3, slot, 0)


def fetch_tap(dilated, weights, sem, place):
    return pltpu.make_async_copy(
        dilated.at[tap_index(TAPS[place - 1])], weights.at[pl.ds(place * W, W)], sem
    )


def outward_kernel(features, dilated, point, *refs):
    row = lax.axis_index("rows")
    out, ordered, weights = refs[0:6], refs[6], refs[7]
    raw, sums, packed, feature_sems, weight_sems = refs[8:]
    loads = []
    for g in range(3):
        rows = pl.ds(g * 192, 192)
        loads.append(pltpu.make_async_copy(features.at[rows], raw.at[rows], feature_sems.at[g]))
        loads[-1].start()
    queue = [
        fetch_tap(dilated, weights, weight_sems.at[q], place)
        for q, place in enumerate((*range(4, 28), 1, 2, 3))
    ]
    queue.append(pltpu.make_async_copy(point, weights.at[pl.ds(0, W)], weight_sems.at[27]))

    def start_loads(first, last):
        for fetch in queue[first:last]:
            fetch.start()

    start_loads(0, 4)
    order = order_matrix()
    for g in range(3):
        loads[g].wait()
        start_loads((4, 12, 18)[g], (12, 18, 28)[g])
        moved = nn(order, raw[g * 192 : (g + 1) * 192, :]).astype(BF16)
        for m in range(4):
            at = m * BLOCK + g * 48
            ordered[at : at + 48, :] = moved[m * 48 : (m + 1) * 48]

    def product(pair, pairs, first, last):
        for fetch in queue[2 * pair : 2 * (pair + pairs)]:
            fetch.wait()
        at = OUT_AT + pair * 128
        return nt(ordered[first * BLOCK : last * BLOCK, :], weights[at : at + pairs * 128, :])

    d = product(0, 2, 0, 4)
    sums[2] = d[:, :128]
    sums[0] = d[:, 128:]
    d = product(2, 2, 0, 3)
    sums[2, 3 * BLOCK :, :] = sums[2, 3 * BLOCK :, :] + d[:BLOCK, :128]
    sums[0, BLOCK:, :] = sums[0, BLOCK:, :] + d[:, 128:]
    d = product(4, 2, 1, 4)
    sums[2, :BLOCK, :] = sums[2, :BLOCK, :] + d[2 * BLOCK :, :128]
    sums[0, : 3 * BLOCK, :] = sums[0, : 3 * BLOCK, :] + d[:, 128:]
    low = low_lanes((HALF, 128))

    def pack(k):
        top, bottom = sums[k, :HALF, :], sums[k, HALF:, :]
        halves = (
            jnp.where(low, top, pltpu.roll(bottom, W, 1)),
            jnp.where(low, pltpu.roll(top, W, 1), bottom),
        )
        for way, value in enumerate(halves):
            value, power = scaled(value)
            packed[k + 3 * way, :HALF, :] = value
            packed[k + 3 * way, HALF:, :] = jnp.broadcast_to(power, (SENT - HALF, 128))

    pack(2)
    pack(0)
    d = product(6, 3, 0, 4)
    sums[1] = d[:, :128]
    sums[1, 2 * BLOCK :, :] = sums[1, 2 * BLOCK :, :] + d[: 2 * BLOCK, 128:256]
    sums[1, : 2 * BLOCK, :] = sums[1, : 2 * BLOCK, :] + d[2 * BLOCK :, 256:]
    pack(1)
    for n, x in enumerate(SWAPS):
        out[n][...] = packed[outward_slot(row, x)]
    for fetch in queue[18:]:
        fetch.wait()


def outward_sums(features, dilated, point):
    return pl.pallas_call(
        outward_kernel,
        out_shape=[jax.ShapeDtypeStruct((SENT, 128), F32)] * 6
        + [pltpu.VMEM((PIXELS, CHANNELS), BF16), pltpu.VMEM((28 * W, CHANNELS), BF16)],
        in_specs=[pl.BlockSpec(memory_space=pltpu.HBM)] * 3,
        out_specs=[pl.BlockSpec(memory_space=pltpu.VMEM)] * 8,
        scratch_shapes=[
            pltpu.VMEM((PIXELS, CHANNELS), BF16),
            pltpu.VMEM((3, PIXELS, 128), F32),
            pltpu.VMEM((6, SENT, 128), F32),
            pltpu.SemaphoreType.DMA((3,)),
            pltpu.SemaphoreType.DMA((28,)),
        ],
        compiler_params=pltpu.CompilerParams(vmem_limit_bytes=28 * 2**20),
        name="outward_sums",
    )(features, dilated, point)


def own_kernel(ordered, weights, bias, *outs):
    d = nt(ordered[...], weights[:256, :])
    for part, out in enumerate(outs):
        line = jnp.concatenate([bias[k : k + 1, :] for k in PARTS[part]], 1)
        out[...] = d[:, part * 128 : part * 128 + 128] + line
    low = low_lanes((PIXELS, 128))

    def add(first, value, k):
        part = k % 2
        rows = slice(first * BLOCK, first * BLOCK + value.shape[0])
        mask, value = low[: value.shape[0]], value[:, part * 128 : part * 128 + 128]
        kept = jnp.where(mask, value, 0.0) if k == 1 else jnp.where(mask, 0.0, value)
        outs[part][rows, :] = outs[part][rows, :] + kept

    d = nt(ordered[: 3 * BLOCK, :], weights[LEFT_AT - W : LEFT_AT + 3 * W, :])
    for k in (1, 2, 3):
        add(k, d[: (4 - k) * BLOCK], k)
    d = nt(ordered[BLOCK:, :], weights[RIGHT_AT - W : RIGHT_AT + 3 * W, :])
    for k in (1, 2, 3):
        add(0, d[(k - 1) * BLOCK :], k)


def own_sums(ordered, weights, bias):
    return pl.pallas_call(
        own_kernel,
        out_shape=[jax.ShapeDtypeStruct((PIXELS, 128), F32)] * 2,
        in_specs=[pl.BlockSpec(memory_space=pltpu.VMEM)] * 3,
        out_specs=[pl.BlockSpec(memory_space=pltpu.VMEM)] * 2,
        compiler_params=pltpu.CompilerParams(vmem_limit_bytes=18 * 2**20),
        cost_estimate=pl.CostEstimate(flops=10**6, bytes_accessed=10**4, transcendentals=0),
        name="own_sums",
    )(ordered, weights, bias)


def arrival_slot(row, other):
    return jnp.where((other >= 0) & (other < 8), row ^ other, 0)


def gather_arrivals(recv, arrivals, swaps):
    arrivals[0] = jnp.zeros((HALF, 128), arrivals.dtype)
    for n, x in enumerate(swaps):
        arrivals[x] = unscaled(recv[n][...])


def activation_kernel(part, swaps, own, *refs):
    recv, acts, arrivals = refs[: len(swaps)], refs[-2], refs[-1]
    row = lax.axis_index("rows")
    gather_arrivals(recv, arrivals, swaps)
    low = low_lanes((HALF, 128))

    def total(k):
        return arrivals[arrival_slot(row, row - k)] + arrivals[arrival_slot(row, row + k)]

    high = total(PARTS[part][1])
    top, bottom = jnp.where(low, 0.0, pltpu.roll(high, W, 1)), jnp.where(low, 0.0, high)
    if part:
        left = total(PARTS[part][0])
        top = jnp.where(low, left, top)
        bottom = jnp.where(low, pltpu.roll(left, W, 1), bottom)
    acts[:HALF, :] = jnp.maximum(own[:HALF, :] + top, 0.0).astype(BF16)
    acts[HALF:, :] = jnp.maximum(own[HALF:, :] + bottom, 0.0).astype(BF16)


def activations_of(part, swaps, own, received):
    return pl.pallas_call(
        functools.partial(activation_kernel, part, swaps),
        out_shape=jax.ShapeDtypeStruct((PIXELS, 128), BF16),
        in_specs=[pl.BlockSpec(memory_space=pltpu.VMEM)] * (1 + len(swaps)),
        out_specs=pl.BlockSpec(memory_space=pltpu.VMEM),
        scratch_shapes=[pltpu.VMEM((8, HALF, 128), F32)],
        compiler_params=pltpu.CompilerParams(vmem_limit_bytes=8 * 2**20),
        name="activations",
    )(own, *received)


def project_rows(project, who):
    at = pl.multiple_of(who * W, W)
    return jnp.concatenate([project[k, pl.ds(at, W), :] for part in PARTS for k in part], 0)


def both(a, b):
    return jnp.concatenate([a[...], b[...]], 1)


def near_head_kernel(a0, b0, a1, b1, project, bias, cotangent, pre, ordered):
    member = lax.axis_index("filt")
    pre[...] = nn(both(a0, b0), project_rows(project, member)) + bias[...]
    pre[...] = pre[...] + nn(both(a1, b1), project_rows(project, member ^ 1))
    order = order_matrix()
    for g in range(3):
        moved = nn(order, cotangent[g * 192 : (g + 1) * 192, :])
        for m in range(4):
            at = m * BLOCK + g * 48
            ordered[at : at + 48, :] = moved[m * 48 : (m + 1) * 48]


def near_head(own, beside, project, bias, cotangent):
    return pl.pallas_call(
        near_head_kernel,
        out_shape=[jax.ShapeDtypeStruct((PIXELS, 256), F32)] * 2,
        in_specs=[pl.BlockSpec(memory_space=pltpu.VMEM)] * 7,
        out_specs=[pl.BlockSpec(memory_space=pltpu.VMEM)] * 2,
        compiler_params=pltpu.CompilerParams(vmem_limit_bytes=10 * 2**20),
        name="near_head",
    )(*own, *beside, project, bias, cotangent)


def far_head_kernel(a0, b0, a1, b1, a2, b2, a3, b3, project, near, cotangent, *refs):
    output, grads, sends, packed = refs[0], refs[1], refs[2:5], refs[5]
    row, member = lax.axis_index("rows"), lax.axis_index("filt")
    pre = near[...] + nn(both(a2, b2), project_rows(project, member ^ 2))
    pre = pre + nn(both(a3, b3), project_rows(project, member ^ 3))
    output[...] = jnp.maximum(pre, 0.0).astype(BF16)
    head_grad = jnp.where(pre > 0, cotangent[...], 0.0).astype(BF16)
    low = low_lanes((HALF, 128))
    for who, (acts_a, acts_b) in enumerate(((a0, b0), (a1, b1))):
        act_grad = nt(head_grad, project_rows(project, member ^ who))
        a = jnp.where(acts_a[...].astype(F32) > 0, act_grad[:, :128], 0.0)
        b = jnp.where(acts_b[...].astype(F32) > 0, act_grad[:, 128:], 0.0)
        if who == 0:
            grads[:, :128] = a.astype(BF16)
            grads[:, 128:] = b.astype(BF16)
        packed[0, who] = jnp.where(low, b[:HALF], pltpu.roll(b[HALF:], W, 1)).astype(BF16)
        packed[1, who] = jnp.where(low, pltpu.roll(a[:HALF], W, 1), a[HALF:]).astype(BF16)
        packed[2, who] = jnp.where(low, pltpu.roll(b[:HALF], W, 1), b[HALF:]).astype(BF16)
    for n, swaps in enumerate(GRAD_SWAPS):
        apart = jnp.abs((row ^ jnp.where((member & 1) == 0, *swaps)) - row)
        sends[n][...] = packed[jnp.where(apart <= 3, apart - 1, 0)]


def far_head(own, beside, across, corner, project, near, cotangent):
    return pl.pallas_call(
        far_head_kernel,
        out_shape=[jax.ShapeDtypeStruct((PIXELS, 256), BF16)] * 2
        + [jax.ShapeDtypeStruct((2, HALF, 128), BF16)] * 3,
        in_specs=[pl.BlockSpec(memory_space=pltpu.VMEM)] * 11,
        out_specs=[pl.BlockSpec(memory_space=pltpu.VMEM)] * 5,
        scratch_shapes=[pltpu.VMEM((3, 2, HALF, 128), BF16)],
        compiler_params=pltpu.CompilerParams(vmem_limit_bytes=12 * 2**20),
        name="far_head",
    )(*own, *beside, *across, *corner, project, near, cotangent)


def own_output_kernel(output, out):
    member = lax.axis_index("filt")
    mine = jnp.zeros((PIXELS, W), F32)
    for q in range(4):
        mine = jnp.where(member == q, output[:, q * W : (q + 1) * W].astype(F32), mine)

    def put(at, value):
        out[at : at + 192, :] = value

    from_blocks(order_matrix(True), mine.astype(BF16), put)


def own_output(output):
    return pl.pallas_call(
        own_output_kernel,
        out_shape=jax.ShapeDtypeStruct((PIXELS, W), BF16),
        in_specs=[pl.BlockSpec(memory_space=pltpu.VMEM)],
        out_specs=pl.BlockSpec(memory_space=pltpu.VMEM),
        compiler_params=pltpu.CompilerParams(vmem_limit_bytes=6 * 2**20),
        name="own_output",
    )(output)


def spread_kernel(own, *refs):
    recv, handed, stack, arrivals, pairs, twice = refs[:3], refs[3:6], *refs[6:]
    row, member = lax.axis_index("rows"), lax.axis_index("filt")
    arrivals[0] = jnp.zeros((HALF, 128), BF16)
    for n, (even, odd) in enumerate(GRAD_SWAPS):
        first = (member & 1) == 0
        arrivals[jnp.where(first, even, odd)] = recv[n][0]
        arrivals[jnp.where(first, odd, even)] = handed[n][1]
    low = low_lanes((HALF, 128))
    low_all = low_lanes((PIXELS, 128))
    for k in (1, 2, 3):
        p = arrivals[arrival_slot(row, row + k)].astype(F32)
        m = arrivals[arrival_slot(row, row - k)].astype(F32)
        pairs[k - 1, :HALF, :] = jnp.where(low, p, pltpu.roll(m, W, 1)).astype(BF16)
        pairs[k - 1, HALF:, :] = jnp.where(low, pltpu.roll(p, W, 1), m).astype(BF16)
        g = own[:, :128].astype(F32) if k == 2 else own[:, 128:].astype(F32)
        other = pltpu.roll(g, W, 1)
        two = jnp.where(low_all, g, other) if k == 1 else jnp.where(low_all, other, g)
        twice[k - 1] = two.astype(BF16)
    stack[:, : 4 * W] = own[...]
    nothing = jnp.zeros((BLOCK, 128), BF16)

    def block_of(ref, k, source):
        if 0 <= source < 4:
            return ref[k - 1, source * BLOCK : (source + 1) * BLOCK, :]
        return nothing

    for q, (k, j) in enumerate(OUT_PAIRS):
        lanes = slice(OUT_AT + q * 128, OUT_AT + q * 128 + 128)
        for m in range(4):
            stack[m * BLOCK : (m + 1) * BLOCK, lanes] = block_of(pairs, k, m - (j - 1) * k)
    low_block = low_lanes((BLOCK, 128))
    for q, (a, b) in enumerate(((2, 1), (3, -2), (-1, -3))):
        lanes = slice(LEFT_AT + q * 128, LEFT_AT + q * 128 + 128)
        for m in range(4):
            stack[m * BLOCK : (m + 1) * BLOCK, lanes] = jnp.where(
                low_block, block_of(twice, abs(a), m + a), block_of(twice, abs(b), m + b)
            )


def spread(own, received, handed):
    return pl.pallas_call(
        spread_kernel,
        out_shape=pltpu.VMEM((PIXELS, 28 * W), BF16),
        in_specs=[pl.BlockSpec(memory_space=pltpu.VMEM)] * 7,
        out_specs=pl.BlockSpec(memory_space=pltpu.VMEM),
        scratch_shapes=[
            pltpu.VMEM((8, HALF, 128), BF16),
            pltpu.VMEM((3, PIXELS, 128), BF16),
            pltpu.VMEM((3, PIXELS, 128), BF16),
        ],
        compiler_params=pltpu.CompilerParams(vmem_limit_bytes=12 * 2**20),
        name="spread",
    )(own, *received, *handed)


def grad_kernel(flips, stack, weights, *outs):
    member = lax.axis_index("filt")
    for out, flip in zip(outs, flips):
        columns = pl.ds(pl.multiple_of((member ^ flip) * 512, 512), 512)
        out[...] = nn(stack[...], weights[:, columns]).astype(BF16)


def grads_for(flips, stack, weights, scale=1):
    return pl.pallas_call(
        functools.partial(grad_kernel, flips),
        out_shape=[jax.ShapeDtypeStruct((PIXELS, 512), BF16)] * len(flips),
        in_specs=[pl.BlockSpec(memory_space=pltpu.VMEM)] * 2,
        out_specs=[pl.BlockSpec(memory_space=pltpu.VMEM)] * len(flips),
        compiler_params=pltpu.CompilerParams(vmem_limit_bytes=18 * 2**20),
        cost_estimate=pl.CostEstimate(
            flops=2 * PIXELS * 28 * W * 512 * scale, bytes_accessed=10**6, transcendentals=0
        ),
        name="grads_for",
    )(stack, weights)


def last_kernel(a, b, c, out):
    total = a[...].astype(F32) + b[...].astype(F32) + c[...].astype(F32)

    def put(at, value):
        out[at : at + 192, :] = value

    from_blocks(order_matrix(True), total.astype(BF16), put)


def last_sum(a, b, c):
    return pl.pallas_call(
        last_kernel,
        out_shape=jax.ShapeDtypeStruct((PIXELS, 512), BF16),
        in_specs=[pl.BlockSpec(memory_space=pltpu.VMEM)] * 3,
        out_specs=pl.BlockSpec(memory_space=pltpu.VMEM),
        compiler_params=pltpu.CompilerParams(vmem_limit_bytes=10 * 2**20),
        name="last_sum",
    )(a, b, c)


def flipped(x, bit):
    return lax.ppermute(x, "filt", [(i, i ^ bit) for i in range(lax.axis_size("filt"))])


def swapped(x, bits):
    pairs = [(r, r ^ bits) for r in range(8) if abs((r ^ bits) - r) <= 3]
    return lax.ppermute(x, "rows", pairs)


def swapped_by_core(x, bits):
    pairs = [
        (4 * r + member, 4 * (r ^ bits[member % 2]) + member)
        for r in range(8)
        for member in range(4)
        if abs((r ^ bits[member % 2]) - r) <= 3
    ]
    return lax.ppermute(x, ("rows", "filt"), pairs)


def on_device(
    features, point_weight, dilated_weight, branch_bias, project_weight, project_bias, cotangent
):
    flat = features.reshape(PIXELS, CHANNELS)
    dilated = jnp.transpose(dilated_weight, (0, 1, 2, 4, 3)).reshape(27, W, CHANNELS)
    point = point_weight.T
    flat, dilated, point = (
        pltpu.with_memory_space_constraint(x, pltpu.HBM) for x in (flat, dilated, point)
    )
    *sums, ordered, weights = outward_sums(flat, dilated, point)
    received = {
        x: swapped(sums[n].astype(jnp.float16), x).astype(F32) for n, x in enumerate(SWAPS)
    }
    own = own_sums(ordered, weights, branch_bias)
    acts = [
        activations_of(part, swaps, own[part], [received[x] for x in swaps])
        for part, swaps in ((0, SWAPS[:2]), (1, SWAPS[2:]))
    ]
    across = [flipped(x, 2) for x in acts]
    beside = [flipped(x, 1) for x in acts]
    corner = [flipped(x, 1) for x in across]
    near, ordered_cotangent = near_head(
        acts,
        beside,
        project_weight,
        project_bias.reshape(1, 256),
        cotangent.reshape(PIXELS, 256),
    )
    output, grads, *sends = far_head(
        acts, beside, across, corner, project_weight, near, ordered_cotangent
    )
    arrived = [swapped_by_core(sends[n], swaps) for n, swaps in enumerate(GRAD_SWAPS)]
    handed = [flipped(x, 1) for x in arrived]
    stack = spread(grads, arrived, handed)
    (far,) = grads_for((3,), stack, weights)
    far = flipped(far, 1)
    (kept,) = grads_for((2,), stack, weights)
    crossing = (far.astype(F32) + kept.astype(F32)).astype(BF16)
    crossed = flipped(crossing, 2)
    later, output, crossing = lax.optimization_barrier((stack, output, crossing))
    head_output = own_output(output)
    (near,) = grads_for((1,), later, weights)
    near = flipped(near, 1)
    (kept,) = grads_for((0,), later, weights, 8)
    feature_grad = last_sum(kept, near, crossed)
    return head_output.reshape(12, 48, W), feature_grad.reshape(12, 48, 512)


def solution(mesh):
    body = on_device if fits(mesh) else on_device_general
    in_specs = (
        P("rows", None, None),
        P(None, "filt"),
        P(None, None, None, None, "filt"),
        P(None, "filt"),
        P(),
        P(),
        P("rows", None, None),
    )
    out_specs = (P("rows", None, "filt"), P("rows", None, "filt"))
    return jax.shard_map(
        body, mesh=mesh, in_specs=in_specs, out_specs=out_specs, check_vma=False
    )
```

```python
import functools

import jax
import jax.numpy as jnp
from jax import lax
from jax.experimental import pallas as pl
from jax.experimental.pallas import tpu as pltpu
from jax.sharding import PartitionSpec as P

FIRST_DILATION = 12
SECOND_DILATION = 24
THIRD_DILATION = 36


def passed_along(x, axis, by):
    devices = lax.axis_size(axis)
    pairs = [(i, i + by) for i in range(devices) if 0 <= i + by < devices]
    return lax.ppermute(x, axis, pairs)


def shift_columns(field, amount):
    breadth = field.shape[1]
    if amount == 0:
        return field
    padding = [(0, 0)] * field.ndim
    if amount > 0:
        kept = field[:, amount:]
        padding[1] = (0, amount)
    else:
        kept = field[:, : breadth + amount]
        padding[1] = (-amount, 0)
    return jnp.pad(kept, padding)


def fetch_sums(field, offset):
    return passed_along(field, "rows", offset)


def fetch_grads(field, offset):
    return passed_along(field, "rows", offset)


def shift_rows(field, amount, fetcher):
    height = field.shape[0]
    quotient = amount // height

    def extract_block(offset):
        if offset == 0:
            return field
        return fetcher(field, offset)

    return extract_block(quotient)


def make_kernel_taps(variants, dilation_rates):
    stacked = [variants[:, :, 0]]
    for branch, dilation in enumerate(dilation_rates):
        for row_tap in range(3):
            source = variants[:, :, 1 + 3 * branch + row_tap]
            for col_tap in range(3):
                stacked.append(shift_columns(source, -(col_tap - 1) * dilation))
    return jnp.stack(stacked, 2)


def on_device_general(
    features, point_weight, dilated_weight, branch_bias, project_weight, project_bias, cotangent
):
    height, breadth, channels = features.shape
    pixels = height * breadth
    own_width = point_weight.shape[1]
    filters = lax.axis_size("filt")
    member = lax.axis_index("filt")
    branch_outputs = project_weight.shape[2]
    own_out = branch_outputs // filters
    own_channels = channels // filters
    dilation_rates = (FIRST_DILATION, SECOND_DILATION, THIRD_DILATION)
    all_weights = jnp.concatenate(
        [point_weight[None], dilated_weight.reshape(27, channels, own_width)], 0
    )
    flattened = features.reshape(pixels, channels)
    tap_terms = jnp.einsum(
        "pc,tco->pto", flattened, all_weights, preferred_element_type=jnp.float32
    )
    tap_terms = tap_terms.reshape(height, breadth, 28, own_width)
    pre_list = [tap_terms[:, :, 0, :] + branch_bias[0]]
    for branch, dilation in enumerate(dilation_rates):
        summed_result = jnp.zeros((height, breadth, own_width), jnp.float32)
        for row_tap in range(3):
            row_sum = jnp.zeros((height, breadth, own_width), jnp.float32)
            for col_tap in range(3):
                row_sum = row_sum + shift_columns(
                    tap_terms[:, :, 1 + 9 * branch + 3 * row_tap + col_tap, :],
                    (col_tap - 1) * dilation,
                )
            summed_result = summed_result + shift_rows(
                row_sum, -(row_tap - 1) * dilation, fetch_sums
            )
        pre_list.append(summed_result + branch_bias[branch + 1])
    branch_pre = jnp.stack(pre_list, 2)
    activations = jnp.maximum(branch_pre, 0.0).astype(jnp.bfloat16).reshape(pixels, 4 * own_width)
    grouped = project_weight.reshape(4, filters, own_width, branch_outputs)
    own_rows = lax.dynamic_index_in_dim(grouped, member, 1, keepdims=False).reshape(
        4 * own_width, branch_outputs
    )
    flat_cotangent = cotangent.reshape(pixels, branch_outputs)
    ordered = jnp.transpose(grouped, (1, 0, 2, 3)).reshape(filters * 4 * own_width, branch_outputs)
    project_pre = jnp.dot(
        lax.all_gather(activations, "filt", axis=1, tiled=True),
        ordered,
        preferred_element_type=jnp.float32,
    )
    project_pre = project_pre + project_bias
    head_grad = jnp.where(project_pre > 0, flat_cotangent.astype(jnp.float32), 0.0).astype(
        jnp.bfloat16
    )
    own_pre = lax.dynamic_slice_in_dim(project_pre, member * own_out, own_out, 1)
    act_grad = jnp.dot(head_grad, own_rows.T, preferred_element_type=jnp.float32)
    head_output = jnp.maximum(own_pre, 0.0).astype(jnp.bfloat16).reshape(height, breadth, own_out)
    branch_grad = jnp.where(
        branch_pre > 0, act_grad.reshape(height, breadth, 4, own_width), 0.0
    ).astype(jnp.bfloat16)
    variant_list = [branch_grad[:, :, 0, :]]
    for branch, dilation in enumerate(dilation_rates):
        for row_tap in range(3):
            variant_list.append(
                shift_rows(branch_grad[:, :, branch + 1, :], (row_tap - 1) * dilation, fetch_grads)
            )
    variants = jnp.stack(variant_list, 2)
    stacked = make_kernel_taps(variants, dilation_rates).reshape(pixels, 28, own_width)
    input_grad = lax.psum_scatter(
        jnp.einsum("pto,tco->cp", stacked, all_weights, preferred_element_type=jnp.float32),
        "filt",
        scatter_dimension=0,
        tiled=True,
    ).T
    feature_grad = input_grad.astype(jnp.bfloat16).reshape(height, breadth, own_channels)
    return (head_output, feature_grad)


W = 64
BLOCK = 144
PIXELS = 576
HALF = 288
SENT = 304
CHANNELS = 2048
F32 = jnp.float32
BF16 = jnp.bfloat16

OUT_PAIRS = ((3, 1), (1, 1), (3, 0), (1, 0), (3, 2), (1, 2), (2, 1), (2, 0), (2, 2))
TAPS = (
    [(k, 1, 1) for k in (1, 2, 3)]
    + [(k, i, j) for k, j in OUT_PAIRS for i in (0, 2)]
    + [(k, 1, j) for j in (0, 2) for k in (1, 2, 3)]
)
OUT_AT, LEFT_AT, RIGHT_AT = 4 * W, 22 * W, 25 * W
PARTS = ((0, 1), (2, 3))
PART_SWAPS = ((7, 3, 1), (6, 2, 5, 7, 3))
SWAPS = (1, 3, 7, 5, 2, 6)
GRAD_SWAPS = ((1, 3), (5, 7), (2, 6))


def fits(mesh):
    return mesh.shape["rows"] == 8 and mesh.shape["filt"] == 4


def order_matrix(turned=False):
    to = lax.broadcasted_iota(jnp.int32, (192, 192), 1 if turned else 0)
    source = lax.broadcasted_iota(jnp.int32, (192, 192), 0 if turned else 1)

    def parts(value, width):
        return sum((value >= n * width).astype(jnp.int32) for n in (1, 2, 3))

    block = parts(to, 48)
    within = to - 48 * block
    line = parts(within, 12)
    wanted = line * 48 + block * 12 + within - 12 * line
    return (source == wanted).astype(F32).astype(BF16)


def tap_index(tap):
    k, i, j = tap
    return (k - 1) * 9 + i * 3 + j


def nt(a, b):
    return lax.dot_general(a, b, (((1,), (1,)), ((), ())), preferred_element_type=F32)


def nn(a, b):
    return lax.dot_general(a, b, (((1,), (0,)), ((), ())), preferred_element_type=F32)


def from_blocks(order_t, value, write):
    for g in range(3):
        parts = [value[m * BLOCK + g * 48 : m * BLOCK + g * 48 + 48] for m in range(4)]
        write(g * 192, nn(order_t, jnp.concatenate(parts, 0)).astype(BF16))


def low_lanes(shape):
    return lax.broadcasted_iota(jnp.int32, shape, 1) % 128 < W


def scaled(value):
    most = jnp.maximum(jnp.max(jnp.abs(value), axis=0, keepdims=True), 1e-30)
    power = jnp.floor(jnp.log(most) * 1.4426950408889634)
    return value * jnp.exp2(13.0 - power), power


def unscaled(sent):
    return sent[:HALF, :] * jnp.exp2(sent[HALF : HALF + 1, :] - 13.0)


def outward_slot(row, x):
    other = row ^ x
    apart = jnp.abs(other - row)
    slot = apart - 1 + jnp.where(other < row, 3, 0)
    return jnp.where(apart <= 3, slot, 0)


def fetch_tap(dilated, weights, sem, place):
    return pltpu.make_async_copy(
        dilated.at[tap_index(TAPS[place - 1])], weights.at[pl.ds(place * W, W)], sem
    )


def outward_kernel(features, dilated, point, *refs):
    row = lax.axis_index("rows")
    out, ordered, weights = refs[0:6], refs[6], refs[7]
    raw, sums, packed, feature_sems, weight_sems = refs[8:]
    loads = []
    for g in range(3):
        rows = pl.ds(g * 192, 192)
        loads.append(pltpu.make_async_copy(features.at[rows], raw.at[rows], feature_sems.at[g]))
        loads[-1].start()
    queue = [
        fetch_tap(dilated, weights, weight_sems.at[q], place)
        for q, place in enumerate((*range(4, 28), 1, 2, 3))
    ]
    queue.append(pltpu.make_async_copy(point, weights.at[pl.ds(0, W)], weight_sems.at[27]))

    def start_loads(first, last):
        for fetch in queue[first:last]:
            fetch.start()

    start_loads(0, 4)
    order = order_matrix()
    for g in range(3):
        loads[g].wait()
        start_loads((4, 12, 18)[g], (12, 18, 28)[g])
        moved = nn(order, raw[g * 192 : (g + 1) * 192, :]).astype(BF16)
        for m in range(4):
            at = m * BLOCK + g * 48
            ordered[at : at + 48, :] = moved[m * 48 : (m + 1) * 48]

    def product(pair, pairs, first, last):
        for fetch in queue[2 * pair : 2 * (pair + pairs)]:
            fetch.wait()
        at = OUT_AT + pair * 128
        return nt(ordered[first * BLOCK : last * BLOCK, :], weights[at : at + pairs * 128, :])

    d = product(0, 2, 0, 4)
    sums[2] = d[:, :128]
    sums[0] = d[:, 128:]
    d = product(2, 2, 0, 3)
    sums[2, 3 * BLOCK :, :] = sums[2, 3 * BLOCK :, :] + d[:BLOCK, :128]
    sums[0, BLOCK:, :] = sums[0, BLOCK:, :] + d[:, 128:]
    d = product(4, 2, 1, 4)
    sums[2, :BLOCK, :] = sums[2, :BLOCK, :] + d[2 * BLOCK :, :128]
    sums[0, : 3 * BLOCK, :] = sums[0, : 3 * BLOCK, :] + d[:, 128:]
    low = low_lanes((HALF, 128))

    def pack(k):
        top, bottom = sums[k, :HALF, :], sums[k, HALF:, :]
        halves = (
            jnp.where(low, top, pltpu.roll(bottom, W, 1)),
            jnp.where(low, pltpu.roll(top, W, 1), bottom),
        )
        for way, value in enumerate(halves):
            value, power = scaled(value)
            packed[k + 3 * way, :HALF, :] = value
            packed[k + 3 * way, HALF:, :] = jnp.broadcast_to(power, (SENT - HALF, 128))

    pack(2)
    pack(0)
    d = product(6, 3, 0, 4)
    sums[1] = d[:, :128]
    sums[1, 2 * BLOCK :, :] = sums[1, 2 * BLOCK :, :] + d[: 2 * BLOCK, 128:256]
    sums[1, : 2 * BLOCK, :] = sums[1, : 2 * BLOCK, :] + d[2 * BLOCK :, 256:]
    pack(1)
    for n, x in enumerate(SWAPS):
        out[n][...] = packed[outward_slot(row, x)]
    for fetch in queue[18:]:
        fetch.wait()


def outward_sums(features, dilated, point):
    return pl.pallas_call(
        outward_kernel,
        out_shape=[jax.ShapeDtypeStruct((SENT, 128), F32)] * 6
        + [pltpu.VMEM((PIXELS, CHANNELS), BF16), pltpu.VMEM((28 * W, CHANNELS), BF16)],
        in_specs=[pl.BlockSpec(memory_space=pltpu.HBM)] * 3,
        out_specs=[pl.BlockSpec(memory_space=pltpu.VMEM)] * 8,
        scratch_shapes=[
            pltpu.VMEM((PIXELS, CHANNELS), BF16),
            pltpu.VMEM((3, PIXELS, 128), F32),
            pltpu.VMEM((6, SENT, 128), F32),
            pltpu.SemaphoreType.DMA((3,)),
            pltpu.SemaphoreType.DMA((28,)),
        ],
        compiler_params=pltpu.CompilerParams(vmem_limit_bytes=28 * 2**20),
        name="outward_sums",
    )(features, dilated, point)


def own_kernel(ordered, weights, bias, *outs):
    d = nt(ordered[...], weights[:256, :])
    for part, out in enumerate(outs):
        line = jnp.concatenate([bias[k : k + 1, :] for k in PARTS[part]], 1)
        out[...] = d[:, part * 128 : part * 128 + 128] + line
    low = low_lanes((PIXELS, 128))

    def add(first, value, k):
        part = k // 2
        rows = slice(first * BLOCK, first * BLOCK + value.shape[0])
        mask, value = low[: value.shape[0]], value[:, part * 128 : part * 128 + 128]
        kept = jnp.where(mask, value, 0.0) if k == 2 else jnp.where(mask, 0.0, value)
        outs[part][rows, :] = outs[part][rows, :] + kept

    d = nt(ordered[: 3 * BLOCK, :], weights[LEFT_AT - W : LEFT_AT + 3 * W, :])
    for k in (1, 2, 3):
        add(k, d[: (4 - k) * BLOCK], k)
    d = nt(ordered[BLOCK:, :], weights[RIGHT_AT - W : RIGHT_AT + 3 * W, :])
    for k in (1, 2, 3):
        add(0, d[(k - 1) * BLOCK :], k)


def own_sums(ordered, weights, bias):
    return pl.pallas_call(
        own_kernel,
        out_shape=[jax.ShapeDtypeStruct((PIXELS, 128), F32)] * 2,
        in_specs=[pl.BlockSpec(memory_space=pltpu.VMEM)] * 3,
        out_specs=[pl.BlockSpec(memory_space=pltpu.VMEM)] * 2,
        compiler_params=pltpu.CompilerParams(vmem_limit_bytes=18 * 2**20),
        cost_estimate=pl.CostEstimate(flops=10**6, bytes_accessed=10**4, transcendentals=0),
        name="own_sums",
    )(ordered, weights, bias)


def arrival_slot(row, other):
    return jnp.where((other >= 0) & (other < 8), row ^ other, 0)


def gather_arrivals(recv, arrivals, swaps):
    arrivals[0] = jnp.zeros((HALF, 128), arrivals.dtype)
    for n, x in enumerate(swaps):
        arrivals[x] = unscaled(recv[n][...])


def activation_kernel(part, swaps, own, *refs):
    recv, acts, arrivals = refs[: len(swaps)], refs[-2], refs[-1]
    row = lax.axis_index("rows")
    gather_arrivals(recv, arrivals, swaps)
    low = low_lanes((HALF, 128))

    def total(k):
        return arrivals[arrival_slot(row, row - k)] + arrivals[arrival_slot(row, row + k)]

    high = total(PARTS[part][1])
    top, bottom = jnp.where(low, 0.0, pltpu.roll(high, W, 1)), jnp.where(low, 0.0, high)
    if part:
        left = total(PARTS[part][0])
        top = jnp.where(low, left, top)
        bottom = jnp.where(low, pltpu.roll(left, W, 1), bottom)
    acts[:HALF, :] = jnp.maximum(own[:HALF, :] + top, 0.0).astype(BF16)
    acts[HALF:, :] = jnp.maximum(own[HALF:, :] + bottom, 0.0).astype(BF16)


def activations_of(part, swaps, own, received):
    return pl.pallas_call(
        functools.partial(activation_kernel, part, swaps),
        out_shape=jax.ShapeDtypeStruct((PIXELS, 128), BF16),
        in_specs=[pl.BlockSpec(memory_space=pltpu.VMEM)] * (1 + len(swaps)),
        out_specs=pl.BlockSpec(memory_space=pltpu.VMEM),
        scratch_shapes=[pltpu.VMEM((8, HALF, 128), F32)],
        compiler_params=pltpu.CompilerParams(vmem_limit_bytes=8 * 2**20),
        name="activations",
    )(own, *received)


def project_rows(project, who):
    at = pl.multiple_of(who * W, W)
    return jnp.concatenate([project[k, pl.ds(at, W), :] for part in PARTS for k in part], 0)


def both(a, b):
    return jnp.concatenate([a[...], b[...]], 1)


def near_head_kernel(a0, b0, a1, b1, project, bias, cotangent, pre, ordered):
    member = lax.axis_index("filt")
    pre[...] = nn(both(a0, b0), project_rows(project, member)) + bias[...]
    pre[...] = pre[...] + nn(both(a1, b1), project_rows(project, member ^ 1))
    order = order_matrix()
    for g in range(3):
        moved = nn(order, cotangent[g * 192 : (g + 1) * 192, :])
        for m in range(4):
            at = m * BLOCK + g * 48
            ordered[at : at + 48, :] = moved[m * 48 : (m + 1) * 48]


def near_head(own, beside, project, bias, cotangent):
    return pl.pallas_call(
        near_head_kernel,
        out_shape=[jax.ShapeDtypeStruct((PIXELS, 256), F32)] * 2,
        in_specs=[pl.BlockSpec(memory_space=pltpu.VMEM)] * 7,
        out_specs=[pl.BlockSpec(memory_space=pltpu.VMEM)] * 2,
        compiler_params=pltpu.CompilerParams(vmem_limit_bytes=10 * 2**20),
        name="near_head",
    )(*own, *beside, project, bias, cotangent)


def far_head_kernel(a0, b0, a1, b1, a2, b2, a3, b3, project, near, cotangent, *refs):
    output, grads, sends, packed = refs[0], refs[1], refs[2:5], refs[5]
    row, member = lax.axis_index("rows"), lax.axis_index("filt")
    pre = near[...] + nn(both(a2, b2), project_rows(project, member ^ 2))
    pre = pre + nn(both(a3, b3), project_rows(project, member ^ 3))
    output[...] = jnp.maximum(pre, 0.0).astype(BF16)
    head_grad = jnp.where(pre > 0, cotangent[...], 0.0).astype(BF16)
    low = low_lanes((HALF, 128))
    for who, (acts_a, acts_b) in enumerate(((a0, b0), (a1, b1))):
        act_grad = nt(head_grad, project_rows(project, member ^ who))
        a = jnp.where(acts_a[...].astype(F32) > 0, act_grad[:, :128], 0.0)
        b = jnp.where(acts_b[...].astype(F32) > 0, act_grad[:, 128:], 0.0)
        if who == 0:
            grads[:, :128] = a.astype(BF16)
            grads[:, 128:] = b.astype(BF16)
        packed[0, who] = jnp.where(low, pltpu.roll(a[:HALF], W, 1), a[HALF:]).astype(BF16)
        packed[1, who] = jnp.where(low, b[:HALF], pltpu.roll(b[HALF:], W, 1)).astype(BF16)
        packed[2, who] = jnp.where(low, pltpu.roll(b[:HALF], W, 1), b[HALF:]).astype(BF16)
    for n, swaps in enumerate(GRAD_SWAPS):
        apart = jnp.abs((row ^ jnp.where((member & 1) == 0, *swaps)) - row)
        sends[n][...] = packed[jnp.where(apart <= 3, apart - 1, 0)]


def far_head(own, beside, across, corner, project, near, cotangent):
    return pl.pallas_call(
        far_head_kernel,
        out_shape=[jax.ShapeDtypeStruct((PIXELS, 256), BF16)] * 2
        + [jax.ShapeDtypeStruct((2, HALF, 128), BF16)] * 3,
        in_specs=[pl.BlockSpec(memory_space=pltpu.VMEM)] * 11,
        out_specs=[pl.BlockSpec(memory_space=pltpu.VMEM)] * 5,
        scratch_shapes=[pltpu.VMEM((3, 2, HALF, 128), BF16)],
        compiler_params=pltpu.CompilerParams(vmem_limit_bytes=12 * 2**20),
        name="far_head",
    )(*own, *beside, *across, *corner, project, near, cotangent)


def own_output_kernel(output, out):
    member = lax.axis_index("filt")
    mine = jnp.zeros((PIXELS, W), F32)
    for q in range(4):
        mine = jnp.where(member == q, output[:, q * W : (q + 1) * W].astype(F32), mine)

    def put(at, value):
        out[at : at + 192, :] = value

    from_blocks(order_matrix(True), mine.astype(BF16), put)


def own_output(output):
    return pl.pallas_call(
        own_output_kernel,
        out_shape=jax.ShapeDtypeStruct((PIXELS, W), BF16),
        in_specs=[pl.BlockSpec(memory_space=pltpu.VMEM)],
        out_specs=pl.BlockSpec(memory_space=pltpu.VMEM),
        compiler_params=pltpu.CompilerParams(vmem_limit_bytes=6 * 2**20),
        name="own_output",
    )(output)


def spread_kernel(own, *refs):
    recv, handed, stack, arrivals, pairs, twice = refs[:3], refs[3:6], *refs[6:]
    row, member = lax.axis_index("rows"), lax.axis_index("filt")
    arrivals[0] = jnp.zeros((HALF, 128), BF16)
    for n, (even, odd) in enumerate(GRAD_SWAPS):
        first = (member & 1) == 0
        arrivals[jnp.where(first, even, odd)] = recv[n][0]
        arrivals[jnp.where(first, odd, even)] = handed[n][1]
    low = low_lanes((HALF, 128))
    low_all = low_lanes((PIXELS, 128))
    for k in (1, 2, 3):
        p = arrivals[arrival_slot(row, row + k)].astype(F32)
        m = arrivals[arrival_slot(row, row - k)].astype(F32)
        pairs[k - 1, :HALF, :] = jnp.where(low, p, pltpu.roll(m, W, 1)).astype(BF16)
        pairs[k - 1, HALF:, :] = jnp.where(low, pltpu.roll(p, W, 1), m).astype(BF16)
        g = own[:, :128].astype(F32) if k == 1 else own[:, 128:].astype(F32)
        other = pltpu.roll(g, W, 1)
        two = jnp.where(low_all, g, other) if k == 2 else jnp.where(low_all, other, g)
        twice[k - 1] = two.astype(BF16)
    stack[:, : 4 * W] = own[...]
    nothing = jnp.zeros((BLOCK, 128), BF16)

    def block_of(ref, k, source):
        if 0 <= source < 4:
            return ref[k - 1, source * BLOCK : (source + 1) * BLOCK, :]
        return nothing

    for q, (k, j) in enumerate(OUT_PAIRS):
        lanes = slice(OUT_AT + q * 128, OUT_AT + q * 128 + 128)
        for m in range(4):
            stack[m * BLOCK : (m + 1) * BLOCK, lanes] = block_of(pairs, k, m - (j - 1) * k)
    low_block = low_lanes((BLOCK, 128))
    for q, (a, b) in enumerate(((1, 2), (3, -1), (-2, -3))):
        lanes = slice(LEFT_AT + q * 128, LEFT_AT + q * 128 + 128)
        for m in range(4):
            stack[m * BLOCK : (m + 1) * BLOCK, lanes] = jnp.where(
                low_block, block_of(twice, abs(a), m + a), block_of(twice, abs(b), m + b)
            )


def spread(own, received, handed):
    return pl.pallas_call(
        spread_kernel,
        out_shape=pltpu.VMEM((PIXELS, 28 * W), BF16),
        in_specs=[pl.BlockSpec(memory_space=pltpu.VMEM)] * 7,
        out_specs=pl.BlockSpec(memory_space=pltpu.VMEM),
        scratch_shapes=[
            pltpu.VMEM((8, HALF, 128), BF16),
            pltpu.VMEM((3, PIXELS, 128), BF16),
            pltpu.VMEM((3, PIXELS, 128), BF16),
        ],
        compiler_params=pltpu.CompilerParams(vmem_limit_bytes=12 * 2**20),
        name="spread",
    )(own, *received, *handed)


def grad_kernel(flips, stack, weights, *outs):
    member = lax.axis_index("filt")
    for out, flip in zip(outs, flips):
        columns = pl.ds(pl.multiple_of((member ^ flip) * 512, 512), 512)
        out[...] = nn(stack[...], weights[:, columns]).astype(BF16)


def grads_for(flips, stack, weights, scale=1):
    return pl.pallas_call(
        functools.partial(grad_kernel, flips),
        out_shape=[jax.ShapeDtypeStruct((PIXELS, 512), BF16)] * len(flips),
        in_specs=[pl.BlockSpec(memory_space=pltpu.VMEM)] * 2,
        out_specs=[pl.BlockSpec(memory_space=pltpu.VMEM)] * len(flips),
        compiler_params=pltpu.CompilerParams(vmem_limit_bytes=18 * 2**20),
        cost_estimate=pl.CostEstimate(
            flops=2 * PIXELS * 28 * W * 512 * scale, bytes_accessed=10**6, transcendentals=0
        ),
        name="grads_for",
    )(stack, weights)


def last_kernel(a, b, c, out):
    total = a[...].astype(F32) + b[...].astype(F32) + c[...].astype(F32)

    def put(at, value):
        out[at : at + 192, :] = value

    from_blocks(order_matrix(True), total.astype(BF16), put)


def last_sum(a, b, c):
    return pl.pallas_call(
        last_kernel,
        out_shape=jax.ShapeDtypeStruct((PIXELS, 512), BF16),
        in_specs=[pl.BlockSpec(memory_space=pltpu.VMEM)] * 3,
        out_specs=pl.BlockSpec(memory_space=pltpu.VMEM),
        compiler_params=pltpu.CompilerParams(vmem_limit_bytes=10 * 2**20),
        name="last_sum",
    )(a, b, c)


def flipped(x, bit):
    return lax.ppermute(x, "filt", [(i, i ^ bit) for i in range(lax.axis_size("filt"))])


def swapped(x, bits):
    pairs = [(r, r ^ bits) for r in range(8) if abs((r ^ bits) - r) <= 3]
    return lax.ppermute(x, "rows", pairs)


def swapped_by_core(x, bits):
    pairs = [
        (4 * r + member, 4 * (r ^ bits[member % 2]) + member)
        for r in range(8)
        for member in range(4)
        if abs((r ^ bits[member % 2]) - r) <= 3
    ]
    return lax.ppermute(x, ("rows", "filt"), pairs)


def on_device(
    features, point_weight, dilated_weight, branch_bias, project_weight, project_bias, cotangent
):
    flat = features.reshape(PIXELS, CHANNELS)
    dilated = jnp.transpose(dilated_weight, (0, 1, 2, 4, 3)).reshape(27, W, CHANNELS)
    point = point_weight.T
    flat, dilated, point = (
        pltpu.with_memory_space_constraint(x, pltpu.HBM) for x in (flat, dilated, point)
    )
    *sums, ordered, weights = outward_sums(flat, dilated, point)
    received = {
        x: swapped(sums[n].astype(jnp.float16), x).astype(F32) for n, x in enumerate(SWAPS)
    }
    own = own_sums(ordered, weights, branch_bias)
    acts = [
        activations_of(part, swaps, own[part], [received[x] for x in swaps])
        for part, swaps in enumerate(PART_SWAPS)
    ]
    across = [flipped(x, 2) for x in acts]
    beside = [flipped(x, 1) for x in acts]
    corner = [flipped(x, 1) for x in across]
    near, ordered_cotangent = near_head(
        acts,
        beside,
        project_weight,
        project_bias.reshape(1, 256),
        cotangent.reshape(PIXELS, 256),
    )
    output, grads, *sends = far_head(
        acts, beside, across, corner, project_weight, near, ordered_cotangent
    )
    arrived = [swapped_by_core(sends[n], swaps) for n, swaps in enumerate(GRAD_SWAPS)]
    handed = [flipped(x, 1) for x in arrived]
    stack = spread(grads, arrived, handed)
    (far,) = grads_for((3,), stack, weights)
    far = flipped(far, 1)
    (kept,) = grads_for((2,), stack, weights)
    crossing = (far.astype(F32) + kept.astype(F32)).astype(BF16)
    crossed = flipped(crossing, 2)
    later, output, crossing = lax.optimization_barrier((stack, output, crossing))
    head_output = own_output(output)
    (near,) = grads_for((1,), later, weights)
    near = flipped(near, 1)
    (kept,) = grads_for((0,), later, weights, 8)
    feature_grad = last_sum(kept, near, crossed)
    return head_output.reshape(12, 48, W), feature_grad.reshape(12, 48, 512)


def solution(mesh):
    body = on_device if fits(mesh) else on_device_general
    in_specs = (
        P("rows", None, None),
        P(None, "filt"),
        P(None, None, None, None, "filt"),
        P(None, "filt"),
        P(),
        P(),
        P("rows", None, None),
    )
    out_specs = (P("rows", None, "filt"), P("rows", None, "filt"))
    return jax.shard_map(
        body, mesh=mesh, in_specs=in_specs, out_specs=out_specs, check_vma=False
    )
```

```python
import functools

import jax
import jax.numpy as jnp
from jax import lax
from jax.experimental import pallas as pl
from jax.experimental.pallas import tpu as pltpu
from jax.sharding import PartitionSpec as P

FIRST_DILATION = 12
SECOND_DILATION = 24
THIRD_DILATION = 36


def passed_along(x, axis, by):
    devices = lax.axis_size(axis)
    pairs = [(i, i + by) for i in range(devices) if 0 <= i + by < devices]
    return lax.ppermute(x, axis, pairs)


def shift_columns(field, amount):
    breadth = field.shape[1]
    if amount == 0:
        return field
    padding = [(0, 0)] * field.ndim
    if amount > 0:
        kept = field[:, amount:]
        padding[1] = (0, amount)
    else:
        kept = field[:, : breadth + amount]
        padding[1] = (-amount, 0)
    return jnp.pad(kept, padding)


def fetch_sums(field, offset):
    return passed_along(field, "rows", offset)


def fetch_grads(field, offset):
    return passed_along(field, "rows", offset)


def shift_rows(field, amount, fetcher):
    height = field.shape[0]
    quotient = amount // height

    def extract_block(offset):
        if offset == 0:
            return field
        return fetcher(field, offset)

    return extract_block(quotient)


def make_kernel_taps(variants, dilation_rates):
    stacked = [variants[:, :, 0]]
    for branch, dilation in enumerate(dilation_rates):
        for row_tap in range(3):
            source = variants[:, :, 1 + 3 * branch + row_tap]
            for col_tap in range(3):
                stacked.append(shift_columns(source, -(col_tap - 1) * dilation))
    return jnp.stack(stacked, 2)


def on_device_general(
    features, point_weight, dilated_weight, branch_bias, project_weight, project_bias, cotangent
):
    height, breadth, channels = features.shape
    pixels = height * breadth
    own_width = point_weight.shape[1]
    filters = lax.axis_size("filt")
    member = lax.axis_index("filt")
    branch_outputs = project_weight.shape[2]
    own_out = branch_outputs // filters
    own_channels = channels // filters
    dilation_rates = (FIRST_DILATION, SECOND_DILATION, THIRD_DILATION)
    all_weights = jnp.concatenate(
        [point_weight[None], dilated_weight.reshape(27, channels, own_width)], 0
    )
    flattened = features.reshape(pixels, channels)
    tap_terms = jnp.einsum(
        "pc,tco->pto", flattened, all_weights, preferred_element_type=jnp.float32
    )
    tap_terms = tap_terms.reshape(height, breadth, 28, own_width)
    pre_list = [tap_terms[:, :, 0, :] + branch_bias[0]]
    for branch, dilation in enumerate(dilation_rates):
        summed_result = jnp.zeros((height, breadth, own_width), jnp.float32)
        for row_tap in range(3):
            row_sum = jnp.zeros((height, breadth, own_width), jnp.float32)
            for col_tap in range(3):
                row_sum = row_sum + shift_columns(
                    tap_terms[:, :, 1 + 9 * branch + 3 * row_tap + col_tap, :],
                    (col_tap - 1) * dilation,
                )
            summed_result = summed_result + shift_rows(
                row_sum, -(row_tap - 1) * dilation, fetch_sums
            )
        pre_list.append(summed_result + branch_bias[branch + 1])
    branch_pre = jnp.stack(pre_list, 2)
    activations = jnp.maximum(branch_pre, 0.0).astype(jnp.bfloat16).reshape(pixels, 4 * own_width)
    grouped = project_weight.reshape(4, filters, own_width, branch_outputs)
    own_rows = lax.dynamic_index_in_dim(grouped, member, 1, keepdims=False).reshape(
        4 * own_width, branch_outputs
    )
    flat_cotangent = cotangent.reshape(pixels, branch_outputs)
    ordered = jnp.transpose(grouped, (1, 0, 2, 3)).reshape(filters * 4 * own_width, branch_outputs)
    project_pre = jnp.dot(
        lax.all_gather(activations, "filt", axis=1, tiled=True),
        ordered,
        preferred_element_type=jnp.float32,
    )
    project_pre = project_pre + project_bias
    head_grad = jnp.where(project_pre > 0, flat_cotangent.astype(jnp.float32), 0.0).astype(
        jnp.bfloat16
    )
    own_pre = lax.dynamic_slice_in_dim(project_pre, member * own_out, own_out, 1)
    act_grad = jnp.dot(head_grad, own_rows.T, preferred_element_type=jnp.float32)
    head_output = jnp.maximum(own_pre, 0.0).astype(jnp.bfloat16).reshape(height, breadth, own_out)
    branch_grad = jnp.where(
        branch_pre > 0, act_grad.reshape(height, breadth, 4, own_width), 0.0
    ).astype(jnp.bfloat16)
    variant_list = [branch_grad[:, :, 0, :]]
    for branch, dilation in enumerate(dilation_rates):
        for row_tap in range(3):
            variant_list.append(
                shift_rows(branch_grad[:, :, branch + 1, :], (row_tap - 1) * dilation, fetch_grads)
            )
    variants = jnp.stack(variant_list, 2)
    stacked = make_kernel_taps(variants, dilation_rates).reshape(pixels, 28, own_width)
    input_grad = lax.psum_scatter(
        jnp.einsum("pto,tco->cp", stacked, all_weights, preferred_element_type=jnp.float32),
        "filt",
        scatter_dimension=0,
        tiled=True,
    ).T
    feature_grad = input_grad.astype(jnp.bfloat16).reshape(height, breadth, own_channels)
    return (head_output, feature_grad)


W = 64
BLOCK = 144
PIXELS = 576
HALF = 288
SENT = 304
CHANNELS = 2048
F32 = jnp.float32
BF16 = jnp.bfloat16

OUT_PAIRS = ((3, 1), (1, 1), (3, 0), (1, 0), (3, 2), (1, 2), (2, 1), (2, 0), (2, 2))
TAPS = (
    [(k, 1, 1) for k in (1, 2, 3)]
    + [(k, i, j) for k, j in OUT_PAIRS for i in (0, 2)]
    + [(k, 1, j) for j in (0, 2) for k in (1, 2, 3)]
)
OUT_AT, LEFT_AT, RIGHT_AT = 4 * W, 22 * W, 25 * W
PARTS = ((0, 1), (2, 3))
PART_SWAPS = ((7, 3, 1), (6, 2, 5, 7, 3))
SWAPS = (1, 3, 7, 5, 2, 6)
GRAD_SWAPS = ((1, 3), (5, 7), (2, 6))


def fits(mesh):
    return mesh.shape["rows"] == 8 and mesh.shape["filt"] == 4


def order_matrix(turned=False):
    to = lax.broadcasted_iota(jnp.int32, (192, 192), 1 if turned else 0)
    source = lax.broadcasted_iota(jnp.int32, (192, 192), 0 if turned else 1)

    def parts(value, width):
        return sum((value >= n * width).astype(jnp.int32) for n in (1, 2, 3))

    block = parts(to, 48)
    within = to - 48 * block
    line = parts(within, 12)
    wanted = line * 48 + block * 12 + within - 12 * line
    return (source == wanted).astype(F32).astype(BF16)


def tap_index(tap):
    k, i, j = tap
    return (k - 1) * 9 + i * 3 + j


def nt(a, b):
    return lax.dot_general(a, b, (((1,), (1,)), ((), ())), preferred_element_type=F32)


def nn(a, b):
    return lax.dot_general(a, b, (((1,), (0,)), ((), ())), preferred_element_type=F32)


def from_blocks(order_t, value, write):
    for g in range(3):
        parts = [value[m * BLOCK + g * 48 : m * BLOCK + g * 48 + 48] for m in range(4)]
        write(g * 192, nn(order_t, jnp.concatenate(parts, 0)).astype(BF16))


def low_lanes(shape):
    return lax.broadcasted_iota(jnp.int32, shape, 1) % 128 < W


def scaled(value):
    most = jnp.maximum(jnp.max(jnp.abs(value), axis=0, keepdims=True), 1e-30)
    power = jnp.floor(jnp.log(most) * 1.4426950408889634)
    return value * jnp.exp2(13.0 - power), power


def unscaled(sent):
    return sent[:HALF, :] * jnp.exp2(sent[HALF : HALF + 1, :] - 13.0)


def outward_slot(row, x):
    other = row ^ x
    apart = jnp.abs(other - row)
    slot = apart - 1 + jnp.where(other < row, 3, 0)
    return jnp.where(apart <= 3, slot, 0)


def fetch_tap(dilated, weights, sem, place):
    return pltpu.make_async_copy(
        dilated.at[tap_index(TAPS[place - 1])], weights.at[pl.ds(place * W, W)], sem
    )


def outward_kernel(features, dilated, point, *refs):
    row = lax.axis_index("rows")
    out, ordered, weights = refs[0:6], refs[6], refs[7]
    raw, sums, packed, feature_sems, weight_sems = refs[8:]
    loads = []
    for g in range(3):
        rows = pl.ds(g * 192, 192)
        loads.append(pltpu.make_async_copy(features.at[rows], raw.at[rows], feature_sems.at[g]))
        loads[-1].start()
    queue = [
        fetch_tap(dilated, weights, weight_sems.at[q], place)
        for q, place in enumerate((*range(4, 28), 1, 2, 3))
    ]
    queue.append(pltpu.make_async_copy(point, weights.at[pl.ds(0, W)], weight_sems.at[27]))

    def start_loads(first, last):
        for fetch in queue[first:last]:
            fetch.start()

    start_loads(0, 4)
    order = order_matrix()
    for g in range(3):
        loads[g].wait()
        start_loads((4, 12, 18)[g], (12, 18, 28)[g])
        moved = nn(order, raw[g * 192 : (g + 1) * 192, :]).astype(BF16)
        for m in range(4):
            at = m * BLOCK + g * 48
            ordered[at : at + 48, :] = moved[m * 48 : (m + 1) * 48]

    def product(pair, pairs, first, last):
        for fetch in queue[2 * pair : 2 * (pair + pairs)]:
            fetch.wait()
        at = OUT_AT + pair * 128
        return nt(ordered[first * BLOCK : last * BLOCK, :], weights[at : at + pairs * 128, :])

    d = product(0, 2, 0, 4)
    sums[2] = d[:, :128]
    sums[0] = d[:, 128:]
    d = product(2, 2, 0, 3)
    sums[2, 3 * BLOCK :, :] = sums[2, 3 * BLOCK :, :] + d[:BLOCK, :128]
    sums[0, BLOCK:, :] = sums[0, BLOCK:, :] + d[:, 128:]
    d = product(4, 2, 1, 4)
    sums[2, :BLOCK, :] = sums[2, :BLOCK, :] + d[2 * BLOCK :, :128]
    sums[0, : 3 * BLOCK, :] = sums[0, : 3 * BLOCK, :] + d[:, 128:]
    low = low_lanes((HALF, 128))

    def pack(k):
        top, bottom = sums[k, :HALF, :], sums[k, HALF:, :]
        halves = (
            jnp.where(low, top, pltpu.roll(bottom, W, 1)),
            jnp.where(low, pltpu.roll(top, W, 1), bottom),
        )
        for way, value in enumerate(halves):
            value, power = scaled(value)
            packed[k + 3 * way, :HALF, :] = value
            packed[k + 3 * way, HALF:, :] = jnp.broadcast_to(power, (SENT - HALF, 128))

    pack(2)
    pack(0)
    d = product(6, 3, 0, 4)
    sums[1] = d[:, :128]
    sums[1, 2 * BLOCK :, :] = sums[1, 2 * BLOCK :, :] + d[: 2 * BLOCK, 128:256]
    sums[1, : 2 * BLOCK, :] = sums[1, : 2 * BLOCK, :] + d[2 * BLOCK :, 256:]
    pack(1)
    for n, x in enumerate(SWAPS):
        out[n][...] = packed[outward_slot(row, x)]
    for fetch in queue[18:]:
        fetch.wait()


def outward_sums(features, dilated, point):
    return pl.pallas_call(
        outward_kernel,
        out_shape=[jax.ShapeDtypeStruct((SENT, 128), F32)] * 6
        + [pltpu.VMEM((PIXELS, CHANNELS), BF16), pltpu.VMEM((28 * W, CHANNELS), BF16)],
        in_specs=[pl.BlockSpec(memory_space=pltpu.HBM)] * 3,
        out_specs=[pl.BlockSpec(memory_space=pltpu.VMEM)] * 8,
        scratch_shapes=[
            pltpu.VMEM((PIXELS, CHANNELS), BF16),
            pltpu.VMEM((3, PIXELS, 128), F32),
            pltpu.VMEM((6, SENT, 128), F32),
            pltpu.SemaphoreType.DMA((3,)),
            pltpu.SemaphoreType.DMA((28,)),
        ],
        compiler_params=pltpu.CompilerParams(vmem_limit_bytes=28 * 2**20),
        name="outward_sums",
    )(features, dilated, point)


def own_kernel(ordered, weights, bias, *outs):
    d = nt(ordered[...], weights[:256, :])
    for part, out in enumerate(outs):
        line = jnp.concatenate([bias[k : k + 1, :] for k in PARTS[part]], 1)
        out[...] = d[:, part * 128 : part * 128 + 128] + line
    low = low_lanes((PIXELS, 128))

    def add(first, value, k):
        part = k // 2
        rows = slice(first * BLOCK, first * BLOCK + value.shape[0])
        mask, value = low[: value.shape[0]], value[:, part * 128 : part * 128 + 128]
        kept = jnp.where(mask, value, 0.0) if k == 2 else jnp.where(mask, 0.0, value)
        outs[part][rows, :] = outs[part][rows, :] + kept

    d = nt(ordered[: 3 * BLOCK, :], weights[LEFT_AT - W : LEFT_AT + 3 * W, :])
    for k in (1, 2, 3):
        add(k, d[: (4 - k) * BLOCK], k)
    d = nt(ordered[BLOCK:, :], weights[RIGHT_AT - W : RIGHT_AT + 3 * W, :])
    for k in (1, 2, 3):
        add(0, d[(k - 1) * BLOCK :], k)


def own_sums(ordered, weights, bias):
    return pl.pallas_call(
        own_kernel,
        out_shape=[jax.ShapeDtypeStruct((PIXELS, 128), F32)] * 2,
        in_specs=[pl.BlockSpec(memory_space=pltpu.VMEM)] * 3,
        out_specs=[pl.BlockSpec(memory_space=pltpu.VMEM)] * 2,
        compiler_params=pltpu.CompilerParams(vmem_limit_bytes=18 * 2**20),
        cost_estimate=pl.CostEstimate(flops=10**6, bytes_accessed=10**4, transcendentals=0),
        name="own_sums",
    )(ordered, weights, bias)


def arrival_slot(row, other):
    return jnp.where((other >= 0) & (other < 8), row ^ other, 0)


def gather_arrivals(recv, arrivals, swaps):
    arrivals[0] = jnp.zeros((HALF, 128), arrivals.dtype)
    for n, x in enumerate(swaps):
        arrivals[x] = unscaled(recv[n][...])


def activation_kernel(part, swaps, own, *refs):
    recv, acts, arrivals = refs[: len(swaps)], refs[-2], refs[-1]
    row = lax.axis_index("rows")
    gather_arrivals(recv, arrivals, swaps)
    low = low_lanes((HALF, 128))

    def total(k):
        return arrivals[arrival_slot(row, row - k)] + arrivals[arrival_slot(row, row + k)]

    high = total(PARTS[part][1])
    top, bottom = jnp.where(low, 0.0, pltpu.roll(high, W, 1)), jnp.where(low, 0.0, high)
    if part:
        left = total(PARTS[part][0])
        top = jnp.where(low, left, top)
        bottom = jnp.where(low, pltpu.roll(left, W, 1), bottom)
    acts[:HALF, :] = jnp.maximum(own[:HALF, :] + top, 0.0).astype(BF16)
    acts[HALF:, :] = jnp.maximum(own[HALF:, :] + bottom, 0.0).astype(BF16)


def activations_of(part, swaps, own, received):
    return pl.pallas_call(
        functools.partial(activation_kernel, part, swaps),
        out_shape=jax.ShapeDtypeStruct((PIXELS, 128), BF16),
        in_specs=[pl.BlockSpec(memory_space=pltpu.VMEM)] * (1 + len(swaps)),
        out_specs=pl.BlockSpec(memory_space=pltpu.VMEM),
        scratch_shapes=[pltpu.VMEM((8, HALF, 128), F32)],
        compiler_params=pltpu.CompilerParams(vmem_limit_bytes=8 * 2**20),
        name="activations",
    )(own, *received)


def project_rows(project, who):
    at = pl.multiple_of(who * W, W)
    return jnp.concatenate([project[k, pl.ds(at, W), :] for part in PARTS for k in part], 0)


def both(a, b):
    return jnp.concatenate([a[...], b[...]], 1)


def near_head_kernel(a0, b0, a1, b1, project, bias, cotangent, pre, ordered):
    member = lax.axis_index("filt")
    pre[...] = nn(both(a0, b0), project_rows(project, member)) + bias[...]
    pre[...] = pre[...] + nn(both(a1, b1), project_rows(project, member ^ 1))
    order = order_matrix()
    for g in range(3):
        moved = nn(order, cotangent[g * 192 : (g + 1) * 192, :])
        for m in range(4):
            at = m * BLOCK + g * 48
            ordered[at : at + 48, :] = moved[m * 48 : (m + 1) * 48]


def near_head(own, beside, project, bias, cotangent):
    return pl.pallas_call(
        near_head_kernel,
        out_shape=[jax.ShapeDtypeStruct((PIXELS, 256), F32)] * 2,
        in_specs=[pl.BlockSpec(memory_space=pltpu.VMEM)] * 7,
        out_specs=[pl.BlockSpec(memory_space=pltpu.VMEM)] * 2,
        compiler_params=pltpu.CompilerParams(vmem_limit_bytes=10 * 2**20),
        name="near_head",
    )(*own, *beside, project, bias, cotangent)


def far_head_kernel(a0, b0, a1, b1, a2, b2, a3, b3, project, near, cotangent, *refs):
    output, grads, sends, packed = refs[0], refs[1], refs[2:5], refs[5]
    row, member = lax.axis_index("rows"), lax.axis_index("filt")
    pre = near[...] + nn(both(a2, b2), project_rows(project, member ^ 2))
    pre = pre + nn(both(a3, b3), project_rows(project, member ^ 3))
    output[...] = jnp.maximum(pre, 0.0).astype(BF16)
    head_grad = jnp.where(pre > 0, cotangent[...], 0.0).astype(BF16)
    low = low_lanes((HALF, 128))
    for who, (acts_a, acts_b) in enumerate(((a0, b0), (a1, b1))):
        act_grad = nt(head_grad, project_rows(project, member ^ who))
        a = jnp.where(acts_a[...].astype(F32) > 0, act_grad[:, :128], 0.0)
        b = jnp.where(acts_b[...].astype(F32) > 0, act_grad[:, 128:], 0.0)
        if who == 0:
            grads[:, :128] = a.astype(BF16)
            grads[:, 128:] = b.astype(BF16)
        packed[0, who] = jnp.where(low, pltpu.roll(a[:HALF], W, 1), a[HALF:]).astype(BF16)
        packed[1, who] = jnp.where(low, b[:HALF], pltpu.roll(b[HALF:], W, 1)).astype(BF16)
        packed[2, who] = jnp.where(low, pltpu.roll(b[:HALF], W, 1), b[HALF:]).astype(BF16)
    for n, swaps in enumerate(GRAD_SWAPS):
        apart = jnp.abs((row ^ jnp.where((member & 1) == 0, *swaps)) - row)
        sends[n][...] = packed[jnp.where(apart <= 3, apart - 1, 0)]


def far_head(own, beside, across, corner, project, near, cotangent):
    return pl.pallas_call(
        far_head_kernel,
        out_shape=[jax.ShapeDtypeStruct((PIXELS, 256), BF16)] * 2
        + [jax.ShapeDtypeStruct((2, HALF, 128), BF16)] * 3,
        in_specs=[pl.BlockSpec(memory_space=pltpu.VMEM)] * 11,
        out_specs=[pl.BlockSpec(memory_space=pltpu.VMEM)] * 5,
        scratch_shapes=[pltpu.VMEM((3, 2, HALF, 128), BF16)],
        compiler_params=pltpu.CompilerParams(vmem_limit_bytes=12 * 2**20),
        name="far_head",
    )(*own, *beside, *across, *corner, project, near, cotangent)


def own_output_kernel(output, out):
    member = lax.axis_index("filt")
    mine = jnp.zeros((PIXELS, W), F32)
    for q in range(4):
        mine = jnp.where(member == q, output[:, q * W : (q + 1) * W].astype(F32), mine)

    def put(at, value):
        out[at : at + 192, :] = value

    from_blocks(order_matrix(True), mine.astype(BF16), put)


def own_output(output):
    return pl.pallas_call(
        own_output_kernel,
        out_shape=jax.ShapeDtypeStruct((PIXELS, W), BF16),
        in_specs=[pl.BlockSpec(memory_space=pltpu.VMEM)],
        out_specs=pl.BlockSpec(memory_space=pltpu.VMEM),
        compiler_params=pltpu.CompilerParams(vmem_limit_bytes=6 * 2**20),
        name="own_output",
    )(output)


def spread_kernel(own, *refs):
    recv, handed, stack, arrivals, pairs, twice = refs[:3], refs[3:6], *refs[6:]
    row, member = lax.axis_index("rows"), lax.axis_index("filt")
    arrivals[0] = jnp.zeros((HALF, 128), BF16)
    for n, (even, odd) in enumerate(GRAD_SWAPS):
        first = (member & 1) == 0
        arrivals[jnp.where(first, even, odd)] = recv[n][0]
        arrivals[jnp.where(first, odd, even)] = handed[n][1]
    low = low_lanes((HALF, 128))
    low_all = low_lanes((PIXELS, 128))
    for k in (1, 2, 3):
        p = arrivals[arrival_slot(row, row + k)].astype(F32)
        m = arrivals[arrival_slot(row, row - k)].astype(F32)
        pairs[k - 1, :HALF, :] = jnp.where(low, p, pltpu.roll(m, W, 1)).astype(BF16)
        pairs[k - 1, HALF:, :] = jnp.where(low, pltpu.roll(p, W, 1), m).astype(BF16)
        g = own[:, :128].astype(F32) if k == 1 else own[:, 128:].astype(F32)
        other = pltpu.roll(g, W, 1)
        two = jnp.where(low_all, g, other) if k == 2 else jnp.where(low_all, other, g)
        twice[k - 1] = two.astype(BF16)
    stack[:, : 4 * W] = own[...]
    nothing = jnp.zeros((BLOCK, 128), BF16)

    def block_of(ref, k, source):
        if 0 <= source < 4:
            return ref[k - 1, source * BLOCK : (source + 1) * BLOCK, :]
        return nothing

    for q, (k, j) in enumerate(OUT_PAIRS):
        lanes = slice(OUT_AT + q * 128, OUT_AT + q * 128 + 128)
        for m in range(4):
            stack[m * BLOCK : (m + 1) * BLOCK, lanes] = block_of(pairs, k, m - (j - 1) * k)
    low_block = low_lanes((BLOCK, 128))
    for q, (a, b) in enumerate(((1, 2), (3, -1), (-2, -3))):
        lanes = slice(LEFT_AT + q * 128, LEFT_AT + q * 128 + 128)
        for m in range(4):
            stack[m * BLOCK : (m + 1) * BLOCK, lanes] = jnp.where(
                low_block, block_of(twice, abs(a), m + a), block_of(twice, abs(b), m + b)
            )


def spread(own, received, handed):
    return pl.pallas_call(
        spread_kernel,
        out_shape=pltpu.VMEM((PIXELS, 28 * W), BF16),
        in_specs=[pl.BlockSpec(memory_space=pltpu.VMEM)] * 7,
        out_specs=pl.BlockSpec(memory_space=pltpu.VMEM),
        scratch_shapes=[
            pltpu.VMEM((8, HALF, 128), BF16),
            pltpu.VMEM((3, PIXELS, 128), BF16),
            pltpu.VMEM((3, PIXELS, 128), BF16),
        ],
        compiler_params=pltpu.CompilerParams(vmem_limit_bytes=12 * 2**20),
        name="spread",
    )(own, *received, *handed)


def grad_kernel(flips, stack, weights, *outs):
    member = lax.axis_index("filt")
    for out, flip in zip(outs, flips):
        columns = pl.ds(pl.multiple_of((member ^ flip) * 512, 512), 512)
        out[...] = nn(stack[...], weights[:, columns]).astype(BF16)


def grads_for(flips, stack, weights, scale=1):
    return pl.pallas_call(
        functools.partial(grad_kernel, flips),
        out_shape=[jax.ShapeDtypeStruct((PIXELS, 512), BF16)] * len(flips),
        in_specs=[pl.BlockSpec(memory_space=pltpu.VMEM)] * 2,
        out_specs=[pl.BlockSpec(memory_space=pltpu.VMEM)] * len(flips),
        compiler_params=pltpu.CompilerParams(vmem_limit_bytes=18 * 2**20),
        cost_estimate=pl.CostEstimate(
            flops=2 * PIXELS * 28 * W * 512 * scale, bytes_accessed=10**6, transcendentals=0
        ),
        name="grads_for",
    )(stack, weights)


def last_kernel(a, b, c, out):
    total = a[...].astype(F32) + b[...].astype(F32) + c[...].astype(F32)

    def put(at, value):
        out[at : at + 192, :] = value

    from_blocks(order_matrix(True), total.astype(BF16), put)


def last_sum(a, b, c):
    return pl.pallas_call(
        last_kernel,
        out_shape=jax.ShapeDtypeStruct((PIXELS, 512), BF16),
        in_specs=[pl.BlockSpec(memory_space=pltpu.VMEM)] * 3,
        out_specs=pl.BlockSpec(memory_space=pltpu.VMEM),
        compiler_params=pltpu.CompilerParams(vmem_limit_bytes=10 * 2**20),
        name="last_sum",
    )(a, b, c)


def flipped(x, bit):
    return lax.ppermute(x, "filt", [(i, i ^ bit) for i in range(lax.axis_size("filt"))])


def partner(r, bits):
    return r ^ bits if abs((r ^ bits) - r) <= 3 else r


def swapped(x, bits):
    return lax.ppermute(x, "rows", [(r, partner(r, bits)) for r in range(8)])


def swapped_by_core(x, bits):
    pairs = [
        (4 * r + member, 4 * partner(r, bits[member % 2]) + member)
        for r in range(8)
        for member in range(4)
    ]
    return lax.ppermute(x, ("rows", "filt"), pairs)


def on_device(
    features, point_weight, dilated_weight, branch_bias, project_weight, project_bias, cotangent
):
    flat = features.reshape(PIXELS, CHANNELS)
    dilated = jnp.transpose(dilated_weight, (0, 1, 2, 4, 3)).reshape(27, W, CHANNELS)
    point = point_weight.T
    flat, dilated, point = (
        pltpu.with_memory_space_constraint(x, pltpu.HBM) for x in (flat, dilated, point)
    )
    *sums, ordered, weights = outward_sums(flat, dilated, point)
    received = {
        x: swapped(sums[n].astype(jnp.float16), x).astype(F32) for n, x in enumerate(SWAPS)
    }
    own = own_sums(ordered, weights, branch_bias)
    acts = [
        activations_of(part, swaps, own[part], [received[x] for x in swaps])
        for part, swaps in enumerate(PART_SWAPS)
    ]
    across = [flipped(x, 2) for x in acts]
    beside = [flipped(x, 1) for x in acts]
    corner = [flipped(x, 1) for x in across]
    near, ordered_cotangent = near_head(
        acts,
        beside,
        project_weight,
        project_bias.reshape(1, 256),
        cotangent.reshape(PIXELS, 256),
    )
    output, grads, *sends = far_head(
        acts, beside, across, corner, project_weight, near, ordered_cotangent
    )
    arrived = [swapped_by_core(sends[n], swaps) for n, swaps in enumerate(GRAD_SWAPS)]
    handed = [flipped(x, 1) for x in arrived]
    stack = spread(grads, arrived, handed)
    (far,) = grads_for((3,), stack, weights)
    far = flipped(far, 1)
    (kept,) = grads_for((2,), stack, weights)
    crossing = (far.astype(F32) + kept.astype(F32)).astype(BF16)
    crossed = flipped(crossing, 2)
    later, output, crossing = lax.optimization_barrier((stack, output, crossing))
    head_output = own_output(output)
    (near,) = grads_for((1,), later, weights)
    near = flipped(near, 1)
    (kept,) = grads_for((0,), later, weights, 8)
    feature_grad = last_sum(kept, near, crossed)
    return head_output.reshape(12, 48, W), feature_grad.reshape(12, 48, 512)


def solution(mesh):
    body = on_device if fits(mesh) else on_device_general
    in_specs = (
        P("rows", None, None),
        P(None, "filt"),
        P(None, None, None, None, "filt"),
        P(None, "filt"),
        P(),
        P(),
        P("rows", None, None),
    )
    out_specs = (P("rows", None, "filt"), P("rows", None, "filt"))
    return jax.shard_map(
        body, mesh=mesh, in_specs=in_specs, out_specs=out_specs, check_vma=False
    )
```

```python
import functools

import jax
import jax.numpy as jnp
from jax import lax
from jax.experimental import pallas as pl
from jax.experimental.pallas import tpu as pltpu
from jax.sharding import PartitionSpec as P

FIRST_DILATION = 12
SECOND_DILATION = 24
THIRD_DILATION = 36


def passed_along(x, axis, by):
    devices = lax.axis_size(axis)
    pairs = [(i, i + by) for i in range(devices) if 0 <= i + by < devices]
    return lax.ppermute(x, axis, pairs)


def shift_columns(field, amount):
    breadth = field.shape[1]
    if amount == 0:
        return field
    padding = [(0, 0)] * field.ndim
    if amount > 0:
        kept = field[:, amount:]
        padding[1] = (0, amount)
    else:
        kept = field[:, : breadth + amount]
        padding[1] = (-amount, 0)
    return jnp.pad(kept, padding)


def fetch_sums(field, offset):
    return passed_along(field, "rows", offset)


def fetch_grads(field, offset):
    return passed_along(field, "rows", offset)


def shift_rows(field, amount, fetcher):
    height = field.shape[0]
    quotient = amount // height

    def extract_block(offset):
        if offset == 0:
            return field
        return fetcher(field, offset)

    return extract_block(quotient)


def make_kernel_taps(variants, dilation_rates):
    stacked = [variants[:, :, 0]]
    for branch, dilation in enumerate(dilation_rates):
        for row_tap in range(3):
            source = variants[:, :, 1 + 3 * branch + row_tap]
            for col_tap in range(3):
                stacked.append(shift_columns(source, -(col_tap - 1) * dilation))
    return jnp.stack(stacked, 2)


def on_device_general(
    features, point_weight, dilated_weight, branch_bias, project_weight, project_bias, cotangent
):
    height, breadth, channels = features.shape
    pixels = height * breadth
    own_width = point_weight.shape[1]
    filters = lax.axis_size("filt")
    member = lax.axis_index("filt")
    branch_outputs = project_weight.shape[2]
    own_out = branch_outputs // filters
    own_channels = channels // filters
    dilation_rates = (FIRST_DILATION, SECOND_DILATION, THIRD_DILATION)
    all_weights = jnp.concatenate(
        [point_weight[None], dilated_weight.reshape(27, channels, own_width)], 0
    )
    flattened = features.reshape(pixels, channels)
    tap_terms = jnp.einsum(
        "pc,tco->pto", flattened, all_weights, preferred_element_type=jnp.float32
    )
    tap_terms = tap_terms.reshape(height, breadth, 28, own_width)
    pre_list = [tap_terms[:, :, 0, :] + branch_bias[0]]
    for branch, dilation in enumerate(dilation_rates):
        summed_result = jnp.zeros((height, breadth, own_width), jnp.float32)
        for row_tap in range(3):
            row_sum = jnp.zeros((height, breadth, own_width), jnp.float32)
            for col_tap in range(3):
                row_sum = row_sum + shift_columns(
                    tap_terms[:, :, 1 + 9 * branch + 3 * row_tap + col_tap, :],
                    (col_tap - 1) * dilation,
                )
            summed_result = summed_result + shift_rows(
                row_sum, -(row_tap - 1) * dilation, fetch_sums
            )
        pre_list.append(summed_result + branch_bias[branch + 1])
    branch_pre = jnp.stack(pre_list, 2)
    activations = jnp.maximum(branch_pre, 0.0).astype(jnp.bfloat16).reshape(pixels, 4 * own_width)
    grouped = project_weight.reshape(4, filters, own_width, branch_outputs)
    own_rows = lax.dynamic_index_in_dim(grouped, member, 1, keepdims=False).reshape(
        4 * own_width, branch_outputs
    )
    flat_cotangent = cotangent.reshape(pixels, branch_outputs)
    ordered = jnp.transpose(grouped, (1, 0, 2, 3)).reshape(filters * 4 * own_width, branch_outputs)
    project_pre = jnp.dot(
        lax.all_gather(activations, "filt", axis=1, tiled=True),
        ordered,
        preferred_element_type=jnp.float32,
    )
    project_pre = project_pre + project_bias
    head_grad = jnp.where(project_pre > 0, flat_cotangent.astype(jnp.float32), 0.0).astype(
        jnp.bfloat16
    )
    own_pre = lax.dynamic_slice_in_dim(project_pre, member * own_out, own_out, 1)
    act_grad = jnp.dot(head_grad, own_rows.T, preferred_element_type=jnp.float32)
    head_output = jnp.maximum(own_pre, 0.0).astype(jnp.bfloat16).reshape(height, breadth, own_out)
    branch_grad = jnp.where(
        branch_pre > 0, act_grad.reshape(height, breadth, 4, own_width), 0.0
    ).astype(jnp.bfloat16)
    variant_list = [branch_grad[:, :, 0, :]]
    for branch, dilation in enumerate(dilation_rates):
        for row_tap in range(3):
            variant_list.append(
                shift_rows(branch_grad[:, :, branch + 1, :], (row_tap - 1) * dilation, fetch_grads)
            )
    variants = jnp.stack(variant_list, 2)
    stacked = make_kernel_taps(variants, dilation_rates).reshape(pixels, 28, own_width)
    input_grad = lax.psum_scatter(
        jnp.einsum("pto,tco->cp", stacked, all_weights, preferred_element_type=jnp.float32),
        "filt",
        scatter_dimension=0,
        tiled=True,
    ).T
    feature_grad = input_grad.astype(jnp.bfloat16).reshape(height, breadth, own_channels)
    return (head_output, feature_grad)


W = 64
BLOCK = 144
PIXELS = 576
HALF = 288
SENT = 304
CHANNELS = 2048
F32 = jnp.float32
BF16 = jnp.bfloat16

OUT_PAIRS = ((3, 1), (1, 1), (3, 0), (1, 0), (3, 2), (1, 2), (2, 1), (2, 0), (2, 2))
TAPS = (
    [(k, 1, 1) for k in (1, 2, 3)]
    + [(k, i, j) for k, j in OUT_PAIRS for i in (0, 2)]
    + [(k, 1, j) for j in (0, 2) for k in (1, 2, 3)]
)
OUT_AT, LEFT_AT, RIGHT_AT = 4 * W, 22 * W, 25 * W
PARTS = ((0, 1), (2, 3))
PART_SWAPS = ((7, 3, 1), (6, 2, 5, 7, 3))
SWAPS = (1, 3, 7, 5, 2, 6)
GRAD_SWAPS = ((1, 3), (5, 7), (2, 6))


def fits(mesh):
    return mesh.shape["rows"] == 8 and mesh.shape["filt"] == 4


def order_matrix(turned=False):
    to = lax.broadcasted_iota(jnp.int32, (192, 192), 1 if turned else 0)
    source = lax.broadcasted_iota(jnp.int32, (192, 192), 0 if turned else 1)

    def parts(value, width):
        return sum((value >= n * width).astype(jnp.int32) for n in (1, 2, 3))

    block = parts(to, 48)
    within = to - 48 * block
    line = parts(within, 12)
    wanted = line * 48 + block * 12 + within - 12 * line
    return (source == wanted).astype(F32).astype(BF16)


def tap_index(tap):
    k, i, j = tap
    return (k - 1) * 9 + i * 3 + j


def nt(a, b):
    return lax.dot_general(a, b, (((1,), (1,)), ((), ())), preferred_element_type=F32)


def nn(a, b):
    return lax.dot_general(a, b, (((1,), (0,)), ((), ())), preferred_element_type=F32)


def from_blocks(order_t, value, write):
    for g in range(3):
        parts = [value[m * BLOCK + g * 48 : m * BLOCK + g * 48 + 48] for m in range(4)]
        write(g * 192, nn(order_t, jnp.concatenate(parts, 0)).astype(BF16))


def low_lanes(shape):
    return lax.broadcasted_iota(jnp.int32, shape, 1) % 128 < W


def scaled(value):
    most = jnp.maximum(jnp.max(jnp.abs(value), axis=0, keepdims=True), 1e-30)
    power = jnp.floor(jnp.log(most) * 1.4426950408889634)
    return value * jnp.exp2(13.0 - power), power


def unscaled(sent):
    return sent[:HALF, :] * jnp.exp2(sent[HALF : HALF + 1, :] - 13.0)


def outward_slot(row, x):
    other = row ^ x
    apart = jnp.abs(other - row)
    slot = apart - 1 + jnp.where(other < row, 3, 0)
    return jnp.where(apart <= 3, slot, 0)


def fetch_tap(dilated, weights, sem, place):
    return pltpu.make_async_copy(
        dilated.at[tap_index(TAPS[place - 1])], weights.at[pl.ds(place * W, W)], sem
    )


def outward_kernel(features, dilated, point, *refs):
    row = lax.axis_index("rows")
    out, ordered, weights = refs[0:6], refs[6], refs[7]
    raw, sums, packed, feature_sems, weight_sems = refs[8:]
    loads = []
    for g in range(3):
        rows = pl.ds(g * 192, 192)
        loads.append(pltpu.make_async_copy(features.at[rows], raw.at[rows], feature_sems.at[g]))
        loads[-1].start()
    queue = [
        fetch_tap(dilated, weights, weight_sems.at[q], place)
        for q, place in enumerate((*range(4, 28), 1, 2, 3))
    ]
    queue.append(pltpu.make_async_copy(point, weights.at[pl.ds(0, W)], weight_sems.at[27]))

    def start_loads(first, last):
        for fetch in queue[first:last]:
            fetch.start()

    start_loads(0, 4)
    order = order_matrix()
    for g in range(3):
        loads[g].wait()
        start_loads((4, 12, 18)[g], (12, 18, 28)[g])
        moved = nn(order, raw[g * 192 : (g + 1) * 192, :]).astype(BF16)
        for m in range(4):
            at = m * BLOCK + g * 48
            ordered[at : at + 48, :] = moved[m * 48 : (m + 1) * 48]

    def product(pair, pairs, first, last):
        for fetch in queue[2 * pair : 2 * (pair + pairs)]:
            fetch.wait()
        at = OUT_AT + pair * 128
        return nt(ordered[first * BLOCK : last * BLOCK, :], weights[at : at + pairs * 128, :])

    d = product(0, 2, 0, 4)
    sums[2] = d[:, :128]
    sums[0] = d[:, 128:]
    d = product(2, 2, 0, 3)
    sums[2, 3 * BLOCK :, :] = sums[2, 3 * BLOCK :, :] + d[:BLOCK, :128]
    sums[0, BLOCK:, :] = sums[0, BLOCK:, :] + d[:, 128:]
    d = product(4, 2, 1, 4)
    sums[2, :BLOCK, :] = sums[2, :BLOCK, :] + d[2 * BLOCK :, :128]
    sums[0, : 3 * BLOCK, :] = sums[0, : 3 * BLOCK, :] + d[:, 128:]
    low = low_lanes((HALF, 128))

    def pack(k):
        top, bottom = sums[k, :HALF, :], sums[k, HALF:, :]
        halves = (
            jnp.where(low, top, pltpu.roll(bottom, W, 1)),
            jnp.where(low, pltpu.roll(top, W, 1), bottom),
        )
        for way, value in enumerate(halves):
            value, power = scaled(value)
            packed[k + 3 * way, :HALF, :] = value
            packed[k + 3 * way, HALF:, :] = jnp.broadcast_to(power, (SENT - HALF, 128))

    pack(2)
    pack(0)
    d = product(6, 3, 0, 4)
    sums[1] = d[:, :128]
    sums[1, 2 * BLOCK :, :] = sums[1, 2 * BLOCK :, :] + d[: 2 * BLOCK, 128:256]
    sums[1, : 2 * BLOCK, :] = sums[1, : 2 * BLOCK, :] + d[2 * BLOCK :, 256:]
    pack(1)
    for n, x in enumerate(SWAPS):
        out[n][...] = packed[outward_slot(row, x)]
    for fetch in queue[18:]:
        fetch.wait()


def outward_sums(features, dilated, point):
    return pl.pallas_call(
        outward_kernel,
        out_shape=[jax.ShapeDtypeStruct((SENT, 128), F32)] * 6
        + [pltpu.VMEM((PIXELS, CHANNELS), BF16), pltpu.VMEM((28 * W, CHANNELS), BF16)],
        in_specs=[pl.BlockSpec(memory_space=pltpu.HBM)] * 3,
        out_specs=[pl.BlockSpec(memory_space=pltpu.VMEM)] * 8,
        scratch_shapes=[
            pltpu.VMEM((PIXELS, CHANNELS), BF16),
            pltpu.VMEM((3, PIXELS, 128), F32),
            pltpu.VMEM((6, SENT, 128), F32),
            pltpu.SemaphoreType.DMA((3,)),
            pltpu.SemaphoreType.DMA((28,)),
        ],
        compiler_params=pltpu.CompilerParams(vmem_limit_bytes=28 * 2**20),
        name="outward_sums",
    )(features, dilated, point)


def own_kernel(ordered, weights, bias, *outs):
    d = nt(ordered[...], weights[:256, :])
    for part, out in enumerate(outs):
        line = jnp.concatenate([bias[k : k + 1, :] for k in PARTS[part]], 1)
        out[...] = d[:, part * 128 : part * 128 + 128] + line
    low = low_lanes((PIXELS, 128))

    def add(first, value, k):
        part = k // 2
        rows = slice(first * BLOCK, first * BLOCK + value.shape[0])
        mask, value = low[: value.shape[0]], value[:, part * 128 : part * 128 + 128]
        kept = jnp.where(mask, value, 0.0) if k == 2 else jnp.where(mask, 0.0, value)
        outs[part][rows, :] = outs[part][rows, :] + kept

    d = nt(ordered[: 3 * BLOCK, :], weights[LEFT_AT - W : LEFT_AT + 3 * W, :])
    for k in (1, 2, 3):
        add(k, d[: (4 - k) * BLOCK], k)
    d = nt(ordered[BLOCK:, :], weights[RIGHT_AT - W : RIGHT_AT + 3 * W, :])
    for k in (1, 2, 3):
        add(0, d[(k - 1) * BLOCK :], k)


def own_sums(ordered, weights, bias):
    return pl.pallas_call(
        own_kernel,
        out_shape=[jax.ShapeDtypeStruct((PIXELS, 128), F32)] * 2,
        in_specs=[pl.BlockSpec(memory_space=pltpu.VMEM)] * 3,
        out_specs=[pl.BlockSpec(memory_space=pltpu.VMEM)] * 2,
        compiler_params=pltpu.CompilerParams(vmem_limit_bytes=18 * 2**20),
        cost_estimate=pl.CostEstimate(flops=10**6, bytes_accessed=10**4, transcendentals=0),
        name="own_sums",
    )(ordered, weights, bias)


def arrival_slot(row, other):
    return jnp.where((other >= 0) & (other < 8), row ^ other, 0)


def gather_arrivals(recv, arrivals, swaps):
    arrivals[0] = jnp.zeros((HALF, 128), arrivals.dtype)
    for n, x in enumerate(swaps):
        arrivals[x] = unscaled(recv[n][...])


def activation_kernel(part, swaps, own, *refs):
    recv, acts, arrivals = refs[: len(swaps)], refs[-2], refs[-1]
    row = lax.axis_index("rows")
    gather_arrivals(recv, arrivals, swaps)
    low = low_lanes((HALF, 128))

    def total(k):
        return arrivals[arrival_slot(row, row - k)] + arrivals[arrival_slot(row, row + k)]

    high = total(PARTS[part][1])
    top, bottom = jnp.where(low, 0.0, pltpu.roll(high, W, 1)), jnp.where(low, 0.0, high)
    if part:
        left = total(PARTS[part][0])
        top = jnp.where(low, left, top)
        bottom = jnp.where(low, pltpu.roll(left, W, 1), bottom)
    acts[:HALF, :] = jnp.maximum(own[:HALF, :] + top, 0.0).astype(BF16)
    acts[HALF:, :] = jnp.maximum(own[HALF:, :] + bottom, 0.0).astype(BF16)


def activations_of(part, swaps, own, received):
    return pl.pallas_call(
        functools.partial(activation_kernel, part, swaps),
        out_shape=jax.ShapeDtypeStruct((PIXELS, 128), BF16),
        in_specs=[pl.BlockSpec(memory_space=pltpu.VMEM)] * (1 + len(swaps)),
        out_specs=pl.BlockSpec(memory_space=pltpu.VMEM),
        scratch_shapes=[pltpu.VMEM((8, HALF, 128), F32)],
        compiler_params=pltpu.CompilerParams(vmem_limit_bytes=8 * 2**20),
        name="activations",
    )(own, *received)


def project_rows(project, who):
    at = pl.multiple_of(who * W, W)
    return jnp.concatenate([project[k, pl.ds(at, W), :] for part in PARTS for k in part], 0)


def both(a, b):
    return jnp.concatenate([a[...], b[...]], 1)


def near_head_kernel(a0, b0, a1, b1, project, bias, cotangent, pre, ordered):
    member = lax.axis_index("filt")
    pre[...] = nn(both(a0, b0), project_rows(project, member)) + bias[...]
    pre[...] = pre[...] + nn(both(a1, b1), project_rows(project, member ^ 1))
    order = order_matrix()
    for g in range(3):
        moved = nn(order, cotangent[g * 192 : (g + 1) * 192, :])
        for m in range(4):
            at = m * BLOCK + g * 48
            ordered[at : at + 48, :] = moved[m * 48 : (m + 1) * 48]


def near_head(own, beside, project, bias, cotangent):
    return pl.pallas_call(
        near_head_kernel,
        out_shape=[jax.ShapeDtypeStruct((PIXELS, 256), F32)] * 2,
        in_specs=[pl.BlockSpec(memory_space=pltpu.VMEM)] * 7,
        out_specs=[pl.BlockSpec(memory_space=pltpu.VMEM)] * 2,
        compiler_params=pltpu.CompilerParams(vmem_limit_bytes=10 * 2**20),
        name="near_head",
    )(*own, *beside, project, bias, cotangent)


def far_head_kernel(a0, b0, a1, b1, a2, b2, a3, b3, project, near, cotangent, *refs):
    output, grads, sends, packed = refs[0], refs[1], refs[2:5], refs[5]
    row, member = lax.axis_index("rows"), lax.axis_index("filt")
    pre = near[...] + nn(both(a2, b2), project_rows(project, member ^ 2))
    pre = pre + nn(both(a3, b3), project_rows(project, member ^ 3))
    output[...] = jnp.maximum(pre, 0.0).astype(BF16)
    head_grad = jnp.where(pre > 0, cotangent[...], 0.0).astype(BF16)
    low = low_lanes((HALF, 128))
    for who, (acts_a, acts_b) in enumerate(((a0, b0), (a1, b1))):
        act_grad = nt(head_grad, project_rows(project, member ^ who))
        a = jnp.where(acts_a[...].astype(F32) > 0, act_grad[:, :128], 0.0)
        b = jnp.where(acts_b[...].astype(F32) > 0, act_grad[:, 128:], 0.0)
        if who == 0:
            grads[:, :128] = a.astype(BF16)
            grads[:, 128:] = b.astype(BF16)
        packed[0, who] = jnp.where(low, pltpu.roll(a[:HALF], W, 1), a[HALF:]).astype(BF16)
        packed[1, who] = jnp.where(low, b[:HALF], pltpu.roll(b[HALF:], W, 1)).astype(BF16)
        packed[2, who] = jnp.where(low, pltpu.roll(b[:HALF], W, 1), b[HALF:]).astype(BF16)
    for n, swaps in enumerate(GRAD_SWAPS):
        apart = jnp.abs((row ^ jnp.where((member & 1) == 0, *swaps)) - row)
        sends[n][...] = packed[jnp.where(apart <= 3, apart - 1, 0)]


def far_head(own, beside, across, corner, project, near, cotangent):
    return pl.pallas_call(
        far_head_kernel,
        out_shape=[jax.ShapeDtypeStruct((PIXELS, 256), BF16)] * 2
        + [jax.ShapeDtypeStruct((2, HALF, 128), BF16)] * 3,
        in_specs=[pl.BlockSpec(memory_space=pltpu.VMEM)] * 11,
        out_specs=[pl.BlockSpec(memory_space=pltpu.VMEM)] * 5,
        scratch_shapes=[pltpu.VMEM((3, 2, HALF, 128), BF16)],
        compiler_params=pltpu.CompilerParams(vmem_limit_bytes=12 * 2**20),
        name="far_head",
    )(*own, *beside, *across, *corner, project, near, cotangent)


def own_output_kernel(output, out):
    member = lax.axis_index("filt")
    mine = jnp.zeros((PIXELS, W), F32)
    for q in range(4):
        mine = jnp.where(member == q, output[:, q * W : (q + 1) * W].astype(F32), mine)

    def put(at, value):
        out[at : at + 192, :] = value

    from_blocks(order_matrix(True), mine.astype(BF16), put)


def own_output(output):
    return pl.pallas_call(
        own_output_kernel,
        out_shape=jax.ShapeDtypeStruct((PIXELS, W), BF16),
        in_specs=[pl.BlockSpec(memory_space=pltpu.VMEM)],
        out_specs=pl.BlockSpec(memory_space=pltpu.VMEM),
        compiler_params=pltpu.CompilerParams(vmem_limit_bytes=6 * 2**20),
        name="own_output",
    )(output)


def spread_kernel(own, *refs):
    recv, handed, stack, arrivals, pairs, twice = refs[:3], refs[3:6], *refs[6:]
    row, member = lax.axis_index("rows"), lax.axis_index("filt")
    arrivals[0] = jnp.zeros((HALF, 128), BF16)
    for n, (even, odd) in enumerate(GRAD_SWAPS):
        first = (member & 1) == 0
        arrivals[jnp.where(first, even, odd)] = recv[n][0]
        arrivals[jnp.where(first, odd, even)] = handed[n][1]
    low = low_lanes((HALF, 128))
    low_all = low_lanes((PIXELS, 128))
    for k in (1, 2, 3):
        p = arrivals[arrival_slot(row, row + k)].astype(F32)
        m = arrivals[arrival_slot(row, row - k)].astype(F32)
        pairs[k - 1, :HALF, :] = jnp.where(low, p, pltpu.roll(m, W, 1)).astype(BF16)
        pairs[k - 1, HALF:, :] = jnp.where(low, pltpu.roll(p, W, 1), m).astype(BF16)
        g = own[:, :128].astype(F32) if k == 1 else own[:, 128:].astype(F32)
        other = pltpu.roll(g, W, 1)
        two = jnp.where(low_all, g, other) if k == 2 else jnp.where(low_all, other, g)
        twice[k - 1] = two.astype(BF16)
    stack[:, : 4 * W] = own[...]
    nothing = jnp.zeros((BLOCK, 128), BF16)

    def block_of(ref, k, source):
        if 0 <= source < 4:
            return ref[k - 1, source * BLOCK : (source + 1) * BLOCK, :]
        return nothing

    for q, (k, j) in enumerate(OUT_PAIRS):
        lanes = slice(OUT_AT + q * 128, OUT_AT + q * 128 + 128)
        for m in range(4):
            stack[m * BLOCK : (m + 1) * BLOCK, lanes] = block_of(pairs, k, m - (j - 1) * k)
    low_block = low_lanes((BLOCK, 128))
    for q, (a, b) in enumerate(((1, 2), (3, -1), (-2, -3))):
        lanes = slice(LEFT_AT + q * 128, LEFT_AT + q * 128 + 128)
        for m in range(4):
            stack[m * BLOCK : (m + 1) * BLOCK, lanes] = jnp.where(
                low_block, block_of(twice, abs(a), m + a), block_of(twice, abs(b), m + b)
            )


def spread(own, received, handed):
    return pl.pallas_call(
        spread_kernel,
        out_shape=pltpu.VMEM((PIXELS, 28 * W), BF16),
        in_specs=[pl.BlockSpec(memory_space=pltpu.VMEM)] * 7,
        out_specs=pl.BlockSpec(memory_space=pltpu.VMEM),
        scratch_shapes=[
            pltpu.VMEM((8, HALF, 128), BF16),
            pltpu.VMEM((3, PIXELS, 128), BF16),
            pltpu.VMEM((3, PIXELS, 128), BF16),
        ],
        compiler_params=pltpu.CompilerParams(vmem_limit_bytes=12 * 2**20),
        name="spread",
    )(own, *received, *handed)


def grad_kernel(flips, stack, weights, *outs):
    member = lax.axis_index("filt")
    for out, flip in zip(outs, flips):
        columns = pl.ds(pl.multiple_of((member ^ flip) * 512, 512), 512)
        out[...] = nn(stack[...], weights[:, columns]).astype(BF16)


def grads_for(flips, stack, weights, scale=1):
    return pl.pallas_call(
        functools.partial(grad_kernel, flips),
        out_shape=[jax.ShapeDtypeStruct((PIXELS, 512), BF16)] * len(flips),
        in_specs=[pl.BlockSpec(memory_space=pltpu.VMEM)] * 2,
        out_specs=[pl.BlockSpec(memory_space=pltpu.VMEM)] * len(flips),
        compiler_params=pltpu.CompilerParams(vmem_limit_bytes=18 * 2**20),
        cost_estimate=pl.CostEstimate(
            flops=2 * PIXELS * 28 * W * 512 * scale, bytes_accessed=10**6, transcendentals=0
        ),
        name="grads_for",
    )(stack, weights)


def last_kernel(a, b, c, out):
    total = a[...].astype(F32) + b[...].astype(F32) + c[...].astype(F32)

    def put(at, value):
        out[at : at + 192, :] = value

    from_blocks(order_matrix(True), total.astype(BF16), put)


def last_sum(a, b, c):
    return pl.pallas_call(
        last_kernel,
        out_shape=jax.ShapeDtypeStruct((PIXELS, 512), BF16),
        in_specs=[pl.BlockSpec(memory_space=pltpu.VMEM)] * 3,
        out_specs=pl.BlockSpec(memory_space=pltpu.VMEM),
        compiler_params=pltpu.CompilerParams(vmem_limit_bytes=10 * 2**20),
        name="last_sum",
    )(a, b, c)


def flipped(x, bit):
    return lax.ppermute(x, "filt", [(i, i ^ bit) for i in range(lax.axis_size("filt"))])


def partner(r, bits):
    return r ^ bits if abs((r ^ bits) - r) <= 3 else r ^ {5: 2, 6: 1, 7: 1}[bits]


def swapped(x, bits):
    return lax.ppermute(x, "rows", [(r, partner(r, bits)) for r in range(8)])


def swapped_by_core(x, bits):
    pairs = [
        (4 * r + member, 4 * partner(r, bits[member % 2]) + member)
        for r in range(8)
        for member in range(4)
    ]
    return lax.ppermute(x, ("rows", "filt"), pairs)


def on_device(
    features, point_weight, dilated_weight, branch_bias, project_weight, project_bias, cotangent
):
    flat = features.reshape(PIXELS, CHANNELS)
    dilated = jnp.transpose(dilated_weight, (0, 1, 2, 4, 3)).reshape(27, W, CHANNELS)
    point = point_weight.T
    flat, dilated, point = (
        pltpu.with_memory_space_constraint(x, pltpu.HBM) for x in (flat, dilated, point)
    )
    *sums, ordered, weights = outward_sums(flat, dilated, point)
    received = {
        x: swapped(sums[n].astype(jnp.float16), x).astype(F32) for n, x in enumerate(SWAPS)
    }
    own = own_sums(ordered, weights, branch_bias)
    acts = [
        activations_of(part, swaps, own[part], [received[x] for x in swaps])
        for part, swaps in enumerate(PART_SWAPS)
    ]
    across = [flipped(x, 2) for x in acts]
    beside = [flipped(x, 1) for x in acts]
    corner = [flipped(x, 1) for x in across]
    near, ordered_cotangent = near_head(
        acts,
        beside,
        project_weight,
        project_bias.reshape(1, 256),
        cotangent.reshape(PIXELS, 256),
    )
    output, grads, *sends = far_head(
        acts, beside, across, corner, project_weight, near, ordered_cotangent
    )
    arrived = [swapped_by_core(sends[n], swaps) for n, swaps in enumerate(GRAD_SWAPS)]
    handed = [flipped(x, 1) for x in arrived]
    stack = spread(grads, arrived, handed)
    (far,) = grads_for((3,), stack, weights)
    far = flipped(far, 1)
    (kept,) = grads_for((2,), stack, weights)
    crossing = (far.astype(F32) + kept.astype(F32)).astype(BF16)
    crossed = flipped(crossing, 2)
    later, output, crossing = lax.optimization_barrier((stack, output, crossing))
    head_output = own_output(output)
    (near,) = grads_for((1,), later, weights)
    near = flipped(near, 1)
    (kept,) = grads_for((0,), later, weights, 8)
    feature_grad = last_sum(kept, near, crossed)
    return head_output.reshape(12, 48, W), feature_grad.reshape(12, 48, 512)


def solution(mesh):
    body = on_device if fits(mesh) else on_device_general
    in_specs = (
        P("rows", None, None),
        P(None, "filt"),
        P(None, None, None, None, "filt"),
        P(None, "filt"),
        P(),
        P(),
        P("rows", None, None),
    )
    out_specs = (P("rows", None, "filt"), P("rows", None, "filt"))
    return jax.shard_map(
        body, mesh=mesh, in_specs=in_specs, out_specs=out_specs, check_vma=False
    )
```

```python
import functools

import jax
import jax.numpy as jnp
from jax import lax
from jax.experimental import pallas as pl
from jax.experimental.pallas import tpu as pltpu
from jax.sharding import PartitionSpec as P

FIRST_DILATION = 12
SECOND_DILATION = 24
THIRD_DILATION = 36


def passed_along(x, axis, by):
    devices = lax.axis_size(axis)
    pairs = [(i, i + by) for i in range(devices) if 0 <= i + by < devices]
    return lax.ppermute(x, axis, pairs)


def shift_columns(field, amount):
    breadth = field.shape[1]
    if amount == 0:
        return field
    padding = [(0, 0)] * field.ndim
    if amount > 0:
        kept = field[:, amount:]
        padding[1] = (0, amount)
    else:
        kept = field[:, : breadth + amount]
        padding[1] = (-amount, 0)
    return jnp.pad(kept, padding)


def fetch_sums(field, offset):
    return passed_along(field, "rows", offset)


def fetch_grads(field, offset):
    return passed_along(field, "rows", offset)


def shift_rows(field, amount, fetcher):
    height = field.shape[0]
    quotient = amount // height

    def extract_block(offset):
        if offset == 0:
            return field
        return fetcher(field, offset)

    return extract_block(quotient)


def make_kernel_taps(variants, dilation_rates):
    stacked = [variants[:, :, 0]]
    for branch, dilation in enumerate(dilation_rates):
        for row_tap in range(3):
            source = variants[:, :, 1 + 3 * branch + row_tap]
            for col_tap in range(3):
                stacked.append(shift_columns(source, -(col_tap - 1) * dilation))
    return jnp.stack(stacked, 2)


def on_device_general(
    features, point_weight, dilated_weight, branch_bias, project_weight, project_bias, cotangent
):
    height, breadth, channels = features.shape
    pixels = height * breadth
    own_width = point_weight.shape[1]
    filters = lax.axis_size("filt")
    member = lax.axis_index("filt")
    branch_outputs = project_weight.shape[2]
    own_out = branch_outputs // filters
    own_channels = channels // filters
    dilation_rates = (FIRST_DILATION, SECOND_DILATION, THIRD_DILATION)
    all_weights = jnp.concatenate(
        [point_weight[None], dilated_weight.reshape(27, channels, own_width)], 0
    )
    flattened = features.reshape(pixels, channels)
    tap_terms = jnp.einsum(
        "pc,tco->pto", flattened, all_weights, preferred_element_type=jnp.float32
    )
    tap_terms = tap_terms.reshape(height, breadth, 28, own_width)
    pre_list = [tap_terms[:, :, 0, :] + branch_bias[0]]
    for branch, dilation in enumerate(dilation_rates):
        summed_result = jnp.zeros((height, breadth, own_width), jnp.float32)
        for row_tap in range(3):
            row_sum = jnp.zeros((height, breadth, own_width), jnp.float32)
            for col_tap in range(3):
                row_sum = row_sum + shift_columns(
                    tap_terms[:, :, 1 + 9 * branch + 3 * row_tap + col_tap, :],
                    (col_tap - 1) * dilation,
                )
            summed_result = summed_result + shift_rows(
                row_sum, -(row_tap - 1) * dilation, fetch_sums
            )
        pre_list.append(summed_result + branch_bias[branch + 1])
    branch_pre = jnp.stack(pre_list, 2)
    activations = jnp.maximum(branch_pre, 0.0).astype(jnp.bfloat16).reshape(pixels, 4 * own_width)
    grouped = project_weight.reshape(4, filters, own_width, branch_outputs)
    own_rows = lax.dynamic_index_in_dim(grouped, member, 1, keepdims=False).reshape(
        4 * own_width, branch_outputs
    )
    flat_cotangent = cotangent.reshape(pixels, branch_outputs)
    ordered = jnp.transpose(grouped, (1, 0, 2, 3)).reshape(filters * 4 * own_width, branch_outputs)
    project_pre = jnp.dot(
        lax.all_gather(activations, "filt", axis=1, tiled=True),
        ordered,
        preferred_element_type=jnp.float32,
    )
    project_pre = project_pre + project_bias
    head_grad = jnp.where(project_pre > 0, flat_cotangent.astype(jnp.float32), 0.0).astype(
        jnp.bfloat16
    )
    own_pre = lax.dynamic_slice_in_dim(project_pre, member * own_out, own_out, 1)
    act_grad = jnp.dot(head_grad, own_rows.T, preferred_element_type=jnp.float32)
    head_output = jnp.maximum(own_pre, 0.0).astype(jnp.bfloat16).reshape(height, breadth, own_out)
    branch_grad = jnp.where(
        branch_pre > 0, act_grad.reshape(height, breadth, 4, own_width), 0.0
    ).astype(jnp.bfloat16)
    variant_list = [branch_grad[:, :, 0, :]]
    for branch, dilation in enumerate(dilation_rates):
        for row_tap in range(3):
            variant_list.append(
                shift_rows(branch_grad[:, :, branch + 1, :], (row_tap - 1) * dilation, fetch_grads)
            )
    variants = jnp.stack(variant_list, 2)
    stacked = make_kernel_taps(variants, dilation_rates).reshape(pixels, 28, own_width)
    input_grad = lax.psum_scatter(
        jnp.einsum("pto,tco->cp", stacked, all_weights, preferred_element_type=jnp.float32),
        "filt",
        scatter_dimension=0,
        tiled=True,
    ).T
    feature_grad = input_grad.astype(jnp.bfloat16).reshape(height, breadth, own_channels)
    return (head_output, feature_grad)


W = 64
BLOCK = 144
PIXELS = 576
HALF = 288
SENT = 304
CHANNELS = 2048
F32 = jnp.float32
BF16 = jnp.bfloat16

OUT_PAIRS = ((3, 1), (1, 1), (3, 0), (1, 0), (3, 2), (1, 2), (2, 1), (2, 0), (2, 2))
TAPS = (
    [(k, 1, 1) for k in (1, 2, 3)]
    + [(k, i, j) for k, j in OUT_PAIRS for i in (0, 2)]
    + [(k, 1, j) for j in (0, 2) for k in (1, 2, 3)]
)
OUT_AT, LEFT_AT, RIGHT_AT = 4 * W, 22 * W, 25 * W
PARTS = ((0, 1), (2, 3))
PART_SWAPS = ((7, 3, 1), (6, 2, 5, 7, 3))
SWAPS = (1, 3, 7, 5, 2, 6)
GRAD_SWAPS = ((1, 3), (5, 7), (2, 6))


def fits(mesh):
    return mesh.shape["rows"] == 8 and mesh.shape["filt"] == 4


def order_matrix(turned=False):
    to = lax.broadcasted_iota(jnp.int32, (192, 192), 1 if turned else 0)
    source = lax.broadcasted_iota(jnp.int32, (192, 192), 0 if turned else 1)

    def parts(value, width):
        return sum((value >= n * width).astype(jnp.int32) for n in (1, 2, 3))

    block = parts(to, 48)
    within = to - 48 * block
    line = parts(within, 12)
    wanted = line * 48 + block * 12 + within - 12 * line
    return (source == wanted).astype(F32).astype(BF16)


def tap_index(tap):
    k, i, j = tap
    return (k - 1) * 9 + i * 3 + j


def nt(a, b):
    return lax.dot_general(a, b, (((1,), (1,)), ((), ())), preferred_element_type=F32)


def nn(a, b):
    return lax.dot_general(a, b, (((1,), (0,)), ((), ())), preferred_element_type=F32)


def from_blocks(order_t, value, write):
    for g in range(3):
        parts = [value[m * BLOCK + g * 48 : m * BLOCK + g * 48 + 48] for m in range(4)]
        write(g * 192, nn(order_t, jnp.concatenate(parts, 0)).astype(BF16))


def low_lanes(shape):
    return lax.broadcasted_iota(jnp.int32, shape, 1) % 128 < W


def scaled(value):
    most = jnp.maximum(jnp.max(jnp.abs(value), axis=0, keepdims=True), 1e-30)
    power = jnp.floor(jnp.log(most) * 1.4426950408889634)
    return value * jnp.exp2(13.0 - power), power


def unscaled(sent):
    return sent[:HALF, :] * jnp.exp2(sent[HALF : HALF + 1, :] - 13.0)


def outward_slot(row, x):
    other = row ^ x
    apart = jnp.abs(other - row)
    slot = apart - 1 + jnp.where(other < row, 3, 0)
    return jnp.where(apart <= 3, slot, 0)


def fetch_tap(dilated, weights, sem, place):
    return pltpu.make_async_copy(
        dilated.at[tap_index(TAPS[place - 1])], weights.at[pl.ds(place * W, W)], sem
    )


def outward_kernel(features, dilated, point, *refs):
    row = lax.axis_index("rows")
    out, ordered, weights = refs[0:6], refs[6], refs[7]
    raw, sums, packed, feature_sems, weight_sems = refs[8:]
    loads = []
    for g in range(3):
        rows = pl.ds(g * 192, 192)
        loads.append(pltpu.make_async_copy(features.at[rows], raw.at[rows], feature_sems.at[g]))
        loads[-1].start()
    queue = [
        fetch_tap(dilated, weights, weight_sems.at[q], place)
        for q, place in enumerate((*range(4, 28), 1, 2, 3))
    ]
    queue.append(pltpu.make_async_copy(point, weights.at[pl.ds(0, W)], weight_sems.at[27]))

    def start_loads(first, last):
        for fetch in queue[first:last]:
            fetch.start()

    start_loads(0, 4)
    order = order_matrix()
    for g in range(3):
        loads[g].wait()
        start_loads((4, 12, 18)[g], (12, 18, 28)[g])
        moved = nn(order, raw[g * 192 : (g + 1) * 192, :]).astype(BF16)
        for m in range(4):
            at = m * BLOCK + g * 48
            ordered[at : at + 48, :] = moved[m * 48 : (m + 1) * 48]

    def product(pair, pairs, first, last):
        for fetch in queue[2 * pair : 2 * (pair + pairs)]:
            fetch.wait()
        at = OUT_AT + pair * 128
        return nt(ordered[first * BLOCK : last * BLOCK, :], weights[at : at + pairs * 128, :])

    d = product(0, 2, 0, 4)
    sums[2] = d[:, :128]
    sums[0] = d[:, 128:]
    d = product(2, 2, 0, 3)
    sums[2, 3 * BLOCK :, :] = sums[2, 3 * BLOCK :, :] + d[:BLOCK, :128]
    sums[0, BLOCK:, :] = sums[0, BLOCK:, :] + d[:, 128:]
    d = product(4, 2, 1, 4)
    sums[2, :BLOCK, :] = sums[2, :BLOCK, :] + d[2 * BLOCK :, :128]
    sums[0, : 3 * BLOCK, :] = sums[0, : 3 * BLOCK, :] + d[:, 128:]
    low = low_lanes((HALF, 128))

    def pack(k):
        top, bottom = sums[k, :HALF, :], sums[k, HALF:, :]
        halves = (
            jnp.where(low, top, pltpu.roll(bottom, W, 1)),
            jnp.where(low, pltpu.roll(top, W, 1), bottom),
        )
        for way, value in enumerate(halves):
            value, power = scaled(value)
            packed[k + 3 * way, :HALF, :] = value
            packed[k + 3 * way, HALF:, :] = jnp.broadcast_to(power, (SENT - HALF, 128))

    pack(2)
    pack(0)
    d = product(6, 3, 0, 4)
    sums[1] = d[:, :128]
    sums[1, 2 * BLOCK :, :] = sums[1, 2 * BLOCK :, :] + d[: 2 * BLOCK, 128:256]
    sums[1, : 2 * BLOCK, :] = sums[1, : 2 * BLOCK, :] + d[2 * BLOCK :, 256:]
    pack(1)
    for n, x in enumerate(SWAPS):
        out[n][...] = packed[outward_slot(row, x)]
    for fetch in queue[18:]:
        fetch.wait()


def outward_sums(features, dilated, point):
    return pl.pallas_call(
        outward_kernel,
        out_shape=[jax.ShapeDtypeStruct((SENT, 128), F32)] * 6
        + [pltpu.VMEM((PIXELS, CHANNELS), BF16), pltpu.VMEM((28 * W, CHANNELS), BF16)],
        in_specs=[pl.BlockSpec(memory_space=pltpu.HBM)] * 3,
        out_specs=[pl.BlockSpec(memory_space=pltpu.VMEM)] * 8,
        scratch_shapes=[
            pltpu.VMEM((PIXELS, CHANNELS), BF16),
            pltpu.VMEM((3, PIXELS, 128), F32),
            pltpu.VMEM((6, SENT, 128), F32),
            pltpu.SemaphoreType.DMA((3,)),
            pltpu.SemaphoreType.DMA((28,)),
        ],
        compiler_params=pltpu.CompilerParams(vmem_limit_bytes=28 * 2**20),
        name="outward_sums",
    )(features, dilated, point)


def own_kernel(ordered, weights, bias, *outs):
    d = nt(ordered[...], weights[:256, :])
    for part, out in enumerate(outs):
        line = jnp.concatenate([bias[k : k + 1, :] for k in PARTS[part]], 1)
        out[...] = d[:, part * 128 : part * 128 + 128] + line
    low = low_lanes((PIXELS, 128))

    def add(first, value, k):
        part = k // 2
        rows = slice(first * BLOCK, first * BLOCK + value.shape[0])
        mask, value = low[: value.shape[0]], value[:, part * 128 : part * 128 + 128]
        kept = jnp.where(mask, value, 0.0) if k == 2 else jnp.where(mask, 0.0, value)
        outs[part][rows, :] = outs[part][rows, :] + kept

    d = nt(ordered[: 3 * BLOCK, :], weights[LEFT_AT - W : LEFT_AT + 3 * W, :])
    for k in (1, 2, 3):
        add(k, d[: (4 - k) * BLOCK], k)
    d = nt(ordered[BLOCK:, :], weights[RIGHT_AT - W : RIGHT_AT + 3 * W, :])
    for k in (1, 2, 3):
        add(0, d[(k - 1) * BLOCK :], k)


def own_sums(ordered, weights, bias):
    return pl.pallas_call(
        own_kernel,
        out_shape=[jax.ShapeDtypeStruct((PIXELS, 128), F32)] * 2,
        in_specs=[pl.BlockSpec(memory_space=pltpu.VMEM)] * 3,
        out_specs=[pl.BlockSpec(memory_space=pltpu.VMEM)] * 2,
        compiler_params=pltpu.CompilerParams(vmem_limit_bytes=18 * 2**20),
        cost_estimate=pl.CostEstimate(flops=10**6, bytes_accessed=10**4, transcendentals=0),
        name="own_sums",
    )(ordered, weights, bias)


def arrival_slot(row, other):
    return jnp.where((other >= 0) & (other < 8), row ^ other, 0)


def gather_arrivals(recv, arrivals, swaps):
    arrivals[0] = jnp.zeros((HALF, 128), arrivals.dtype)
    for n, x in enumerate(swaps):
        arrivals[x] = unscaled(recv[n][...])


def activation_kernel(part, swaps, own, *refs):
    recv, acts, arrivals = refs[: len(swaps)], refs[-2], refs[-1]
    row = lax.axis_index("rows")
    gather_arrivals(recv, arrivals, swaps)
    low = low_lanes((HALF, 128))

    def total(k):
        return arrivals[arrival_slot(row, row - k)] + arrivals[arrival_slot(row, row + k)]

    high = total(PARTS[part][1])
    top, bottom = jnp.where(low, 0.0, pltpu.roll(high, W, 1)), jnp.where(low, 0.0, high)
    if part:
        left = total(PARTS[part][0])
        top = jnp.where(low, left, top)
        bottom = jnp.where(low, pltpu.roll(left, W, 1), bottom)
    acts[:HALF, :] = jnp.maximum(own[:HALF, :] + top, 0.0).astype(BF16)
    acts[HALF:, :] = jnp.maximum(own[HALF:, :] + bottom, 0.0).astype(BF16)


def activations_of(part, swaps, own, received):
    return pl.pallas_call(
        functools.partial(activation_kernel, part, swaps),
        out_shape=jax.ShapeDtypeStruct((PIXELS, 128), BF16),
        in_specs=[pl.BlockSpec(memory_space=pltpu.VMEM)] * (1 + len(swaps)),
        out_specs=pl.BlockSpec(memory_space=pltpu.VMEM),
        scratch_shapes=[pltpu.VMEM((8, HALF, 128), F32)],
        compiler_params=pltpu.CompilerParams(vmem_limit_bytes=8 * 2**20),
        name="activations",
    )(own, *received)


def project_rows(project, who):
    at = pl.multiple_of(who * W, W)
    return jnp.concatenate([project[k, pl.ds(at, W), :] for part in PARTS for k in part], 0)


def both(a, b):
    return jnp.concatenate([a[...], b[...]], 1)


def near_head_kernel(a0, b0, a1, b1, project, bias, cotangent, pre, ordered):
    member = lax.axis_index("filt")
    pre[...] = nn(both(a0, b0), project_rows(project, member)) + bias[...]
    pre[...] = pre[...] + nn(both(a1, b1), project_rows(project, member ^ 1))
    order = order_matrix()
    for g in range(3):
        moved = nn(order, cotangent[g * 192 : (g + 1) * 192, :])
        for m in range(4):
            at = m * BLOCK + g * 48
            ordered[at : at + 48, :] = moved[m * 48 : (m + 1) * 48]


def near_head(own, beside, project, bias, cotangent):
    return pl.pallas_call(
        near_head_kernel,
        out_shape=[jax.ShapeDtypeStruct((PIXELS, 256), F32)] * 2,
        in_specs=[pl.BlockSpec(memory_space=pltpu.VMEM)] * 7,
        out_specs=[pl.BlockSpec(memory_space=pltpu.VMEM)] * 2,
        compiler_params=pltpu.CompilerParams(vmem_limit_bytes=10 * 2**20),
        name="near_head",
    )(*own, *beside, project, bias, cotangent)


def far_head_kernel(a0, b0, a1, b1, a2, b2, a3, b3, project, near, cotangent, *refs):
    output, grads, sends, packed = refs[0], refs[1], refs[2:5], refs[5]
    row, member = lax.axis_index("rows"), lax.axis_index("filt")
    pre = near[...] + nn(both(a2, b2), project_rows(project, member ^ 2))
    pre = pre + nn(both(a3, b3), project_rows(project, member ^ 3))
    output[...] = jnp.maximum(pre, 0.0).astype(BF16)
    head_grad = jnp.where(pre > 0, cotangent[...], 0.0).astype(BF16)
    low = low_lanes((HALF, 128))
    for who, (acts_a, acts_b) in enumerate(((a0, b0), (a1, b1))):
        act_grad = nt(head_grad, project_rows(project, member ^ who))
        a = jnp.where(acts_a[...].astype(F32) > 0, act_grad[:, :128], 0.0)
        b = jnp.where(acts_b[...].astype(F32) > 0, act_grad[:, 128:], 0.0)
        if who == 0:
            grads[:, :128] = a.astype(BF16)
            grads[:, 128:] = b.astype(BF16)
        packed[0, who] = jnp.where(low, pltpu.roll(a[:HALF], W, 1), a[HALF:]).astype(BF16)
        packed[1, who] = jnp.where(low, b[:HALF], pltpu.roll(b[HALF:], W, 1)).astype(BF16)
        packed[2, who] = jnp.where(low, pltpu.roll(b[:HALF], W, 1), b[HALF:]).astype(BF16)
    for n, swaps in enumerate(GRAD_SWAPS):
        apart = jnp.abs((row ^ jnp.where((member & 1) == 0, *swaps)) - row)
        sends[n][...] = packed[jnp.where(apart <= 3, apart - 1, 0)]


def far_head(own, beside, across, corner, project, near, cotangent):
    return pl.pallas_call(
        far_head_kernel,
        out_shape=[jax.ShapeDtypeStruct((PIXELS, 256), BF16)] * 2
        + [jax.ShapeDtypeStruct((2, HALF, 128), BF16)] * 3,
        in_specs=[pl.BlockSpec(memory_space=pltpu.VMEM)] * 11,
        out_specs=[pl.BlockSpec(memory_space=pltpu.VMEM)] * 5,
        scratch_shapes=[pltpu.VMEM((3, 2, HALF, 128), BF16)],
        compiler_params=pltpu.CompilerParams(vmem_limit_bytes=12 * 2**20),
        name="far_head",
    )(*own, *beside, *across, *corner, project, near, cotangent)


def own_output_kernel(output, out):
    member = lax.axis_index("filt")
    mine = jnp.zeros((PIXELS, W), F32)
    for q in range(4):
        mine = jnp.where(member == q, output[:, q * W : (q + 1) * W].astype(F32), mine)

    def put(at, value):
        out[at : at + 192, :] = value

    from_blocks(order_matrix(True), mine.astype(BF16), put)


def own_output(output):
    return pl.pallas_call(
        own_output_kernel,
        out_shape=jax.ShapeDtypeStruct((PIXELS, W), BF16),
        in_specs=[pl.BlockSpec(memory_space=pltpu.VMEM)],
        out_specs=pl.BlockSpec(memory_space=pltpu.VMEM),
        compiler_params=pltpu.CompilerParams(vmem_limit_bytes=6 * 2**20),
        name="own_output",
    )(output)


def spread_kernel(own, *refs):
    recv, handed, stack, arrivals, pairs, twice = refs[:3], refs[3:6], *refs[6:]
    row, member = lax.axis_index("rows"), lax.axis_index("filt")
    arrivals[0] = jnp.zeros((HALF, 128), BF16)
    for n, (even, odd) in enumerate(GRAD_SWAPS):
        first = (member & 1) == 0
        arrivals[jnp.where(first, even, odd)] = recv[n][0]
        arrivals[jnp.where(first, odd, even)] = handed[n][1]
    low = low_lanes((HALF, 128))
    low_all = low_lanes((PIXELS, 128))
    for k in (1, 2, 3):
        p = arrivals[arrival_slot(row, row + k)].astype(F32)
        m = arrivals[arrival_slot(row, row - k)].astype(F32)
        pairs[k - 1, :HALF, :] = jnp.where(low, p, pltpu.roll(m, W, 1)).astype(BF16)
        pairs[k - 1, HALF:, :] = jnp.where(low, pltpu.roll(p, W, 1), m).astype(BF16)
        g = own[:, :128].astype(F32) if k == 1 else own[:, 128:].astype(F32)
        other = pltpu.roll(g, W, 1)
        two = jnp.where(low_all, g, other) if k == 2 else jnp.where(low_all, other, g)
        twice[k - 1] = two.astype(BF16)
    stack[:, : 4 * W] = own[...]
    nothing = jnp.zeros((BLOCK, 128), BF16)

    def block_of(ref, k, source):
        if 0 <= source < 4:
            return ref[k - 1, source * BLOCK : (source + 1) * BLOCK, :]
        return nothing

    for q, (k, j) in enumerate(OUT_PAIRS):
        lanes = slice(OUT_AT + q * 128, OUT_AT + q * 128 + 128)
        for m in range(4):
            stack[m * BLOCK : (m + 1) * BLOCK, lanes] = block_of(pairs, k, m - (j - 1) * k)
    low_block = low_lanes((BLOCK, 128))
    for q, (a, b) in enumerate(((1, 2), (3, -1), (-2, -3))):
        lanes = slice(LEFT_AT + q * 128, LEFT_AT + q * 128 + 128)
        for m in range(4):
            stack[m * BLOCK : (m + 1) * BLOCK, lanes] = jnp.where(
                low_block, block_of(twice, abs(a), m + a), block_of(twice, abs(b), m + b)
            )


def spread(own, received, handed):
    return pl.pallas_call(
        spread_kernel,
        out_shape=pltpu.VMEM((PIXELS, 28 * W), BF16),
        in_specs=[pl.BlockSpec(memory_space=pltpu.VMEM)] * 7,
        out_specs=pl.BlockSpec(memory_space=pltpu.VMEM),
        scratch_shapes=[
            pltpu.VMEM((8, HALF, 128), BF16),
            pltpu.VMEM((3, PIXELS, 128), BF16),
            pltpu.VMEM((3, PIXELS, 128), BF16),
        ],
        compiler_params=pltpu.CompilerParams(vmem_limit_bytes=12 * 2**20),
        name="spread",
    )(own, *received, *handed)


def grad_kernel(flips, stack, weights, *outs):
    member = lax.axis_index("filt")
    for out, flip in zip(outs, flips):
        columns = pl.ds(pl.multiple_of((member ^ flip) * 512, 512), 512)
        out[...] = nn(stack[...], weights[:, columns]).astype(BF16)


def grads_for(flips, stack, weights, scale=1):
    return pl.pallas_call(
        functools.partial(grad_kernel, flips),
        out_shape=[jax.ShapeDtypeStruct((PIXELS, 512), BF16)] * len(flips),
        in_specs=[pl.BlockSpec(memory_space=pltpu.VMEM)] * 2,
        out_specs=[pl.BlockSpec(memory_space=pltpu.VMEM)] * len(flips),
        compiler_params=pltpu.CompilerParams(vmem_limit_bytes=18 * 2**20),
        cost_estimate=pl.CostEstimate(
            flops=2 * PIXELS * 28 * W * 512 * scale, bytes_accessed=10**6, transcendentals=0
        ),
        name="grads_for",
    )(stack, weights)


def last_kernel(a, b, c, out):
    total = a[...].astype(F32) + b[...].astype(F32) + c[...].astype(F32)

    def put(at, value):
        out[at : at + 192, :] = value

    from_blocks(order_matrix(True), total.astype(BF16), put)


def last_sum(a, b, c):
    return pl.pallas_call(
        last_kernel,
        out_shape=jax.ShapeDtypeStruct((PIXELS, 512), BF16),
        in_specs=[pl.BlockSpec(memory_space=pltpu.VMEM)] * 3,
        out_specs=pl.BlockSpec(memory_space=pltpu.VMEM),
        compiler_params=pltpu.CompilerParams(vmem_limit_bytes=10 * 2**20),
        name="last_sum",
    )(a, b, c)


def flipped(x, bit):
    return lax.ppermute(x, "filt", [(i, i ^ bit) for i in range(lax.axis_size("filt"))])


def partner(r, member, bits):
    if abs((r ^ bits) - r) <= 3:
        return 4 * (r ^ bits) + member
    return 4 * r + (member ^ 2)


def swapped(x, *bits):
    pairs = [
        (4 * r + member, partner(r, member, bits[member % len(bits)]))
        for r in range(8)
        for member in range(4)
    ]
    return lax.ppermute(x, ("rows", "filt"), pairs)


def on_device(
    features, point_weight, dilated_weight, branch_bias, project_weight, project_bias, cotangent
):
    flat = features.reshape(PIXELS, CHANNELS)
    dilated = jnp.transpose(dilated_weight, (0, 1, 2, 4, 3)).reshape(27, W, CHANNELS)
    point = point_weight.T
    flat, dilated, point = (
        pltpu.with_memory_space_constraint(x, pltpu.HBM) for x in (flat, dilated, point)
    )
    *sums, ordered, weights = outward_sums(flat, dilated, point)
    received = {
        x: swapped(sums[n].astype(jnp.float16), x).astype(F32) for n, x in enumerate(SWAPS)
    }
    own = own_sums(ordered, weights, branch_bias)
    acts = [
        activations_of(part, swaps, own[part], [received[x] for x in swaps])
        for part, swaps in enumerate(PART_SWAPS)
    ]
    across = [flipped(x, 2) for x in acts]
    beside = [flipped(x, 1) for x in acts]
    corner = [flipped(x, 1) for x in across]
    near, ordered_cotangent = near_head(
        acts,
        beside,
        project_weight,
        project_bias.reshape(1, 256),
        cotangent.reshape(PIXELS, 256),
    )
    output, grads, *sends = far_head(
        acts, beside, across, corner, project_weight, near, ordered_cotangent
    )
    arrived = [swapped(sends[n], *swaps) for n, swaps in enumerate(GRAD_SWAPS)]
    handed = [flipped(x, 1) for x in arrived]
    stack = spread(grads, arrived, handed)
    (far,) = grads_for((3,), stack, weights)
    far = flipped(far, 1)
    (kept,) = grads_for((2,), stack, weights)
    crossing = (far.astype(F32) + kept.astype(F32)).astype(BF16)
    crossed = flipped(crossing, 2)
    later, output, crossing = lax.optimization_barrier((stack, output, crossing))
    head_output = own_output(output)
    (near,) = grads_for((1,), later, weights)
    near = flipped(near, 1)
    (kept,) = grads_for((0,), later, weights, 8)
    feature_grad = last_sum(kept, near, crossed)
    return head_output.reshape(12, 48, W), feature_grad.reshape(12, 48, 512)


def solution(mesh):
    body = on_device if fits(mesh) else on_device_general
    in_specs = (
        P("rows", None, None),
        P(None, "filt"),
        P(None, None, None, None, "filt"),
        P(None, "filt"),
        P(),
        P(),
        P("rows", None, None),
    )
    out_specs = (P("rows", None, "filt"), P("rows", None, "filt"))
    return jax.shard_map(
        body, mesh=mesh, in_specs=in_specs, out_specs=out_specs, check_vma=False
    )
```

```python
import functools

import jax
import jax.numpy as jnp
from jax import lax
from jax.experimental import pallas as pl
from jax.experimental.pallas import tpu as pltpu
from jax.sharding import PartitionSpec as P

FIRST_DILATION = 12
SECOND_DILATION = 24
THIRD_DILATION = 36


def passed_along(x, axis, by):
    devices = lax.axis_size(axis)
    pairs = [(i, i + by) for i in range(devices) if 0 <= i + by < devices]
    return lax.ppermute(x, axis, pairs)


def shift_columns(field, amount):
    breadth = field.shape[1]
    if amount == 0:
        return field
    padding = [(0, 0)] * field.ndim
    if amount > 0:
        kept = field[:, amount:]
        padding[1] = (0, amount)
    else:
        kept = field[:, : breadth + amount]
        padding[1] = (-amount, 0)
    return jnp.pad(kept, padding)


def fetch_sums(field, offset):
    return passed_along(field, "rows", offset)


def fetch_grads(field, offset):
    return passed_along(field, "rows", offset)


def shift_rows(field, amount, fetcher):
    height = field.shape[0]
    quotient = amount // height

    def extract_block(offset):
        if offset == 0:
            return field
        return fetcher(field, offset)

    return extract_block(quotient)


def make_kernel_taps(variants, dilation_rates):
    stacked = [variants[:, :, 0]]
    for branch, dilation in enumerate(dilation_rates):
        for row_tap in range(3):
            source = variants[:, :, 1 + 3 * branch + row_tap]
            for col_tap in range(3):
                stacked.append(shift_columns(source, -(col_tap - 1) * dilation))
    return jnp.stack(stacked, 2)


def on_device_general(
    features, point_weight, dilated_weight, branch_bias, project_weight, project_bias, cotangent
):
    height, breadth, channels = features.shape
    pixels = height * breadth
    own_width = point_weight.shape[1]
    filters = lax.axis_size("filt")
    member = lax.axis_index("filt")
    branch_outputs = project_weight.shape[2]
    own_out = branch_outputs // filters
    own_channels = channels // filters
    dilation_rates = (FIRST_DILATION, SECOND_DILATION, THIRD_DILATION)
    all_weights = jnp.concatenate(
        [point_weight[None], dilated_weight.reshape(27, channels, own_width)], 0
    )
    flattened = features.reshape(pixels, channels)
    tap_terms = jnp.einsum(
        "pc,tco->pto", flattened, all_weights, preferred_element_type=jnp.float32
    )
    tap_terms = tap_terms.reshape(height, breadth, 28, own_width)
    pre_list = [tap_terms[:, :, 0, :] + branch_bias[0]]
    for branch, dilation in enumerate(dilation_rates):
        summed_result = jnp.zeros((height, breadth, own_width), jnp.float32)
        for row_tap in range(3):
            row_sum = jnp.zeros((height, breadth, own_width), jnp.float32)
            for col_tap in range(3):
                row_sum = row_sum + shift_columns(
                    tap_terms[:, :, 1 + 9 * branch + 3 * row_tap + col_tap, :],
                    (col_tap - 1) * dilation,
                )
            summed_result = summed_result + shift_rows(
                row_sum, -(row_tap - 1) * dilation, fetch_sums
            )
        pre_list.append(summed_result + branch_bias[branch + 1])
    branch_pre = jnp.stack(pre_list, 2)
    activations = jnp.maximum(branch_pre, 0.0).astype(jnp.bfloat16).reshape(pixels, 4 * own_width)
    grouped = project_weight.reshape(4, filters, own_width, branch_outputs)
    own_rows = lax.dynamic_index_in_dim(grouped, member, 1, keepdims=False).reshape(
        4 * own_width, branch_outputs
    )
    flat_cotangent = cotangent.reshape(pixels, branch_outputs)
    ordered = jnp.transpose(grouped, (1, 0, 2, 3)).reshape(filters * 4 * own_width, branch_outputs)
    project_pre = jnp.dot(
        lax.all_gather(activations, "filt", axis=1, tiled=True),
        ordered,
        preferred_element_type=jnp.float32,
    )
    project_pre = project_pre + project_bias
    head_grad = jnp.where(project_pre > 0, flat_cotangent.astype(jnp.float32), 0.0).astype(
        jnp.bfloat16
    )
    own_pre = lax.dynamic_slice_in_dim(project_pre, member * own_out, own_out, 1)
    act_grad = jnp.dot(head_grad, own_rows.T, preferred_element_type=jnp.float32)
    head_output = jnp.maximum(own_pre, 0.0).astype(jnp.bfloat16).reshape(height, breadth, own_out)
    branch_grad = jnp.where(
        branch_pre > 0, act_grad.reshape(height, breadth, 4, own_width), 0.0
    ).astype(jnp.bfloat16)
    variant_list = [branch_grad[:, :, 0, :]]
    for branch, dilation in enumerate(dilation_rates):
        for row_tap in range(3):
            variant_list.append(
                shift_rows(branch_grad[:, :, branch + 1, :], (row_tap - 1) * dilation, fetch_grads)
            )
    variants = jnp.stack(variant_list, 2)
    stacked = make_kernel_taps(variants, dilation_rates).reshape(pixels, 28, own_width)
    input_grad = lax.psum_scatter(
        jnp.einsum("pto,tco->cp", stacked, all_weights, preferred_element_type=jnp.float32),
        "filt",
        scatter_dimension=0,
        tiled=True,
    ).T
    feature_grad = input_grad.astype(jnp.bfloat16).reshape(height, breadth, own_channels)
    return (head_output, feature_grad)


W = 64
BLOCK = 144
PIXELS = 576
HALF = 288
SENT = 304
CHANNELS = 2048
F32 = jnp.float32
BF16 = jnp.bfloat16

OUT_PAIRS = ((3, 1), (1, 1), (3, 0), (1, 0), (3, 2), (1, 2), (2, 1), (2, 0), (2, 2))
TAPS = (
    [(k, 1, 1) for k in (1, 2, 3)]
    + [(k, i, j) for k, j in OUT_PAIRS for i in (0, 2)]
    + [(k, 1, j) for j in (0, 2) for k in (1, 2, 3)]
)
OUT_AT, LEFT_AT, RIGHT_AT = 4 * W, 22 * W, 25 * W
PARTS = ((0, 1), (2, 3))
PART_SWAPS = ((7, 3, 1), (6, 2, 5, 7, 3))
SWAPS = (1, 3, 7, 5, 2, 6)
GRAD_SWAPS = ((5, 7), (2, 6), (1, 3))


def fits(mesh):
    return mesh.shape["rows"] == 8 and mesh.shape["filt"] == 4


def order_matrix(turned=False):
    to = lax.broadcasted_iota(jnp.int32, (192, 192), 1 if turned else 0)
    source = lax.broadcasted_iota(jnp.int32, (192, 192), 0 if turned else 1)

    def parts(value, width):
        return sum((value >= n * width).astype(jnp.int32) for n in (1, 2, 3))

    block = parts(to, 48)
    within = to - 48 * block
    line = parts(within, 12)
    wanted = line * 48 + block * 12 + within - 12 * line
    return (source == wanted).astype(F32).astype(BF16)


def tap_index(tap):
    k, i, j = tap
    return (k - 1) * 9 + i * 3 + j


def nt(a, b):
    return lax.dot_general(a, b, (((1,), (1,)), ((), ())), preferred_element_type=F32)


def nn(a, b):
    return lax.dot_general(a, b, (((1,), (0,)), ((), ())), preferred_element_type=F32)


def from_blocks(order_t, value, write):
    for g in range(3):
        parts = [value[m * BLOCK + g * 48 : m * BLOCK + g * 48 + 48] for m in range(4)]
        write(g * 192, nn(order_t, jnp.concatenate(parts, 0)).astype(BF16))


def low_lanes(shape):
    return lax.broadcasted_iota(jnp.int32, shape, 1) % 128 < W


def scaled(value):
    most = jnp.maximum(jnp.max(jnp.abs(value), axis=0, keepdims=True), 1e-30)
    power = jnp.floor(jnp.log(most) * 1.4426950408889634)
    return value * jnp.exp2(13.0 - power), power


def unscaled(sent):
    return sent[:HALF, :] * jnp.exp2(sent[HALF : HALF + 1, :] - 13.0)


def outward_slot(row, x):
    other = row ^ x
    apart = jnp.abs(other - row)
    slot = apart - 1 + jnp.where(other < row, 3, 0)
    return jnp.where(apart <= 3, slot, 0)


def fetch_tap(dilated, weights, sem, place):
    return pltpu.make_async_copy(
        dilated.at[tap_index(TAPS[place - 1])], weights.at[pl.ds(place * W, W)], sem
    )


def outward_kernel(features, dilated, point, *refs):
    row = lax.axis_index("rows")
    out, ordered, weights = refs[0:6], refs[6], refs[7]
    raw, sums, packed, feature_sems, weight_sems = refs[8:]
    loads = []
    for g in range(3):
        rows = pl.ds(g * 192, 192)
        loads.append(pltpu.make_async_copy(features.at[rows], raw.at[rows], feature_sems.at[g]))
        loads[-1].start()
    queue = [
        fetch_tap(dilated, weights, weight_sems.at[q], place)
        for q, place in enumerate((*range(4, 28), 1, 2, 3))
    ]
    queue.append(pltpu.make_async_copy(point, weights.at[pl.ds(0, W)], weight_sems.at[27]))

    def start_loads(first, last):
        for fetch in queue[first:last]:
            fetch.start()

    start_loads(0, 4)
    order = order_matrix()
    for g in range(3):
        loads[g].wait()
        start_loads((4, 12, 18)[g], (12, 18, 28)[g])
        moved = nn(order, raw[g * 192 : (g + 1) * 192, :]).astype(BF16)
        for m in range(4):
            at = m * BLOCK + g * 48
            ordered[at : at + 48, :] = moved[m * 48 : (m + 1) * 48]

    def product(pair, pairs, first, last):
        for fetch in queue[2 * pair : 2 * (pair + pairs)]:
            fetch.wait()
        at = OUT_AT + pair * 128
        return nt(ordered[first * BLOCK : last * BLOCK, :], weights[at : at + pairs * 128, :])

    d = product(0, 2, 0, 4)
    sums[2] = d[:, :128]
    sums[0] = d[:, 128:]
    d = product(2, 2, 0, 3)
    sums[2, 3 * BLOCK :, :] = sums[2, 3 * BLOCK :, :] + d[:BLOCK, :128]
    sums[0, BLOCK:, :] = sums[0, BLOCK:, :] + d[:, 128:]
    d = product(4, 2, 1, 4)
    sums[2, :BLOCK, :] = sums[2, :BLOCK, :] + d[2 * BLOCK :, :128]
    sums[0, : 3 * BLOCK, :] = sums[0, : 3 * BLOCK, :] + d[:, 128:]
    low = low_lanes((HALF, 128))

    def pack(k):
        top, bottom = sums[k, :HALF, :], sums[k, HALF:, :]
        halves = (
            jnp.where(low, top, pltpu.roll(bottom, W, 1)),
            jnp.where(low, pltpu.roll(top, W, 1), bottom),
        )
        for way, value in enumerate(halves):
            value, power = scaled(value)
            packed[k + 3 * way, :HALF, :] = value
            packed[k + 3 * way, HALF:, :] = jnp.broadcast_to(power, (SENT - HALF, 128))

    pack(2)
    pack(0)
    d = product(6, 3, 0, 4)
    sums[1] = d[:, :128]
    sums[1, 2 * BLOCK :, :] = sums[1, 2 * BLOCK :, :] + d[: 2 * BLOCK, 128:256]
    sums[1, : 2 * BLOCK, :] = sums[1, : 2 * BLOCK, :] + d[2 * BLOCK :, 256:]
    pack(1)
    for n, x in enumerate(SWAPS):
        out[n][...] = packed[outward_slot(row, x)]
    for fetch in queue[18:]:
        fetch.wait()


def outward_sums(features, dilated, point):
    return pl.pallas_call(
        outward_kernel,
        out_shape=[jax.ShapeDtypeStruct((SENT, 128), F32)] * 6
        + [pltpu.VMEM((PIXELS, CHANNELS), BF16), pltpu.VMEM((28 * W, CHANNELS), BF16)],
        in_specs=[pl.BlockSpec(memory_space=pltpu.HBM)] * 3,
        out_specs=[pl.BlockSpec(memory_space=pltpu.VMEM)] * 8,
        scratch_shapes=[
            pltpu.VMEM((PIXELS, CHANNELS), BF16),
            pltpu.VMEM((3, PIXELS, 128), F32),
            pltpu.VMEM((6, SENT, 128), F32),
            pltpu.SemaphoreType.DMA((3,)),
            pltpu.SemaphoreType.DMA((28,)),
        ],
        compiler_params=pltpu.CompilerParams(vmem_limit_bytes=28 * 2**20),
        name="outward_sums",
    )(features, dilated, point)


def own_kernel(ordered, weights, bias, *outs):
    d = nt(ordered[...], weights[:256, :])
    for part, out in enumerate(outs):
        line = jnp.concatenate([bias[k : k + 1, :] for k in PARTS[part]], 1)
        out[...] = d[:, part * 128 : part * 128 + 128] + line
    low = low_lanes((PIXELS, 128))

    def add(first, value, k):
        part = k // 2
        rows = slice(first * BLOCK, first * BLOCK + value.shape[0])
        mask, value = low[: value.shape[0]], value[:, part * 128 : part * 128 + 128]
        kept = jnp.where(mask, value, 0.0) if k == 2 else jnp.where(mask, 0.0, value)
        outs[part][rows, :] = outs[part][rows, :] + kept

    d = nt(ordered[: 3 * BLOCK, :], weights[LEFT_AT - W : LEFT_AT + 3 * W, :])
    for k in (1, 2, 3):
        add(k, d[: (4 - k) * BLOCK], k)
    d = nt(ordered[BLOCK:, :], weights[RIGHT_AT - W : RIGHT_AT + 3 * W, :])
    for k in (1, 2, 3):
        add(0, d[(k - 1) * BLOCK :], k)


def own_sums(ordered, weights, bias):
    return pl.pallas_call(
        own_kernel,
        out_shape=[jax.ShapeDtypeStruct((PIXELS, 128), F32)] * 2,
        in_specs=[pl.BlockSpec(memory_space=pltpu.VMEM)] * 3,
        out_specs=[pl.BlockSpec(memory_space=pltpu.VMEM)] * 2,
        compiler_params=pltpu.CompilerParams(vmem_limit_bytes=18 * 2**20),
        cost_estimate=pl.CostEstimate(flops=10**6, bytes_accessed=10**4, transcendentals=0),
        name="own_sums",
    )(ordered, weights, bias)


def arrival_slot(row, other):
    return jnp.where((other >= 0) & (other < 8), row ^ other, 0)


def gather_arrivals(recv, arrivals, swaps):
    arrivals[0] = jnp.zeros((HALF, 128), arrivals.dtype)
    for n, x in enumerate(swaps):
        arrivals[x] = unscaled(recv[n][...])


def activation_kernel(part, swaps, own, *refs):
    recv, acts, arrivals = refs[: len(swaps)], refs[-2], refs[-1]
    row = lax.axis_index("rows")
    gather_arrivals(recv, arrivals, swaps)
    low = low_lanes((HALF, 128))

    def total(k):
        return arrivals[arrival_slot(row, row - k)] + arrivals[arrival_slot(row, row + k)]

    high = total(PARTS[part][1])
    top, bottom = jnp.where(low, 0.0, pltpu.roll(high, W, 1)), jnp.where(low, 0.0, high)
    if part:
        left = total(PARTS[part][0])
        top = jnp.where(low, left, top)
        bottom = jnp.where(low, pltpu.roll(left, W, 1), bottom)
    acts[:HALF, :] = jnp.maximum(own[:HALF, :] + top, 0.0).astype(BF16)
    acts[HALF:, :] = jnp.maximum(own[HALF:, :] + bottom, 0.0).astype(BF16)


def activations_of(part, swaps, own, received):
    return pl.pallas_call(
        functools.partial(activation_kernel, part, swaps),
        out_shape=jax.ShapeDtypeStruct((PIXELS, 128), BF16),
        in_specs=[pl.BlockSpec(memory_space=pltpu.VMEM)] * (1 + len(swaps)),
        out_specs=pl.BlockSpec(memory_space=pltpu.VMEM),
        scratch_shapes=[pltpu.VMEM((8, HALF, 128), F32)],
        compiler_params=pltpu.CompilerParams(vmem_limit_bytes=8 * 2**20),
        name="activations",
    )(own, *received)


def project_rows(project, who):
    at = pl.multiple_of(who * W, W)
    return jnp.concatenate([project[k, pl.ds(at, W), :] for part in PARTS for k in part], 0)


def both(a, b):
    return jnp.concatenate([a[...], b[...]], 1)


def near_head_kernel(a0, b0, a1, b1, project, bias, cotangent, pre, ordered):
    member = lax.axis_index("filt")
    pre[...] = nn(both(a0, b0), project_rows(project, member)) + bias[...]
    pre[...] = pre[...] + nn(both(a1, b1), project_rows(project, member ^ 1))
    order = order_matrix()
    for g in range(3):
        moved = nn(order, cotangent[g * 192 : (g + 1) * 192, :])
        for m in range(4):
            at = m * BLOCK + g * 48
            ordered[at : at + 48, :] = moved[m * 48 : (m + 1) * 48]


def near_head(own, beside, project, bias, cotangent):
    return pl.pallas_call(
        near_head_kernel,
        out_shape=[jax.ShapeDtypeStruct((PIXELS, 256), F32)] * 2,
        in_specs=[pl.BlockSpec(memory_space=pltpu.VMEM)] * 7,
        out_specs=[pl.BlockSpec(memory_space=pltpu.VMEM)] * 2,
        compiler_params=pltpu.CompilerParams(vmem_limit_bytes=10 * 2**20),
        name="near_head",
    )(*own, *beside, project, bias, cotangent)


def far_head_kernel(a0, b0, a1, b1, a2, b2, a3, b3, project, near, cotangent, *refs):
    output, grads, sends, packed = refs[0], refs[1], refs[2:5], refs[5]
    row, member = lax.axis_index("rows"), lax.axis_index("filt")
    pre = near[...] + nn(both(a2, b2), project_rows(project, member ^ 2))
    pre = pre + nn(both(a3, b3), project_rows(project, member ^ 3))
    output[...] = jnp.maximum(pre, 0.0).astype(BF16)
    head_grad = jnp.where(pre > 0, cotangent[...], 0.0).astype(BF16)
    low = low_lanes((HALF, 128))
    for who, (acts_a, acts_b) in enumerate(((a0, b0), (a1, b1))):
        act_grad = nt(head_grad, project_rows(project, member ^ who))
        a = jnp.where(acts_a[...].astype(F32) > 0, act_grad[:, :128], 0.0)
        b = jnp.where(acts_b[...].astype(F32) > 0, act_grad[:, 128:], 0.0)
        if who == 0:
            grads[:, :128] = a.astype(BF16)
            grads[:, 128:] = b.astype(BF16)
        packed[0, who] = jnp.where(low, pltpu.roll(a[:HALF], W, 1), a[HALF:]).astype(BF16)
        packed[1, who] = jnp.where(low, b[:HALF], pltpu.roll(b[HALF:], W, 1)).astype(BF16)
        packed[2, who] = jnp.where(low, pltpu.roll(b[:HALF], W, 1), b[HALF:]).astype(BF16)
    for n, swaps in enumerate(GRAD_SWAPS):
        apart = jnp.abs((row ^ jnp.where((member & 1) == 0, *swaps)) - row)
        sends[n][...] = packed[jnp.where(apart <= 3, apart - 1, 0)]


def far_head(own, beside, across, corner, project, near, cotangent):
    return pl.pallas_call(
        far_head_kernel,
        out_shape=[jax.ShapeDtypeStruct((PIXELS, 256), BF16)] * 2
        + [jax.ShapeDtypeStruct((2, HALF, 128), BF16)] * 3,
        in_specs=[pl.BlockSpec(memory_space=pltpu.VMEM)] * 11,
        out_specs=[pl.BlockSpec(memory_space=pltpu.VMEM)] * 5,
        scratch_shapes=[pltpu.VMEM((3, 2, HALF, 128), BF16)],
        compiler_params=pltpu.CompilerParams(vmem_limit_bytes=12 * 2**20),
        name="far_head",
    )(*own, *beside, *across, *corner, project, near, cotangent)


def own_output_kernel(output, out):
    member = lax.axis_index("filt")
    mine = jnp.zeros((PIXELS, W), F32)
    for q in range(4):
        mine = jnp.where(member == q, output[:, q * W : (q + 1) * W].astype(F32), mine)

    def put(at, value):
        out[at : at + 192, :] = value

    from_blocks(order_matrix(True), mine.astype(BF16), put)


def own_output(output):
    return pl.pallas_call(
        own_output_kernel,
        out_shape=jax.ShapeDtypeStruct((PIXELS, W), BF16),
        in_specs=[pl.BlockSpec(memory_space=pltpu.VMEM)],
        out_specs=pl.BlockSpec(memory_space=pltpu.VMEM),
        compiler_params=pltpu.CompilerParams(vmem_limit_bytes=6 * 2**20),
        name="own_output",
    )(output)


def spread_kernel(own, *refs):
    recv, handed, stack, arrivals, pairs, twice = refs[:3], refs[3:6], *refs[6:]
    row, member = lax.axis_index("rows"), lax.axis_index("filt")
    arrivals[0] = jnp.zeros((HALF, 128), BF16)
    for n, (even, odd) in enumerate(GRAD_SWAPS):
        first = (member & 1) == 0
        arrivals[jnp.where(first, even, odd)] = recv[n][0]
        arrivals[jnp.where(first, odd, even)] = handed[n][1]
    low = low_lanes((HALF, 128))
    low_all = low_lanes((PIXELS, 128))
    for k in (1, 2, 3):
        p = arrivals[arrival_slot(row, row + k)].astype(F32)
        m = arrivals[arrival_slot(row, row - k)].astype(F32)
        pairs[k - 1, :HALF, :] = jnp.where(low, p, pltpu.roll(m, W, 1)).astype(BF16)
        pairs[k - 1, HALF:, :] = jnp.where(low, pltpu.roll(p, W, 1), m).astype(BF16)
        g = own[:, :128].astype(F32) if k == 1 else own[:, 128:].astype(F32)
        other = pltpu.roll(g, W, 1)
        two = jnp.where(low_all, g, other) if k == 2 else jnp.where(low_all, other, g)
        twice[k - 1] = two.astype(BF16)
    stack[:, : 4 * W] = own[...]
    nothing = jnp.zeros((BLOCK, 128), BF16)

    def block_of(ref, k, source):
        if 0 <= source < 4:
            return ref[k - 1, source * BLOCK : (source + 1) * BLOCK, :]
        return nothing

    for q, (k, j) in enumerate(OUT_PAIRS):
        lanes = slice(OUT_AT + q * 128, OUT_AT + q * 128 + 128)
        for m in range(4):
            stack[m * BLOCK : (m + 1) * BLOCK, lanes] = block_of(pairs, k, m - (j - 1) * k)
    low_block = low_lanes((BLOCK, 128))
    for q, (a, b) in enumerate(((1, 2), (3, -1), (-2, -3))):
        lanes = slice(LEFT_AT + q * 128, LEFT_AT + q * 128 + 128)
        for m in range(4):
            stack[m * BLOCK : (m + 1) * BLOCK, lanes] = jnp.where(
                low_block, block_of(twice, abs(a), m + a), block_of(twice, abs(b), m + b)
            )


def spread(own, received, handed):
    return pl.pallas_call(
        spread_kernel,
        out_shape=pltpu.VMEM((PIXELS, 28 * W), BF16),
        in_specs=[pl.BlockSpec(memory_space=pltpu.VMEM)] * 7,
        out_specs=pl.BlockSpec(memory_space=pltpu.VMEM),
        scratch_shapes=[
            pltpu.VMEM((8, HALF, 128), BF16),
            pltpu.VMEM((3, PIXELS, 128), BF16),
            pltpu.VMEM((3, PIXELS, 128), BF16),
        ],
        compiler_params=pltpu.CompilerParams(vmem_limit_bytes=12 * 2**20),
        name="spread",
    )(own, *received, *handed)


def grad_kernel(flips, stack, weights, *outs):
    member = lax.axis_index("filt")
    for out, flip in zip(outs, flips):
        columns = pl.ds(pl.multiple_of((member ^ flip) * 512, 512), 512)
        out[...] = nn(stack[...], weights[:, columns]).astype(BF16)


def grads_for(flips, stack, weights, scale=1):
    return pl.pallas_call(
        functools.partial(grad_kernel, flips),
        out_shape=[jax.ShapeDtypeStruct((PIXELS, 512), BF16)] * len(flips),
        in_specs=[pl.BlockSpec(memory_space=pltpu.VMEM)] * 2,
        out_specs=[pl.BlockSpec(memory_space=pltpu.VMEM)] * len(flips),
        compiler_params=pltpu.CompilerParams(vmem_limit_bytes=18 * 2**20),
        cost_estimate=pl.CostEstimate(
            flops=2 * PIXELS * 28 * W * 512 * scale, bytes_accessed=10**6, transcendentals=0
        ),
        name="grads_for",
    )(stack, weights)


def last_kernel(a, b, c, out):
    total = a[...].astype(F32) + b[...].astype(F32) + c[...].astype(F32)

    def put(at, value):
        out[at : at + 192, :] = value

    from_blocks(order_matrix(True), total.astype(BF16), put)


def last_sum(a, b, c):
    return pl.pallas_call(
        last_kernel,
        out_shape=jax.ShapeDtypeStruct((PIXELS, 512), BF16),
        in_specs=[pl.BlockSpec(memory_space=pltpu.VMEM)] * 3,
        out_specs=pl.BlockSpec(memory_space=pltpu.VMEM),
        compiler_params=pltpu.CompilerParams(vmem_limit_bytes=10 * 2**20),
        name="last_sum",
    )(a, b, c)


def flipped(x, bit):
    return lax.ppermute(x, "filt", [(i, i ^ bit) for i in range(lax.axis_size("filt"))])


def partner(r, bits):
    return r ^ bits if abs((r ^ bits) - r) <= 3 else r ^ {5: 2, 6: 1, 7: 1}[bits]


def swapped(x, bits):
    return lax.ppermute(x, "rows", [(r, partner(r, bits)) for r in range(8)])


def swapped_by_core(x, bits):
    pairs = [
        (4 * r + member, 4 * partner(r, bits[member % 2]) + member)
        for r in range(8)
        for member in range(4)
    ]
    return lax.ppermute(x, ("rows", "filt"), pairs)


def on_device(
    features, point_weight, dilated_weight, branch_bias, project_weight, project_bias, cotangent
):
    flat = features.reshape(PIXELS, CHANNELS)
    dilated = jnp.transpose(dilated_weight, (0, 1, 2, 4, 3)).reshape(27, W, CHANNELS)
    point = point_weight.T
    flat, dilated, point = (
        pltpu.with_memory_space_constraint(x, pltpu.HBM) for x in (flat, dilated, point)
    )
    *sums, ordered, weights = outward_sums(flat, dilated, point)
    received = {
        x: swapped(sums[n].astype(jnp.float16), x).astype(F32) for n, x in enumerate(SWAPS)
    }
    own = own_sums(ordered, weights, branch_bias)
    acts = [
        activations_of(part, swaps, own[part], [received[x] for x in swaps])
        for part, swaps in enumerate(PART_SWAPS)
    ]
    across = [flipped(x, 2) for x in acts]
    beside = [flipped(x, 1) for x in acts]
    corner = [flipped(x, 1) for x in across]
    near, ordered_cotangent = near_head(
        acts,
        beside,
        project_weight,
        project_bias.reshape(1, 256),
        cotangent.reshape(PIXELS, 256),
    )
    output, grads, *sends = far_head(
        acts, beside, across, corner, project_weight, near, ordered_cotangent
    )
    arrived = [swapped_by_core(sends[n], swaps) for n, swaps in enumerate(GRAD_SWAPS)]
    handed = [flipped(x, 1) for x in arrived]
    stack = spread(grads, arrived, handed)
    (far,) = grads_for((3,), stack, weights)
    far = flipped(far, 1)
    (kept,) = grads_for((2,), stack, weights)
    crossing = (far.astype(F32) + kept.astype(F32)).astype(BF16)
    crossed = flipped(crossing, 2)
    later, output, crossing = lax.optimization_barrier((stack, output, crossing))
    head_output = own_output(output)
    (near,) = grads_for((1,), later, weights)
    near = flipped(near, 1)
    (kept,) = grads_for((0,), later, weights, 8)
    feature_grad = last_sum(kept, near, crossed)
    return head_output.reshape(12, 48, W), feature_grad.reshape(12, 48, 512)


def solution(mesh):
    body = on_device if fits(mesh) else on_device_general
    in_specs = (
        P("rows", None, None),
        P(None, "filt"),
        P(None, None, None, None, "filt"),
        P(None, "filt"),
        P(),
        P(),
        P("rows", None, None),
    )
    out_specs = (P("rows", None, "filt"), P("rows", None, "filt"))
    return jax.shard_map(
        body, mesh=mesh, in_specs=in_specs, out_specs=out_specs, check_vma=False
    )
```

```python
import functools

import jax
import jax.numpy as jnp
from jax import lax
from jax.experimental import pallas as pl
from jax.experimental.pallas import tpu as pltpu
from jax.sharding import PartitionSpec as P

FIRST_DILATION = 12
SECOND_DILATION = 24
THIRD_DILATION = 36


def passed_along(x, axis, by):
    devices = lax.axis_size(axis)
    pairs = [(i, i + by) for i in range(devices) if 0 <= i + by < devices]
    return lax.ppermute(x, axis, pairs)


def shift_columns(field, amount):
    breadth = field.shape[1]
    if amount == 0:
        return field
    padding = [(0, 0)] * field.ndim
    if amount > 0:
        kept = field[:, amount:]
        padding[1] = (0, amount)
    else:
        kept = field[:, : breadth + amount]
        padding[1] = (-amount, 0)
    return jnp.pad(kept, padding)


def fetch_sums(field, offset):
    return passed_along(field, "rows", offset)


def fetch_grads(field, offset):
    return passed_along(field, "rows", offset)


def shift_rows(field, amount, fetcher):
    height = field.shape[0]
    quotient = amount // height

    def extract_block(offset):
        if offset == 0:
            return field
        return fetcher(field, offset)

    return extract_block(quotient)


def make_kernel_taps(variants, dilation_rates):
    stacked = [variants[:, :, 0]]
    for branch, dilation in enumerate(dilation_rates):
        for row_tap in range(3):
            source = variants[:, :, 1 + 3 * branch + row_tap]
            for col_tap in range(3):
                stacked.append(shift_columns(source, -(col_tap - 1) * dilation))
    return jnp.stack(stacked, 2)


def on_device_general(
    features, point_weight, dilated_weight, branch_bias, project_weight, project_bias, cotangent
):
    height, breadth, channels = features.shape
    pixels = height * breadth
    own_width = point_weight.shape[1]
    filters = lax.axis_size("filt")
    member = lax.axis_index("filt")
    branch_outputs = project_weight.shape[2]
    own_out = branch_outputs // filters
    own_channels = channels // filters
    dilation_rates = (FIRST_DILATION, SECOND_DILATION, THIRD_DILATION)
    all_weights = jnp.concatenate(
        [point_weight[None], dilated_weight.reshape(27, channels, own_width)], 0
    )
    flattened = features.reshape(pixels, channels)
    tap_terms = jnp.einsum(
        "pc,tco->pto", flattened, all_weights, preferred_element_type=jnp.float32
    )
    tap_terms = tap_terms.reshape(height, breadth, 28, own_width)
    pre_list = [tap_terms[:, :, 0, :] + branch_bias[0]]
    for branch, dilation in enumerate(dilation_rates):
        summed_result = jnp.zeros((height, breadth, own_width), jnp.float32)
        for row_tap in range(3):
            row_sum = jnp.zeros((height, breadth, own_width), jnp.float32)
            for col_tap in range(3):
                row_sum = row_sum + shift_columns(
                    tap_terms[:, :, 1 + 9 * branch + 3 * row_tap + col_tap, :],
                    (col_tap - 1) * dilation,
                )
            summed_result = summed_result + shift_rows(
                row_sum, -(row_tap - 1) * dilation, fetch_sums
            )
        pre_list.append(summed_result + branch_bias[branch + 1])
    branch_pre = jnp.stack(pre_list, 2)
    activations = jnp.maximum(branch_pre, 0.0).astype(jnp.bfloat16).reshape(pixels, 4 * own_width)
    grouped = project_weight.reshape(4, filters, own_width, branch_outputs)
    own_rows = lax.dynamic_index_in_dim(grouped, member, 1, keepdims=False).reshape(
        4 * own_width, branch_outputs
    )
    flat_cotangent = cotangent.reshape(pixels, branch_outputs)
    ordered = jnp.transpose(grouped, (1, 0, 2, 3)).reshape(filters * 4 * own_width, branch_outputs)
    project_pre = jnp.dot(
        lax.all_gather(activations, "filt", axis=1, tiled=True),
        ordered,
        preferred_element_type=jnp.float32,
    )
    project_pre = project_pre + project_bias
    head_grad = jnp.where(project_pre > 0, flat_cotangent.astype(jnp.float32), 0.0).astype(
        jnp.bfloat16
    )
    own_pre = lax.dynamic_slice_in_dim(project_pre, member * own_out, own_out, 1)
    act_grad = jnp.dot(head_grad, own_rows.T, preferred_element_type=jnp.float32)
    head_output = jnp.maximum(own_pre, 0.0).astype(jnp.bfloat16).reshape(height, breadth, own_out)
    branch_grad = jnp.where(
        branch_pre > 0, act_grad.reshape(height, breadth, 4, own_width), 0.0
    ).astype(jnp.bfloat16)
    variant_list = [branch_grad[:, :, 0, :]]
    for branch, dilation in enumerate(dilation_rates):
        for row_tap in range(3):
            variant_list.append(
                shift_rows(branch_grad[:, :, branch + 1, :], (row_tap - 1) * dilation, fetch_grads)
            )
    variants = jnp.stack(variant_list, 2)
    stacked = make_kernel_taps(variants, dilation_rates).reshape(pixels, 28, own_width)
    input_grad = lax.psum_scatter(
        jnp.einsum("pto,tco->cp", stacked, all_weights, preferred_element_type=jnp.float32),
        "filt",
        scatter_dimension=0,
        tiled=True,
    ).T
    feature_grad = input_grad.astype(jnp.bfloat16).reshape(height, breadth, own_channels)
    return (head_output, feature_grad)


W = 64
BLOCK = 144
PIXELS = 576
HALF = 288
SENT = 304
CHANNELS = 2048
F32 = jnp.float32
BF16 = jnp.bfloat16

OUT_PAIRS = ((3, 1), (1, 1), (3, 0), (1, 0), (3, 2), (1, 2), (2, 1), (2, 0), (2, 2))
TAPS = (
    [(k, 1, 1) for k in (1, 2, 3)]
    + [(k, i, j) for k, j in OUT_PAIRS for i in (0, 2)]
    + [(k, 1, j) for j in (0, 2) for k in (1, 2, 3)]
)
OUT_AT, LEFT_AT, RIGHT_AT = 4 * W, 22 * W, 25 * W
PARTS = ((0, 1), (2, 3))
PART_SWAPS = ((7, 3, 1), (6, 2, 5, 7, 3))
SWAPS = (1, 3, 7, 5, 2, 6)
GRAD_SWAPS = (1, 3, 7, 5, 2, 6)


def fits(mesh):
    return mesh.shape["rows"] == 8 and mesh.shape["filt"] == 4


def order_matrix(turned=False):
    to = lax.broadcasted_iota(jnp.int32, (192, 192), 1 if turned else 0)
    source = lax.broadcasted_iota(jnp.int32, (192, 192), 0 if turned else 1)

    def parts(value, width):
        return sum((value >= n * width).astype(jnp.int32) for n in (1, 2, 3))

    block = parts(to, 48)
    within = to - 48 * block
    line = parts(within, 12)
    wanted = line * 48 + block * 12 + within - 12 * line
    return (source == wanted).astype(F32).astype(BF16)


def tap_index(tap):
    k, i, j = tap
    return (k - 1) * 9 + i * 3 + j


def nt(a, b):
    return lax.dot_general(a, b, (((1,), (1,)), ((), ())), preferred_element_type=F32)


def nn(a, b):
    return lax.dot_general(a, b, (((1,), (0,)), ((), ())), preferred_element_type=F32)


def from_blocks(order_t, value, write):
    for g in range(3):
        parts = [value[m * BLOCK + g * 48 : m * BLOCK + g * 48 + 48] for m in range(4)]
        write(g * 192, nn(order_t, jnp.concatenate(parts, 0)).astype(BF16))


def low_lanes(shape):
    return lax.broadcasted_iota(jnp.int32, shape, 1) % 128 < W


def scaled(value):
    most = jnp.maximum(jnp.max(jnp.abs(value), axis=0, keepdims=True), 1e-30)
    power = jnp.floor(jnp.log(most) * 1.4426950408889634)
    return value * jnp.exp2(13.0 - power), power


def unscaled(sent):
    return sent[:HALF, :] * jnp.exp2(sent[HALF : HALF + 1, :] - 13.0)


def outward_slot(row, x):
    other = row ^ x
    apart = jnp.abs(other - row)
    slot = apart - 1 + jnp.where(other < row, 3, 0)
    return jnp.where(apart <= 3, slot, 0)


def fetch_tap(dilated, weights, sem, place):
    return pltpu.make_async_copy(
        dilated.at[tap_index(TAPS[place - 1])], weights.at[pl.ds(place * W, W)], sem
    )


def outward_kernel(features, dilated, point, *refs):
    row = lax.axis_index("rows")
    out, ordered, weights = refs[0:6], refs[6], refs[7]
    raw, sums, packed, feature_sems, weight_sems = refs[8:]
    loads = []
    for g in range(3):
        rows = pl.ds(g * 192, 192)
        loads.append(pltpu.make_async_copy(features.at[rows], raw.at[rows], feature_sems.at[g]))
        loads[-1].start()
    queue = [
        fetch_tap(dilated, weights, weight_sems.at[q], place)
        for q, place in enumerate((*range(4, 28), 1, 2, 3))
    ]
    queue.append(pltpu.make_async_copy(point, weights.at[pl.ds(0, W)], weight_sems.at[27]))

    def start_loads(first, last):
        for fetch in queue[first:last]:
            fetch.start()

    start_loads(0, 4)
    order = order_matrix()
    for g in range(3):
        loads[g].wait()
        start_loads((4, 12, 18)[g], (12, 18, 28)[g])
        moved = nn(order, raw[g * 192 : (g + 1) * 192, :]).astype(BF16)
        for m in range(4):
            at = m * BLOCK + g * 48
            ordered[at : at + 48, :] = moved[m * 48 : (m + 1) * 48]

    def product(pair, pairs, first, last):
        for fetch in queue[2 * pair : 2 * (pair + pairs)]:
            fetch.wait()
        at = OUT_AT + pair * 128
        return nt(ordered[first * BLOCK : last * BLOCK, :], weights[at : at + pairs * 128, :])

    d = product(0, 2, 0, 4)
    sums[2] = d[:, :128]
    sums[0] = d[:, 128:]
    d = product(2, 2, 0, 3)
    sums[2, 3 * BLOCK :, :] = sums[2, 3 * BLOCK :, :] + d[:BLOCK, :128]
    sums[0, BLOCK:, :] = sums[0, BLOCK:, :] + d[:, 128:]
    d = product(4, 2, 1, 4)
    sums[2, :BLOCK, :] = sums[2, :BLOCK, :] + d[2 * BLOCK :, :128]
    sums[0, : 3 * BLOCK, :] = sums[0, : 3 * BLOCK, :] + d[:, 128:]
    low = low_lanes((HALF, 128))

    def pack(k):
        top, bottom = sums[k, :HALF, :], sums[k, HALF:, :]
        halves = (
            jnp.where(low, top, pltpu.roll(bottom, W, 1)),
            jnp.where(low, pltpu.roll(top, W, 1), bottom),
        )
        for way, value in enumerate(halves):
            value, power = scaled(value)
            packed[k + 3 * way, :HALF, :] = value
            packed[k + 3 * way, HALF:, :] = jnp.broadcast_to(power, (SENT - HALF, 128))

    pack(2)
    pack(0)
    d = product(6, 3, 0, 4)
    sums[1] = d[:, :128]
    sums[1, 2 * BLOCK :, :] = sums[1, 2 * BLOCK :, :] + d[: 2 * BLOCK, 128:256]
    sums[1, : 2 * BLOCK, :] = sums[1, : 2 * BLOCK, :] + d[2 * BLOCK :, 256:]
    pack(1)
    for n, x in enumerate(SWAPS):
        out[n][...] = packed[outward_slot(row, x)]
    for fetch in queue[18:]:
        fetch.wait()


def outward_sums(features, dilated, point):
    return pl.pallas_call(
        outward_kernel,
        out_shape=[jax.ShapeDtypeStruct((SENT, 128), F32)] * 6
        + [pltpu.VMEM((PIXELS, CHANNELS), BF16), pltpu.VMEM((28 * W, CHANNELS), BF16)],
        in_specs=[pl.BlockSpec(memory_space=pltpu.HBM)] * 3,
        out_specs=[pl.BlockSpec(memory_space=pltpu.VMEM)] * 8,
        scratch_shapes=[
            pltpu.VMEM((PIXELS, CHANNELS), BF16),
            pltpu.VMEM((3, PIXELS, 128), F32),
            pltpu.VMEM((6, SENT, 128), F32),
            pltpu.SemaphoreType.DMA((3,)),
            pltpu.SemaphoreType.DMA((28,)),
        ],
        compiler_params=pltpu.CompilerParams(vmem_limit_bytes=28 * 2**20),
        name="outward_sums",
    )(features, dilated, point)


def own_kernel(ordered, weights, bias, *outs):
    d = nt(ordered[...], weights[:256, :])
    for part, out in enumerate(outs):
        line = jnp.concatenate([bias[k : k + 1, :] for k in PARTS[part]], 1)
        out[...] = d[:, part * 128 : part * 128 + 128] + line
    low = low_lanes((PIXELS, 128))

    def add(first, value, k):
        part = k // 2
        rows = slice(first * BLOCK, first * BLOCK + value.shape[0])
        mask, value = low[: value.shape[0]], value[:, part * 128 : part * 128 + 128]
        kept = jnp.where(mask, value, 0.0) if k == 2 else jnp.where(mask, 0.0, value)
        outs[part][rows, :] = outs[part][rows, :] + kept

    d = nt(ordered[: 3 * BLOCK, :], weights[LEFT_AT - W : LEFT_AT + 3 * W, :])
    for k in (1, 2, 3):
        add(k, d[: (4 - k) * BLOCK], k)
    d = nt(ordered[BLOCK:, :], weights[RIGHT_AT - W : RIGHT_AT + 3 * W, :])
    for k in (1, 2, 3):
        add(0, d[(k - 1) * BLOCK :], k)


def own_sums(ordered, weights, bias):
    return pl.pallas_call(
        own_kernel,
        out_shape=[jax.ShapeDtypeStruct((PIXELS, 128), F32)] * 2,
        in_specs=[pl.BlockSpec(memory_space=pltpu.VMEM)] * 3,
        out_specs=[pl.BlockSpec(memory_space=pltpu.VMEM)] * 2,
        compiler_params=pltpu.CompilerParams(vmem_limit_bytes=18 * 2**20),
        cost_estimate=pl.CostEstimate(flops=10**6, bytes_accessed=10**4, transcendentals=0),
        name="own_sums",
    )(ordered, weights, bias)


def arrival_slot(row, other):
    return jnp.where((other >= 0) & (other < 8), row ^ other, 0)


def gather_arrivals(recv, arrivals, swaps):
    arrivals[0] = jnp.zeros((HALF, 128), arrivals.dtype)
    for n, x in enumerate(swaps):
        arrivals[x] = unscaled(recv[n][...])


def activation_kernel(part, swaps, own, *refs):
    recv, acts, arrivals = refs[: len(swaps)], refs[-2], refs[-1]
    row = lax.axis_index("rows")
    gather_arrivals(recv, arrivals, swaps)
    low = low_lanes((HALF, 128))

    def total(k):
        return arrivals[arrival_slot(row, row - k)] + arrivals[arrival_slot(row, row + k)]

    high = total(PARTS[part][1])
    top, bottom = jnp.where(low, 0.0, pltpu.roll(high, W, 1)), jnp.where(low, 0.0, high)
    if part:
        left = total(PARTS[part][0])
        top = jnp.where(low, left, top)
        bottom = jnp.where(low, pltpu.roll(left, W, 1), bottom)
    acts[:HALF, :] = jnp.maximum(own[:HALF, :] + top, 0.0).astype(BF16)
    acts[HALF:, :] = jnp.maximum(own[HALF:, :] + bottom, 0.0).astype(BF16)


def activations_of(part, swaps, own, received):
    return pl.pallas_call(
        functools.partial(activation_kernel, part, swaps),
        out_shape=jax.ShapeDtypeStruct((PIXELS, 128), BF16),
        in_specs=[pl.BlockSpec(memory_space=pltpu.VMEM)] * (1 + len(swaps)),
        out_specs=pl.BlockSpec(memory_space=pltpu.VMEM),
        scratch_shapes=[pltpu.VMEM((8, HALF, 128), F32)],
        compiler_params=pltpu.CompilerParams(vmem_limit_bytes=8 * 2**20),
        name="activations",
    )(own, *received)


def project_rows(project, who):
    at = pl.multiple_of(who * W, W)
    return jnp.concatenate([project[k, pl.ds(at, W), :] for part in PARTS for k in part], 0)


def both(a, b):
    return jnp.concatenate([a[...], b[...]], 1)


def near_head_kernel(a0, b0, a1, b1, project, bias, cotangent, pre, ordered):
    member = lax.axis_index("filt")
    pre[...] = nn(both(a0, b0), project_rows(project, member)) + bias[...]
    pre[...] = pre[...] + nn(both(a1, b1), project_rows(project, member ^ 1))
    order = order_matrix()
    for g in range(3):
        moved = nn(order, cotangent[g * 192 : (g + 1) * 192, :])
        for m in range(4):
            at = m * BLOCK + g * 48
            ordered[at : at + 48, :] = moved[m * 48 : (m + 1) * 48]


def near_head(own, beside, project, bias, cotangent):
    return pl.pallas_call(
        near_head_kernel,
        out_shape=[jax.ShapeDtypeStruct((PIXELS, 256), F32)] * 2,
        in_specs=[pl.BlockSpec(memory_space=pltpu.VMEM)] * 7,
        out_specs=[pl.BlockSpec(memory_space=pltpu.VMEM)] * 2,
        compiler_params=pltpu.CompilerParams(vmem_limit_bytes=10 * 2**20),
        name="near_head",
    )(*own, *beside, project, bias, cotangent)


def far_head_kernel(a0, b0, a2, b2, a3, b3, project, near, cotangent, *refs):
    output, grads, sends, packed = refs[0], refs[1], refs[2:8], refs[8]
    row, member = lax.axis_index("rows"), lax.axis_index("filt")
    pre = near[...] + nn(both(a2, b2), project_rows(project, member ^ 2))
    pre = pre + nn(both(a3, b3), project_rows(project, member ^ 3))
    output[...] = jnp.maximum(pre, 0.0).astype(BF16)
    head_grad = jnp.where(pre > 0, cotangent[...], 0.0).astype(BF16)
    act_grad = nt(head_grad, project_rows(project, member))
    a = jnp.where(a0[...].astype(F32) > 0, act_grad[:, :128], 0.0)
    b = jnp.where(b0[...].astype(F32) > 0, act_grad[:, 128:], 0.0)
    grads[:, :128] = a.astype(BF16)
    grads[:, 128:] = b.astype(BF16)
    low = low_lanes((HALF, 128))
    packed[0] = jnp.where(low, pltpu.roll(a[:HALF], W, 1), a[HALF:]).astype(BF16)
    packed[1] = jnp.where(low, b[:HALF], pltpu.roll(b[HALF:], W, 1)).astype(BF16)
    packed[2] = jnp.where(low, pltpu.roll(b[:HALF], W, 1), b[HALF:]).astype(BF16)
    for n, x in enumerate(GRAD_SWAPS):
        apart = jnp.abs((row ^ x) - row)
        sends[n][...] = packed[jnp.where(apart <= 3, apart - 1, 0)]


def far_head(own, across, corner, project, near, cotangent):
    return pl.pallas_call(
        far_head_kernel,
        out_shape=[jax.ShapeDtypeStruct((PIXELS, 256), BF16)] * 2
        + [jax.ShapeDtypeStruct((HALF, 128), BF16)] * 6,
        in_specs=[pl.BlockSpec(memory_space=pltpu.VMEM)] * 9,
        out_specs=[pl.BlockSpec(memory_space=pltpu.VMEM)] * 8,
        scratch_shapes=[pltpu.VMEM((3, HALF, 128), BF16)],
        compiler_params=pltpu.CompilerParams(vmem_limit_bytes=12 * 2**20),
        name="far_head",
    )(*own, *across, *corner, project, near, cotangent)


def own_output_kernel(output, out):
    member = lax.axis_index("filt")
    mine = jnp.zeros((PIXELS, W), F32)
    for q in range(4):
        mine = jnp.where(member == q, output[:, q * W : (q + 1) * W].astype(F32), mine)

    def put(at, value):
        out[at : at + 192, :] = value

    from_blocks(order_matrix(True), mine.astype(BF16), put)


def own_output(output):
    return pl.pallas_call(
        own_output_kernel,
        out_shape=jax.ShapeDtypeStruct((PIXELS, W), BF16),
        in_specs=[pl.BlockSpec(memory_space=pltpu.VMEM)],
        out_specs=pl.BlockSpec(memory_space=pltpu.VMEM),
        compiler_params=pltpu.CompilerParams(vmem_limit_bytes=6 * 2**20),
        name="own_output",
    )(output)


def spread_kernel(own, *refs):
    recv, stack, arrivals, pairs, twice = refs[:6], *refs[6:]
    row = lax.axis_index("rows")
    arrivals[0] = jnp.zeros((HALF, 128), BF16)
    for n, x in enumerate(GRAD_SWAPS):
        arrivals[x] = recv[n][...]
    low = low_lanes((HALF, 128))
    low_all = low_lanes((PIXELS, 128))
    for k in (1, 2, 3):
        p = arrivals[arrival_slot(row, row + k)].astype(F32)
        m = arrivals[arrival_slot(row, row - k)].astype(F32)
        pairs[k - 1, :HALF, :] = jnp.where(low, p, pltpu.roll(m, W, 1)).astype(BF16)
        pairs[k - 1, HALF:, :] = jnp.where(low, pltpu.roll(p, W, 1), m).astype(BF16)
        g = own[:, :128].astype(F32) if k == 1 else own[:, 128:].astype(F32)
        other = pltpu.roll(g, W, 1)
        two = jnp.where(low_all, g, other) if k == 2 else jnp.where(low_all, other, g)
        twice[k - 1] = two.astype(BF16)
    stack[:, : 4 * W] = own[...]
    nothing = jnp.zeros((BLOCK, 128), BF16)

    def block_of(ref, k, source):
        if 0 <= source < 4:
            return ref[k - 1, source * BLOCK : (source + 1) * BLOCK, :]
        return nothing

    for q, (k, j) in enumerate(OUT_PAIRS):
        lanes = slice(OUT_AT + q * 128, OUT_AT + q * 128 + 128)
        for m in range(4):
            stack[m * BLOCK : (m + 1) * BLOCK, lanes] = block_of(pairs, k, m - (j - 1) * k)
    low_block = low_lanes((BLOCK, 128))
    for q, (a, b) in enumerate(((1, 2), (3, -1), (-2, -3))):
        lanes = slice(LEFT_AT + q * 128, LEFT_AT + q * 128 + 128)
        for m in range(4):
            stack[m * BLOCK : (m + 1) * BLOCK, lanes] = jnp.where(
                low_block, block_of(twice, abs(a), m + a), block_of(twice, abs(b), m + b)
            )


def spread(own, received):
    return pl.pallas_call(
        spread_kernel,
        out_shape=pltpu.VMEM((PIXELS, 28 * W), BF16),
        in_specs=[pl.BlockSpec(memory_space=pltpu.VMEM)] * 7,
        out_specs=pl.BlockSpec(memory_space=pltpu.VMEM),
        scratch_shapes=[
            pltpu.VMEM((8, HALF, 128), BF16),
            pltpu.VMEM((3, PIXELS, 128), BF16),
            pltpu.VMEM((3, PIXELS, 128), BF16),
        ],
        compiler_params=pltpu.CompilerParams(vmem_limit_bytes=12 * 2**20),
        name="spread",
    )(own, *received)


def grad_kernel(flips, stack, weights, *outs):
    member = lax.axis_index("filt")
    for out, flip in zip(outs, flips):
        columns = pl.ds(pl.multiple_of((member ^ flip) * 512, 512), 512)
        out[...] = nn(stack[...], weights[:, columns]).astype(BF16)


def grads_for(flips, stack, weights, scale=1):
    return pl.pallas_call(
        functools.partial(grad_kernel, flips),
        out_shape=[jax.ShapeDtypeStruct((PIXELS, 512), BF16)] * len(flips),
        in_specs=[pl.BlockSpec(memory_space=pltpu.VMEM)] * 2,
        out_specs=[pl.BlockSpec(memory_space=pltpu.VMEM)] * len(flips),
        compiler_params=pltpu.CompilerParams(vmem_limit_bytes=18 * 2**20),
        cost_estimate=pl.CostEstimate(
            flops=2 * PIXELS * 28 * W * 512 * scale, bytes_accessed=10**6, transcendentals=0
        ),
        name="grads_for",
    )(stack, weights)


def last_kernel(a, b, c, out):
    total = a[...].astype(F32) + b[...].astype(F32) + c[...].astype(F32)

    def put(at, value):
        out[at : at + 192, :] = value

    from_blocks(order_matrix(True), total.astype(BF16), put)


def last_sum(a, b, c):
    return pl.pallas_call(
        last_kernel,
        out_shape=jax.ShapeDtypeStruct((PIXELS, 512), BF16),
        in_specs=[pl.BlockSpec(memory_space=pltpu.VMEM)] * 3,
        out_specs=pl.BlockSpec(memory_space=pltpu.VMEM),
        compiler_params=pltpu.CompilerParams(vmem_limit_bytes=10 * 2**20),
        name="last_sum",
    )(a, b, c)


def flipped(x, bit):
    return lax.ppermute(x, "filt", [(i, i ^ bit) for i in range(lax.axis_size("filt"))])


def partner(r, bits):
    return r ^ bits if abs((r ^ bits) - r) <= 3 else r ^ {5: 2, 6: 1, 7: 1}[bits]


def swapped(x, bits):
    return lax.ppermute(x, "rows", [(r, partner(r, bits)) for r in range(8)])


def on_device(
    features, point_weight, dilated_weight, branch_bias, project_weight, project_bias, cotangent
):
    flat = features.reshape(PIXELS, CHANNELS)
    dilated = jnp.transpose(dilated_weight, (0, 1, 2, 4, 3)).reshape(27, W, CHANNELS)
    point = point_weight.T
    flat, dilated, point = (
        pltpu.with_memory_space_constraint(x, pltpu.HBM) for x in (flat, dilated, point)
    )
    *sums, ordered, weights = outward_sums(flat, dilated, point)
    received = {
        x: swapped(sums[n].astype(jnp.float16), x).astype(F32) for n, x in enumerate(SWAPS)
    }
    own = own_sums(ordered, weights, branch_bias)
    acts = [
        activations_of(part, swaps, own[part], [received[x] for x in swaps])
        for part, swaps in enumerate(PART_SWAPS)
    ]
    across = [flipped(x, 2) for x in acts]
    beside = [flipped(x, 1) for x in acts]
    corner = [flipped(x, 1) for x in across]
    near, ordered_cotangent = near_head(
        acts,
        beside,
        project_weight,
        project_bias.reshape(1, 256),
        cotangent.reshape(PIXELS, 256),
    )
    output, grads, *sends = far_head(
        acts, across, corner, project_weight, near, ordered_cotangent
    )
    arrived = [swapped(sends[n], x) for n, x in enumerate(GRAD_SWAPS)]
    stack = spread(grads, arrived)
    (far,) = grads_for((3,), stack, weights)
    far = flipped(far, 1)
    (kept,) = grads_for((2,), stack, weights)
    crossing = (far.astype(F32) + kept.astype(F32)).astype(BF16)
    crossed = flipped(crossing, 2)
    later, output, crossing = lax.optimization_barrier((stack, output, crossing))
    head_output = own_output(output)
    (near,) = grads_for((1,), later, weights)
    near = flipped(near, 1)
    (kept,) = grads_for((0,), later, weights, 8)
    feature_grad = last_sum(kept, near, crossed)
    return head_output.reshape(12, 48, W), feature_grad.reshape(12, 48, 512)


def solution(mesh):
    body = on_device if fits(mesh) else on_device_general
    in_specs = (
        P("rows", None, None),
        P(None, "filt"),
        P(None, None, None, None, "filt"),
        P(None, "filt"),
        P(),
        P(),
        P("rows", None, None),
    )
    out_specs = (P("rows", None, "filt"), P("rows", None, "filt"))
    return jax.shard_map(
        body, mesh=mesh, in_specs=in_specs, out_specs=out_specs, check_vma=False
    )
```

```python
import functools

import jax
import jax.numpy as jnp
from jax import lax
from jax.experimental import pallas as pl
from jax.experimental.pallas import tpu as pltpu
from jax.sharding import PartitionSpec as P

FIRST_DILATION = 12
SECOND_DILATION = 24
THIRD_DILATION = 36


def passed_along(x, axis, by):
    devices = lax.axis_size(axis)
    pairs = [(i, i + by) for i in range(devices) if 0 <= i + by < devices]
    return lax.ppermute(x, axis, pairs)


def shift_columns(field, amount):
    breadth = field.shape[1]
    if amount == 0:
        return field
    padding = [(0, 0)] * field.ndim
    if amount > 0:
        kept = field[:, amount:]
        padding[1] = (0, amount)
    else:
        kept = field[:, : breadth + amount]
        padding[1] = (-amount, 0)
    return jnp.pad(kept, padding)


def fetch_sums(field, offset):
    return passed_along(field, "rows", offset)


def fetch_grads(field, offset):
    return passed_along(field, "rows", offset)


def shift_rows(field, amount, fetcher):
    height = field.shape[0]
    quotient = amount // height

    def extract_block(offset):
        if offset == 0:
            return field
        return fetcher(field, offset)

    return extract_block(quotient)


def make_kernel_taps(variants, dilation_rates):
    stacked = [variants[:, :, 0]]
    for branch, dilation in enumerate(dilation_rates):
        for row_tap in range(3):
            source = variants[:, :, 1 + 3 * branch + row_tap]
            for col_tap in range(3):
                stacked.append(shift_columns(source, -(col_tap - 1) * dilation))
    return jnp.stack(stacked, 2)


def on_device_general(
    features, point_weight, dilated_weight, branch_bias, project_weight, project_bias, cotangent
):
    height, breadth, channels = features.shape
    pixels = height * breadth
    own_width = point_weight.shape[1]
    filters = lax.axis_size("filt")
    member = lax.axis_index("filt")
    branch_outputs = project_weight.shape[2]
    own_out = branch_outputs // filters
    own_channels = channels // filters
    dilation_rates = (FIRST_DILATION, SECOND_DILATION, THIRD_DILATION)
    all_weights = jnp.concatenate(
        [point_weight[None], dilated_weight.reshape(27, channels, own_width)], 0
    )
    flattened = features.reshape(pixels, channels)
    tap_terms = jnp.einsum(
        "pc,tco->pto", flattened, all_weights, preferred_element_type=jnp.float32
    )
    tap_terms = tap_terms.reshape(height, breadth, 28, own_width)
    pre_list = [tap_terms[:, :, 0, :] + branch_bias[0]]
    for branch, dilation in enumerate(dilation_rates):
        summed_result = jnp.zeros((height, breadth, own_width), jnp.float32)
        for row_tap in range(3):
            row_sum = jnp.zeros((height, breadth, own_width), jnp.float32)
            for col_tap in range(3):
                row_sum = row_sum + shift_columns(
                    tap_terms[:, :, 1 + 9 * branch + 3 * row_tap + col_tap, :],
                    (col_tap - 1) * dilation,
                )
            summed_result = summed_result + shift_rows(
                row_sum, -(row_tap - 1) * dilation, fetch_sums
            )
        pre_list.append(summed_result + branch_bias[branch + 1])
    branch_pre = jnp.stack(pre_list, 2)
    activations = jnp.maximum(branch_pre, 0.0).astype(jnp.bfloat16).reshape(pixels, 4 * own_width)
    grouped = project_weight.reshape(4, filters, own_width, branch_outputs)
    own_rows = lax.dynamic_index_in_dim(grouped, member, 1, keepdims=False).reshape(
        4 * own_width, branch_outputs
    )
    flat_cotangent = cotangent.reshape(pixels, branch_outputs)
    ordered = jnp.transpose(grouped, (1, 0, 2, 3)).reshape(filters * 4 * own_width, branch_outputs)
    project_pre = jnp.dot(
        lax.all_gather(activations, "filt", axis=1, tiled=True),
        ordered,
        preferred_element_type=jnp.float32,
    )
    project_pre = project_pre + project_bias
    head_grad = jnp.where(project_pre > 0, flat_cotangent.astype(jnp.float32), 0.0).astype(
        jnp.bfloat16
    )
    own_pre = lax.dynamic_slice_in_dim(project_pre, member * own_out, own_out, 1)
    act_grad = jnp.dot(head_grad, own_rows.T, preferred_element_type=jnp.float32)
    head_output = jnp.maximum(own_pre, 0.0).astype(jnp.bfloat16).reshape(height, breadth, own_out)
    branch_grad = jnp.where(
        branch_pre > 0, act_grad.reshape(height, breadth, 4, own_width), 0.0
    ).astype(jnp.bfloat16)
    variant_list = [branch_grad[:, :, 0, :]]
    for branch, dilation in enumerate(dilation_rates):
        for row_tap in range(3):
            variant_list.append(
                shift_rows(branch_grad[:, :, branch + 1, :], (row_tap - 1) * dilation, fetch_grads)
            )
    variants = jnp.stack(variant_list, 2)
    stacked = make_kernel_taps(variants, dilation_rates).reshape(pixels, 28, own_width)
    input_grad = lax.psum_scatter(
        jnp.einsum("pto,tco->cp", stacked, all_weights, preferred_element_type=jnp.float32),
        "filt",
        scatter_dimension=0,
        tiled=True,
    ).T
    feature_grad = input_grad.astype(jnp.bfloat16).reshape(height, breadth, own_channels)
    return (head_output, feature_grad)


W = 64
BLOCK = 144
PIXELS = 576
HALF = 288
SENT = 304
CHANNELS = 2048
F32 = jnp.float32
BF16 = jnp.bfloat16

OUT_PAIRS = ((3, 1), (1, 1), (3, 0), (1, 0), (3, 2), (1, 2), (2, 1), (2, 0), (2, 2))
TAPS = (
    [(k, 1, 1) for k in (1, 2, 3)]
    + [(k, i, j) for k, j in OUT_PAIRS for i in (0, 2)]
    + [(k, 1, j) for j in (0, 2) for k in (1, 2, 3)]
)
OUT_AT, LEFT_AT, RIGHT_AT = 4 * W, 22 * W, 25 * W
PARTS = ((0, 1), (2, 3))
PART_SWAPS = ((7, 3, 1), (6, 2, 5, 7, 3))
SWAPS = (1, 3, 7, 5, 2, 6)
GRAD_SWAPS = (7, 5, 6, 3, 1, 2)


def fits(mesh):
    return mesh.shape["rows"] == 8 and mesh.shape["filt"] == 4


def order_matrix(turned=False):
    to = lax.broadcasted_iota(jnp.int32, (192, 192), 1 if turned else 0)
    source = lax.broadcasted_iota(jnp.int32, (192, 192), 0 if turned else 1)

    def parts(value, width):
        return sum((value >= n * width).astype(jnp.int32) for n in (1, 2, 3))

    block = parts(to, 48)
    within = to - 48 * block
    line = parts(within, 12)
    wanted = line * 48 + block * 12 + within - 12 * line
    return (source == wanted).astype(F32).astype(BF16)


def tap_index(tap):
    k, i, j = tap
    return (k - 1) * 9 + i * 3 + j


def nt(a, b):
    return lax.dot_general(a, b, (((1,), (1,)), ((), ())), preferred_element_type=F32)


def nn(a, b):
    return lax.dot_general(a, b, (((1,), (0,)), ((), ())), preferred_element_type=F32)


def from_blocks(order_t, value, write):
    for g in range(3):
        parts = [value[m * BLOCK + g * 48 : m * BLOCK + g * 48 + 48] for m in range(4)]
        write(g * 192, nn(order_t, jnp.concatenate(parts, 0)).astype(BF16))


def low_lanes(shape):
    return lax.broadcasted_iota(jnp.int32, shape, 1) % 128 < W


def scaled(value):
    most = jnp.maximum(jnp.max(jnp.abs(value), axis=0, keepdims=True), 1e-30)
    power = jnp.floor(jnp.log(most) * 1.4426950408889634)
    return value * jnp.exp2(13.0 - power), power


def unscaled(sent):
    return sent[:HALF, :] * jnp.exp2(sent[HALF : HALF + 1, :] - 13.0)


def outward_slot(row, x):
    other = row ^ x
    apart = jnp.abs(other - row)
    slot = apart - 1 + jnp.where(other < row, 3, 0)
    return jnp.where(apart <= 3, slot, 0)


def fetch_tap(dilated, weights, sem, place):
    return pltpu.make_async_copy(
        dilated.at[tap_index(TAPS[place - 1])], weights.at[pl.ds(place * W, W)], sem
    )


def outward_kernel(features, dilated, point, *refs):
    row = lax.axis_index("rows")
    out, ordered, weights = refs[0:6], refs[6], refs[7]
    raw, sums, packed, feature_sems, weight_sems = refs[8:]
    loads = []
    for g in range(3):
        rows = pl.ds(g * 192, 192)
        loads.append(pltpu.make_async_copy(features.at[rows], raw.at[rows], feature_sems.at[g]))
        loads[-1].start()
    queue = [
        fetch_tap(dilated, weights, weight_sems.at[q], place)
        for q, place in enumerate((*range(4, 28), 1, 2, 3))
    ]
    queue.append(pltpu.make_async_copy(point, weights.at[pl.ds(0, W)], weight_sems.at[27]))

    def start_loads(first, last):
        for fetch in queue[first:last]:
            fetch.start()

    start_loads(0, 4)
    order = order_matrix()
    for g in range(3):
        loads[g].wait()
        start_loads((4, 12, 18)[g], (12, 18, 28)[g])
        moved = nn(order, raw[g * 192 : (g + 1) * 192, :]).astype(BF16)
        for m in range(4):
            at = m * BLOCK + g * 48
            ordered[at : at + 48, :] = moved[m * 48 : (m + 1) * 48]

    def product(pair, pairs, first, last):
        for fetch in queue[2 * pair : 2 * (pair + pairs)]:
            fetch.wait()
        at = OUT_AT + pair * 128
        return nt(ordered[first * BLOCK : last * BLOCK, :], weights[at : at + pairs * 128, :])

    d = product(0, 2, 0, 4)
    sums[2] = d[:, :128]
    sums[0] = d[:, 128:]
    d = product(2, 2, 0, 3)
    sums[2, 3 * BLOCK :, :] = sums[2, 3 * BLOCK :, :] + d[:BLOCK, :128]
    sums[0, BLOCK:, :] = sums[0, BLOCK:, :] + d[:, 128:]
    d = product(4, 2, 1, 4)
    sums[2, :BLOCK, :] = sums[2, :BLOCK, :] + d[2 * BLOCK :, :128]
    sums[0, : 3 * BLOCK, :] = sums[0, : 3 * BLOCK, :] + d[:, 128:]
    low = low_lanes((HALF, 128))

    def pack(k):
        top, bottom = sums[k, :HALF, :], sums[k, HALF:, :]
        halves = (
            jnp.where(low, top, pltpu.roll(bottom, W, 1)),
            jnp.where(low, pltpu.roll(top, W, 1), bottom),
        )
        for way, value in enumerate(halves):
            value, power = scaled(value)
            packed[k + 3 * way, :HALF, :] = value
            packed[k + 3 * way, HALF:, :] = jnp.broadcast_to(power, (SENT - HALF, 128))

    pack(2)
    pack(0)
    d = product(6, 3, 0, 4)
    sums[1] = d[:, :128]
    sums[1, 2 * BLOCK :, :] = sums[1, 2 * BLOCK :, :] + d[: 2 * BLOCK, 128:256]
    sums[1, : 2 * BLOCK, :] = sums[1, : 2 * BLOCK, :] + d[2 * BLOCK :, 256:]
    pack(1)
    for n, x in enumerate(SWAPS):
        out[n][...] = packed[outward_slot(row, x)]
    for fetch in queue[18:]:
        fetch.wait()


def outward_sums(features, dilated, point):
    return pl.pallas_call(
        outward_kernel,
        out_shape=[jax.ShapeDtypeStruct((SENT, 128), F32)] * 6
        + [pltpu.VMEM((PIXELS, CHANNELS), BF16), pltpu.VMEM((28 * W, CHANNELS), BF16)],
        in_specs=[pl.BlockSpec(memory_space=pltpu.HBM)] * 3,
        out_specs=[pl.BlockSpec(memory_space=pltpu.VMEM)] * 8,
        scratch_shapes=[
            pltpu.VMEM((PIXELS, CHANNELS), BF16),
            pltpu.VMEM((3, PIXELS, 128), F32),
            pltpu.VMEM((6, SENT, 128), F32),
            pltpu.SemaphoreType.DMA((3,)),
            pltpu.SemaphoreType.DMA((28,)),
        ],
        compiler_params=pltpu.CompilerParams(vmem_limit_bytes=28 * 2**20),
        name="outward_sums",
    )(features, dilated, point)


def own_kernel(ordered, weights, bias, *outs):
    d = nt(ordered[...], weights[:256, :])
    for part, out in enumerate(outs):
        line = jnp.concatenate([bias[k : k + 1, :] for k in PARTS[part]], 1)
        out[...] = d[:, part * 128 : part * 128 + 128] + line
    low = low_lanes((PIXELS, 128))

    def add(first, value, k):
        part = k // 2
        rows = slice(first * BLOCK, first * BLOCK + value.shape[0])
        mask, value = low[: value.shape[0]], value[:, part * 128 : part * 128 + 128]
        kept = jnp.where(mask, value, 0.0) if k == 2 else jnp.where(mask, 0.0, value)
        outs[part][rows, :] = outs[part][rows, :] + kept

    d = nt(ordered[: 3 * BLOCK, :], weights[LEFT_AT - W : LEFT_AT + 3 * W, :])
    for k in (1, 2, 3):
        add(k, d[: (4 - k) * BLOCK], k)
    d = nt(ordered[BLOCK:, :], weights[RIGHT_AT - W : RIGHT_AT + 3 * W, :])
    for k in (1, 2, 3):
        add(0, d[(k - 1) * BLOCK :], k)


def own_sums(ordered, weights, bias):
    return pl.pallas_call(
        own_kernel,
        out_shape=[jax.ShapeDtypeStruct((PIXELS, 128), F32)] * 2,
        in_specs=[pl.BlockSpec(memory_space=pltpu.VMEM)] * 3,
        out_specs=[pl.BlockSpec(memory_space=pltpu.VMEM)] * 2,
        compiler_params=pltpu.CompilerParams(vmem_limit_bytes=18 * 2**20),
        cost_estimate=pl.CostEstimate(flops=10**6, bytes_accessed=10**4, transcendentals=0),
        name="own_sums",
    )(ordered, weights, bias)


def arrival_slot(row, other):
    return jnp.where((other >= 0) & (other < 8), row ^ other, 0)


def gather_arrivals(recv, arrivals, swaps):
    arrivals[0] = jnp.zeros((HALF, 128), arrivals.dtype)
    for n, x in enumerate(swaps):
        arrivals[x] = unscaled(recv[n][...])


def activation_kernel(part, swaps, own, *refs):
    recv, acts, arrivals = refs[: len(swaps)], refs[-2], refs[-1]
    row = lax.axis_index("rows")
    gather_arrivals(recv, arrivals, swaps)
    low = low_lanes((HALF, 128))

    def total(k):
        return arrivals[arrival_slot(row, row - k)] + arrivals[arrival_slot(row, row + k)]

    high = total(PARTS[part][1])
    top, bottom = jnp.where(low, 0.0, pltpu.roll(high, W, 1)), jnp.where(low, 0.0, high)
    if part:
        left = total(PARTS[part][0])
        top = jnp.where(low, left, top)
        bottom = jnp.where(low, pltpu.roll(left, W, 1), bottom)
    acts[:HALF, :] = jnp.maximum(own[:HALF, :] + top, 0.0).astype(BF16)
    acts[HALF:, :] = jnp.maximum(own[HALF:, :] + bottom, 0.0).astype(BF16)


def activations_of(part, swaps, own, received):
    return pl.pallas_call(
        functools.partial(activation_kernel, part, swaps),
        out_shape=jax.ShapeDtypeStruct((PIXELS, 128), BF16),
        in_specs=[pl.BlockSpec(memory_space=pltpu.VMEM)] * (1 + len(swaps)),
        out_specs=pl.BlockSpec(memory_space=pltpu.VMEM),
        scratch_shapes=[pltpu.VMEM((8, HALF, 128), F32)],
        compiler_params=pltpu.CompilerParams(vmem_limit_bytes=8 * 2**20),
        name="activations",
    )(own, *received)


def project_rows(project, who):
    at = pl.multiple_of(who * W, W)
    return jnp.concatenate([project[k, pl.ds(at, W), :] for part in PARTS for k in part], 0)


def both(a, b):
    return jnp.concatenate([a[...], b[...]], 1)


def near_head_kernel(a0, b0, a1, b1, project, bias, cotangent, pre, ordered):
    member = lax.axis_index("filt")
    pre[...] = nn(both(a0, b0), project_rows(project, member)) + bias[...]
    pre[...] = pre[...] + nn(both(a1, b1), project_rows(project, member ^ 1))
    order = order_matrix()
    for g in range(3):
        moved = nn(order, cotangent[g * 192 : (g + 1) * 192, :])
        for m in range(4):
            at = m * BLOCK + g * 48
            ordered[at : at + 48, :] = moved[m * 48 : (m + 1) * 48]


def near_head(own, beside, project, bias, cotangent):
    return pl.pallas_call(
        near_head_kernel,
        out_shape=[jax.ShapeDtypeStruct((PIXELS, 256), F32)] * 2,
        in_specs=[pl.BlockSpec(memory_space=pltpu.VMEM)] * 7,
        out_specs=[pl.BlockSpec(memory_space=pltpu.VMEM)] * 2,
        compiler_params=pltpu.CompilerParams(vmem_limit_bytes=10 * 2**20),
        name="near_head",
    )(*own, *beside, project, bias, cotangent)


def far_head_kernel(a0, b0, a2, b2, a3, b3, project, near, cotangent, *refs):
    output, grads, sends, packed = refs[0], refs[1], refs[2:8], refs[8]
    row, member = lax.axis_index("rows"), lax.axis_index("filt")
    pre = near[...] + nn(both(a2, b2), project_rows(project, member ^ 2))
    pre = pre + nn(both(a3, b3), project_rows(project, member ^ 3))
    output[...] = jnp.maximum(pre, 0.0).astype(BF16)
    head_grad = jnp.where(pre > 0, cotangent[...], 0.0).astype(BF16)
    act_grad = nt(head_grad, project_rows(project, member))
    a = jnp.where(a0[...].astype(F32) > 0, act_grad[:, :128], 0.0)
    b = jnp.where(b0[...].astype(F32) > 0, act_grad[:, 128:], 0.0)
    grads[:, :128] = a.astype(BF16)
    grads[:, 128:] = b.astype(BF16)
    low = low_lanes((HALF, 128))
    packed[0] = jnp.where(low, pltpu.roll(a[:HALF], W, 1), a[HALF:]).astype(BF16)
    packed[1] = jnp.where(low, b[:HALF], pltpu.roll(b[HALF:], W, 1)).astype(BF16)
    packed[2] = jnp.where(low, pltpu.roll(b[:HALF], W, 1), b[HALF:]).astype(BF16)
    for n, x in enumerate(GRAD_SWAPS):
        apart = jnp.abs((row ^ x) - row)
        sends[n][...] = packed[jnp.where(apart <= 3, apart - 1, 0)]


def far_head(own, across, corner, project, near, cotangent):
    return pl.pallas_call(
        far_head_kernel,
        out_shape=[jax.ShapeDtypeStruct((PIXELS, 256), BF16)] * 2
        + [jax.ShapeDtypeStruct((HALF, 128), BF16)] * 6,
        in_specs=[pl.BlockSpec(memory_space=pltpu.VMEM)] * 9,
        out_specs=[pl.BlockSpec(memory_space=pltpu.VMEM)] * 8,
        scratch_shapes=[pltpu.VMEM((3, HALF, 128), BF16)],
        compiler_params=pltpu.CompilerParams(vmem_limit_bytes=12 * 2**20),
        name="far_head",
    )(*own, *across, *corner, project, near, cotangent)


def own_output_kernel(output, out):
    member = lax.axis_index("filt")
    mine = jnp.zeros((PIXELS, W), F32)
    for q in range(4):
        mine = jnp.where(member == q, output[:, q * W : (q + 1) * W].astype(F32), mine)

    def put(at, value):
        out[at : at + 192, :] = value

    from_blocks(order_matrix(True), mine.astype(BF16), put)


def own_output(output):
    return pl.pallas_call(
        own_output_kernel,
        out_shape=jax.ShapeDtypeStruct((PIXELS, W), BF16),
        in_specs=[pl.BlockSpec(memory_space=pltpu.VMEM)],
        out_specs=pl.BlockSpec(memory_space=pltpu.VMEM),
        compiler_params=pltpu.CompilerParams(vmem_limit_bytes=6 * 2**20),
        name="own_output",
    )(output)


def spread_kernel(own, *refs):
    recv, stack, arrivals, pairs, twice = refs[:6], *refs[6:]
    row = lax.axis_index("rows")
    arrivals[0] = jnp.zeros((HALF, 128), BF16)
    for n, x in enumerate(GRAD_SWAPS):
        arrivals[x] = recv[n][...]
    low = low_lanes((HALF, 128))
    low_all = low_lanes((PIXELS, 128))
    for k in (1, 2, 3):
        p = arrivals[arrival_slot(row, row + k)].astype(F32)
        m = arrivals[arrival_slot(row, row - k)].astype(F32)
        pairs[k - 1, :HALF, :] = jnp.where(low, p, pltpu.roll(m, W, 1)).astype(BF16)
        pairs[k - 1, HALF:, :] = jnp.where(low, pltpu.roll(p, W, 1), m).astype(BF16)
        g = own[:, :128].astype(F32) if k == 1 else own[:, 128:].astype(F32)
        other = pltpu.roll(g, W, 1)
        two = jnp.where(low_all, g, other) if k == 2 else jnp.where(low_all, other, g)
        twice[k - 1] = two.astype(BF16)
    stack[:, : 4 * W] = own[...]
    nothing = jnp.zeros((BLOCK, 128), BF16)

    def block_of(ref, k, source):
        if 0 <= source < 4:
            return ref[k - 1, source * BLOCK : (source + 1) * BLOCK, :]
        return nothing

    for q, (k, j) in enumerate(OUT_PAIRS):
        lanes = slice(OUT_AT + q * 128, OUT_AT + q * 128 + 128)
        for m in range(4):
            stack[m * BLOCK : (m + 1) * BLOCK, lanes] = block_of(pairs, k, m - (j - 1) * k)
    low_block = low_lanes((BLOCK, 128))
    for q, (a, b) in enumerate(((1, 2), (3, -1), (-2, -3))):
        lanes = slice(LEFT_AT + q * 128, LEFT_AT + q * 128 + 128)
        for m in range(4):
            stack[m * BLOCK : (m + 1) * BLOCK, lanes] = jnp.where(
                low_block, block_of(twice, abs(a), m + a), block_of(twice, abs(b), m + b)
            )


def spread(own, received):
    return pl.pallas_call(
        spread_kernel,
        out_shape=pltpu.VMEM((PIXELS, 28 * W), BF16),
        in_specs=[pl.BlockSpec(memory_space=pltpu.VMEM)] * 7,
        out_specs=pl.BlockSpec(memory_space=pltpu.VMEM),
        scratch_shapes=[
            pltpu.VMEM((8, HALF, 128), BF16),
            pltpu.VMEM((3, PIXELS, 128), BF16),
            pltpu.VMEM((3, PIXELS, 128), BF16),
        ],
        compiler_params=pltpu.CompilerParams(vmem_limit_bytes=12 * 2**20),
        name="spread",
    )(own, *received)


def grad_kernel(flip, first, stack, weights, out):
    member = lax.axis_index("filt")
    columns = pl.ds(pl.multiple_of((member ^ flip) * 512 + first, 256), out.shape[1])
    out[...] = nn(stack[...], weights[:, columns]).astype(BF16)


def grads_for(flip, stack, weights, first=0, width=512, scale=1):
    return pl.pallas_call(
        functools.partial(grad_kernel, flip, first),
        out_shape=jax.ShapeDtypeStruct((PIXELS, width), BF16),
        in_specs=[pl.BlockSpec(memory_space=pltpu.VMEM)] * 2,
        out_specs=pl.BlockSpec(memory_space=pltpu.VMEM),
        compiler_params=pltpu.CompilerParams(vmem_limit_bytes=18 * 2**20),
        cost_estimate=pl.CostEstimate(
            flops=2 * PIXELS * 28 * W * width * scale, bytes_accessed=10**6, transcendentals=0
        ),
        name="grads_for",
    )(stack, weights)


def last_kernel(a, b, c, d, out):
    total = a[...].astype(F32) + b[...].astype(F32) + both(c, d).astype(F32)

    def put(at, value):
        out[at : at + 192, :] = value

    from_blocks(order_matrix(True), total.astype(BF16), put)


def last_sum(a, b, c, d):
    return pl.pallas_call(
        last_kernel,
        out_shape=jax.ShapeDtypeStruct((PIXELS, 512), BF16),
        in_specs=[pl.BlockSpec(memory_space=pltpu.VMEM)] * 4,
        out_specs=pl.BlockSpec(memory_space=pltpu.VMEM),
        compiler_params=pltpu.CompilerParams(vmem_limit_bytes=10 * 2**20),
        name="last_sum",
    )(a, b, c, d)


def flipped(x, bit):
    return lax.ppermute(x, "filt", [(i, i ^ bit) for i in range(lax.axis_size("filt"))])


def partner(r, bits):
    return r ^ bits if abs((r ^ bits) - r) <= 3 else r ^ {5: 2, 6: 1, 7: 1}[bits]


def swapped(x, bits):
    return lax.ppermute(x, "rows", [(r, partner(r, bits)) for r in range(8)])


def on_device(
    features, point_weight, dilated_weight, branch_bias, project_weight, project_bias, cotangent
):
    flat = features.reshape(PIXELS, CHANNELS)
    dilated = jnp.transpose(dilated_weight, (0, 1, 2, 4, 3)).reshape(27, W, CHANNELS)
    point = point_weight.T
    flat, dilated, point = (
        pltpu.with_memory_space_constraint(x, pltpu.HBM) for x in (flat, dilated, point)
    )
    *sums, ordered, weights = outward_sums(flat, dilated, point)
    received = {
        x: swapped(sums[n].astype(jnp.float16), x).astype(F32) for n, x in enumerate(SWAPS)
    }
    own = own_sums(ordered, weights, branch_bias)
    acts = [
        activations_of(part, swaps, own[part], [received[x] for x in swaps])
        for part, swaps in enumerate(PART_SWAPS)
    ]
    across = [flipped(x, 2) for x in acts]
    beside = [flipped(x, 1) for x in acts]
    corner = [flipped(x, 1) for x in across]
    near, ordered_cotangent = near_head(
        acts,
        beside,
        project_weight,
        project_bias.reshape(1, 256),
        cotangent.reshape(PIXELS, 256),
    )
    output, grads, *sends = far_head(
        acts, across, corner, project_weight, near, ordered_cotangent
    )
    arrived = [swapped(sends[n], x) for n, x in enumerate(GRAD_SWAPS)]
    stack = spread(grads, arrived)
    far = [flipped(grads_for(3, stack, weights, at, 256), 1) for at in (0, 256)]
    kept = grads_for(2, stack, weights, 0, 256)
    crossing = (far[0].astype(F32) + kept.astype(F32)).astype(BF16)
    crossed = [flipped(crossing, 2)]
    later, crossing = lax.optimization_barrier((stack, crossing))
    kept = grads_for(2, later, weights, 256, 256)
    crossing = (far[1].astype(F32) + kept.astype(F32)).astype(BF16)
    crossed.append(flipped(crossing, 2))
    later, output, crossing = lax.optimization_barrier((stack, output, crossing))
    head_output = own_output(output)
    near = flipped(grads_for(1, later, weights), 1)
    kept = grads_for(0, later, weights, scale=8)
    feature_grad = last_sum(kept, near, *crossed)
    return head_output.reshape(12, 48, W), feature_grad.reshape(12, 48, 512)


def solution(mesh):
    body = on_device if fits(mesh) else on_device_general
    in_specs = (
        P("rows", None, None),
        P(None, "filt"),
        P(None, None, None, None, "filt"),
        P(None, "filt"),
        P(),
        P(),
        P("rows", None, None),
    )
    out_specs = (P("rows", None, "filt"), P("rows", None, "filt"))
    return jax.shard_map(
        body, mesh=mesh, in_specs=in_specs, out_specs=out_specs, check_vma=False
    )
```

```python
import functools

import jax
import jax.numpy as jnp
from jax import lax
from jax.experimental import pallas as pl
from jax.experimental.pallas import tpu as pltpu
from jax.sharding import PartitionSpec as P

FIRST_DILATION = 12
SECOND_DILATION = 24
THIRD_DILATION = 36


def passed_along(x, axis, by):
    devices = lax.axis_size(axis)
    pairs = [(i, i + by) for i in range(devices) if 0 <= i + by < devices]
    return lax.ppermute(x, axis, pairs)


def shift_columns(field, amount):
    breadth = field.shape[1]
    if amount == 0:
        return field
    padding = [(0, 0)] * field.ndim
    if amount > 0:
        kept = field[:, amount:]
        padding[1] = (0, amount)
    else:
        kept = field[:, : breadth + amount]
        padding[1] = (-amount, 0)
    return jnp.pad(kept, padding)


def fetch_sums(field, offset):
    return passed_along(field, "rows", offset)


def fetch_grads(field, offset):
    return passed_along(field, "rows", offset)


def shift_rows(field, amount, fetcher):
    height = field.shape[0]
    quotient = amount // height

    def extract_block(offset):
        if offset == 0:
            return field
        return fetcher(field, offset)

    return extract_block(quotient)


def make_kernel_taps(variants, dilation_rates):
    stacked = [variants[:, :, 0]]
    for branch, dilation in enumerate(dilation_rates):
        for row_tap in range(3):
            source = variants[:, :, 1 + 3 * branch + row_tap]
            for col_tap in range(3):
                stacked.append(shift_columns(source, -(col_tap - 1) * dilation))
    return jnp.stack(stacked, 2)


def on_device_general(
    features, point_weight, dilated_weight, branch_bias, project_weight, project_bias, cotangent
):
    height, breadth, channels = features.shape
    pixels = height * breadth
    own_width = point_weight.shape[1]
    filters = lax.axis_size("filt")
    member = lax.axis_index("filt")
    branch_outputs = project_weight.shape[2]
    own_out = branch_outputs // filters
    own_channels = channels // filters
    dilation_rates = (FIRST_DILATION, SECOND_DILATION, THIRD_DILATION)
    all_weights = jnp.concatenate(
        [point_weight[None], dilated_weight.reshape(27, channels, own_width)], 0
    )
    flattened = features.reshape(pixels, channels)
    tap_terms = jnp.einsum(
        "pc,tco->pto", flattened, all_weights, preferred_element_type=jnp.float32
    )
    tap_terms = tap_terms.reshape(height, breadth, 28, own_width)
    pre_list = [tap_terms[:, :, 0, :] + branch_bias[0]]
    for branch, dilation in enumerate(dilation_rates):
        summed_result = jnp.zeros((height, breadth, own_width), jnp.float32)
        for row_tap in range(3):
            row_sum = jnp.zeros((height, breadth, own_width), jnp.float32)
            for col_tap in range(3):
                row_sum = row_sum + shift_columns(
                    tap_terms[:, :, 1 + 9 * branch + 3 * row_tap + col_tap, :],
                    (col_tap - 1) * dilation,
                )
            summed_result = summed_result + shift_rows(
                row_sum, -(row_tap - 1) * dilation, fetch_sums
            )
        pre_list.append(summed_result + branch_bias[branch + 1])
    branch_pre = jnp.stack(pre_list, 2)
    activations = jnp.maximum(branch_pre, 0.0).astype(jnp.bfloat16).reshape(pixels, 4 * own_width)
    grouped = project_weight.reshape(4, filters, own_width, branch_outputs)
    own_rows = lax.dynamic_index_in_dim(grouped, member, 1, keepdims=False).reshape(
        4 * own_width, branch_outputs
    )
    flat_cotangent = cotangent.reshape(pixels, branch_outputs)
    ordered = jnp.transpose(grouped, (1, 0, 2, 3)).reshape(filters * 4 * own_width, branch_outputs)
    project_pre = jnp.dot(
        lax.all_gather(activations, "filt", axis=1, tiled=True),
        ordered,
        preferred_element_type=jnp.float32,
    )
    project_pre = project_pre + project_bias
    head_grad = jnp.where(project_pre > 0, flat_cotangent.astype(jnp.float32), 0.0).astype(
        jnp.bfloat16
    )
    own_pre = lax.dynamic_slice_in_dim(project_pre, member * own_out, own_out, 1)
    act_grad = jnp.dot(head_grad, own_rows.T, preferred_element_type=jnp.float32)
    head_output = jnp.maximum(own_pre, 0.0).astype(jnp.bfloat16).reshape(height, breadth, own_out)
    branch_grad = jnp.where(
        branch_pre > 0, act_grad.reshape(height, breadth, 4, own_width), 0.0
    ).astype(jnp.bfloat16)
    variant_list = [branch_grad[:, :, 0, :]]
    for branch, dilation in enumerate(dilation_rates):
        for row_tap in range(3):
            variant_list.append(
                shift_rows(branch_grad[:, :, branch + 1, :], (row_tap - 1) * dilation, fetch_grads)
            )
    variants = jnp.stack(variant_list, 2)
    stacked = make_kernel_taps(variants, dilation_rates).reshape(pixels, 28, own_width)
    input_grad = lax.psum_scatter(
        jnp.einsum("pto,tco->cp", stacked, all_weights, preferred_element_type=jnp.float32),
        "filt",
        scatter_dimension=0,
        tiled=True,
    ).T
    feature_grad = input_grad.astype(jnp.bfloat16).reshape(height, breadth, own_channels)
    return (head_output, feature_grad)


W = 64
BLOCK = 144
PIXELS = 576
HALF = 288
SENT = 304
CHANNELS = 2048
F32 = jnp.float32
BF16 = jnp.bfloat16

OUT_PAIRS = ((3, 1), (1, 1), (3, 0), (1, 0), (3, 2), (1, 2), (2, 1), (2, 0), (2, 2))
TAPS = (
    [(k, 1, 1) for k in (1, 2, 3)]
    + [(k, i, j) for k, j in OUT_PAIRS for i in (0, 2)]
    + [(k, 1, j) for j in (0, 2) for k in (1, 2, 3)]
)
OUT_AT, LEFT_AT, RIGHT_AT = 4 * W, 22 * W, 25 * W
PARTS = ((0, 1), (2, 3))
PART_SWAPS = ((7, 3, 1), (6, 2, 5, 7, 3))
SWAPS = (1, 3, 7, 5, 2, 6)
GRAD_SWAPS = (7, 5, 6, 3, 1, 2)


def fits(mesh):
    return mesh.shape["rows"] == 8 and mesh.shape["filt"] == 4


def order_matrix(turned=False):
    to = lax.broadcasted_iota(jnp.int32, (192, 192), 1 if turned else 0)
    source = lax.broadcasted_iota(jnp.int32, (192, 192), 0 if turned else 1)

    def parts(value, width):
        return sum((value >= n * width).astype(jnp.int32) for n in (1, 2, 3))

    block = parts(to, 48)
    within = to - 48 * block
    line = parts(within, 12)
    wanted = line * 48 + block * 12 + within - 12 * line
    return (source == wanted).astype(F32).astype(BF16)


def tap_index(tap):
    k, i, j = tap
    return (k - 1) * 9 + i * 3 + j


def nt(a, b):
    return lax.dot_general(a, b, (((1,), (1,)), ((), ())), preferred_element_type=F32)


def nn(a, b):
    return lax.dot_general(a, b, (((1,), (0,)), ((), ())), preferred_element_type=F32)


def from_blocks(order_t, value, write):
    for g in range(3):
        parts = [value[m * BLOCK + g * 48 : m * BLOCK + g * 48 + 48] for m in range(4)]
        write(g * 192, nn(order_t, jnp.concatenate(parts, 0)).astype(BF16))


def low_lanes(shape):
    return lax.broadcasted_iota(jnp.int32, shape, 1) % 128 < W


def scaled(value):
    most = jnp.maximum(jnp.max(jnp.abs(value), axis=0, keepdims=True), 1e-30)
    power = jnp.floor(jnp.log(most) * 1.4426950408889634)
    return value * jnp.exp2(13.0 - power), power


def unscaled(sent):
    return sent[:HALF, :] * jnp.exp2(sent[HALF : HALF + 1, :] - 13.0)


def outward_slot(row, x):
    other = row ^ x
    apart = jnp.abs(other - row)
    slot = apart - 1 + jnp.where(other < row, 3, 0)
    return jnp.where(apart <= 3, slot, 0)


def fetch_tap(dilated, weights, sem, place):
    return pltpu.make_async_copy(
        dilated.at[tap_index(TAPS[place - 1])], weights.at[pl.ds(place * W, W)], sem
    )


def outward_kernel(features, dilated, point, *refs):
    row = lax.axis_index("rows")
    out, ordered, weights = refs[0:6], refs[6], refs[7]
    raw, sums, packed, feature_sems, weight_sems = refs[8:]
    loads = []
    for g in range(12):
        rows = pl.ds(g * 48, 48)
        loads.append(pltpu.make_async_copy(features.at[rows], raw.at[rows], feature_sems.at[g]))
        loads[-1].start()
    queue = [
        fetch_tap(dilated, weights, weight_sems.at[q], place)
        for q, place in enumerate((*range(4, 28), 1, 2, 3))
    ]
    queue.append(pltpu.make_async_copy(point, weights.at[pl.ds(0, W)], weight_sems.at[27]))

    def start_loads(first, last):
        for fetch in queue[first:last]:
            fetch.start()

    order = order_matrix()
    for g in range(3):
        for load in loads[4 * g : 4 * g + 4]:
            load.wait()
        start_loads((0, 8, 18)[g], (8, 18, 28)[g])
        moved = nn(order, raw[g * 192 : (g + 1) * 192, :]).astype(BF16)
        for m in range(4):
            at = m * BLOCK + g * 48
            ordered[at : at + 48, :] = moved[m * 48 : (m + 1) * 48]

    def product(pair, pairs, first, last):
        for fetch in queue[2 * pair : 2 * (pair + pairs)]:
            fetch.wait()
        at = OUT_AT + pair * 128
        return nt(ordered[first * BLOCK : last * BLOCK, :], weights[at : at + pairs * 128, :])

    d = product(0, 2, 0, 4)
    sums[2] = d[:, :128]
    sums[0] = d[:, 128:]
    d = product(2, 2, 0, 3)
    sums[2, 3 * BLOCK :, :] = sums[2, 3 * BLOCK :, :] + d[:BLOCK, :128]
    sums[0, BLOCK:, :] = sums[0, BLOCK:, :] + d[:, 128:]
    d = product(4, 2, 1, 4)
    sums[2, :BLOCK, :] = sums[2, :BLOCK, :] + d[2 * BLOCK :, :128]
    sums[0, : 3 * BLOCK, :] = sums[0, : 3 * BLOCK, :] + d[:, 128:]
    low = low_lanes((HALF, 128))

    def pack(k):
        top, bottom = sums[k, :HALF, :], sums[k, HALF:, :]
        halves = (
            jnp.where(low, top, pltpu.roll(bottom, W, 1)),
            jnp.where(low, pltpu.roll(top, W, 1), bottom),
        )
        for way, value in enumerate(halves):
            value, power = scaled(value)
            packed[k + 3 * way, :HALF, :] = value
            packed[k + 3 * way, HALF:, :] = jnp.broadcast_to(power, (SENT - HALF, 128))

    pack(2)
    pack(0)
    d = product(6, 3, 0, 4)
    sums[1] = d[:, :128]
    sums[1, 2 * BLOCK :, :] = sums[1, 2 * BLOCK :, :] + d[: 2 * BLOCK, 128:256]
    sums[1, : 2 * BLOCK, :] = sums[1, : 2 * BLOCK, :] + d[2 * BLOCK :, 256:]
    pack(1)
    for n, x in enumerate(SWAPS):
        out[n][...] = packed[outward_slot(row, x)]
    for fetch in queue[18:]:
        fetch.wait()


def outward_sums(features, dilated, point):
    return pl.pallas_call(
        outward_kernel,
        out_shape=[jax.ShapeDtypeStruct((SENT, 128), F32)] * 6
        + [pltpu.VMEM((PIXELS, CHANNELS), BF16), pltpu.VMEM((28 * W, CHANNELS), BF16)],
        in_specs=[pl.BlockSpec(memory_space=pltpu.HBM)] * 3,
        out_specs=[pl.BlockSpec(memory_space=pltpu.VMEM)] * 8,
        scratch_shapes=[
            pltpu.VMEM((PIXELS, CHANNELS), BF16),
            pltpu.VMEM((3, PIXELS, 128), F32),
            pltpu.VMEM((6, SENT, 128), F32),
            pltpu.SemaphoreType.DMA((12,)),
            pltpu.SemaphoreType.DMA((28,)),
        ],
        compiler_params=pltpu.CompilerParams(vmem_limit_bytes=28 * 2**20),
        name="outward_sums",
    )(features, dilated, point)


def own_kernel(ordered, weights, bias, *outs):
    d = nt(ordered[...], weights[:256, :])
    for part, out in enumerate(outs):
        line = jnp.concatenate([bias[k : k + 1, :] for k in PARTS[part]], 1)
        out[...] = d[:, part * 128 : part * 128 + 128] + line
    low = low_lanes((PIXELS, 128))

    def add(first, value, k):
        part = k // 2
        rows = slice(first * BLOCK, first * BLOCK + value.shape[0])
        mask, value = low[: value.shape[0]], value[:, part * 128 : part * 128 + 128]
        kept = jnp.where(mask, value, 0.0) if k == 2 else jnp.where(mask, 0.0, value)
        outs[part][rows, :] = outs[part][rows, :] + kept

    d = nt(ordered[: 3 * BLOCK, :], weights[LEFT_AT - W : LEFT_AT + 3 * W, :])
    for k in (1, 2, 3):
        add(k, d[: (4 - k) * BLOCK], k)
    d = nt(ordered[BLOCK:, :], weights[RIGHT_AT - W : RIGHT_AT + 3 * W, :])
    for k in (1, 2, 3):
        add(0, d[(k - 1) * BLOCK :], k)


def own_sums(ordered, weights, bias):
    return pl.pallas_call(
        own_kernel,
        out_shape=[jax.ShapeDtypeStruct((PIXELS, 128), F32)] * 2,
        in_specs=[pl.BlockSpec(memory_space=pltpu.VMEM)] * 3,
        out_specs=[pl.BlockSpec(memory_space=pltpu.VMEM)] * 2,
        compiler_params=pltpu.CompilerParams(vmem_limit_bytes=18 * 2**20),
        cost_estimate=pl.CostEstimate(flops=10**6, bytes_accessed=10**4, transcendentals=0),
        name="own_sums",
    )(ordered, weights, bias)


def arrival_slot(row, other):
    return jnp.where((other >= 0) & (other < 8), row ^ other, 0)


def gather_arrivals(recv, arrivals, swaps):
    arrivals[0] = jnp.zeros((HALF, 128), arrivals.dtype)
    for n, x in enumerate(swaps):
        arrivals[x] = unscaled(recv[n][...])


def activation_kernel(part, swaps, own, *refs):
    recv, acts, arrivals = refs[: len(swaps)], refs[-2], refs[-1]
    row = lax.axis_index("rows")
    gather_arrivals(recv, arrivals, swaps)
    low = low_lanes((HALF, 128))

    def total(k):
        return arrivals[arrival_slot(row, row - k)] + arrivals[arrival_slot(row, row + k)]

    high = total(PARTS[part][1])
    top, bottom = jnp.where(low, 0.0, pltpu.roll(high, W, 1)), jnp.where(low, 0.0, high)
    if part:
        left = total(PARTS[part][0])
        top = jnp.where(low, left, top)
        bottom = jnp.where(low, pltpu.roll(left, W, 1), bottom)
    acts[:HALF, :] = jnp.maximum(own[:HALF, :] + top, 0.0).astype(BF16)
    acts[HALF:, :] = jnp.maximum(own[HALF:, :] + bottom, 0.0).astype(BF16)


def activations_of(part, swaps, own, received):
    return pl.pallas_call(
        functools.partial(activation_kernel, part, swaps),
        out_shape=jax.ShapeDtypeStruct((PIXELS, 128), BF16),
        in_specs=[pl.BlockSpec(memory_space=pltpu.VMEM)] * (1 + len(swaps)),
        out_specs=pl.BlockSpec(memory_space=pltpu.VMEM),
        scratch_shapes=[pltpu.VMEM((8, HALF, 128), F32)],
        compiler_params=pltpu.CompilerParams(vmem_limit_bytes=8 * 2**20),
        name="activations",
    )(own, *received)


def project_rows(project, who):
    at = pl.multiple_of(who * W, W)
    return jnp.concatenate([project[k, pl.ds(at, W), :] for part in PARTS for k in part], 0)


def both(a, b):
    return jnp.concatenate([a[...], b[...]], 1)


def near_head_kernel(a0, b0, a1, b1, project, bias, cotangent, pre, ordered):
    member = lax.axis_index("filt")
    pre[...] = nn(both(a0, b0), project_rows(project, member)) + bias[...]
    pre[...] = pre[...] + nn(both(a1, b1), project_rows(project, member ^ 1))
    order = order_matrix()
    for g in range(3):
        moved = nn(order, cotangent[g * 192 : (g + 1) * 192, :])
        for m in range(4):
            at = m * BLOCK + g * 48
            ordered[at : at + 48, :] = moved[m * 48 : (m + 1) * 48]


def near_head(own, beside, project, bias, cotangent):
    return pl.pallas_call(
        near_head_kernel,
        out_shape=[jax.ShapeDtypeStruct((PIXELS, 256), F32)] * 2,
        in_specs=[pl.BlockSpec(memory_space=pltpu.VMEM)] * 7,
        out_specs=[pl.BlockSpec(memory_space=pltpu.VMEM)] * 2,
        compiler_params=pltpu.CompilerParams(vmem_limit_bytes=10 * 2**20),
        name="near_head",
    )(*own, *beside, project, bias, cotangent)


def far_head_kernel(a0, b0, a2, b2, a3, b3, project, near, cotangent, *refs):
    output, grads, sends, packed = refs[0], refs[1], refs[2:8], refs[8]
    row, member = lax.axis_index("rows"), lax.axis_index("filt")
    pre = near[...] + nn(both(a2, b2), project_rows(project, member ^ 2))
    pre = pre + nn(both(a3, b3), project_rows(project, member ^ 3))
    output[...] = jnp.maximum(pre, 0.0).astype(BF16)
    head_grad = jnp.where(pre > 0, cotangent[...], 0.0).astype(BF16)
    act_grad = nt(head_grad, project_rows(project, member))
    a = jnp.where(a0[...].astype(F32) > 0, act_grad[:, :128], 0.0)
    b = jnp.where(b0[...].astype(F32) > 0, act_grad[:, 128:], 0.0)
    grads[:, :128] = a.astype(BF16)
    grads[:, 128:] = b.astype(BF16)
    low = low_lanes((HALF, 128))
    packed[0] = jnp.where(low, pltpu.roll(a[:HALF], W, 1), a[HALF:]).astype(BF16)
    packed[1] = jnp.where(low, b[:HALF], pltpu.roll(b[HALF:], W, 1)).astype(BF16)
    packed[2] = jnp.where(low, pltpu.roll(b[:HALF], W, 1), b[HALF:]).astype(BF16)
    for n, x in enumerate(GRAD_SWAPS):
        apart = jnp.abs((row ^ x) - row)
        sends[n][...] = packed[jnp.where(apart <= 3, apart - 1, 0)]


def far_head(own, across, corner, project, near, cotangent):
    return pl.pallas_call(
        far_head_kernel,
        out_shape=[jax.ShapeDtypeStruct((PIXELS, 256), BF16)] * 2
        + [jax.ShapeDtypeStruct((HALF, 128), BF16)] * 6,
        in_specs=[pl.BlockSpec(memory_space=pltpu.VMEM)] * 9,
        out_specs=[pl.BlockSpec(memory_space=pltpu.VMEM)] * 8,
        scratch_shapes=[pltpu.VMEM((3, HALF, 128), BF16)],
        compiler_params=pltpu.CompilerParams(vmem_limit_bytes=12 * 2**20),
        name="far_head",
    )(*own, *across, *corner, project, near, cotangent)


def own_output_kernel(output, out):
    member = lax.axis_index("filt")
    mine = jnp.zeros((PIXELS, W), F32)
    for q in range(4):
        mine = jnp.where(member == q, output[:, q * W : (q + 1) * W].astype(F32), mine)

    def put(at, value):
        out[at : at + 192, :] = value

    from_blocks(order_matrix(True), mine.astype(BF16), put)


def own_output(output):
    return pl.pallas_call(
        own_output_kernel,
        out_shape=jax.ShapeDtypeStruct((PIXELS, W), BF16),
        in_specs=[pl.BlockSpec(memory_space=pltpu.VMEM)],
        out_specs=pl.BlockSpec(memory_space=pltpu.VMEM),
        compiler_params=pltpu.CompilerParams(vmem_limit_bytes=6 * 2**20),
        name="own_output",
    )(output)


def spread_kernel(own, *refs):
    recv, stack, arrivals, pairs, twice = refs[:6], *refs[6:]
    row = lax.axis_index("rows")
    arrivals[0] = jnp.zeros((HALF, 128), BF16)
    for n, x in enumerate(GRAD_SWAPS):
        arrivals[x] = recv[n][...]
    low = low_lanes((HALF, 128))
    low_all = low_lanes((PIXELS, 128))
    for k in (1, 2, 3):
        p = arrivals[arrival_slot(row, row + k)].astype(F32)
        m = arrivals[arrival_slot(row, row - k)].astype(F32)
        pairs[k - 1, :HALF, :] = jnp.where(low, p, pltpu.roll(m, W, 1)).astype(BF16)
        pairs[k - 1, HALF:, :] = jnp.where(low, pltpu.roll(p, W, 1), m).astype(BF16)
        g = own[:, :128].astype(F32) if k == 1 else own[:, 128:].astype(F32)
        other = pltpu.roll(g, W, 1)
        two = jnp.where(low_all, g, other) if k == 2 else jnp.where(low_all, other, g)
        twice[k - 1] = two.astype(BF16)
    stack[:, : 4 * W] = own[...]
    nothing = jnp.zeros((BLOCK, 128), BF16)

    def block_of(ref, k, source):
        if 0 <= source < 4:
            return ref[k - 1, source * BLOCK : (source + 1) * BLOCK, :]
        return nothing

    for q, (k, j) in enumerate(OUT_PAIRS):
        lanes = slice(OUT_AT + q * 128, OUT_AT + q * 128 + 128)
        for m in range(4):
            stack[m * BLOCK : (m + 1) * BLOCK, lanes] = block_of(pairs, k, m - (j - 1) * k)
    low_block = low_lanes((BLOCK, 128))
    for q, (a, b) in enumerate(((1, 2), (3, -1), (-2, -3))):
        lanes = slice(LEFT_AT + q * 128, LEFT_AT + q * 128 + 128)
        for m in range(4):
            stack[m * BLOCK : (m + 1) * BLOCK, lanes] = jnp.where(
                low_block, block_of(twice, abs(a), m + a), block_of(twice, abs(b), m + b)
            )


def spread(own, received):
    return pl.pallas_call(
        spread_kernel,
        out_shape=pltpu.VMEM((PIXELS, 28 * W), BF16),
        in_specs=[pl.BlockSpec(memory_space=pltpu.VMEM)] * 7,
        out_specs=pl.BlockSpec(memory_space=pltpu.VMEM),
        scratch_shapes=[
            pltpu.VMEM((8, HALF, 128), BF16),
            pltpu.VMEM((3, PIXELS, 128), BF16),
            pltpu.VMEM((3, PIXELS, 128), BF16),
        ],
        compiler_params=pltpu.CompilerParams(vmem_limit_bytes=12 * 2**20),
        name="spread",
    )(own, *received)


def grad_kernel(flip, first, stack, weights, out):
    member = lax.axis_index("filt")
    columns = pl.ds(pl.multiple_of((member ^ flip) * 512 + first, 256), out.shape[1])
    out[...] = nn(stack[...], weights[:, columns]).astype(BF16)


def grads_for(flip, stack, weights, first=0, width=512, scale=1):
    return pl.pallas_call(
        functools.partial(grad_kernel, flip, first),
        out_shape=jax.ShapeDtypeStruct((PIXELS, width), BF16),
        in_specs=[pl.BlockSpec(memory_space=pltpu.VMEM)] * 2,
        out_specs=pl.BlockSpec(memory_space=pltpu.VMEM),
        compiler_params=pltpu.CompilerParams(vmem_limit_bytes=18 * 2**20),
        cost_estimate=pl.CostEstimate(
            flops=2 * PIXELS * 28 * W * width * scale, bytes_accessed=10**6, transcendentals=0
        ),
        name="grads_for",
    )(stack, weights)


def last_kernel(a, b, c, d, out):
    total = a[...].astype(F32) + b[...].astype(F32) + both(c, d).astype(F32)

    def put(at, value):
        out[at : at + 192, :] = value

    from_blocks(order_matrix(True), total.astype(BF16), put)


def last_sum(a, b, c, d):
    return pl.pallas_call(
        last_kernel,
        out_shape=jax.ShapeDtypeStruct((PIXELS, 512), BF16),
        in_specs=[pl.BlockSpec(memory_space=pltpu.VMEM)] * 4,
        out_specs=pl.BlockSpec(memory_space=pltpu.VMEM),
        compiler_params=pltpu.CompilerParams(vmem_limit_bytes=10 * 2**20),
        name="last_sum",
    )(a, b, c, d)


def flipped(x, bit):
    return lax.ppermute(x, "filt", [(i, i ^ bit) for i in range(lax.axis_size("filt"))])


def partner(r, bits):
    return r ^ bits if abs((r ^ bits) - r) <= 3 else r ^ {5: 2, 6: 1, 7: 1}[bits]


def swapped(x, bits):
    return lax.ppermute(x, "rows", [(r, partner(r, bits)) for r in range(8)])


def on_device(
    features, point_weight, dilated_weight, branch_bias, project_weight, project_bias, cotangent
):
    flat = features.reshape(PIXELS, CHANNELS)
    dilated = jnp.transpose(dilated_weight, (0, 1, 2, 4, 3)).reshape(27, W, CHANNELS)
    point = point_weight.T
    flat, dilated, point = (
        pltpu.with_memory_space_constraint(x, pltpu.HBM) for x in (flat, dilated, point)
    )
    *sums, ordered, weights = outward_sums(flat, dilated, point)
    received = {
        x: swapped(sums[n].astype(jnp.float16), x).astype(F32) for n, x in enumerate(SWAPS)
    }
    own = own_sums(ordered, weights, branch_bias)
    acts = [
        activations_of(part, swaps, own[part], [received[x] for x in swaps])
        for part, swaps in enumerate(PART_SWAPS)
    ]
    across = [flipped(x, 2) for x in acts]
    beside = [flipped(x, 1) for x in acts]
    corner = [flipped(x, 1) for x in across]
    near, ordered_cotangent = near_head(
        acts,
        beside,
        project_weight,
        project_bias.reshape(1, 256),
        cotangent.reshape(PIXELS, 256),
    )
    output, grads, *sends = far_head(
        acts, across, corner, project_weight, near, ordered_cotangent
    )
    arrived = [swapped(sends[n], x) for n, x in enumerate(GRAD_SWAPS)]
    stack = spread(grads, arrived)
    far = [flipped(grads_for(3, stack, weights, at, 256), 1) for at in (0, 256)]
    kept = grads_for(2, stack, weights, 0, 256)
    crossing = (far[0].astype(F32) + kept.astype(F32)).astype(BF16)
    crossed = [flipped(crossing, 2)]
    later, crossing = lax.optimization_barrier((stack, crossing))
    kept = grads_for(2, later, weights, 256, 256)
    crossing = (far[1].astype(F32) + kept.astype(F32)).astype(BF16)
    crossed.append(flipped(crossing, 2))
    later, output, crossing = lax.optimization_barrier((stack, output, crossing))
    head_output = own_output(output)
    near = flipped(grads_for(1, later, weights), 1)
    kept = grads_for(0, later, weights, scale=8)
    feature_grad = last_sum(kept, near, *crossed)
    return head_output.reshape(12, 48, W), feature_grad.reshape(12, 48, 512)


def solution(mesh):
    body = on_device if fits(mesh) else on_device_general
    in_specs = (
        P("rows", None, None),
        P(None, "filt"),
        P(None, None, None, None, "filt"),
        P(None, "filt"),
        P(),
        P(),
        P("rows", None, None),
    )
    out_specs = (P("rows", None, "filt"), P("rows", None, "filt"))
    return jax.shard_map(
        body, mesh=mesh, in_specs=in_specs, out_specs=out_specs, check_vma=False
    )
```

```python
import functools

import jax
import jax.numpy as jnp
from jax import lax
from jax.experimental import pallas as pl
from jax.experimental.pallas import tpu as pltpu
from jax.sharding import PartitionSpec as P

FIRST_DILATION = 12
SECOND_DILATION = 24
THIRD_DILATION = 36


def passed_along(x, axis, by):
    devices = lax.axis_size(axis)
    pairs = [(i, i + by) for i in range(devices) if 0 <= i + by < devices]
    return lax.ppermute(x, axis, pairs)


def shift_columns(field, amount):
    breadth = field.shape[1]
    if amount == 0:
        return field
    padding = [(0, 0)] * field.ndim
    if amount > 0:
        kept = field[:, amount:]
        padding[1] = (0, amount)
    else:
        kept = field[:, : breadth + amount]
        padding[1] = (-amount, 0)
    return jnp.pad(kept, padding)


def fetch_sums(field, offset):
    return passed_along(field, "rows", offset)


def fetch_grads(field, offset):
    return passed_along(field, "rows", offset)


def shift_rows(field, amount, fetcher):
    height = field.shape[0]
    quotient = amount // height

    def extract_block(offset):
        if offset == 0:
            return field
        return fetcher(field, offset)

    return extract_block(quotient)


def make_kernel_taps(variants, dilation_rates):
    stacked = [variants[:, :, 0]]
    for branch, dilation in enumerate(dilation_rates):
        for row_tap in range(3):
            source = variants[:, :, 1 + 3 * branch + row_tap]
            for col_tap in range(3):
                stacked.append(shift_columns(source, -(col_tap - 1) * dilation))
    return jnp.stack(stacked, 2)


def on_device_general(
    features, point_weight, dilated_weight, branch_bias, project_weight, project_bias, cotangent
):
    height, breadth, channels = features.shape
    pixels = height * breadth
    own_width = point_weight.shape[1]
    filters = lax.axis_size("filt")
    member = lax.axis_index("filt")
    branch_outputs = project_weight.shape[2]
    own_out = branch_outputs // filters
    own_channels = channels // filters
    dilation_rates = (FIRST_DILATION, SECOND_DILATION, THIRD_DILATION)
    all_weights = jnp.concatenate(
        [point_weight[None], dilated_weight.reshape(27, channels, own_width)], 0
    )
    flattened = features.reshape(pixels, channels)
    tap_terms = jnp.einsum(
        "pc,tco->pto", flattened, all_weights, preferred_element_type=jnp.float32
    )
    tap_terms = tap_terms.reshape(height, breadth, 28, own_width)
    pre_list = [tap_terms[:, :, 0, :] + branch_bias[0]]
    for branch, dilation in enumerate(dilation_rates):
        summed_result = jnp.zeros((height, breadth, own_width), jnp.float32)
        for row_tap in range(3):
            row_sum = jnp.zeros((height, breadth, own_width), jnp.float32)
            for col_tap in range(3):
                row_sum = row_sum + shift_columns(
                    tap_terms[:, :, 1 + 9 * branch + 3 * row_tap + col_tap, :],
                    (col_tap - 1) * dilation,
                )
            summed_result = summed_result + shift_rows(
                row_sum, -(row_tap - 1) * dilation, fetch_sums
            )
        pre_list.append(summed_result + branch_bias[branch + 1])
    branch_pre = jnp.stack(pre_list, 2)
    activations = jnp.maximum(branch_pre, 0.0).astype(jnp.bfloat16).reshape(pixels, 4 * own_width)
    grouped = project_weight.reshape(4, filters, own_width, branch_outputs)
    own_rows = lax.dynamic_index_in_dim(grouped, member, 1, keepdims=False).reshape(
        4 * own_width, branch_outputs
    )
    flat_cotangent = cotangent.reshape(pixels, branch_outputs)
    ordered = jnp.transpose(grouped, (1, 0, 2, 3)).reshape(filters * 4 * own_width, branch_outputs)
    project_pre = jnp.dot(
        lax.all_gather(activations, "filt", axis=1, tiled=True),
        ordered,
        preferred_element_type=jnp.float32,
    )
    project_pre = project_pre + project_bias
    head_grad = jnp.where(project_pre > 0, flat_cotangent.astype(jnp.float32), 0.0).astype(
        jnp.bfloat16
    )
    own_pre = lax.dynamic_slice_in_dim(project_pre, member * own_out, own_out, 1)
    act_grad = jnp.dot(head_grad, own_rows.T, preferred_element_type=jnp.float32)
    head_output = jnp.maximum(own_pre, 0.0).astype(jnp.bfloat16).reshape(height, breadth, own_out)
    branch_grad = jnp.where(
        branch_pre > 0, act_grad.reshape(height, breadth, 4, own_width), 0.0
    ).astype(jnp.bfloat16)
    variant_list = [branch_grad[:, :, 0, :]]
    for branch, dilation in enumerate(dilation_rates):
        for row_tap in range(3):
            variant_list.append(
                shift_rows(branch_grad[:, :, branch + 1, :], (row_tap - 1) * dilation, fetch_grads)
            )
    variants = jnp.stack(variant_list, 2)
    stacked = make_kernel_taps(variants, dilation_rates).reshape(pixels, 28, own_width)
    input_grad = lax.psum_scatter(
        jnp.einsum("pto,tco->cp", stacked, all_weights, preferred_element_type=jnp.float32),
        "filt",
        scatter_dimension=0,
        tiled=True,
    ).T
    feature_grad = input_grad.astype(jnp.bfloat16).reshape(height, breadth, own_channels)
    return (head_output, feature_grad)


W = 64
BLOCK = 144
PIXELS = 576
HALF = 288
SENT = 304
CHANNELS = 2048
F32 = jnp.float32
BF16 = jnp.bfloat16

OUT_PAIRS = ((3, 1), (1, 1), (3, 0), (1, 0), (3, 2), (1, 2), (2, 1), (2, 0), (2, 2))
TAPS = (
    [(k, 1, 1) for k in (1, 2, 3)]
    + [(k, i, j) for k, j in OUT_PAIRS for i in (0, 2)]
    + [(k, 1, j) for j in (0, 2) for k in (1, 2, 3)]
)
OUT_AT, LEFT_AT, RIGHT_AT = 4 * W, 22 * W, 25 * W
PARTS = ((0, 1), (2, 3))
PART_SWAPS = ((7, 3, 1), (6, 2, 5, 7, 3))
SWAPS = (1, 3, 7, 5, 2, 6)
GRAD_SWAPS = (7, 5, 6, 3, 1, 2)


def fits(mesh):
    return mesh.shape["rows"] == 8 and mesh.shape["filt"] == 4


def order_matrix(turned=False):
    to = lax.broadcasted_iota(jnp.int32, (192, 192), 1 if turned else 0)
    source = lax.broadcasted_iota(jnp.int32, (192, 192), 0 if turned else 1)

    def parts(value, width):
        return sum((value >= n * width).astype(jnp.int32) for n in (1, 2, 3))

    block = parts(to, 48)
    within = to - 48 * block
    line = parts(within, 12)
    wanted = line * 48 + block * 12 + within - 12 * line
    return (source == wanted).astype(F32).astype(BF16)


def tap_index(tap):
    k, i, j = tap
    return (k - 1) * 9 + i * 3 + j


def nt(a, b):
    return lax.dot_general(a, b, (((1,), (1,)), ((), ())), preferred_element_type=F32)


def nn(a, b):
    return lax.dot_general(a, b, (((1,), (0,)), ((), ())), preferred_element_type=F32)


def from_blocks(order_t, value, write):
    for g in range(3):
        parts = [value[m * BLOCK + g * 48 : m * BLOCK + g * 48 + 48] for m in range(4)]
        write(g * 192, nn(order_t, jnp.concatenate(parts, 0)).astype(BF16))


def low_lanes(shape):
    return lax.broadcasted_iota(jnp.int32, shape, 1) % 128 < W


def scaled(value):
    most = jnp.maximum(jnp.max(jnp.abs(value), axis=0, keepdims=True), 1e-30)
    power = jnp.floor(jnp.log(most) * 1.4426950408889634)
    return value * jnp.exp2(13.0 - power), power


def unscaled(sent):
    return sent[:HALF, :] * jnp.exp2(sent[HALF : HALF + 1, :] - 13.0)


def outward_slot(row, x):
    other = row ^ x
    apart = jnp.abs(other - row)
    slot = apart - 1 + jnp.where(other < row, 3, 0)
    return jnp.where(apart <= 3, slot, 0)


def fetch_tap(dilated, weights, sem, place):
    return pltpu.make_async_copy(
        dilated.at[tap_index(TAPS[place - 1])], weights.at[pl.ds(place * W, W)], sem
    )


def outward_kernel(features, dilated, point, *refs):
    row = lax.axis_index("rows")
    out, ordered, weights = refs[0:6], refs[6], refs[7]
    raw, sums, packed, feature_sems, weight_sems = refs[8:]
    loads = []
    for g in range(3):
        rows = pl.ds(g * 192, 192)
        loads.append(pltpu.make_async_copy(features.at[rows], raw.at[rows], feature_sems.at[g]))
        loads[-1].start()
    queue = [
        fetch_tap(dilated, weights, weight_sems.at[q], place)
        for q, place in enumerate((*range(4, 28), 1, 2, 3))
    ]
    queue.append(pltpu.make_async_copy(point, weights.at[pl.ds(0, W)], weight_sems.at[27]))

    def start_loads(first, last):
        for fetch in queue[first:last]:
            fetch.start()

    start_loads(0, 4)
    order = order_matrix()
    for g in range(3):
        loads[g].wait()
        start_loads((4, 12, 18)[g], (12, 18, 28)[g])
        moved = nn(order, raw[g * 192 : (g + 1) * 192, :]).astype(BF16)
        for m in range(4):
            at = m * BLOCK + g * 48
            ordered[at : at + 48, :] = moved[m * 48 : (m + 1) * 48]

    def product(pair, pairs, first, last):
        for fetch in queue[2 * pair : 2 * (pair + pairs)]:
            fetch.wait()
        at = OUT_AT + pair * 128
        return nt(ordered[first * BLOCK : last * BLOCK, :], weights[at : at + pairs * 128, :])

    d = product(0, 2, 0, 4)
    sums[2] = d[:, :128]
    sums[0] = d[:, 128:]
    d = product(2, 2, 0, 3)
    sums[2, 3 * BLOCK :, :] = sums[2, 3 * BLOCK :, :] + d[:BLOCK, :128]
    sums[0, BLOCK:, :] = sums[0, BLOCK:, :] + d[:, 128:]
    d = product(4, 2, 1, 4)
    sums[2, :BLOCK, :] = sums[2, :BLOCK, :] + d[2 * BLOCK :, :128]
    sums[0, : 3 * BLOCK, :] = sums[0, : 3 * BLOCK, :] + d[:, 128:]
    low = low_lanes((HALF, 128))

    def pack(k):
        top, bottom = sums[k, :HALF, :], sums[k, HALF:, :]
        halves = (
            jnp.where(low, top, pltpu.roll(bottom, W, 1)),
            jnp.where(low, pltpu.roll(top, W, 1), bottom),
        )
        for way, value in enumerate(halves):
            value, power = scaled(value)
            packed[k + 3 * way, :HALF, :] = value
            packed[k + 3 * way, HALF:, :] = jnp.broadcast_to(power, (SENT - HALF, 128))

    pack(2)
    pack(0)
    d = product(6, 3, 0, 4)
    sums[1] = d[:, :128]
    sums[1, 2 * BLOCK :, :] = sums[1, 2 * BLOCK :, :] + d[: 2 * BLOCK, 128:256]
    sums[1, : 2 * BLOCK, :] = sums[1, : 2 * BLOCK, :] + d[2 * BLOCK :, 256:]
    pack(1)
    for n, x in enumerate(SWAPS):
        out[n][...] = packed[outward_slot(row, x)]
    for fetch in queue[18:]:
        fetch.wait()


def outward_sums(features, dilated, point):
    return pl.pallas_call(
        outward_kernel,
        out_shape=[jax.ShapeDtypeStruct((SENT, 128), F32)] * 6
        + [pltpu.VMEM((PIXELS, CHANNELS), BF16), pltpu.VMEM((28 * W, CHANNELS), BF16)],
        in_specs=[pl.BlockSpec(memory_space=pltpu.HBM)] * 3,
        out_specs=[pl.BlockSpec(memory_space=pltpu.VMEM)] * 8,
        scratch_shapes=[
            pltpu.VMEM((PIXELS, CHANNELS), BF16),
            pltpu.VMEM((3, PIXELS, 128), F32),
            pltpu.VMEM((6, SENT, 128), F32),
            pltpu.SemaphoreType.DMA((3,)),
            pltpu.SemaphoreType.DMA((28,)),
        ],
        compiler_params=pltpu.CompilerParams(vmem_limit_bytes=28 * 2**20),
        name="outward_sums",
    )(features, dilated, point)


def own_kernel(ordered, weights, bias, *outs):
    d = nt(ordered[...], weights[:256, :])
    for part, out in enumerate(outs):
        line = jnp.concatenate([bias[k : k + 1, :] for k in PARTS[part]], 1)
        out[...] = d[:, part * 128 : part * 128 + 128] + line
    low = low_lanes((PIXELS, 128))

    def add(first, value, k):
        part = k // 2
        rows = slice(first * BLOCK, first * BLOCK + value.shape[0])
        mask, value = low[: value.shape[0]], value[:, part * 128 : part * 128 + 128]
        kept = jnp.where(mask, value, 0.0) if k == 2 else jnp.where(mask, 0.0, value)
        outs[part][rows, :] = outs[part][rows, :] + kept

    d = nt(ordered[: 3 * BLOCK, :], weights[LEFT_AT - W : LEFT_AT + 3 * W, :])
    for k in (1, 2, 3):
        add(k, d[: (4 - k) * BLOCK], k)
    d = nt(ordered[BLOCK:, :], weights[RIGHT_AT - W : RIGHT_AT + 3 * W, :])
    for k in (1, 2, 3):
        add(0, d[(k - 1) * BLOCK :], k)


def own_sums(ordered, weights, bias):
    return pl.pallas_call(
        own_kernel,
        out_shape=[jax.ShapeDtypeStruct((PIXELS, 128), F32)] * 2,
        in_specs=[pl.BlockSpec(memory_space=pltpu.VMEM)] * 3,
        out_specs=[pl.BlockSpec(memory_space=pltpu.VMEM)] * 2,
        compiler_params=pltpu.CompilerParams(vmem_limit_bytes=18 * 2**20),
        cost_estimate=pl.CostEstimate(flops=10**6, bytes_accessed=10**4, transcendentals=0),
        name="own_sums",
    )(ordered, weights, bias)


def arrival_slot(row, other):
    return jnp.where((other >= 0) & (other < 8), row ^ other, 0)


def gather_arrivals(recv, arrivals, swaps):
    arrivals[0] = jnp.zeros((HALF, 128), arrivals.dtype)
    for n, x in enumerate(swaps):
        arrivals[x] = unscaled(recv[n][...])


def activation_kernel(part, swaps, own, *refs):
    recv, acts, arrivals = refs[: len(swaps)], refs[-2], refs[-1]
    row = lax.axis_index("rows")
    gather_arrivals(recv, arrivals, swaps)
    low = low_lanes((HALF, 128))

    def total(k):
        return arrivals[arrival_slot(row, row - k)] + arrivals[arrival_slot(row, row + k)]

    high = total(PARTS[part][1])
    top, bottom = jnp.where(low, 0.0, pltpu.roll(high, W, 1)), jnp.where(low, 0.0, high)
    if part:
        left = total(PARTS[part][0])
        top = jnp.where(low, left, top)
        bottom = jnp.where(low, pltpu.roll(left, W, 1), bottom)
    acts[:HALF, :] = jnp.maximum(own[:HALF, :] + top, 0.0).astype(BF16)
    acts[HALF:, :] = jnp.maximum(own[HALF:, :] + bottom, 0.0).astype(BF16)


def activations_of(part, swaps, own, received):
    return pl.pallas_call(
        functools.partial(activation_kernel, part, swaps),
        out_shape=jax.ShapeDtypeStruct((PIXELS, 128), BF16),
        in_specs=[pl.BlockSpec(memory_space=pltpu.VMEM)] * (1 + len(swaps)),
        out_specs=pl.BlockSpec(memory_space=pltpu.VMEM),
        scratch_shapes=[pltpu.VMEM((8, HALF, 128), F32)],
        compiler_params=pltpu.CompilerParams(vmem_limit_bytes=8 * 2**20),
        name="activations",
    )(own, *received)


def project_rows(project, who):
    at = pl.multiple_of(who * W, W)
    return jnp.concatenate([project[k, pl.ds(at, W), :] for part in PARTS for k in part], 0)


def both(a, b):
    return jnp.concatenate([a[...], b[...]], 1)


def near_head_kernel(a0, b0, a1, b1, project, bias, cotangent, pre, ordered):
    member = lax.axis_index("filt")
    pre[...] = nn(both(a0, b0), project_rows(project, member)) + bias[...]
    pre[...] = pre[...] + nn(both(a1, b1), project_rows(project, member ^ 1))
    order = order_matrix()
    for g in range(3):
        moved = nn(order, cotangent[g * 192 : (g + 1) * 192, :])
        for m in range(4):
            at = m * BLOCK + g * 48
            ordered[at : at + 48, :] = moved[m * 48 : (m + 1) * 48]


def near_head(own, beside, project, bias, cotangent):
    return pl.pallas_call(
        near_head_kernel,
        out_shape=[jax.ShapeDtypeStruct((PIXELS, 256), F32)] * 2,
        in_specs=[pl.BlockSpec(memory_space=pltpu.VMEM)] * 7,
        out_specs=[pl.BlockSpec(memory_space=pltpu.VMEM)] * 2,
        compiler_params=pltpu.CompilerParams(vmem_limit_bytes=10 * 2**20),
        name="near_head",
    )(*own, *beside, project, bias, cotangent)


def far_head_kernel(a0, b0, a2, b2, a3, b3, project, near, cotangent, *refs):
    output, grads, sends, packed = refs[0], refs[1], refs[2:8], refs[8]
    row, member = lax.axis_index("rows"), lax.axis_index("filt")
    pre = near[...] + nn(both(a2, b2), project_rows(project, member ^ 2))
    pre = pre + nn(both(a3, b3), project_rows(project, member ^ 3))
    output[...] = jnp.maximum(pre, 0.0).astype(BF16)
    head_grad = jnp.where(pre > 0, cotangent[...], 0.0).astype(BF16)
    act_grad = nt(head_grad, project_rows(project, member))
    a = jnp.where(a0[...].astype(F32) > 0, act_grad[:, :128], 0.0)
    b = jnp.where(b0[...].astype(F32) > 0, act_grad[:, 128:], 0.0)
    grads[:, :128] = a.astype(BF16)
    grads[:, 128:] = b.astype(BF16)
    low = low_lanes((HALF, 128))
    packed[0] = jnp.where(low, pltpu.roll(a[:HALF], W, 1), a[HALF:]).astype(BF16)
    packed[1] = jnp.where(low, b[:HALF], pltpu.roll(b[HALF:], W, 1)).astype(BF16)
    packed[2] = jnp.where(low, pltpu.roll(b[:HALF], W, 1), b[HALF:]).astype(BF16)
    for n, x in enumerate(GRAD_SWAPS):
        apart = jnp.abs((row ^ x) - row)
        sends[n][...] = packed[jnp.where(apart <= 3, apart - 1, 0)]


def far_head(own, across, corner, project, near, cotangent):
    return pl.pallas_call(
        far_head_kernel,
        out_shape=[jax.ShapeDtypeStruct((PIXELS, 256), BF16)] * 2
        + [jax.ShapeDtypeStruct((HALF, 128), BF16)] * 6,
        in_specs=[pl.BlockSpec(memory_space=pltpu.VMEM)] * 9,
        out_specs=[pl.BlockSpec(memory_space=pltpu.VMEM)] * 8,
        scratch_shapes=[pltpu.VMEM((3, HALF, 128), BF16)],
        compiler_params=pltpu.CompilerParams(vmem_limit_bytes=12 * 2**20),
        name="far_head",
    )(*own, *across, *corner, project, near, cotangent)


def own_output_kernel(output, out):
    member = lax.axis_index("filt")
    mine = jnp.zeros((PIXELS, W), F32)
    for q in range(4):
        mine = jnp.where(member == q, output[:, q * W : (q + 1) * W].astype(F32), mine)

    def put(at, value):
        out[at : at + 192, :] = value

    from_blocks(order_matrix(True), mine.astype(BF16), put)


def own_output(output):
    return pl.pallas_call(
        own_output_kernel,
        out_shape=jax.ShapeDtypeStruct((PIXELS, W), BF16),
        in_specs=[pl.BlockSpec(memory_space=pltpu.VMEM)],
        out_specs=pl.BlockSpec(memory_space=pltpu.VMEM),
        compiler_params=pltpu.CompilerParams(vmem_limit_bytes=6 * 2**20),
        name="own_output",
    )(output)


def spread_kernel(own, *refs):
    recv, stack, arrivals, pairs, twice = refs[:6], *refs[6:]
    row = lax.axis_index("rows")
    arrivals[0] = jnp.zeros((HALF, 128), BF16)
    for n, x in enumerate(GRAD_SWAPS):
        arrivals[x] = recv[n][...]
    low = low_lanes((HALF, 128))
    low_all = low_lanes((PIXELS, 128))
    for k in (1, 2, 3):
        p = arrivals[arrival_slot(row, row + k)].astype(F32)
        m = arrivals[arrival_slot(row, row - k)].astype(F32)
        pairs[k - 1, :HALF, :] = jnp.where(low, p, pltpu.roll(m, W, 1)).astype(BF16)
        pairs[k - 1, HALF:, :] = jnp.where(low, pltpu.roll(p, W, 1), m).astype(BF16)
        g = own[:, :128].astype(F32) if k == 1 else own[:, 128:].astype(F32)
        other = pltpu.roll(g, W, 1)
        two = jnp.where(low_all, g, other) if k == 2 else jnp.where(low_all, other, g)
        twice[k - 1] = two.astype(BF16)
    stack[:, : 4 * W] = own[...]
    nothing = jnp.zeros((BLOCK, 128), BF16)

    def block_of(ref, k, source):
        if 0 <= source < 4:
            return ref[k - 1, source * BLOCK : (source + 1) * BLOCK, :]
        return nothing

    for q, (k, j) in enumerate(OUT_PAIRS):
        lanes = slice(OUT_AT + q * 128, OUT_AT + q * 128 + 128)
        for m in range(4):
            stack[m * BLOCK : (m + 1) * BLOCK, lanes] = block_of(pairs, k, m - (j - 1) * k)
    low_block = low_lanes((BLOCK, 128))
    for q, (a, b) in enumerate(((1, 2), (3, -1), (-2, -3))):
        lanes = slice(LEFT_AT + q * 128, LEFT_AT + q * 128 + 128)
        for m in range(4):
            stack[m * BLOCK : (m + 1) * BLOCK, lanes] = jnp.where(
                low_block, block_of(twice, abs(a), m + a), block_of(twice, abs(b), m + b)
            )


def spread(own, received):
    return pl.pallas_call(
        spread_kernel,
        out_shape=pltpu.VMEM((PIXELS, 28 * W), BF16),
        in_specs=[pl.BlockSpec(memory_space=pltpu.VMEM)] * 7,
        out_specs=pl.BlockSpec(memory_space=pltpu.VMEM),
        scratch_shapes=[
            pltpu.VMEM((8, HALF, 128), BF16),
            pltpu.VMEM((3, PIXELS, 128), BF16),
            pltpu.VMEM((3, PIXELS, 128), BF16),
        ],
        compiler_params=pltpu.CompilerParams(vmem_limit_bytes=12 * 2**20),
        name="spread",
    )(own, *received)


def grad_kernel(flip, first, stack, weights, out):
    member = lax.axis_index("filt")
    columns = pl.ds(pl.multiple_of((member ^ flip) * 512 + first, 256), out.shape[1])
    out[...] = nn(stack[...], weights[:, columns]).astype(BF16)


def grads_for(flip, stack, weights, first=0, width=512, scale=1):
    return pl.pallas_call(
        functools.partial(grad_kernel, flip, first),
        out_shape=jax.ShapeDtypeStruct((PIXELS, width), BF16),
        in_specs=[pl.BlockSpec(memory_space=pltpu.VMEM)] * 2,
        out_specs=pl.BlockSpec(memory_space=pltpu.VMEM),
        compiler_params=pltpu.CompilerParams(vmem_limit_bytes=18 * 2**20),
        cost_estimate=pl.CostEstimate(
            flops=2 * PIXELS * 28 * W * width * scale, bytes_accessed=10**6, transcendentals=0
        ),
        name="grads_for",
    )(stack, weights)


def last_kernel(a, b, c, d, out, done, sems):
    order = order_matrix(True)
    copies = []
    for g in range(3):
        parts = []
        for m in range(4):
            rows = slice(m * BLOCK + g * 48, m * BLOCK + g * 48 + 48)
            crossed = jnp.concatenate([c[rows, :], d[rows, :]], 1)
            total = a[rows, :].astype(F32) + b[rows, :].astype(F32) + crossed.astype(F32)
            parts.append(total.astype(BF16))
        rows = pl.ds(g * 192, 192)
        done[g * 192 : (g + 1) * 192, :] = nn(order, jnp.concatenate(parts, 0)).astype(BF16)
        copies.append(pltpu.make_async_copy(done.at[rows], out.at[rows], sems.at[g]))
        copies[-1].start()
    for copy in copies:
        copy.wait()


def last_sum(a, b, c, d):
    return pl.pallas_call(
        last_kernel,
        out_shape=jax.ShapeDtypeStruct((PIXELS, 512), BF16),
        in_specs=[pl.BlockSpec(memory_space=pltpu.VMEM)] * 4,
        out_specs=pl.BlockSpec(memory_space=pl.ANY),
        scratch_shapes=[pltpu.VMEM((PIXELS, 512), BF16), pltpu.SemaphoreType.DMA((3,))],
        compiler_params=pltpu.CompilerParams(vmem_limit_bytes=10 * 2**20),
        name="last_sum",
    )(a, b, c, d)


def flipped(x, bit):
    return lax.ppermute(x, "filt", [(i, i ^ bit) for i in range(lax.axis_size("filt"))])


def partner(r, bits):
    return r ^ bits if abs((r ^ bits) - r) <= 3 else r ^ {5: 2, 6: 1, 7: 1}[bits]


def swapped(x, bits):
    return lax.ppermute(x, "rows", [(r, partner(r, bits)) for r in range(8)])


def on_device(
    features, point_weight, dilated_weight, branch_bias, project_weight, project_bias, cotangent
):
    flat = features.reshape(PIXELS, CHANNELS)
    dilated = jnp.transpose(dilated_weight, (0, 1, 2, 4, 3)).reshape(27, W, CHANNELS)
    point = point_weight.T
    flat, dilated, point = (
        pltpu.with_memory_space_constraint(x, pltpu.HBM) for x in (flat, dilated, point)
    )
    *sums, ordered, weights = outward_sums(flat, dilated, point)
    received = {
        x: swapped(sums[n].astype(jnp.float16), x).astype(F32) for n, x in enumerate(SWAPS)
    }
    own = own_sums(ordered, weights, branch_bias)
    acts = [
        activations_of(part, swaps, own[part], [received[x] for x in swaps])
        for part, swaps in enumerate(PART_SWAPS)
    ]
    across = [flipped(x, 2) for x in acts]
    beside = [flipped(x, 1) for x in acts]
    corner = [flipped(x, 1) for x in across]
    near, ordered_cotangent = near_head(
        acts,
        beside,
        project_weight,
        project_bias.reshape(1, 256),
        cotangent.reshape(PIXELS, 256),
    )
    output, grads, *sends = far_head(
        acts, across, corner, project_weight, near, ordered_cotangent
    )
    arrived = [swapped(sends[n], x) for n, x in enumerate(GRAD_SWAPS)]
    stack = spread(grads, arrived)
    far = [flipped(grads_for(3, stack, weights, at, 256), 1) for at in (0, 256)]
    kept = grads_for(2, stack, weights, 0, 256)
    crossing = (far[0].astype(F32) + kept.astype(F32)).astype(BF16)
    crossed = [flipped(crossing, 2)]
    later, crossing = lax.optimization_barrier((stack, crossing))
    kept = grads_for(2, later, weights, 256, 256)
    crossing = (far[1].astype(F32) + kept.astype(F32)).astype(BF16)
    crossed.append(flipped(crossing, 2))
    later, output, crossing = lax.optimization_barrier((stack, output, crossing))
    head_output = own_output(output)
    near = flipped(grads_for(1, later, weights), 1)
    kept = grads_for(0, later, weights, scale=8)
    feature_grad = last_sum(kept, near, *crossed)
    return head_output.reshape(12, 48, W), feature_grad.reshape(12, 48, 512)


def solution(mesh):
    body = on_device if fits(mesh) else on_device_general
    in_specs = (
        P("rows", None, None),
        P(None, "filt"),
        P(None, None, None, None, "filt"),
        P(None, "filt"),
        P(),
        P(),
        P("rows", None, None),
    )
    out_specs = (P("rows", None, "filt"), P("rows", None, "filt"))
    return jax.shard_map(
        body, mesh=mesh, in_specs=in_specs, out_specs=out_specs, check_vma=False
    )
```

```python
import functools

import jax
import jax.numpy as jnp
from jax import lax
from jax.experimental import pallas as pl
from jax.experimental.pallas import tpu as pltpu
from jax.sharding import PartitionSpec as P

FIRST_DILATION = 12
SECOND_DILATION = 24
THIRD_DILATION = 36


def passed_along(x, axis, by):
    devices = lax.axis_size(axis)
    pairs = [(i, i + by) for i in range(devices) if 0 <= i + by < devices]
    return lax.ppermute(x, axis, pairs)


def shift_columns(field, amount):
    breadth = field.shape[1]
    if amount == 0:
        return field
    padding = [(0, 0)] * field.ndim
    if amount > 0:
        kept = field[:, amount:]
        padding[1] = (0, amount)
    else:
        kept = field[:, : breadth + amount]
        padding[1] = (-amount, 0)
    return jnp.pad(kept, padding)


def fetch_sums(field, offset):
    return passed_along(field, "rows", offset)


def fetch_grads(field, offset):
    return passed_along(field, "rows", offset)


def shift_rows(field, amount, fetcher):
    height = field.shape[0]
    quotient = amount // height

    def extract_block(offset):
        if offset == 0:
            return field
        return fetcher(field, offset)

    return extract_block(quotient)


def make_kernel_taps(variants, dilation_rates):
    stacked = [variants[:, :, 0]]
    for branch, dilation in enumerate(dilation_rates):
        for row_tap in range(3):
            source = variants[:, :, 1 + 3 * branch + row_tap]
            for col_tap in range(3):
                stacked.append(shift_columns(source, -(col_tap - 1) * dilation))
    return jnp.stack(stacked, 2)


def on_device_general(
    features, point_weight, dilated_weight, branch_bias, project_weight, project_bias, cotangent
):
    height, breadth, channels = features.shape
    pixels = height * breadth
    own_width = point_weight.shape[1]
    filters = lax.axis_size("filt")
    member = lax.axis_index("filt")
    branch_outputs = project_weight.shape[2]
    own_out = branch_outputs // filters
    own_channels = channels // filters
    dilation_rates = (FIRST_DILATION, SECOND_DILATION, THIRD_DILATION)
    all_weights = jnp.concatenate(
        [point_weight[None], dilated_weight.reshape(27, channels, own_width)], 0
    )
    flattened = features.reshape(pixels, channels)
    tap_terms = jnp.einsum(
        "pc,tco->pto", flattened, all_weights, preferred_element_type=jnp.float32
    )
    tap_terms = tap_terms.reshape(height, breadth, 28, own_width)
    pre_list = [tap_terms[:, :, 0, :] + branch_bias[0]]
    for branch, dilation in enumerate(dilation_rates):
        summed_result = jnp.zeros((height, breadth, own_width), jnp.float32)
        for row_tap in range(3):
            row_sum = jnp.zeros((height, breadth, own_width), jnp.float32)
            for col_tap in range(3):
                row_sum = row_sum + shift_columns(
                    tap_terms[:, :, 1 + 9 * branch + 3 * row_tap + col_tap, :],
                    (col_tap - 1) * dilation,
                )
            summed_result = summed_result + shift_rows(
                row_sum, -(row_tap - 1) * dilation, fetch_sums
            )
        pre_list.append(summed_result + branch_bias[branch + 1])
    branch_pre = jnp.stack(pre_list, 2)
    activations = jnp.maximum(branch_pre, 0.0).astype(jnp.bfloat16).reshape(pixels, 4 * own_width)
    grouped = project_weight.reshape(4, filters, own_width, branch_outputs)
    own_rows = lax.dynamic_index_in_dim(grouped, member, 1, keepdims=False).reshape(
        4 * own_width, branch_outputs
    )
    flat_cotangent = cotangent.reshape(pixels, branch_outputs)
    ordered = jnp.transpose(grouped, (1, 0, 2, 3)).reshape(filters * 4 * own_width, branch_outputs)
    project_pre = jnp.dot(
        lax.all_gather(activations, "filt", axis=1, tiled=True),
        ordered,
        preferred_element_type=jnp.float32,
    )
    project_pre = project_pre + project_bias
    head_grad = jnp.where(project_pre > 0, flat_cotangent.astype(jnp.float32), 0.0).astype(
        jnp.bfloat16
    )
    own_pre = lax.dynamic_slice_in_dim(project_pre, member * own_out, own_out, 1)
    act_grad = jnp.dot(head_grad, own_rows.T, preferred_element_type=jnp.float32)
    head_output = jnp.maximum(own_pre, 0.0).astype(jnp.bfloat16).reshape(height, breadth, own_out)
    branch_grad = jnp.where(
        branch_pre > 0, act_grad.reshape(height, breadth, 4, own_width), 0.0
    ).astype(jnp.bfloat16)
    variant_list = [branch_grad[:, :, 0, :]]
    for branch, dilation in enumerate(dilation_rates):
        for row_tap in range(3):
            variant_list.append(
                shift_rows(branch_grad[:, :, branch + 1, :], (row_tap - 1) * dilation, fetch_grads)
            )
    variants = jnp.stack(variant_list, 2)
    stacked = make_kernel_taps(variants, dilation_rates).reshape(pixels, 28, own_width)
    input_grad = lax.psum_scatter(
        jnp.einsum("pto,tco->cp", stacked, all_weights, preferred_element_type=jnp.float32),
        "filt",
        scatter_dimension=0,
        tiled=True,
    ).T
    feature_grad = input_grad.astype(jnp.bfloat16).reshape(height, breadth, own_channels)
    return (head_output, feature_grad)


W = 64
BLOCK = 144
PIXELS = 576
HALF = 288
SENT = 304
CHANNELS = 2048
F32 = jnp.float32
BF16 = jnp.bfloat16

OUT_PAIRS = ((3, 1), (1, 1), (3, 0), (1, 0), (3, 2), (1, 2), (2, 1), (2, 0), (2, 2))
TAPS = (
    [(k, 1, 1) for k in (1, 2, 3)]
    + [(k, i, j) for k, j in OUT_PAIRS for i in (0, 2)]
    + [(k, 1, j) for j in (0, 2) for k in (1, 2, 3)]
)
OUT_AT, LEFT_AT, RIGHT_AT = 4 * W, 22 * W, 25 * W
PARTS = ((0, 1), (2, 3))
PART_SWAPS = ((7, 3, 1), (6, 2, 5, 7, 3))
SWAPS = (1, 3, 7, 5, 2, 6)
GRAD_SWAPS = (5, 7, 6, 3, 2, 1)


def fits(mesh):
    return mesh.shape["rows"] == 8 and mesh.shape["filt"] == 4


def order_matrix(turned=False):
    to = lax.broadcasted_iota(jnp.int32, (192, 192), 1 if turned else 0)
    source = lax.broadcasted_iota(jnp.int32, (192, 192), 0 if turned else 1)

    def parts(value, width):
        return sum((value >= n * width).astype(jnp.int32) for n in (1, 2, 3))

    block = parts(to, 48)
    within = to - 48 * block
    line = parts(within, 12)
    wanted = line * 48 + block * 12 + within - 12 * line
    return (source == wanted).astype(F32).astype(BF16)


def tap_index(tap):
    k, i, j = tap
    return (k - 1) * 9 + i * 3 + j


def nt(a, b):
    return lax.dot_general(a, b, (((1,), (1,)), ((), ())), preferred_element_type=F32)


def nn(a, b):
    return lax.dot_general(a, b, (((1,), (0,)), ((), ())), preferred_element_type=F32)


def from_blocks(order_t, value, write):
    for g in range(3):
        parts = [value[m * BLOCK + g * 48 : m * BLOCK + g * 48 + 48] for m in range(4)]
        write(g * 192, nn(order_t, jnp.concatenate(parts, 0)).astype(BF16))


def low_lanes(shape):
    return lax.broadcasted_iota(jnp.int32, shape, 1) % 128 < W


def scaled(value):
    most = jnp.maximum(jnp.max(jnp.abs(value), axis=0, keepdims=True), 1e-30)
    power = jnp.floor(jnp.log(most) * 1.4426950408889634)
    return value * jnp.exp2(13.0 - power), power


def unscaled(sent):
    return sent[:HALF, :] * jnp.exp2(sent[HALF : HALF + 1, :] - 13.0)


def outward_slot(row, x):
    other = row ^ x
    apart = jnp.abs(other - row)
    slot = apart - 1 + jnp.where(other < row, 3, 0)
    return jnp.where(apart <= 3, slot, 0)


def fetch_tap(dilated, weights, sem, place):
    return pltpu.make_async_copy(
        dilated.at[tap_index(TAPS[place - 1])], weights.at[pl.ds(place * W, W)], sem
    )


def outward_kernel(features, dilated, point, *refs):
    row = lax.axis_index("rows")
    out, ordered, weights = refs[0:6], refs[6], refs[7]
    raw, sums, packed, feature_sems, weight_sems = refs[8:]
    loads = []
    for g in range(3):
        rows = pl.ds(g * 192, 192)
        loads.append(pltpu.make_async_copy(features.at[rows], raw.at[rows], feature_sems.at[g]))
        loads[-1].start()
    queue = [
        fetch_tap(dilated, weights, weight_sems.at[q], place)
        for q, place in enumerate((*range(4, 28), 1, 2, 3))
    ]
    queue.append(pltpu.make_async_copy(point, weights.at[pl.ds(0, W)], weight_sems.at[27]))

    def start_loads(first, last):
        for fetch in queue[first:last]:
            fetch.start()

    start_loads(0, 4)
    order = order_matrix()
    for g in range(3):
        loads[g].wait()
        start_loads((4, 12, 18)[g], (12, 18, 28)[g])
        moved = nn(order, raw[g * 192 : (g + 1) * 192, :]).astype(BF16)
        for m in range(4):
            at = m * BLOCK + g * 48
            ordered[at : at + 48, :] = moved[m * 48 : (m + 1) * 48]

    def product(pair, pairs, first, last):
        for fetch in queue[2 * pair : 2 * (pair + pairs)]:
            fetch.wait()
        at = OUT_AT + pair * 128
        return nt(ordered[first * BLOCK : last * BLOCK, :], weights[at : at + pairs * 128, :])

    d = product(0, 2, 0, 4)
    sums[2] = d[:, :128]
    sums[0] = d[:, 128:]
    d = product(2, 2, 0, 3)
    sums[2, 3 * BLOCK :, :] = sums[2, 3 * BLOCK :, :] + d[:BLOCK, :128]
    sums[0, BLOCK:, :] = sums[0, BLOCK:, :] + d[:, 128:]
    d = product(4, 2, 1, 4)
    sums[2, :BLOCK, :] = sums[2, :BLOCK, :] + d[2 * BLOCK :, :128]
    sums[0, : 3 * BLOCK, :] = sums[0, : 3 * BLOCK, :] + d[:, 128:]
    low = low_lanes((HALF, 128))

    def pack(k):
        top, bottom = sums[k, :HALF, :], sums[k, HALF:, :]
        halves = (
            jnp.where(low, top, pltpu.roll(bottom, W, 1)),
            jnp.where(low, pltpu.roll(top, W, 1), bottom),
        )
        for way, value in enumerate(halves):
            value, power = scaled(value)
            packed[k + 3 * way, :HALF, :] = value
            packed[k + 3 * way, HALF:, :] = jnp.broadcast_to(power, (SENT - HALF, 128))

    pack(2)
    pack(0)
    d = product(6, 3, 0, 4)
    sums[1] = d[:, :128]
    sums[1, 2 * BLOCK :, :] = sums[1, 2 * BLOCK :, :] + d[: 2 * BLOCK, 128:256]
    sums[1, : 2 * BLOCK, :] = sums[1, : 2 * BLOCK, :] + d[2 * BLOCK :, 256:]
    pack(1)
    for n, x in enumerate(SWAPS):
        out[n][...] = packed[outward_slot(row, x)]
    for fetch in queue[18:]:
        fetch.wait()


def outward_sums(features, dilated, point):
    return pl.pallas_call(
        outward_kernel,
        out_shape=[jax.ShapeDtypeStruct((SENT, 128), F32)] * 6
        + [pltpu.VMEM((PIXELS, CHANNELS), BF16), pltpu.VMEM((28 * W, CHANNELS), BF16)],
        in_specs=[pl.BlockSpec(memory_space=pltpu.HBM)] * 3,
        out_specs=[pl.BlockSpec(memory_space=pltpu.VMEM)] * 8,
        scratch_shapes=[
            pltpu.VMEM((PIXELS, CHANNELS), BF16),
            pltpu.VMEM((3, PIXELS, 128), F32),
            pltpu.VMEM((6, SENT, 128), F32),
            pltpu.SemaphoreType.DMA((3,)),
            pltpu.SemaphoreType.DMA((28,)),
        ],
        compiler_params=pltpu.CompilerParams(vmem_limit_bytes=28 * 2**20),
        name="outward_sums",
    )(features, dilated, point)


def own_kernel(ordered, weights, bias, *outs):
    d = nt(ordered[...], weights[:256, :])
    for part, out in enumerate(outs):
        line = jnp.concatenate([bias[k : k + 1, :] for k in PARTS[part]], 1)
        out[...] = d[:, part * 128 : part * 128 + 128] + line
    low = low_lanes((PIXELS, 128))

    def add(first, value, k):
        part = k // 2
        rows = slice(first * BLOCK, first * BLOCK + value.shape[0])
        mask, value = low[: value.shape[0]], value[:, part * 128 : part * 128 + 128]
        kept = jnp.where(mask, value, 0.0) if k == 2 else jnp.where(mask, 0.0, value)
        outs[part][rows, :] = outs[part][rows, :] + kept

    d = nt(ordered[: 3 * BLOCK, :], weights[LEFT_AT - W : LEFT_AT + 3 * W, :])
    for k in (1, 2, 3):
        add(k, d[: (4 - k) * BLOCK], k)
    d = nt(ordered[BLOCK:, :], weights[RIGHT_AT - W : RIGHT_AT + 3 * W, :])
    for k in (1, 2, 3):
        add(0, d[(k - 1) * BLOCK :], k)


def own_sums(ordered, weights, bias):
    return pl.pallas_call(
        own_kernel,
        out_shape=[jax.ShapeDtypeStruct((PIXELS, 128), F32)] * 2,
        in_specs=[pl.BlockSpec(memory_space=pltpu.VMEM)] * 3,
        out_specs=[pl.BlockSpec(memory_space=pltpu.VMEM)] * 2,
        compiler_params=pltpu.CompilerParams(vmem_limit_bytes=18 * 2**20),
        cost_estimate=pl.CostEstimate(flops=10**6, bytes_accessed=10**4, transcendentals=0),
        name="own_sums",
    )(ordered, weights, bias)


def arrival_slot(row, other):
    return jnp.where((other >= 0) & (other < 8), row ^ other, 0)


def gather_arrivals(recv, arrivals, swaps):
    arrivals[0] = jnp.zeros((HALF, 128), arrivals.dtype)
    for n, x in enumerate(swaps):
        arrivals[x] = unscaled(recv[n][...])


def activation_kernel(part, swaps, own, *refs):
    recv, acts, arrivals = refs[: len(swaps)], refs[-2], refs[-1]
    row = lax.axis_index("rows")
    gather_arrivals(recv, arrivals, swaps)
    low = low_lanes((HALF, 128))

    def total(k):
        return arrivals[arrival_slot(row, row - k)] + arrivals[arrival_slot(row, row + k)]

    high = total(PARTS[part][1])
    top, bottom = jnp.where(low, 0.0, pltpu.roll(high, W, 1)), jnp.where(low, 0.0, high)
    if part:
        left = total(PARTS[part][0])
        top = jnp.where(low, left, top)
        bottom = jnp.where(low, pltpu.roll(left, W, 1), bottom)
    acts[:HALF, :] = jnp.maximum(own[:HALF, :] + top, 0.0).astype(BF16)
    acts[HALF:, :] = jnp.maximum(own[HALF:, :] + bottom, 0.0).astype(BF16)


def activations_of(part, swaps, own, received):
    return pl.pallas_call(
        functools.partial(activation_kernel, part, swaps),
        out_shape=jax.ShapeDtypeStruct((PIXELS, 128), BF16),
        in_specs=[pl.BlockSpec(memory_space=pltpu.VMEM)] * (1 + len(swaps)),
        out_specs=pl.BlockSpec(memory_space=pltpu.VMEM),
        scratch_shapes=[pltpu.VMEM((8, HALF, 128), F32)],
        compiler_params=pltpu.CompilerParams(vmem_limit_bytes=8 * 2**20),
        name="activations",
    )(own, *received)


def project_rows(project, who):
    at = pl.multiple_of(who * W, W)
    return jnp.concatenate([project[k, pl.ds(at, W), :] for part in PARTS for k in part], 0)


def both(a, b):
    return jnp.concatenate([a[...], b[...]], 1)


def near_head_kernel(a0, b0, a1, b1, project, bias, cotangent, pre, ordered):
    member = lax.axis_index("filt")
    pre[...] = nn(both(a0, b0), project_rows(project, member)) + bias[...]
    pre[...] = pre[...] + nn(both(a1, b1), project_rows(project, member ^ 1))
    order = order_matrix()
    for g in range(3):
        moved = nn(order, cotangent[g * 192 : (g + 1) * 192, :])
        for m in range(4):
            at = m * BLOCK + g * 48
            ordered[at : at + 48, :] = moved[m * 48 : (m + 1) * 48]


def near_head(own, beside, project, bias, cotangent):
    return pl.pallas_call(
        near_head_kernel,
        out_shape=[jax.ShapeDtypeStruct((PIXELS, 256), F32)] * 2,
        in_specs=[pl.BlockSpec(memory_space=pltpu.VMEM)] * 7,
        out_specs=[pl.BlockSpec(memory_space=pltpu.VMEM)] * 2,
        compiler_params=pltpu.CompilerParams(vmem_limit_bytes=10 * 2**20),
        name="near_head",
    )(*own, *beside, project, bias, cotangent)


def far_head_kernel(a0, b0, a2, b2, a3, b3, project, near, cotangent, *refs):
    output, grads, sends, packed = refs[0], refs[1], refs[2:8], refs[8]
    row, member = lax.axis_index("rows"), lax.axis_index("filt")
    pre = near[...] + nn(both(a2, b2), project_rows(project, member ^ 2))
    pre = pre + nn(both(a3, b3), project_rows(project, member ^ 3))
    output[...] = jnp.maximum(pre, 0.0).astype(BF16)
    head_grad = jnp.where(pre > 0, cotangent[...], 0.0).astype(BF16)
    act_grad = nt(head_grad, project_rows(project, member))
    a = jnp.where(a0[...].astype(F32) > 0, act_grad[:, :128], 0.0)
    b = jnp.where(b0[...].astype(F32) > 0, act_grad[:, 128:], 0.0)
    grads[:, :128] = a.astype(BF16)
    grads[:, 128:] = b.astype(BF16)
    low = low_lanes((HALF, 128))
    packed[0] = jnp.where(low, pltpu.roll(a[:HALF], W, 1), a[HALF:]).astype(BF16)
    packed[1] = jnp.where(low, b[:HALF], pltpu.roll(b[HALF:], W, 1)).astype(BF16)
    packed[2] = jnp.where(low, pltpu.roll(b[:HALF], W, 1), b[HALF:]).astype(BF16)
    for n, x in enumerate(GRAD_SWAPS):
        apart = jnp.abs((row ^ x) - row)
        sends[n][...] = packed[jnp.where(apart <= 3, apart - 1, 0)]


def far_head(own, across, corner, project, near, cotangent):
    return pl.pallas_call(
        far_head_kernel,
        out_shape=[jax.ShapeDtypeStruct((PIXELS, 256), BF16)] * 2
        + [jax.ShapeDtypeStruct((HALF, 128), BF16)] * 6,
        in_specs=[pl.BlockSpec(memory_space=pltpu.VMEM)] * 9,
        out_specs=[pl.BlockSpec(memory_space=pltpu.VMEM)] * 8,
        scratch_shapes=[pltpu.VMEM((3, HALF, 128), BF16)],
        compiler_params=pltpu.CompilerParams(vmem_limit_bytes=12 * 2**20),
        name="far_head",
    )(*own, *across, *corner, project, near, cotangent)


def own_output_kernel(output, out):
    member = lax.axis_index("filt")
    mine = jnp.zeros((PIXELS, W), F32)
    for q in range(4):
        mine = jnp.where(member == q, output[:, q * W : (q + 1) * W].astype(F32), mine)

    def put(at, value):
        out[at : at + 192, :] = value

    from_blocks(order_matrix(True), mine.astype(BF16), put)


def own_output(output):
    return pl.pallas_call(
        own_output_kernel,
        out_shape=jax.ShapeDtypeStruct((PIXELS, W), BF16),
        in_specs=[pl.BlockSpec(memory_space=pltpu.VMEM)],
        out_specs=pl.BlockSpec(memory_space=pltpu.VMEM),
        compiler_params=pltpu.CompilerParams(vmem_limit_bytes=6 * 2**20),
        name="own_output",
    )(output)


def spread_kernel(own, *refs):
    recv, stack, arrivals, pairs, twice = refs[:6], *refs[6:]
    row = lax.axis_index("rows")
    arrivals[0] = jnp.zeros((HALF, 128), BF16)
    for n, x in enumerate(GRAD_SWAPS):
        arrivals[x] = recv[n][...]
    low = low_lanes((HALF, 128))
    low_all = low_lanes((PIXELS, 128))
    for k in (1, 2, 3):
        p = arrivals[arrival_slot(row, row + k)].astype(F32)
        m = arrivals[arrival_slot(row, row - k)].astype(F32)
        pairs[k - 1, :HALF, :] = jnp.where(low, p, pltpu.roll(m, W, 1)).astype(BF16)
        pairs[k - 1, HALF:, :] = jnp.where(low, pltpu.roll(p, W, 1), m).astype(BF16)
        g = own[:, :128].astype(F32) if k == 1 else own[:, 128:].astype(F32)
        other = pltpu.roll(g, W, 1)
        two = jnp.where(low_all, g, other) if k == 2 else jnp.where(low_all, other, g)
        twice[k - 1] = two.astype(BF16)
    stack[:, : 4 * W] = own[...]
    nothing = jnp.zeros((BLOCK, 128), BF16)

    def block_of(ref, k, source):
        if 0 <= source < 4:
            return ref[k - 1, source * BLOCK : (source + 1) * BLOCK, :]
        return nothing

    for q, (k, j) in enumerate(OUT_PAIRS):
        lanes = slice(OUT_AT + q * 128, OUT_AT + q * 128 + 128)
        for m in range(4):
            stack[m * BLOCK : (m + 1) * BLOCK, lanes] = block_of(pairs, k, m - (j - 1) * k)
    low_block = low_lanes((BLOCK, 128))
    for q, (a, b) in enumerate(((1, 2), (3, -1), (-2, -3))):
        lanes = slice(LEFT_AT + q * 128, LEFT_AT + q * 128 + 128)
        for m in range(4):
            stack[m * BLOCK : (m + 1) * BLOCK, lanes] = jnp.where(
                low_block, block_of(twice, abs(a), m + a), block_of(twice, abs(b), m + b)
            )


def spread(own, received):
    return pl.pallas_call(
        spread_kernel,
        out_shape=pltpu.VMEM((PIXELS, 28 * W), BF16),
        in_specs=[pl.BlockSpec(memory_space=pltpu.VMEM)] * 7,
        out_specs=pl.BlockSpec(memory_space=pltpu.VMEM),
        scratch_shapes=[
            pltpu.VMEM((8, HALF, 128), BF16),
            pltpu.VMEM((3, PIXELS, 128), BF16),
            pltpu.VMEM((3, PIXELS, 128), BF16),
        ],
        compiler_params=pltpu.CompilerParams(vmem_limit_bytes=12 * 2**20),
        name="spread",
    )(own, *received)


def grad_kernel(flip, first, stack, weights, out):
    member = lax.axis_index("filt")
    columns = pl.ds(pl.multiple_of((member ^ flip) * 512 + first, 256), out.shape[1])
    out[...] = nn(stack[...], weights[:, columns]).astype(BF16)


def grads_for(flip, stack, weights, first=0, width=512, scale=1):
    return pl.pallas_call(
        functools.partial(grad_kernel, flip, first),
        out_shape=jax.ShapeDtypeStruct((PIXELS, width), BF16),
        in_specs=[pl.BlockSpec(memory_space=pltpu.VMEM)] * 2,
        out_specs=pl.BlockSpec(memory_space=pltpu.VMEM),
        compiler_params=pltpu.CompilerParams(vmem_limit_bytes=18 * 2**20),
        cost_estimate=pl.CostEstimate(
            flops=2 * PIXELS * 28 * W * width * scale, bytes_accessed=10**6, transcendentals=0
        ),
        name="grads_for",
    )(stack, weights)


def last_kernel(a, b, c, d, out, done, sems):
    order = order_matrix(True)
    copies = []
    for g in range(3):
        parts = []
        for m in range(4):
            rows = slice(m * BLOCK + g * 48, m * BLOCK + g * 48 + 48)
            crossed = jnp.concatenate([c[rows, :], d[rows, :]], 1)
            total = a[rows, :].astype(F32) + b[rows, :].astype(F32) + crossed.astype(F32)
            parts.append(total.astype(BF16))
        rows = pl.ds(g * 192, 192)
        done[g * 192 : (g + 1) * 192, :] = nn(order, jnp.concatenate(parts, 0)).astype(BF16)
        copies.append(pltpu.make_async_copy(done.at[rows], out.at[rows], sems.at[g]))
        copies[-1].start()
    for copy in copies:
        copy.wait()


def last_sum(a, b, c, d):
    return pl.pallas_call(
        last_kernel,
        out_shape=jax.ShapeDtypeStruct((PIXELS, 512), BF16),
        in_specs=[pl.BlockSpec(memory_space=pltpu.VMEM)] * 4,
        out_specs=pl.BlockSpec(memory_space=pl.ANY),
        scratch_shapes=[pltpu.VMEM((PIXELS, 512), BF16), pltpu.SemaphoreType.DMA((3,))],
        compiler_params=pltpu.CompilerParams(vmem_limit_bytes=10 * 2**20),
        name="last_sum",
    )(a, b, c, d)


def flipped(x, bit):
    return lax.ppermute(x, "filt", [(i, i ^ bit) for i in range(lax.axis_size("filt"))])


def partner(r, bits):
    return r ^ bits if abs((r ^ bits) - r) <= 3 else r ^ {5: 2, 6: 1, 7: 1}[bits]


def swapped(x, bits):
    return lax.ppermute(x, "rows", [(r, partner(r, bits)) for r in range(8)])


def on_device(
    features, point_weight, dilated_weight, branch_bias, project_weight, project_bias, cotangent
):
    flat = features.reshape(PIXELS, CHANNELS)
    dilated = jnp.transpose(dilated_weight, (0, 1, 2, 4, 3)).reshape(27, W, CHANNELS)
    point = point_weight.T
    flat, dilated, point = (
        pltpu.with_memory_space_constraint(x, pltpu.HBM) for x in (flat, dilated, point)
    )
    *sums, ordered, weights = outward_sums(flat, dilated, point)
    received = {
        x: swapped(sums[n].astype(jnp.float16), x).astype(F32) for n, x in enumerate(SWAPS)
    }
    own = own_sums(ordered, weights, branch_bias)
    acts = [
        activations_of(part, swaps, own[part], [received[x] for x in swaps])
        for part, swaps in enumerate(PART_SWAPS)
    ]
    across = [flipped(x, 2) for x in acts]
    beside = [flipped(x, 1) for x in acts]
    corner = [flipped(x, 1) for x in across]
    near, ordered_cotangent = near_head(
        acts,
        beside,
        project_weight,
        project_bias.reshape(1, 256),
        cotangent.reshape(PIXELS, 256),
    )
    output, grads, *sends = far_head(
        acts, across, corner, project_weight, near, ordered_cotangent
    )
    arrived = [swapped(sends[n], x) for n, x in enumerate(GRAD_SWAPS)]
    stack = spread(grads, arrived)
    far = [flipped(grads_for(3, stack, weights, at, 256), 1) for at in (0, 256)]
    kept = grads_for(2, stack, weights, 0, 256)
    crossing = (far[0].astype(F32) + kept.astype(F32)).astype(BF16)
    crossed = [flipped(crossing, 2)]
    later, crossing = lax.optimization_barrier((stack, crossing))
    kept = grads_for(2, later, weights, 256, 256)
    crossing = (far[1].astype(F32) + kept.astype(F32)).astype(BF16)
    crossed.append(flipped(crossing, 2))
    later, output, crossing = lax.optimization_barrier((stack, output, crossing))
    head_output = own_output(output)
    near = flipped(grads_for(1, later, weights), 1)
    kept = grads_for(0, later, weights, scale=8)
    feature_grad = last_sum(kept, near, *crossed)
    return head_output.reshape(12, 48, W), feature_grad.reshape(12, 48, 512)


def solution(mesh):
    body = on_device if fits(mesh) else on_device_general
    in_specs = (
        P("rows", None, None),
        P(None, "filt"),
        P(None, None, None, None, "filt"),
        P(None, "filt"),
        P(),
        P(),
        P("rows", None, None),
    )
    out_specs = (P("rows", None, "filt"), P("rows", None, "filt"))
    return jax.shard_map(
        body, mesh=mesh, in_specs=in_specs, out_specs=out_specs, check_vma=False
    )
```
